32 devices in a mesh: groups: 2 (over y), tm: 8 (over z, x), chan: 2 (over core).
Axes of the slice: x: 2, y: 2, z: 4, core: 2. Of those that a mesh axis runs over, the one named last changes fastest.
Arguments:
- strain: bfloat16 [32768, 2048], P(('groups', 'tm'), 'chan'), parts along dimension 0
Outputs:
- covariance: float32 [2048, 2048], P(('groups', 'tm'), 'chan'), parts along dimension 0
- segment_auto: float32 [256, 2048], P(('groups', 'tm'), 'chan'), parts along dimension 0
There are 2 independent parts, one for each index of `groups`. The reference program is written for one: setup_inputs(seed, part) draws one part's arguments, and reference() takes and returns one part's arrays. A program takes and returns all parts, laid end to end along the dimension named above; each array names one. Nothing has to cross between parts.
All inputs are finite; a program needn't handle non-finite values.
Results may differ from the reference program's by a relative error of at most 0.0003.
Values may be sent and summed in bfloat16 or wider, within the bound.
No kernel may reach another device: no remote copies, remote signals or barrier semaphores. Data moves between devices by JAX's collectives and lax.ppermute only.
A program may use at most 64 MiB of HBM per device.

```python
import math
import jax
import jax.numpy as jnp
from jax import lax

C = 2048
LAGS = 16
REF = 64
TS = 2048
N_TM = 8


def draw_strain(key, part):
    key = jax.random.fold_in(key, 11)
    key_freq, key_phase, key_shape, key_noise, key_gain = jax.random.split(key, 5)
    rows = TS * N_TM
    angular = jnp.exp(jax.random.uniform(key_freq, (24,), jnp.float32, math.log(0.05), math.log(1.2)))
    phases = jax.random.uniform(key_phase, (24,), jnp.float32, 0.0, 2.0 * math.pi)
    mode_shapes = jax.random.normal(key_shape, (24, C), jnp.float32)
    times_axis = jnp.arange(rows, dtype=jnp.float32)
    modal_wave = jnp.sin(times_axis[:, None] * angular[None, :] + phases[None, :])
    signal = jnp.dot(modal_wave, mode_shapes, precision=lax.Precision.HIGHEST) / math.sqrt(24.0)
    envelope = 1.0 + 0.8 * times_axis / rows
    noise_part = 0.8 * jax.random.normal(key_noise, (rows, C), jnp.float32)
    channel_gain = jnp.exp(jax.random.uniform(key_gain, (C,), jnp.float32, 0.0, math.log(10.0)))
    return ((signal + noise_part) * envelope[:, None] * channel_gain[None, :]).astype(jnp.bfloat16)


def setup_inputs(seed: int = 0, part: int = 0) -> dict:
    keys = jax.random.split(jax.random.key(seed), 2)
    part_splits = jax.random.split(jax.random.fold_in(keys[1], part), 2)
    return {
        "strain": draw_strain(jax.random.fold_in(jax.random.fold_in(keys[1], part), 71), part),
    }


def stack_lags(ref_cols, lags):
    pieces = [jnp.pad(ref_cols, ((offset, lags - 1 - offset), (0, 0))) for offset in range(lags)]
    return jnp.concatenate(pieces, axis=1)

def auto_rows(extended, block_rows, lags, rows):
    block_wide = block_rows.astype(jnp.float32)
    return jnp.stack([lax.optimization_barrier(jnp.sum(extended[offset:offset + rows].astype(jnp.float32) * block_wide, axis=0)) for offset in range(lags)])

def reference(strain):
    slab_rows = strain.shape[0]
    width = strain.shape[1]
    halfref = REF // 2
    wide = strain.astype(jnp.float32)
    mean_sq = lax.optimization_barrier(jnp.sum(wide * wide, axis=0)) / slab_rows
    inv_rms = 1.0 / jnp.sqrt(mean_sq + 1e-06)
    ref_scale = jnp.concatenate([inv_rms[:halfref], inv_rms[width // 2:width // 2 + halfref]])
    blocks = strain.reshape(N_TM, TS, width)
    lead_rows = blocks[:, :LAGS - 1]
    tail_rows = jnp.concatenate([lead_rows[1:], jnp.zeros((1, LAGS - 1, width), strain.dtype)], axis=0)

    def accumulate(running, inputs_pair):
        block_rows, next_rows = inputs_pair
        extended = jnp.concatenate([block_rows, next_rows], axis=0)
        ref_cols = jnp.concatenate([block_rows[:, :halfref], block_rows[:, width // 2:width // 2 + halfref]], axis=1)
        toeplitz = stack_lags(ref_cols, LAGS)
        product = lax.dot_general(toeplitz, extended, (((0,), (0,)), ((), ())), preferred_element_type=jnp.float32)
        return (running + product, auto_rows(extended, block_rows, LAGS, TS))
    summed, auto_lags = lax.scan(accumulate, jnp.zeros((LAGS * REF, width), jnp.float32), (blocks, tail_rows))
    pair_counts = slab_rows - jnp.arange(LAGS, dtype=jnp.float32)
    row_scale = jnp.tile(ref_scale, LAGS) / jnp.repeat(pair_counts, REF)
    covariance = summed * inv_rms[None, :] * row_scale[:, None]
    segment_auto = auto_lags.reshape(N_TM * LAGS, width) * (inv_rms * inv_rms)[None, :] / TS
    return (covariance, segment_auto)
```

```python
import functools

import jax
import jax.numpy as jnp
import numpy as np
from jax import lax
from jax.experimental import pallas as pl
from jax.experimental.pallas import tpu as pltpu
from jax.sharding import PartitionSpec as P

LAGS = 16
REF = 64
HALF = REF // 2
HALO = 128
LANES = 128
VMEM_BYTES = 48 * 1024 * 1024


def passed_along(value, axis, steps):
    count = lax.axis_size(axis)
    initial, last = (max(0, -steps), min(count, count - steps))
    return lax.ppermute(value, axis, [(source, source + steps) for source in range(initial, last)])


def exchanged(value, axis, bit):
    count = lax.axis_size(axis)
    return lax.ppermute(value, axis, [(source, source ^ bit) for source in range(count)])


def summed_over(value, axis):
    bit = 1
    while bit < lax.axis_size(axis):
        value = value + exchanged(value, axis, bit)
        bit *= 2
    return value


def lag_products_kernel(place, order, strain, own, other, halo_own, halo_other, keep, send, shifted):
    chan, near = place[0], place[1]
    slot = pl.program_id(0)
    rows = strain.shape[0]
    chunk = keep.shape[1]

    @pl.when(slot == 0)
    def _():
        for refs, halo, half in ((own, halo_own, chan), (other, halo_other, 1 - chan)):
            long = jnp.concatenate([halo[...], refs[...]], axis=1).astype(jnp.float32)
            for lag in range(LAGS):
                start = pl.multiple_of(lag * REF + half * HALF, HALF)
                piece = long[:, HALO - lag : HALO - lag + rows]
                shifted[pl.ds(start, HALF), :] = piece.astype(jnp.bfloat16)

    start = pl.multiple_of(order[slot] * 2 * chunk, 2 * chunk)
    product = jnp.dot(
        shifted[pl.ds(start, 2 * chunk), :], strain[...], preferred_element_type=jnp.float32
    )
    keep[0] = jnp.where(near == 0, product[:chunk], product[chunk:])
    send[0] = jnp.where(near == 0, product[chunk:], product[:chunk])


def lag_products(place, order, strain, own, other, halo_own, halo_other, chunk):
    slots = order.shape[0]
    rows, width = strain.shape
    whole = lambda array: pl.BlockSpec(array.shape, lambda slot, *_: (0, 0))
    block = pl.BlockSpec((1, chunk, width), lambda slot, *_: (slot, 0, 0))
    shape = jax.ShapeDtypeStruct((slots, chunk, width), jnp.float32)
    return pl.pallas_call(
        lag_products_kernel,
        grid_spec=pltpu.PrefetchScalarGridSpec(
            num_scalar_prefetch=2,
            grid=(slots,),
            in_specs=[whole(array) for array in (strain, own, other, halo_own, halo_other)],
            out_specs=[block, block],
            scratch_shapes=[pltpu.VMEM((LAGS * REF, rows), jnp.bfloat16)],
        ),
        out_shape=[shape, shape],
        compiler_params=pltpu.CompilerParams(vmem_limit_bytes=VMEM_BYTES),
        cost_estimate=pl.CostEstimate(
            flops=2 * slots * 2 * chunk * rows * width,
            bytes_accessed=rows * width * 2 + slots * 2 * chunk * width * 4,
            transcendentals=0,
        ),
        name="lag_products",
    )(place, order, strain, own, other, halo_own, halo_other)


def segment_kernel(strain, tail, out, wide):
    rows, lanes = strain.shape
    pitch = rows // 8
    for lane in range(0, lanes, LANES):
        wide[:rows, :] = strain[:, lane : lane + LANES].astype(jnp.float32)
        wide[rows:, :] = tail[:, lane : lane + LANES].astype(jnp.float32)
        taken = lambda first: wide[pl.ds(first, 8, stride=pitch), :]

        def step(index, carry):
            window, sums = carry
            window = window + (taken(index + LAGS - 1),)
            sums = tuple(total + window[0] * window[lag] for lag, total in enumerate(sums))
            return window[1:], sums

        window = tuple(taken(first) for first in range(LAGS - 1))
        zero = jnp.zeros((8, LANES), jnp.float32)
        _, sums = lax.fori_loop(0, pitch, step, (window, (zero,) * LAGS), unroll=16)
        out[:, lane : lane + LANES] = jnp.concatenate(
            [jnp.sum(total, axis=0, keepdims=True) for total in sums], axis=0
        )


def segment_rows(strain, tail, block):
    rows, width = strain.shape
    return pl.pallas_call(
        segment_kernel,
        grid=(width // block,),
        in_specs=[
            pl.BlockSpec((rows, block), lambda index: (0, index)),
            pl.BlockSpec((LAGS, block), lambda index: (0, index)),
        ],
        out_specs=pl.BlockSpec((LAGS, block), lambda index: (0, index)),
        out_shape=jax.ShapeDtypeStruct((LAGS, width), jnp.float32),
        scratch_shapes=[pltpu.VMEM((rows + LAGS, LANES), jnp.float32)],
        compiler_params=pltpu.CompilerParams(vmem_limit_bytes=VMEM_BYTES),
        cost_estimate=pl.CostEstimate(
            flops=2 * LAGS * rows * width, bytes_accessed=rows * width * 2, transcendentals=0
        ),
        name="segment_rows",
    )(strain, tail)


def chosen(array, index):
    return lax.dynamic_index_in_dim(array, index, 0, keepdims=False)


def scattered_sums(keep, send, order):
    count = keep.shape[0]
    far = lax.axis_index("tm") // 2
    table = np.argsort(order, axis=1)
    arrived = []
    right = left = None
    for step in range(count):
        arrived.append(keep[step] + exchanged(send[step], "tm", 1))
        if step == count - 1:
            return arrived[step] + right + left
        stacked = jnp.stack(arrived)
        ahead = np.clip(count - 1 + np.arange(count) - step, 0, count - 1)
        back = np.clip(step + np.arange(count) - count + 1, 0, count - 1)
        slot_ahead = jnp.asarray(np.minimum(table[np.arange(count), ahead], step), jnp.int32)[far]
        slot_back = jnp.asarray(np.minimum(table[np.arange(count), back], step), jnp.int32)[far]
        to_right = chosen(stacked, slot_ahead)
        to_left = chosen(stacked, slot_back)
        if step:
            to_right = to_right + right
            to_left = to_left + left
        right = lax.ppermute(
            to_right, "tm", [(2 * z + x, 2 * z + 2 + x) for z in range(min(step + 1, count - 1)) for x in range(2)]
        )
        left = lax.ppermute(
            to_left, "tm", [(2 * z + x, 2 * z - 2 + x) for z in range(max(count - 1 - step, 1), count) for x in range(2)]
        )


def send_order(count):
    places = np.arange(count)
    return np.stack([np.argsort(-np.abs(places - place), kind="stable") for place in places]).astype(np.int32)


def local(strain):
    rows, width = strain.shape
    count = lax.axis_size("tm")
    chan = lax.axis_index("chan")
    time = lax.axis_index("tm")
    slab_rows = rows * count
    rows_dev = LAGS * REF // count
    pairs = count // 2

    own = strain[:, :HALF].T
    edge = own[:, rows - HALO :]
    other = exchanged(own, "chan", 1)
    halo_own = passed_along(edge, "tm", 1)
    halo_other = exchanged(halo_own, "chan", 1)
    tail = passed_along(strain[:LAGS], "tm", -1)

    place = jnp.stack([chan, time % 2]).astype(jnp.int32)
    products = functools.partial(
        lag_products,
        place,
        strain=strain,
        own=own,
        other=other,
        halo_own=halo_own,
        halo_other=halo_other,
        chunk=rows_dev,
    )

    wide = strain.astype(jnp.float32)
    power = jnp.sum(wide * wide, axis=0)
    power_other = jnp.sum(jnp.square(other.astype(jnp.float32)), axis=1)
    power = summed_over(jnp.concatenate([power, power_other]), "tm")
    inv = 1.0 / jnp.sqrt(power / slab_rows + 1e-06)
    own_scale = inv[:width]
    ref_scale = jnp.where(
        chan == 0,
        jnp.concatenate([inv[:HALF], inv[width:]]),
        jnp.concatenate([inv[width:], inv[:HALF]]),
    )

    if pairs <= 4:
        order = send_order(pairs)
        mine = jnp.asarray(order)[time // 2]
        first = products(order=mine[:1])
        rest = products(order=mine[1:])
        keep = [first[0][0]] + [rest[0][slot] for slot in range(pairs - 1)]
        send = [first[1][0]] + [rest[1][slot] for slot in range(pairs - 1)]
        summed = scattered_sums(jnp.stack(keep), send, order)
    else:
        keep, send = products(order=jnp.arange(pairs, dtype=jnp.int32))
        near = (time % 2)[None, None, None]
        blocks = jnp.stack([jnp.where(near == 0, keep, send), jnp.where(near == 0, send, keep)], axis=1)
        summed = lax.psum_scatter(
            blocks.reshape(LAGS * REF, width), "tm", scatter_dimension=0, tiled=True
        )

    row = time * rows_dev + jnp.arange(rows_dev, dtype=jnp.int32)
    denom = (slab_rows - row // REF).astype(jnp.float32)
    row_scale = ref_scale[row % REF] / denom
    covariance = summed * own_scale[None, :] * row_scale[:, None]

    auto = segment_rows(strain, tail, 256)
    segment_auto = auto * (own_scale * own_scale)[None, :] / rows
    return (covariance, segment_auto)


def solution(mesh):
    in_specs = (P(("groups", "tm"), "chan"),)
    out_specs = (P(("groups", "tm"), "chan"), P(("groups", "tm"), "chan"))
    return jax.shard_map(local, mesh=mesh, in_specs=in_specs, out_specs=out_specs, check_vma=False)
```

```python
import jax
import jax.numpy as jnp
from jax import lax
from jax.experimental import pallas as pl
from jax.experimental.pallas import tpu as pltpu
from jax.sharding import PartitionSpec as P

LAGS = 16
REF = 64
HALF = REF // 2
HALO = 128
LANES = 128
GROUP = 4
POWER = 16
CODE_SCALE = 2.0 ** (126 / POWER)
TINY = 1e-35
VMEM_BYTES = 48 * 1024 * 1024


def passed_along(value, axis, steps):
    count = lax.axis_size(axis)
    initial, last = (max(0, -steps), min(count, count - steps))
    return lax.ppermute(value, axis, [(source, source + steps) for source in range(initial, last)])


def exchanged(value, axis, bit):
    count = lax.axis_size(axis)
    return lax.ppermute(value, axis, [(source, source ^ bit) for source in range(count)])


def passed_across(value):
    count = lax.axis_size("tm")
    route = [(2 * t + c, 2 * t + 2 + (1 - c)) for t in range(count - 1) for c in range(2)]
    return lax.ppermute(value, ("tm", "chan"), route)


def as_column(row):
    size = row.shape[1]
    eye = lax.broadcasted_iota(jnp.int32, (size, size), 0) == lax.broadcasted_iota(jnp.int32, (size, size), 1)
    return jnp.sum(jnp.where(eye, row, 0.0), axis=1, keepdims=True)


def as_row(column):
    size = column.shape[0]
    eye = lax.broadcasted_iota(jnp.int32, (size, size), 0) == lax.broadcasted_iota(jnp.int32, (size, size), 1)
    return jnp.sum(jnp.where(eye, column, 0.0), axis=0, keepdims=True)


def for_chunk(ref_column, rows):
    return jnp.concatenate([ref_column] * (rows // REF), axis=0)


def bounds(powers):
    return (
        jnp.maximum(powers[0:1, :], TINY),
        jnp.maximum(as_column(powers[2:3, :LANES])[:REF], TINY),
    )


def coded(values, channel_bound, ref_bound):
    ref_column = for_chunk(lax.rsqrt(ref_bound) * CODE_SCALE, values.shape[0])
    power = values * lax.rsqrt(channel_bound) * ref_column
    for _ in range(4):
        power = power * jnp.abs(power)
    return power.astype(jnp.bfloat16)


def expanded(code, channel_bound, ref_bound):
    wide = code.astype(jnp.float32)
    root = jnp.exp2(jnp.log2(jnp.abs(wide)) * (1.0 / POWER))
    ref_column = for_chunk(jnp.sqrt(ref_bound) * (1.0 / CODE_SCALE), code.shape[0])
    return jnp.where(wide < 0.0, -root, root) * jnp.sqrt(channel_bound) * ref_column


def lag_rows(own, other, halo_own, halo_other, chan, first_lag, shifted):
    rows = own.shape[1]
    for refs, halo, half in ((own, halo_own, chan), (other, halo_other, 1 - chan)):
        long = jnp.concatenate([halo[...], refs[...]], axis=1).astype(jnp.float32)
        for index in range(GROUP):
            moved = pltpu.roll(long, first_lag + index, 1)[:, HALO:]
            start = pl.multiple_of(index * REF + half * HALF, HALF)
            shifted[pl.ds(start, HALF), :] = moved.astype(jnp.bfloat16)


def ref_powers(refs, halo):
    squares = jnp.square(refs[...].astype(jnp.float32))
    lane = lax.broadcasted_iota(jnp.int32, (1, HALO), 1)
    edge = jnp.where(lane > HALO - LAGS, jnp.square(halo[...].astype(jnp.float32)), 0.0)
    inside = jnp.sum(squares, axis=1, keepdims=True)
    return inside, inside + jnp.sum(edge, axis=1, keepdims=True)


def first_products_kernel(place, power, strain, own, other, halo_own, halo_other, keep, send, powers, shifted):
    chan, group, near = place[0], place[1], place[2]
    lag_rows(own, other, halo_own, halo_other, chan, group * GROUP, shifted)
    ours = ref_powers(own, halo_own)
    theirs = ref_powers(other, halo_other)
    columns = [
        jnp.where(chan == 0, jnp.concatenate([a, b], axis=0), jnp.concatenate([b, a], axis=0))
        for a, b in zip(ours, theirs)
    ]
    pad = jnp.zeros((1, power.shape[1] - REF), jnp.float32)
    rows = [jnp.concatenate([as_row(column), pad], axis=1) for column in columns]
    powers[...] = jnp.concatenate(
        [power[...]] + rows + [jnp.zeros((5, power.shape[1]), jnp.float32)], axis=0
    )
    product = jnp.dot(shifted[...], strain[...], preferred_element_type=jnp.float32)
    chunk = keep.shape[0]
    keep[...] = jnp.where(near == 0, product[:chunk], product[chunk:])
    other_half = jnp.where(near == 0, product[chunk:], product[:chunk])
    send[...] = coded(other_half, jnp.maximum(power[...], TINY), jnp.maximum(columns[1], TINY))


def first_products(place, power, strain, own, other, halo_own, halo_other, chunk):
    rows, width = strain.shape
    return pl.pallas_call(
        first_products_kernel,
        in_specs=[pl.BlockSpec(memory_space=pltpu.SMEM)] + [pl.BlockSpec(memory_space=pltpu.VMEM)] * 6,
        out_specs=[pl.BlockSpec(memory_space=pltpu.VMEM)] * 3,
        out_shape=[
            jax.ShapeDtypeStruct((chunk, width), jnp.float32),
            jax.ShapeDtypeStruct((chunk, width), jnp.bfloat16),
            jax.ShapeDtypeStruct((8, width), jnp.float32),
        ],
        scratch_shapes=[pltpu.VMEM((GROUP * REF, rows), jnp.bfloat16)],
        compiler_params=pltpu.CompilerParams(vmem_limit_bytes=VMEM_BYTES),
        cost_estimate=pl.CostEstimate(
            flops=2 * 2 * chunk * rows * width, bytes_accessed=rows * width * 2, transcendentals=0
        ),
        name="first_products",
    )(place, power, strain, own, other, halo_own, halo_other)


def later_products_kernel(place, powers, strain, own, other, halo_own, halo_other, *rest):
    chan, near = place[0], place[2]
    shifted = rest[-1]
    channel_bound, ref_bound = bounds(powers)
    for slot in range((len(rest) - 1) // 2):
        keep, send = rest[2 * slot], rest[2 * slot + 1]
        chunk = keep.shape[0]
        lag_rows(own, other, halo_own, halo_other, chan, place[3 + slot] * GROUP, shifted)
        product = jnp.dot(shifted[...], strain[...], preferred_element_type=jnp.float32)
        keep[...] = jnp.where(near == 0, product[:chunk], product[chunk:])
        other_half = jnp.where(near == 0, product[chunk:], product[:chunk])
        send[...] = coded(other_half, channel_bound, ref_bound)


def later_products(place, powers, strain, own, other, halo_own, halo_other, chunk, slots):
    rows, width = strain.shape
    return pl.pallas_call(
        later_products_kernel,
        in_specs=[pl.BlockSpec(memory_space=pltpu.SMEM)] + [pl.BlockSpec(memory_space=pltpu.VMEM)] * 6,
        out_specs=[pl.BlockSpec(memory_space=pltpu.VMEM)] * (2 * slots),
        out_shape=[
            jax.ShapeDtypeStruct((chunk, width), jnp.float32),
            jax.ShapeDtypeStruct((chunk, width), jnp.bfloat16),
        ]
        * slots,
        scratch_shapes=[pltpu.VMEM((GROUP * REF, rows), jnp.bfloat16)],
        compiler_params=pltpu.CompilerParams(vmem_limit_bytes=VMEM_BYTES),
        cost_estimate=pl.CostEstimate(
            flops=2 * 2 * chunk * slots * rows * width, bytes_accessed=rows * width * 2, transcendentals=0
        ),
        name="later_products",
    )(place, powers, strain, own, other, halo_own, halo_other)


def merge_kernel(powers, keep, *rest):
    total = keep[...]
    out = rest[-1]
    for code, sender in zip(rest[:-1:2], rest[1:-1:2]):
        total = total + expanded(code[...], *bounds(sender))
    out[...] = coded(total, *bounds(powers))


def merged(powers, keep, *received):
    return pl.pallas_call(
        merge_kernel,
        out_shape=jax.ShapeDtypeStruct(keep.shape, jnp.bfloat16),
        compiler_params=pltpu.CompilerParams(vmem_limit_bytes=VMEM_BYTES),
        cost_estimate=pl.CostEstimate(flops=0, bytes_accessed=keep.size * 8, transcendentals=0),
        name="merged",
    )(powers, keep, *received)


def finish_kernel(segment, slab_rows, place, powers, auto, keep, *rest):
    covariance, segment_auto = rest[-2:]
    total = keep[...]
    for code, sender in zip(rest[:-2:2], rest[1:-2:2]):
        total = total + expanded(code[...], *bounds(sender))
    chunk = total.shape[0]
    inverse = 1.0 / jnp.sqrt(powers[0:2, :] / slab_rows + 1e-06)
    scale = inverse[0:1]
    ref_scale = for_chunk(as_column(inverse[1:2, :LANES])[:REF], chunk)
    lag = lax.broadcasted_iota(jnp.int32, (chunk, 1), 0) // REF + place[4] * (chunk // REF)
    denom = (slab_rows - lag).astype(jnp.float32)
    covariance[...] = total * scale * (ref_scale / denom)
    segment_auto[...] = auto[...] * (scale * scale) / segment


def finished(segment, slab_rows, place, powers, auto, keep, *received):
    def kernel(*refs):
        finish_kernel(segment, slab_rows, *refs)

    vmem = pl.BlockSpec(memory_space=pltpu.VMEM)
    return pl.pallas_call(
        kernel,
        in_specs=[pl.BlockSpec(memory_space=pltpu.SMEM)] + [vmem] * (3 + len(received)),
        out_specs=[vmem, vmem],
        out_shape=[
            jax.ShapeDtypeStruct(keep.shape, jnp.float32),
            jax.ShapeDtypeStruct(auto.shape, jnp.float32),
        ],
        compiler_params=pltpu.CompilerParams(vmem_limit_bytes=VMEM_BYTES),
        cost_estimate=pl.CostEstimate(flops=0, bytes_accessed=keep.size * 8, transcendentals=0),
        name="finished",
    )(place, powers, auto, keep, *received)


def segment_kernel(strain, tail, out, wide):
    rows, lanes = strain.shape
    pitch = rows // 8
    for lane in range(0, lanes, LANES):
        wide[:rows, :] = strain[:, lane : lane + LANES].astype(jnp.float32)
        wide[rows:, :] = tail[:, lane : lane + LANES].astype(jnp.float32)
        taken = lambda first: wide[pl.ds(first, 8, stride=pitch), :]

        def step(index, carry):
            window, sums = carry
            window = window + (taken(index + LAGS - 1),)
            sums = tuple(total + window[0] * window[lag] for lag, total in enumerate(sums))
            return window[1:], sums

        window = tuple(taken(first) for first in range(LAGS - 1))
        zero = jnp.zeros((8, LANES), jnp.float32)
        _, sums = lax.fori_loop(0, pitch, step, (window, (zero,) * LAGS), unroll=16)
        out[:, lane : lane + LANES] = jnp.concatenate(
            [jnp.sum(total, axis=0, keepdims=True) for total in sums], axis=0
        )


def segment_rows(strain, tail, first, size):
    rows = strain.shape[0]
    return pl.pallas_call(
        segment_kernel,
        grid=(1,),
        in_specs=[
            pl.BlockSpec((rows, size), lambda index: (0, first)),
            pl.BlockSpec((LAGS, size), lambda index: (0, first)),
        ],
        out_specs=pl.BlockSpec((LAGS, size), lambda index: (0, 0)),
        out_shape=jax.ShapeDtypeStruct((LAGS, size), jnp.float32),
        scratch_shapes=[pltpu.VMEM((rows + LAGS, LANES), jnp.float32)],
        compiler_params=pltpu.CompilerParams(vmem_limit_bytes=VMEM_BYTES),
        cost_estimate=pl.CostEstimate(
            flops=64 * LAGS * rows * size, bytes_accessed=rows * size * 2, transcendentals=0
        ),
        name="segment_rows",
    )(strain, tail)


def all_products_kernel(place, strain, own, other, halo_own, halo_other, out, shifted):
    group = pl.program_id(0)
    lag_rows(own, other, halo_own, halo_other, place[0], group * GROUP, shifted)
    out[...] = jnp.dot(shifted[...], strain[...], preferred_element_type=jnp.float32)


def all_products(place, strain, *refs):
    rows, width = strain.shape
    whole = lambda array: pl.BlockSpec(array.shape, lambda group: (0, 0))
    return pl.pallas_call(
        all_products_kernel,
        grid=(LAGS // GROUP,),
        in_specs=[pl.BlockSpec(memory_space=pltpu.SMEM)] + [whole(array) for array in (strain, *refs)],
        out_specs=pl.BlockSpec((GROUP * REF, width), lambda group: (group, 0)),
        out_shape=jax.ShapeDtypeStruct((LAGS * REF, width), jnp.float32),
        scratch_shapes=[pltpu.VMEM((GROUP * REF, rows), jnp.bfloat16)],
        compiler_params=pltpu.CompilerParams(vmem_limit_bytes=VMEM_BYTES),
        name="all_products",
    )(place, strain, *refs)


def local(strain):
    rows, width = strain.shape
    count = lax.axis_size("tm")
    chan = lax.axis_index("chan").astype(jnp.int32)
    time = lax.axis_index("tm").astype(jnp.int32)
    slab_rows = rows * count
    chunk = LAGS * REF // count
    pair = lax.shift_right_logical(time, 1)

    own = strain[:, :HALF].T
    edge = own[:, rows - HALO :]
    other = exchanged(own, "chan", 1)
    halo_own = passed_along(edge, "tm", 1)
    halo_other = passed_across(edge)
    refs = (own, other, halo_own, halo_other)
    tail = passed_along(strain[:LAGS], "tm", -1)

    wide = strain.astype(jnp.float32)
    power = jnp.sum(wide * wide, axis=0, keepdims=True)

    size = 256
    pieces = [segment_rows(strain, tail, first, size) for first in range(width // size)]
    auto = jnp.concatenate(pieces, axis=1)

    if chunk * 2 == GROUP * REF:
        place = jnp.stack([chan, pair ^ 3, time & 1, pair ^ 2, pair ^ 1, pair])
        keep6, send7, powers0 = first_products(place, power, strain, *refs, chunk)
        got7 = exchanged(send7, "tm", 1)
        near0 = exchanged(powers0, "tm", 1)
        powers1 = powers0 + near0
        near1 = exchanged(powers1, "tm", 2)
        powers2 = powers1 + near1
        near2 = exchanged(powers2, "tm", 4)
        powers3 = powers2 + near2
        keep4, send5, keep2, send3, keep0, send1 = later_products(place, powers0, strain, *refs, chunk, 3)
        got5 = exchanged(send5, "tm", 1)
        got3 = exchanged(send3, "tm", 1)
        got1 = exchanged(send1, "tm", 1)
        got6 = exchanged(merged(powers1, keep6, got7, near0), "tm", 2)
        got4 = exchanged(merged(powers2, keep4, got5, near0, got6, near1), "tm", 4)
        got2 = exchanged(merged(powers1, keep2, got3, near0), "tm", 2)
        place = jnp.stack([chan, chan, chan, chan, time])
        covariance, segment_auto = finished(
            rows, slab_rows, place, powers3, auto, keep0, got1, near0, got2, near1, got4, near2
        )
        return (covariance, segment_auto)

    place = jnp.stack([chan, time])
    power_other = jnp.sum(jnp.square(other.astype(jnp.float32)), axis=1)
    power = lax.psum(jnp.concatenate([power[0], power_other]), "tm")
    inv = 1.0 / jnp.sqrt(power / slab_rows + 1e-06)
    scale = inv[:width]
    ref_scale = jnp.where(
        chan == 0,
        jnp.concatenate([inv[:HALF], inv[width:]]),
        jnp.concatenate([inv[width:], inv[:HALF]]),
    )
    products = all_products(place, strain, *refs)
    summed = lax.psum_scatter(products, "tm", scatter_dimension=0, tiled=True)
    row = time * chunk + jnp.arange(chunk, dtype=jnp.int32)
    row_scale = ref_scale[row % REF] / (slab_rows - row // REF).astype(jnp.float32)
    covariance = summed * scale[None, :] * row_scale[:, None]
    segment_auto = auto * (scale * scale)[None, :] / rows
    return (covariance, segment_auto)


def solution(mesh):
    in_specs = (P(("groups", "tm"), "chan"),)
    out_specs = (P(("groups", "tm"), "chan"), P(("groups", "tm"), "chan"))
    return jax.shard_map(local, mesh=mesh, in_specs=in_specs, out_specs=out_specs, check_vma=False)
```

```python
import jax
import jax.numpy as jnp
from jax import lax
from jax.experimental import pallas as pl
from jax.experimental.pallas import tpu as pltpu
from jax.sharding import PartitionSpec as P

LAGS = 16
REF = 64
HALF = REF // 2
LANES = 128
EXTRA = 8
FETCHES = 8
GROUP = 4
POWER = 16
CODE_SCALE = 2.0 ** (126 / POWER)
TINY = 1e-35
VMEM_BYTES = 48 * 1024 * 1024


def passed_along(value, axis, steps):
    count = lax.axis_size(axis)
    initial, last = (max(0, -steps), min(count, count - steps))
    return lax.ppermute(value, axis, [(source, source + steps) for source in range(initial, last)])


def exchanged(value, axis, bit):
    count = lax.axis_size(axis)
    return lax.ppermute(value, axis, [(source, source ^ bit) for source in range(count)])


def as_column(row):
    size = row.shape[1]
    eye = lax.broadcasted_iota(jnp.int32, (size, size), 0) == lax.broadcasted_iota(jnp.int32, (size, size), 1)
    return jnp.sum(jnp.where(eye, row, 0.0), axis=1, keepdims=True)


def as_row(column):
    size = column.shape[0]
    eye = lax.broadcasted_iota(jnp.int32, (size, size), 0) == lax.broadcasted_iota(jnp.int32, (size, size), 1)
    return jnp.sum(jnp.where(eye, column, 0.0), axis=0, keepdims=True)


def for_chunk(ref_column, rows):
    return jnp.concatenate([ref_column] * (rows // REF), axis=0)


def bf16_pieces(value):
    high = value.astype(jnp.bfloat16).astype(jnp.float32)
    middle = (value - high).astype(jnp.bfloat16).astype(jnp.float32)
    return high, middle, value - high - middle


def packed(powers, ref_powers, channel_bound):
    rows = list(bf16_pieces(powers))
    refs = jnp.concatenate(bf16_pieces(ref_powers), axis=1)
    pad = jnp.zeros((1, powers.shape[1] - refs.shape[1]), jnp.float32)
    rows += [jnp.concatenate([refs, pad], axis=1), channel_bound]
    rows += [jnp.zeros_like(powers)] * (EXTRA - len(rows))
    return jnp.concatenate(rows, axis=0).astype(jnp.bfloat16)


def unpacked(block):
    wide = block.astype(jnp.float32)
    powers = wide[0:1] + wide[1:2] + wide[2:3]
    refs = wide[3:4, :LANES] + wide[3:4, LANES : 2 * LANES] + wide[3:4, 2 * LANES : 3 * LANES]
    return powers, refs, wide[4:5]


def rounded_up(value):
    return (value * (1.0 + 2.0**-7)).astype(jnp.bfloat16).astype(jnp.float32)


def coded(values, channel_bound, ref_bound):
    channel = lax.rsqrt(jnp.maximum(channel_bound, TINY))
    refs = lax.rsqrt(jnp.maximum(ref_bound, TINY)) * CODE_SCALE
    power = values * channel * for_chunk(refs, values.shape[0])
    for _ in range(4):
        power = power * jnp.abs(power)
    return power.astype(jnp.bfloat16)


def expanded(code, channel_bound, ref_bound):
    channel = jnp.sqrt(jnp.maximum(channel_bound, TINY))
    refs = jnp.sqrt(jnp.maximum(ref_bound, TINY)) * (1.0 / CODE_SCALE)
    wide = code.astype(jnp.float32)
    root = jnp.exp2(jnp.log2(jnp.abs(wide)) * (1.0 / POWER))
    return jnp.where(wide < 0.0, -root, root) * channel * for_chunk(refs, code.shape[0])


def ref_column(ref_powers):
    return as_column(ref_powers)[:REF]


def prepare_kernel(left, top, own, head):
    own[...] = left[...].astype(jnp.float32).T[:HALF].astype(jnp.bfloat16)
    head[...] = top[...]


def prepared(strain):
    rows, width = strain.shape
    return pl.pallas_call(
        prepare_kernel,
        grid=(1,),
        in_specs=[
            pl.BlockSpec((rows, LANES), lambda index: (0, 0)),
            pl.BlockSpec((LAGS, width), lambda index: (0, 0)),
        ],
        out_specs=[
            pl.BlockSpec((HALF, rows), lambda index: (0, 0)),
            pl.BlockSpec((LAGS, width), lambda index: (0, 0)),
        ],
        out_shape=[
            jax.ShapeDtypeStruct((HALF, rows), strain.dtype),
            jax.ShapeDtypeStruct((LAGS, width), strain.dtype),
        ],
        name="prepared",
    )(strain, strain)


def lag_rows(own, other, chan, first_lag, shifted):
    rows = own.shape[1]
    zeros = jnp.zeros((HALF, LANES), jnp.float32)
    for refs, half in ((own, chan), (other, 1 - chan)):
        long = jnp.concatenate([refs[...].astype(jnp.float32), zeros], axis=1)
        for index in range(GROUP):
            moved = pltpu.roll(long, first_lag + index, 1)
            start = pl.multiple_of(index * REF + half * HALF, HALF)
            shifted[pl.ds(start, HALF), :] = moved.astype(jnp.bfloat16)


def fetches(strain, held, sems):
    step = held.shape[0] // FETCHES
    return [
        pltpu.make_async_copy(
            strain.at[pl.ds(index * step, step)], held.at[pl.ds(index * step, step)], sems.at[index]
        )
        for index in range(FETCHES)
    ]


def product_of(shifted, held, tail, copies):
    rows = held.shape[0]
    total = jnp.dot(
        shifted[:, rows:], tail[...], preferred_element_type=jnp.float32
    )
    step = rows // FETCHES
    for index in range(FETCHES):
        if copies:
            copies[index].wait()
        here = slice(index * step, (index + 1) * step)
        total += jnp.dot(shifted[:, here], held[here, :], preferred_element_type=jnp.float32)
    return total


def padded(tail):
    wide = tail[...]
    return jnp.concatenate([wide, jnp.zeros((LANES - LAGS, wide.shape[1]), wide.dtype)], axis=0)


def first_products_kernel(place, strain, own, other, tail, keep, send, powers, held, shifted, edge, sems):
    chan, group, near = place[0], place[1], place[2]
    copies = fetches(strain, held, sems)
    for copy in copies:
        copy.start()
    edge[...] = padded(tail)
    lag_rows(own, other, chan, group * GROUP, shifted)
    ours, theirs = [
        jnp.sum(jnp.square(refs[...].astype(jnp.float32)), axis=1, keepdims=True) for refs in (own, other)
    ]
    refs = jnp.where(
        chan == 0, jnp.concatenate([ours, theirs], axis=0), jnp.concatenate([theirs, ours], axis=0)
    )
    product = product_of(shifted, held, edge, copies)
    channel = jnp.sum(jnp.square(held[...].astype(jnp.float32)), axis=0, keepdims=True)
    beyond = jnp.sum(jnp.square(tail[...].astype(jnp.float32)), axis=0, keepdims=True)
    bound = rounded_up(channel + beyond)
    pad = jnp.zeros((1, LANES - REF), jnp.float32)
    extra = packed(channel, jnp.concatenate([as_row(refs), pad], axis=1), bound)
    powers[...] = extra
    chunk = keep.shape[0]
    keep[...] = jnp.where(near == 0, product[:chunk], product[chunk:])
    other_half = jnp.where(near == 0, product[chunk:], product[:chunk])
    send[:chunk] = coded(other_half, bound, refs)
    send[chunk:] = extra


def product_scratch(rows, width, *slots):
    return [
        pltpu.VMEM((rows, width), jnp.bfloat16),
        pltpu.VMEM((*slots, GROUP * REF, rows + LANES), jnp.bfloat16),
        pltpu.VMEM((LANES, width), jnp.bfloat16),
        pltpu.SemaphoreType.DMA((FETCHES,)),
    ]


def product_specs(count):
    return [
        pl.BlockSpec(memory_space=pltpu.SMEM),
        pl.BlockSpec(memory_space=pl.ANY),
    ] + [pl.BlockSpec(memory_space=pltpu.VMEM)] * count


def first_products(place, strain, own, other, tail, chunk):
    rows, width = strain.shape
    return pl.pallas_call(
        first_products_kernel,
        in_specs=product_specs(3),
        out_specs=[pl.BlockSpec(memory_space=pltpu.VMEM)] * 3,
        out_shape=[
            jax.ShapeDtypeStruct((chunk, width), jnp.float32),
            jax.ShapeDtypeStruct((chunk + EXTRA, width), jnp.bfloat16),
            jax.ShapeDtypeStruct((EXTRA, width), jnp.bfloat16),
        ],
        scratch_shapes=product_scratch(rows, width),
        compiler_params=pltpu.CompilerParams(vmem_limit_bytes=VMEM_BYTES),
        cost_estimate=pl.CostEstimate(
            flops=2 * 4 * chunk * rows * width, bytes_accessed=rows * width * 2, transcendentals=0
        ),
        name="first_products",
    )(place, strain, own, other, tail)


def later_products_kernel(place, strain, own, other, tail, powers, *rest):
    chan, near = place[0], place[2]
    held, shifted, edge, sems = rest[-4:]
    copies = fetches(strain, held, sems)
    for copy in copies:
        copy.start()
    edge[...] = padded(tail)
    _, ref_powers, bound = unpacked(powers[...])
    refs = ref_column(ref_powers)
    for slot in range((len(rest) - 4) // 2):
        keep, send = rest[2 * slot], rest[2 * slot + 1]
        chunk = keep.shape[0]
        lag_rows(own, other, chan, place[3 + slot] * GROUP, shifted.at[slot])
        product = product_of(shifted.at[slot], held, edge, copies if slot == 0 else None)
        keep[...] = jnp.where(near == 0, product[:chunk], product[chunk:])
        other_half = jnp.where(near == 0, product[chunk:], product[:chunk])
        send[...] = coded(other_half, bound, refs)


def later_products(place, strain, own, other, tail, powers, chunk, slots):
    rows, width = strain.shape
    return pl.pallas_call(
        later_products_kernel,
        in_specs=product_specs(4),
        out_specs=[pl.BlockSpec(memory_space=pltpu.VMEM)] * (2 * slots),
        out_shape=[
            jax.ShapeDtypeStruct((chunk, width), jnp.float32),
            jax.ShapeDtypeStruct((chunk, width), jnp.bfloat16),
        ]
        * slots,
        scratch_shapes=product_scratch(rows, width, slots),
        compiler_params=pltpu.CompilerParams(vmem_limit_bytes=VMEM_BYTES),
        cost_estimate=pl.CostEstimate(
            flops=2 * 4 * chunk * slots * rows * width, bytes_accessed=rows * width * 2, transcendentals=0
        ),
        name="later_products",
    )(place, strain, own, other, tail, powers)


def call_on_blocks(kernel, outs, *arrays, name):
    vmem = pl.BlockSpec(memory_space=pltpu.VMEM)
    smem = pl.BlockSpec(memory_space=pltpu.SMEM)
    return pl.pallas_call(
        kernel,
        in_specs=[smem if array.dtype == jnp.int32 else vmem for array in arrays],
        out_specs=[vmem] * len(outs),
        out_shape=[jax.ShapeDtypeStruct(shape, dtype) for shape, dtype in outs],
        compiler_params=pltpu.CompilerParams(vmem_limit_bytes=VMEM_BYTES),
        cost_estimate=pl.CostEstimate(flops=0, bytes_accessed=2**21, transcendentals=0),
        name=name,
    )(*arrays)


def received(code, powers):
    chunk = code.shape[0] // REF * REF
    _, refs, bound = unpacked(powers[...])
    return expanded(code[:chunk], bound, ref_column(refs))


def joined(powers, arrived):
    ours, ours_refs, ours_bound = unpacked(powers)
    theirs, theirs_refs, theirs_bound = unpacked(arrived)
    bound = rounded_up(ours_bound + theirs_bound)
    return ours + theirs, ours_refs + theirs_refs, bound


def merge_kernel(*refs):
    keep, powers, arrived, out, extra = refs[0], refs[1], refs[2], refs[-2], refs[-1]
    chunk = keep.shape[0]
    total = keep[...] + received(arrived, arrived[chunk:])
    for code, sender in zip(refs[3:-2:2], refs[4:-2:2]):
        total = total + received(code, sender)
    sums, sum_refs, bound = joined(powers[...], arrived[chunk:])
    extra[...] = packed(sums, sum_refs, bound)
    out[:chunk] = coded(total, bound, ref_column(sum_refs))
    out[chunk:] = extra[...]


def merged(keep, powers, arrived, *others):
    chunk, width = keep.shape
    outs = [((chunk + EXTRA, width), jnp.bfloat16), ((EXTRA, width), jnp.bfloat16)]
    return call_on_blocks(merge_kernel, outs, keep, powers, arrived, *others, name="merged")


def resend_kernel(keep, code, sender, powers, out):
    _, refs, bound = unpacked(powers[...])
    out[...] = coded(keep[...] + received(code, sender), bound, ref_column(refs))


def resent(keep, code, sender, powers):
    outs = [(keep.shape, jnp.bfloat16)]
    return call_on_blocks(resend_kernel, outs, keep, code, sender, powers, name="resent")[0]


def add_kernel(keep, code, sender, other, other_sender, out):
    out[...] = keep[...] + received(code, sender) + received(other, other_sender)


def added(*arrays):
    outs = [(arrays[0].shape, jnp.float32)]
    return call_on_blocks(add_kernel, outs, *arrays, name="added")[0]


def finished(segment, slab_rows, place, powers, auto, partial, arrived):
    def kernel(place, powers, auto, partial, arrived, covariance, segment_auto):
        chunk = partial.shape[0]
        total = partial[...] + received(arrived, arrived[chunk:])
        sums, sum_refs, _ = joined(powers[...], arrived[chunk:])
        scale = 1.0 / jnp.sqrt(sums / slab_rows + 1e-06)
        ref_scale = 1.0 / jnp.sqrt(ref_column(sum_refs) / slab_rows + 1e-06)
        lag = lax.broadcasted_iota(jnp.int32, (chunk, 1), 0) // REF + place[0] * (chunk // REF)
        denom = (slab_rows - lag).astype(jnp.float32)
        covariance[...] = total * scale * (for_chunk(ref_scale, chunk) / denom)
        segment_auto[...] = auto[...] * (scale * scale) / segment

    outs = [(partial.shape, jnp.float32), (auto.shape, jnp.float32)]
    return call_on_blocks(kernel, outs, place, powers, auto, partial, arrived, name="finished")


def segment_kernel(strain, tail, out, wide):
    rows, lanes = strain.shape
    pitch = rows // 8
    for lane in range(0, lanes, LANES):
        wide[:rows, :] = strain[:, lane : lane + LANES].astype(jnp.float32)
        wide[rows:, :] = tail[:, lane : lane + LANES].astype(jnp.float32)
        taken = lambda first: wide[pl.ds(first, 8, stride=pitch), :]

        def step(index, carry):
            window, sums = carry
            window = window + (taken(index + LAGS - 1),)
            sums = tuple(total + window[0] * window[lag] for lag, total in enumerate(sums))
            return window[1:], sums

        window = tuple(taken(first) for first in range(LAGS - 1))
        zero = jnp.zeros((8, LANES), jnp.float32)
        _, sums = lax.fori_loop(0, pitch, step, (window, (zero,) * LAGS), unroll=16)
        out[:, lane : lane + LANES] = jnp.concatenate(
            [jnp.sum(total, axis=0, keepdims=True) for total in sums], axis=0
        )


def segment_rows(strain, tail, first, size):
    rows = strain.shape[0]
    return pl.pallas_call(
        segment_kernel,
        grid=(1,),
        in_specs=[
            pl.BlockSpec((rows, size), lambda index: (0, first)),
            pl.BlockSpec((LAGS, size), lambda index: (0, first)),
        ],
        out_specs=pl.BlockSpec((LAGS, size), lambda index: (0, 0)),
        out_shape=jax.ShapeDtypeStruct((LAGS, size), jnp.float32),
        scratch_shapes=[pltpu.VMEM((rows + LAGS, LANES), jnp.float32)],
        compiler_params=pltpu.CompilerParams(vmem_limit_bytes=VMEM_BYTES),
        cost_estimate=pl.CostEstimate(
            flops=64 * LAGS * rows * size, bytes_accessed=rows * size * 2, transcendentals=0
        ),
        name="segment_rows",
    )(strain, tail)


def all_products_kernel(place, strain, own, other, tail, out, held, shifted, edge, sems):
    group = pl.program_id(0)
    copies = fetches(strain, held, sems)
    for copy in copies:
        copy.start()
    edge[...] = padded(tail)
    lag_rows(own, other, place[0], group * GROUP, shifted)
    out[...] = product_of(shifted, held, edge, copies)


def all_products(place, strain, own, other, tail):
    rows, width = strain.shape
    return pl.pallas_call(
        all_products_kernel,
        grid=(LAGS // GROUP,),
        in_specs=product_specs(3),
        out_specs=pl.BlockSpec((GROUP * REF, width), lambda group: (group, 0)),
        out_shape=jax.ShapeDtypeStruct((LAGS * REF, width), jnp.float32),
        scratch_shapes=product_scratch(rows, width),
        compiler_params=pltpu.CompilerParams(vmem_limit_bytes=VMEM_BYTES),
        name="all_products",
    )(place, strain, own, other, tail)


def local(strain):
    rows, width = strain.shape
    count = lax.axis_size("tm")
    chan = lax.axis_index("chan").astype(jnp.int32)
    time = lax.axis_index("tm").astype(jnp.int32)
    slab_rows = rows * count
    chunk = LAGS * REF // count
    pair = lax.shift_right_logical(time, 1)

    own, head = prepared(strain)
    other = exchanged(own, "chan", 1)
    tail = passed_along(head, "tm", -1)

    size = 256
    pieces = [segment_rows(strain, tail, first, size) for first in range(width // size)]
    auto = jnp.concatenate(pieces, axis=1)

    if chunk * 2 == GROUP * REF:
        place = jnp.stack([chan, pair ^ 3, time & 1, pair ^ 2, pair ^ 1, pair])
        keep6, send7, powers0 = first_products(place, strain, own, other, tail, chunk)
        got7 = exchanged(send7, "tm", 1)
        keep4, send5, keep2, send3, keep0, send1 = later_products(
            place, strain, own, other, tail, powers0, chunk, 3
        )
        near0 = got7[chunk:]
        got5 = exchanged(send5, "tm", 1)
        got3 = exchanged(send3, "tm", 1)
        got1 = exchanged(send1, "tm", 1)
        send6, powers1 = merged(keep6, powers0, got7)
        got6 = exchanged(send6, "tm", 2)
        near1 = got6[chunk:]
        send4, powers2 = merged(keep4, powers1, got6, got5, near0)
        got4 = exchanged(send4, "tm", 4)
        got2 = exchanged(resent(keep2, got3, near0, powers1), "tm", 2)
        partial = added(keep0, got1, near0, got2, near1)
        return tuple(finished(rows, slab_rows, time[None], powers2, auto, partial, got4))

    place = jnp.stack([chan, time])
    powers = [jnp.sum(jnp.square(array.astype(jnp.float32)), axis=axis) for array, axis in ((strain, 0), (other, 1))]
    power = lax.psum(jnp.concatenate(powers), "tm")
    inv = 1.0 / jnp.sqrt(power / slab_rows + 1e-06)
    scale = inv[:width]
    ref_scale = jnp.where(
        chan == 0,
        jnp.concatenate([inv[:HALF], inv[width:]]),
        jnp.concatenate([inv[width:], inv[:HALF]]),
    )
    products = all_products(place, strain, own, other, tail)
    summed = lax.psum_scatter(products, "tm", scatter_dimension=0, tiled=True)
    row = time * chunk + jnp.arange(chunk, dtype=jnp.int32)
    row_scale = ref_scale[row % REF] / (slab_rows - row // REF).astype(jnp.float32)
    covariance = summed * scale[None, :] * row_scale[:, None]
    segment_auto = auto * (scale * scale)[None, :] / rows
    return (covariance, segment_auto)


def solution(mesh):
    in_specs = (P(("groups", "tm"), "chan"),)
    out_specs = (P(("groups", "tm"), "chan"), P(("groups", "tm"), "chan"))
    return jax.shard_map(local, mesh=mesh, in_specs=in_specs, out_specs=out_specs, check_vma=False)
```

```python
import jax
import jax.numpy as jnp
from jax import lax
from jax.experimental import pallas as pl
from jax.experimental.pallas import tpu as pltpu
from jax.sharding import PartitionSpec as P

LAGS = 16
REF = 64
HALF = REF // 2
LANES = 128
EXTRA = 8
FETCHES = 8
GROUP = 4
POWER = 16
CODE_SCALE = 2.0 ** (126 / POWER)
TINY = 1e-35
PIECES = 4
VMEM_BYTES = 32 * 1024 * 1024
SMALL = pl.CostEstimate(flops=0, bytes_accessed=1024, transcendentals=0)


def passed_along(value, axis, steps):
    count = lax.axis_size(axis)
    initial, last = (max(0, -steps), min(count, count - steps))
    return lax.ppermute(value, axis, [(source, source + steps) for source in range(initial, last)])


def exchanged(value, axis, bit):
    count = lax.axis_size(axis)
    return lax.ppermute(value, axis, [(source, source ^ bit) for source in range(count)])


def as_column(row):
    size = row.shape[1]
    eye = lax.broadcasted_iota(jnp.int32, (size, size), 0) == lax.broadcasted_iota(jnp.int32, (size, size), 1)
    return jnp.sum(jnp.where(eye, row, 0.0), axis=1, keepdims=True)


def as_row(column):
    size = column.shape[0]
    eye = lax.broadcasted_iota(jnp.int32, (size, size), 0) == lax.broadcasted_iota(jnp.int32, (size, size), 1)
    return jnp.sum(jnp.where(eye, column, 0.0), axis=0, keepdims=True)


def for_chunk(ref_column, rows):
    return jnp.concatenate([ref_column] * (rows // REF), axis=0)


def bf16_pieces(value):
    high = value.astype(jnp.bfloat16).astype(jnp.float32)
    middle = (value - high).astype(jnp.bfloat16).astype(jnp.float32)
    return high, middle, value - high - middle


def packed(powers, ref_powers, channel_bound):
    rows = list(bf16_pieces(powers))
    refs = jnp.concatenate(bf16_pieces(ref_powers), axis=1)
    pad = jnp.zeros((1, powers.shape[1] - refs.shape[1]), jnp.float32)
    rows += [jnp.concatenate([refs, pad], axis=1), channel_bound]
    rows += [jnp.zeros_like(powers)] * (EXTRA - len(rows))
    return jnp.concatenate(rows, axis=0).astype(jnp.bfloat16)


def unpacked(block):
    wide = block.astype(jnp.float32)
    powers = wide[0:1] + wide[1:2] + wide[2:3]
    refs = wide[3:4, :LANES] + wide[3:4, LANES : 2 * LANES] + wide[3:4, 2 * LANES : 3 * LANES]
    return powers, refs, wide[4:5]


def rounded_up(value):
    return (value * (1.0 + 2.0**-7)).astype(jnp.bfloat16).astype(jnp.float32)


def coded(values, channel_bound, ref_bound):
    channel = lax.rsqrt(jnp.maximum(channel_bound, TINY))
    refs = lax.rsqrt(jnp.maximum(ref_bound, TINY)) * CODE_SCALE
    power = values * channel * for_chunk(refs, values.shape[0])
    for _ in range(4):
        power = power * jnp.abs(power)
    return power.astype(jnp.bfloat16)


def expanded(code, channel_bound, ref_bound):
    channel = jnp.sqrt(jnp.maximum(channel_bound, TINY))
    refs = jnp.sqrt(jnp.maximum(ref_bound, TINY)) * (1.0 / CODE_SCALE)
    wide = code.astype(jnp.float32)
    root = jnp.exp2(jnp.log2(jnp.abs(wide)) * (1.0 / POWER))
    return jnp.where(wide < 0.0, -root, root) * channel * for_chunk(refs, code.shape[0])


def ref_column(ref_powers):
    return as_column(ref_powers)[:REF]


def prepare_kernel(strain, own, head, left, sems):
    rows = left.shape[0]
    step = rows // PIECES
    copies = [
        pltpu.make_async_copy(
            strain.at[pl.ds(index * step, step), pl.ds(0, LANES)], left.at[pl.ds(index * step, step)], sems.at[index]
        )
        for index in range(PIECES)
    ]
    copies.append(pltpu.make_async_copy(strain.at[pl.ds(0, LAGS)], head, sems.at[PIECES]))
    for copy in copies:
        copy.start()
    for index in range(PIECES):
        copies[index].wait()
        here = slice(index * step, (index + 1) * step)
        own[:, here] = left[here, :].astype(jnp.float32).T[:HALF].astype(jnp.bfloat16)
    copies[PIECES].wait()


def prepared(strain):
    rows, width = strain.shape
    vmem = pl.BlockSpec(memory_space=pltpu.VMEM)
    return pl.pallas_call(
        prepare_kernel,
        in_specs=[pl.BlockSpec(memory_space=pl.ANY)],
        out_specs=[vmem, vmem],
        out_shape=[pltpu.VMEM((HALF, rows), strain.dtype), pltpu.VMEM((LAGS, width), strain.dtype)],
        scratch_shapes=[pltpu.VMEM((rows, LANES), strain.dtype), pltpu.SemaphoreType.DMA((PIECES + 1,))],
        compiler_params=pltpu.CompilerParams(vmem_limit_bytes=VMEM_BYTES),
        cost_estimate=SMALL,
        name="prepared",
    )(pltpu.with_memory_space_constraint(strain, pltpu.HBM))


def lag_rows(own, other, chan, first_lag, shifted):
    rows = own.shape[1]
    zeros = jnp.zeros((HALF, LANES), jnp.float32)
    for refs, half in ((own, chan), (other, 1 - chan)):
        long = jnp.concatenate([refs[...].astype(jnp.float32), zeros], axis=1)
        for index in range(GROUP):
            moved = pltpu.roll(long, first_lag + index, 1)
            start = pl.multiple_of(index * REF + half * HALF, HALF)
            shifted[pl.ds(start, HALF), :] = moved.astype(jnp.bfloat16)


def loaded_kernel(strain, held, power, sems):
    step = held.shape[0] // FETCHES
    pieces = [slice(index * step, (index + 1) * step) for index in range(FETCHES)]
    copies = [
        pltpu.make_async_copy(strain.at[pl.ds(here.start, step)], held.at[pl.ds(here.start, step)], sems.at[index])
        for index, here in enumerate(pieces)
    ]
    for copy in copies:
        copy.start()
    total = jnp.zeros((8, held.shape[1]), jnp.float32)
    for copy, here in zip(copies, pieces):
        copy.wait()
        squares = jnp.square(held[here, :].astype(jnp.float32))
        total += jnp.sum(squares.reshape(step // 8, 8, held.shape[1]), axis=0)
    power[...] = jnp.sum(total, axis=0, keepdims=True)


def loaded(strain, after):
    rows, width = strain.shape
    vmem = pl.BlockSpec(memory_space=pltpu.VMEM)

    def kernel(strain, after, held, power, sems):
        loaded_kernel(strain, held, power, sems)

    return pl.pallas_call(
        kernel,
        in_specs=[pl.BlockSpec(memory_space=pl.ANY)] * 2,
        out_specs=[vmem, vmem],
        out_shape=[pltpu.VMEM((rows, width), strain.dtype), pltpu.VMEM((1, width), jnp.float32)],
        scratch_shapes=[pltpu.SemaphoreType.DMA((FETCHES,))],
        compiler_params=pltpu.CompilerParams(vmem_limit_bytes=VMEM_BYTES),
        cost_estimate=SMALL,
        name="loaded",
    )(pltpu.with_memory_space_constraint(strain, pltpu.HBM), after)


def product_of(shifted, held, tail):
    rows = held.shape[0]
    total = jnp.dot(shifted[:, :rows], held[...], preferred_element_type=jnp.float32)
    edge = jnp.concatenate([tail[...], jnp.zeros((LANES - LAGS, tail.shape[1]), tail.dtype)], axis=0)
    return total + jnp.dot(shifted[:, rows:], edge, preferred_element_type=jnp.float32)


def first_products_kernel(place, held, power, own, other, tail, keep, send, powers, shifted):
    chan, group, near = place[0], place[1], place[2]
    lag_rows(own, other, chan, group * GROUP, shifted)
    ours, theirs = [
        jnp.sum(jnp.square(refs[...].astype(jnp.float32)), axis=1, keepdims=True) for refs in (own, other)
    ]
    refs = jnp.where(
        chan == 0, jnp.concatenate([ours, theirs], axis=0), jnp.concatenate([theirs, ours], axis=0)
    )
    product = product_of(shifted, held, tail)
    beyond = jnp.sum(jnp.square(tail[...].astype(jnp.float32)), axis=0, keepdims=True)
    bound = rounded_up(power[...] + beyond)
    pad = jnp.zeros((1, LANES - REF), jnp.float32)
    extra = packed(power[...], jnp.concatenate([as_row(refs), pad], axis=1), bound)
    powers[...] = extra
    chunk = keep.shape[0]
    keep[...] = jnp.where(near == 0, product[:chunk], product[chunk:])
    other_half = jnp.where(near == 0, product[chunk:], product[:chunk])
    send[:chunk] = coded(other_half, bound, refs)
    send[chunk:] = extra


def shifted_scratch(rows, *slots):
    return [pltpu.VMEM((*slots, GROUP * REF, rows + LANES), jnp.bfloat16)]


def first_products(place, held, power, own, other, tail, chunk):
    rows, width = held.shape
    outs = [
        ((chunk, width), jnp.float32),
        ((chunk + EXTRA, width), jnp.bfloat16),
        ((EXTRA, width), jnp.bfloat16),
    ]
    return call_on_blocks(
        first_products_kernel,
        outs,
        place,
        held,
        power,
        own,
        other,
        tail,
        name="first_products",
        scratch=shifted_scratch(rows),
    )


def later_products_kernel(place, held, own, other, tail, powers, *rest):
    chan, near = place[0], place[2]
    shifted = rest[-1]
    _, ref_powers, bound = unpacked(powers[...])
    refs = ref_column(ref_powers)
    slots = (len(rest) - 1) // 2
    for slot in range(slots):
        keep, send = rest[2 * slot], rest[2 * slot + 1]
        chunk = keep.shape[0]
        lag_rows(own, other, chan, place[3 + slot] * GROUP, shifted.at[slot])
        product = product_of(shifted.at[slot], held, tail)
        keep[...] = jnp.where(near == 0, product[:chunk], product[chunk:])
        other_half = jnp.where(near == 0, product[chunk:], product[:chunk])
        send[...] = coded(other_half, bound, refs)


def later_products(place, held, own, other, tail, powers, chunk, slots):
    rows, width = held.shape
    return call_on_blocks(
        later_products_kernel,
        [((chunk, width), jnp.float32), ((chunk, width), jnp.bfloat16)] * slots,
        place,
        held,
        own,
        other,
        tail,
        powers,
        name="later_products",
        scratch=shifted_scratch(rows, slots),
    )


def call_on_blocks(kernel, outs, *arrays, name, after=(), scratch=(), space=pltpu.VMEM):
    vmem = pl.BlockSpec(memory_space=pltpu.VMEM)
    smem = pl.BlockSpec(memory_space=pltpu.SMEM)
    count = len(arrays)

    def body(*refs):
        kernel(*refs[:count], *refs[count + len(after) :])

    return pl.pallas_call(
        body,
        in_specs=[smem if array.dtype == jnp.int32 else vmem for array in arrays]
        + [pl.BlockSpec(memory_space=pl.ANY)] * len(after),
        out_specs=[vmem] * len(outs),
        out_shape=[space(shape, dtype) for shape, dtype in outs],
        scratch_shapes=list(scratch),
        compiler_params=pltpu.CompilerParams(vmem_limit_bytes=VMEM_BYTES),
        cost_estimate=SMALL,
        name=name,
    )(*arrays, *after)


def received(code, powers):
    chunk = code.shape[0] // REF * REF
    _, refs, bound = unpacked(powers[...])
    return expanded(code[:chunk], bound, ref_column(refs))


def joined(powers, arrived):
    ours, ours_refs, ours_bound = unpacked(powers)
    theirs, theirs_refs, theirs_bound = unpacked(arrived)
    bound = rounded_up(ours_bound + theirs_bound)
    return ours + theirs, ours_refs + theirs_refs, bound


def merge_kernel(*refs):
    keep, powers, arrived, out, extra = refs[0], refs[1], refs[2], refs[-2], refs[-1]
    chunk = keep.shape[0]
    total = keep[...] + received(arrived, arrived[chunk:])
    for code, sender in zip(refs[3:-2:2], refs[4:-2:2]):
        total = total + received(code, sender)
    sums, sum_refs, bound = joined(powers[...], arrived[chunk:])
    extra[...] = packed(sums, sum_refs, bound)
    out[:chunk] = coded(total, bound, ref_column(sum_refs))
    out[chunk:] = extra[...]


def merged(keep, powers, arrived, *others, after):
    chunk, width = keep.shape
    outs = [((chunk + EXTRA, width), jnp.bfloat16), ((EXTRA, width), jnp.bfloat16)]
    return call_on_blocks(merge_kernel, outs, keep, powers, arrived, *others, name="merged", after=after)


def resend_kernel(keep, code, sender, powers, out):
    _, refs, bound = unpacked(powers[...])
    out[...] = coded(keep[...] + received(code, sender), bound, ref_column(refs))


def resent(keep, code, sender, powers, after):
    outs = [(keep.shape, jnp.bfloat16)]
    return call_on_blocks(resend_kernel, outs, keep, code, sender, powers, name="resent", after=after)[0]


def add_kernel(keep, code, sender, other, other_sender, out):
    out[...] = keep[...] + received(code, sender) + received(other, other_sender)


def added(*arrays, after):
    outs = [(arrays[0].shape, jnp.float32)]
    return call_on_blocks(add_kernel, outs, *arrays, name="added", after=after)[0]


def finished(segment, slab_rows, place, powers, auto, partial, arrived):
    def kernel(place, powers, auto, partial, arrived, covariance, segment_auto):
        chunk = partial.shape[0]
        total = partial[...] + received(arrived, arrived[chunk:])
        sums, sum_refs, _ = joined(powers[...], arrived[chunk:])
        scale = 1.0 / jnp.sqrt(sums / slab_rows + 1e-06)
        ref_scale = 1.0 / jnp.sqrt(ref_column(sum_refs) / slab_rows + 1e-06)
        lag = lax.broadcasted_iota(jnp.int32, (chunk, 1), 0) // REF + place[0] * (chunk // REF)
        denom = (slab_rows - lag).astype(jnp.float32)
        covariance[...] = total * scale * (for_chunk(ref_scale, chunk) / denom)
        segment_auto[...] = auto[...] * (scale * scale) / segment

    outs = [(partial.shape, jnp.float32), (auto.shape, jnp.float32)]
    return call_on_blocks(kernel, outs, place, powers, auto, partial, arrived, name="finished", space=jax.ShapeDtypeStruct)


def segment_kernel(first, strain, tail, out, wide):
    rows = strain.shape[0]
    pitch = rows // 8
    for index in range(out.shape[1] // LANES):
        here = slice(first + index * LANES, first + (index + 1) * LANES)
        wide[:rows, :] = strain[:, here].astype(jnp.float32)
        wide[rows:, :] = tail[:, here].astype(jnp.float32)
        taken = lambda first: wide[pl.ds(first, 8, stride=pitch), :]

        def step(index, carry):
            window, sums = carry
            window = window + (taken(index + LAGS - 1),)
            sums = tuple(total + window[0] * window[lag] for lag, total in enumerate(sums))
            return window[1:], sums

        window = tuple(taken(first) for first in range(LAGS - 1))
        zero = jnp.zeros((8, LANES), jnp.float32)
        _, sums = lax.fori_loop(0, pitch, step, (window, (zero,) * LAGS), unroll=16)
        out[:, index * LANES : (index + 1) * LANES] = jnp.concatenate(
            [jnp.sum(total, axis=0, keepdims=True) for total in sums], axis=0
        )


def segment_rows(held, tail, first, size, after=()):
    rows = held.shape[0]

    def kernel(*refs):
        segment_kernel(first, *refs)

    return call_on_blocks(
        kernel,
        [((LAGS, size), jnp.float32)],
        held,
        tail,
        name="segment_rows",
        after=after,
        scratch=[pltpu.VMEM((rows + LAGS, LANES), jnp.float32)],
    )[0]


def all_products_kernel(place, held, own, other, tail, out, shifted):
    group = pl.program_id(0)
    lag_rows(own, other, place[0], group * GROUP, shifted)
    out[...] = product_of(shifted, held, tail)


def all_products(place, held, own, other, tail):
    rows, width = held.shape
    vmem = pl.BlockSpec(memory_space=pltpu.VMEM)
    return pl.pallas_call(
        all_products_kernel,
        grid=(LAGS // GROUP,),
        in_specs=[pl.BlockSpec(memory_space=pltpu.SMEM)] + [vmem] * 4,
        out_specs=pl.BlockSpec((GROUP * REF, width), lambda group: (group, 0)),
        out_shape=jax.ShapeDtypeStruct((LAGS * REF, width), jnp.float32),
        scratch_shapes=shifted_scratch(rows),
        compiler_params=pltpu.CompilerParams(vmem_limit_bytes=VMEM_BYTES),
        name="all_products",
    )(place, held, own, other, tail)


def local(strain):
    rows, width = strain.shape
    count = lax.axis_size("tm")
    chan = lax.axis_index("chan").astype(jnp.int32)
    time = lax.axis_index("tm").astype(jnp.int32)
    slab_rows = rows * count
    chunk = LAGS * REF // count
    pair = lax.shift_right_logical(time, 1)

    own, head = prepared(strain)
    other = exchanged(own, "chan", 1)
    tail = passed_along(head, "tm", -1)
    held, power = loaded(strain, own)
    size = width // 4

    if chunk * 2 == GROUP * REF:
        place = jnp.stack([chan, pair ^ 3, time & 1, pair ^ 2, pair ^ 1, pair])
        keep6, send7, powers0 = first_products(place, held, power, own, other, tail, chunk)
        got7 = exchanged(send7, "tm", 1)
        keep4, send5, keep2, send3, keep0, send1 = later_products(
            place, held, own, other, tail, powers0, chunk, 3
        )
        near0 = got7[chunk:]
        got5 = exchanged(send5, "tm", 1)
        got3 = exchanged(send3, "tm", 1)
        got1 = exchanged(send1, "tm", 1)
        send6, powers1 = merged(keep6, powers0, got7, after=(send5,))
        got6 = exchanged(send6, "tm", 2)
        near1 = got6[chunk:]
        autos = [segment_rows(held, tail, 0, size, after=(powers1,))]
        send4, powers2 = merged(keep4, powers1, got6, got5, near0, after=(autos[0],))
        got4 = exchanged(send4, "tm", 4)
        send2 = resent(keep2, got3, near0, powers1, after=(powers2,))
        got2 = exchanged(send2, "tm", 2)
        autos += [segment_rows(held, tail, size * index, size, after=(send2,)) for index in (1, 2, 3)]
        partial = added(keep0, got1, near0, got2, near1, after=(autos[1], autos[2]))
        auto = jnp.concatenate(autos, axis=1)
        return tuple(finished(rows, slab_rows, time[None], powers2, auto, partial, got4))

    place = jnp.stack([chan, time])
    auto = jnp.concatenate([segment_rows(held, tail, size * index, size) for index in range(4)], axis=1)
    power_other = jnp.sum(jnp.square(other.astype(jnp.float32)), axis=1)
    power = lax.psum(jnp.concatenate([power[0], power_other]), "tm")
    inv = 1.0 / jnp.sqrt(power / slab_rows + 1e-06)
    scale = inv[:width]
    ref_scale = jnp.where(
        chan == 0,
        jnp.concatenate([inv[:HALF], inv[width:]]),
        jnp.concatenate([inv[width:], inv[:HALF]]),
    )
    products = all_products(place, held, own, other, tail)
    summed = lax.psum_scatter(products, "tm", scatter_dimension=0, tiled=True)
    row = time * chunk + jnp.arange(chunk, dtype=jnp.int32)
    row_scale = ref_scale[row % REF] / (slab_rows - row // REF).astype(jnp.float32)
    covariance = summed * scale[None, :] * row_scale[:, None]
    segment_auto = auto * (scale * scale)[None, :] / rows
    return (covariance, segment_auto)


def solution(mesh):
    in_specs = (P(("groups", "tm"), "chan"),)
    out_specs = (P(("groups", "tm"), "chan"), P(("groups", "tm"), "chan"))
    return jax.shard_map(local, mesh=mesh, in_specs=in_specs, out_specs=out_specs, check_vma=False)
```

```python
import jax
import jax.numpy as jnp
from jax import lax
from jax.experimental import pallas as pl
from jax.experimental.pallas import tpu as pltpu
from jax.sharding import PartitionSpec as P

LAGS = 16
REF = 64
HALF = REF // 2
LANES = 128
EXTRA = 8
FETCHES = 8
GROUP = 4
POWER = 16
CODE_SCALE = 2.0 ** (126 / POWER)
TINY = 1e-35
PIECES = 4
VMEM_BYTES = 32 * 1024 * 1024
SMALL = pl.CostEstimate(flops=0, bytes_accessed=1024, transcendentals=0)


def passed_along(value, axis, steps):
    count = lax.axis_size(axis)
    initial, last = (max(0, -steps), min(count, count - steps))
    return lax.ppermute(value, axis, [(source, source + steps) for source in range(initial, last)])


def exchanged(value, axis, bit):
    count = lax.axis_size(axis)
    return lax.ppermute(value, axis, [(source, source ^ bit) for source in range(count)])


def as_column(row):
    size = row.shape[1]
    eye = lax.broadcasted_iota(jnp.int32, (size, size), 0) == lax.broadcasted_iota(jnp.int32, (size, size), 1)
    return jnp.sum(jnp.where(eye, row, 0.0), axis=1, keepdims=True)


def as_row(column):
    size = column.shape[0]
    eye = lax.broadcasted_iota(jnp.int32, (size, size), 0) == lax.broadcasted_iota(jnp.int32, (size, size), 1)
    return jnp.sum(jnp.where(eye, column, 0.0), axis=0, keepdims=True)


def for_chunk(ref_column, rows):
    return jnp.concatenate([ref_column] * (rows // REF), axis=0)


def bf16_pieces(value):
    high = value.astype(jnp.bfloat16).astype(jnp.float32)
    middle = (value - high).astype(jnp.bfloat16).astype(jnp.float32)
    return high, middle, value - high - middle


def packed(powers, ref_powers, channel_bound):
    rows = list(bf16_pieces(powers))
    refs = jnp.concatenate(bf16_pieces(ref_powers), axis=1)
    pad = jnp.zeros((1, powers.shape[1] - refs.shape[1]), jnp.float32)
    rows += [jnp.concatenate([refs, pad], axis=1), channel_bound]
    rows += [jnp.zeros_like(powers)] * (EXTRA - len(rows))
    return jnp.concatenate(rows, axis=0).astype(jnp.bfloat16)


def unpacked(block):
    wide = block.astype(jnp.float32)
    powers = wide[0:1] + wide[1:2] + wide[2:3]
    refs = wide[3:4, :LANES] + wide[3:4, LANES : 2 * LANES] + wide[3:4, 2 * LANES : 3 * LANES]
    return powers, refs, wide[4:5]


def rounded_up(value):
    return (value * (1.0 + 2.0**-7)).astype(jnp.bfloat16).astype(jnp.float32)


def coded(values, channel_bound, ref_bound):
    channel = lax.rsqrt(jnp.maximum(channel_bound, TINY))
    refs = lax.rsqrt(jnp.maximum(ref_bound, TINY)) * CODE_SCALE
    power = values * channel * for_chunk(refs, values.shape[0])
    for _ in range(4):
        power = power * jnp.abs(power)
    return power.astype(jnp.bfloat16)


def expanded(code, channel_bound, ref_bound):
    channel = jnp.sqrt(jnp.maximum(channel_bound, TINY))
    refs = jnp.sqrt(jnp.maximum(ref_bound, TINY)) * (1.0 / CODE_SCALE)
    wide = code.astype(jnp.float32)
    root = jnp.exp2(jnp.log2(jnp.abs(wide)) * (1.0 / POWER))
    return jnp.where(wide < 0.0, -root, root) * channel * for_chunk(refs, code.shape[0])


def ref_column(ref_powers):
    return as_column(ref_powers)[:REF]


def prepare_kernel(strain, own, head, left, sems):
    rows = left.shape[0]
    step = rows // PIECES
    copies = [
        pltpu.make_async_copy(
            strain.at[pl.ds(index * step, step), pl.ds(0, LANES)], left.at[pl.ds(index * step, step)], sems.at[index]
        )
        for index in range(PIECES)
    ]
    copies.append(pltpu.make_async_copy(strain.at[pl.ds(0, LAGS)], head, sems.at[PIECES]))
    for copy in copies:
        copy.start()
    for index in range(PIECES):
        copies[index].wait()
        here = slice(index * step, (index + 1) * step)
        own[:, here] = left[here, :].astype(jnp.float32).T[:HALF].astype(jnp.bfloat16)
    copies[PIECES].wait()


def prepared(strain):
    rows, width = strain.shape
    vmem = pl.BlockSpec(memory_space=pltpu.VMEM)
    return pl.pallas_call(
        prepare_kernel,
        in_specs=[pl.BlockSpec(memory_space=pl.ANY)],
        out_specs=[vmem, vmem],
        out_shape=[pltpu.VMEM((HALF, rows), strain.dtype), pltpu.VMEM((LAGS, width), strain.dtype)],
        scratch_shapes=[pltpu.VMEM((rows, LANES), strain.dtype), pltpu.SemaphoreType.DMA((PIECES + 1,))],
        compiler_params=pltpu.CompilerParams(vmem_limit_bytes=VMEM_BYTES),
        cost_estimate=SMALL,
        name="prepared",
    )(pltpu.with_memory_space_constraint(strain, pltpu.HBM))


def lag_rows(own, other, group, shifted):
    chan, near = lax.axis_index("chan"), lax.axis_index("tm") & 1
    zeros = jnp.zeros((HALF, LANES), jnp.float32)
    for refs, half in ((own, chan), (other, 1 - chan)):
        long = jnp.concatenate([refs[...].astype(jnp.float32), zeros], axis=1)
        for index in range(GROUP):
            ahead = near if index < GROUP // 2 else 1 - near
            lag = group * GROUP + ahead * (GROUP // 2) + index % (GROUP // 2)
            start = pl.multiple_of(index * REF + half * HALF, HALF)
            shifted[pl.ds(start, HALF), :] = pltpu.roll(long, lag, 1).astype(jnp.bfloat16)


def own_group(bits):
    return lax.shift_right_logical(lax.axis_index("tm").astype(jnp.int32), 1) ^ bits


def loaded_kernel(strain, held, power, sems):
    step = held.shape[0] // FETCHES
    pieces = [slice(index * step, (index + 1) * step) for index in range(FETCHES)]
    copies = [
        pltpu.make_async_copy(strain.at[pl.ds(here.start, step)], held.at[pl.ds(here.start, step)], sems.at[index])
        for index, here in enumerate(pieces)
    ]
    for copy in copies:
        copy.start()
    total = jnp.zeros((8, held.shape[1]), jnp.float32)
    for copy, here in zip(copies, pieces):
        copy.wait()
        squares = jnp.square(held[here, :].astype(jnp.float32))
        total += jnp.sum(squares.reshape(step // 8, 8, held.shape[1]), axis=0)
    power[...] = jnp.sum(total, axis=0, keepdims=True)


def loaded(strain, after):
    rows, width = strain.shape
    vmem = pl.BlockSpec(memory_space=pltpu.VMEM)

    def kernel(strain, after, held, power, sems):
        loaded_kernel(strain, held, power, sems)

    return pl.pallas_call(
        kernel,
        in_specs=[pl.BlockSpec(memory_space=pl.ANY)] * 2,
        out_specs=[vmem, vmem],
        out_shape=[pltpu.VMEM((rows, width), strain.dtype), pltpu.VMEM((1, width), jnp.float32)],
        scratch_shapes=[pltpu.SemaphoreType.DMA((FETCHES,))],
        compiler_params=pltpu.CompilerParams(vmem_limit_bytes=VMEM_BYTES),
        cost_estimate=SMALL,
        name="loaded",
    )(pltpu.with_memory_space_constraint(strain, pltpu.HBM), after)


def edge_of(tail):
    return jnp.concatenate([tail[...], jnp.zeros((LANES - LAGS, tail.shape[1]), tail.dtype)], axis=0)


def product_of(shifted, held, edge, here):
    rows = held.shape[0]
    total = jnp.dot(shifted[:, rows:], edge[:, here], preferred_element_type=jnp.float32)
    return total + jnp.dot(shifted[:, :rows], held[:, here], preferred_element_type=jnp.float32)


def columns(width, step=256):
    return [slice(first, first + step) for first in range(0, width, step)]


def first_products_kernel(held, power, own, other, tail, keep, send, shifted):
    lag_rows(own, other, own_group(3), shifted)
    ours, theirs = [
        jnp.sum(jnp.square(refs[...].astype(jnp.float32)), axis=1, keepdims=True) for refs in (own, other)
    ]
    refs = jnp.where(
        lax.axis_index("chan") == 0,
        jnp.concatenate([ours, theirs], axis=0),
        jnp.concatenate([theirs, ours], axis=0),
    )
    beyond = jnp.sum(jnp.square(tail[...].astype(jnp.float32)), axis=0, keepdims=True)
    bound = rounded_up(power[...] + beyond)
    pad = jnp.zeros((1, LANES - REF), jnp.float32)
    chunk = keep.shape[0]
    send[chunk:] = packed(power[...], jnp.concatenate([as_row(refs), pad], axis=1), bound)
    edge = edge_of(tail)
    for here in columns(held.shape[1]):
        product = product_of(shifted, held, edge, here)
        keep[:, here] = product[:chunk]
        send[:chunk, here] = coded(product[chunk:], bound[:, here], refs)


def shifted_scratch(rows):
    return [pltpu.VMEM((GROUP * REF, rows + LANES), jnp.bfloat16)]


def first_products(held, power, own, other, tail, chunk, after):
    rows, width = held.shape
    outs = [
        ((chunk, width), jnp.float32),
        ((chunk + EXTRA, width), jnp.bfloat16),
    ]
    return call_on_blocks(
        first_products_kernel,
        outs,
        held,
        power,
        own,
        other,
        tail,
        name="first_products",
        after=after,
        scratch=shifted_scratch(rows),
    )


def later_products(bits, held, own, other, tail, powers, chunk, after=()):
    rows, width = held.shape

    def kernel(held, own, other, tail, powers, keep, send, shifted):
        _, ref_powers, bound = sent_powers(powers)
        refs = ref_column(ref_powers)
        lag_rows(own, other, own_group(bits), shifted)
        edge = edge_of(tail)
        for here in columns(width):
            product = product_of(shifted, held, edge, here)
            keep[:, here] = product[:chunk]
            send[:, here] = coded(product[chunk:], bound[:, here], refs)

    return call_on_blocks(
        kernel,
        [((chunk, width), jnp.float32), ((chunk, width), jnp.bfloat16)],
        held,
        own,
        other,
        tail,
        powers,
        name="later_products",
        after=after,
        scratch=shifted_scratch(rows),
    )


def call_on_blocks(kernel, outs, *arrays, name, after=(), scratch=(), space=pltpu.VMEM):
    vmem = pl.BlockSpec(memory_space=pltpu.VMEM)
    count = len(arrays)

    def body(*refs):
        kernel(*refs[:count], *refs[count + len(after) :])

    return pl.pallas_call(
        body,
        in_specs=[vmem] * count + [pl.BlockSpec(memory_space=pl.ANY)] * len(after),
        out_specs=[vmem] * len(outs),
        out_shape=[space(shape, dtype) for shape, dtype in outs],
        scratch_shapes=list(scratch),
        compiler_params=pltpu.CompilerParams(vmem_limit_bytes=VMEM_BYTES),
        cost_estimate=SMALL,
        name=name,
    )(*arrays, *after)


def half_of(width, part):
    return slice(part * width // 2, (part + 1) * width // 2)


def sent_powers(code, here=slice(None)):
    powers, refs, bound = unpacked(code[-EXTRA:])
    return powers[:, here], refs, bound[:, here]


def merge_near(keep, ours, theirs):
    chunk, width = keep.shape

    def kernel(keep, ours, theirs, *outs):
        for part, out in enumerate(outs):
            here = half_of(width, part)
            powers, refs, bound = sent_powers(ours, here)
            their_powers, their_refs, their_bound = sent_powers(theirs, here)
            total = keep[:, here] + expanded(theirs[:chunk, here], their_bound, ref_column(their_refs))
            sums, sum_refs, sum_bound = powers + their_powers, refs + their_refs, rounded_up(bound + their_bound)
            out[chunk:] = packed(sums, sum_refs, sum_bound)
            out[:chunk] = coded(total, sum_bound, ref_column(sum_refs))

    outs = [((chunk + EXTRA, width // 2), jnp.bfloat16)] * 2
    return lambda after: call_on_blocks(kernel, outs, keep, ours, theirs, name="merge_near", after=after)


def merge_far(part, keep, ours, theirs, direct, direct_powers, after):
    chunk, width = keep.shape
    here = half_of(width, part)

    def kernel(keep, ours, theirs, direct, direct_powers, out):
        powers, refs, bound = sent_powers(ours)
        their_powers, their_refs, their_bound = sent_powers(theirs)
        total = keep[:, here] + expanded(theirs[:chunk], their_bound, ref_column(their_refs))
        _, direct_refs, direct_bound = sent_powers(direct_powers, here)
        total += expanded(direct[:, here], direct_bound, ref_column(direct_refs))
        sums, sum_refs, sum_bound = powers + their_powers, refs + their_refs, rounded_up(bound + their_bound)
        out[chunk:] = packed(sums, sum_refs, sum_bound)
        out[:chunk] = coded(total, sum_bound, ref_column(sum_refs))

    outs = [((chunk + EXTRA, width // 2), jnp.bfloat16)]
    return call_on_blocks(
        kernel, outs, keep, ours, theirs, direct, direct_powers, name="merge_far", after=after
    )[0]


def resent(keep, direct, direct_powers, ours, after):
    width = keep.shape[1]

    def kernel(keep, direct, direct_powers, first, second, out):
        for part, powers in enumerate((first, second)):
            here = half_of(width, part)
            _, direct_refs, direct_bound = sent_powers(direct_powers, here)
            _, refs, bound = sent_powers(powers)
            total = keep[:, here] + expanded(direct[:, here], direct_bound, ref_column(direct_refs))
            out[:, here] = coded(total, bound, ref_column(refs))

    outs = [(keep.shape, jnp.bfloat16)]
    return call_on_blocks(kernel, outs, keep, direct, direct_powers, *ours, name="resent", after=after)[0]


def added(keep, direct, direct_powers, near, near_powers, held, tail, size, after):
    rows, width = held.shape

    def kernel(keep, direct, direct_powers, near, first, second, held, tail, out, edge):
        for part, powers in enumerate((first, second)):
            here = half_of(width, part)
            _, direct_refs, direct_bound = sent_powers(direct_powers, here)
            _, refs, bound = sent_powers(powers)
            total = keep[:, here] + expanded(direct[:, here], direct_bound, ref_column(direct_refs))
            out[:, here] = total + expanded(near[:, here], bound, ref_column(refs))
        last = held[rows - LAGS :, :size].astype(jnp.float32)
        beyond = tail[:, :size].astype(jnp.float32)
        place = lax.broadcasted_iota(jnp.int32, last.shape, 0)
        sums = [jnp.zeros((1, size), jnp.float32)]
        for lag in range(1, LAGS):
            pairs = jnp.where(place >= LAGS - lag, last * pltpu.roll(beyond, LAGS - lag, 0), 0.0)
            sums.append(jnp.sum(pairs, axis=0, keepdims=True))
        edge[...] = jnp.concatenate(sums, axis=0)

    outs = [(keep.shape, jnp.float32), ((LAGS, size), jnp.float32)]
    return call_on_blocks(
        kernel, outs, keep, direct, direct_powers, near, *near_powers, held, tail, name="added", after=after
    )


def finished(slab_rows, segment, partial, edge, ours, theirs, autos):
    chunk, width = partial.shape

    def kernel(partial, edge, *refs):
        ours, theirs, autos, (covariance, segment_auto) = refs[:2], refs[2:4], refs[4:-2], refs[-2:]
        first_lag = lax.axis_index("tm").astype(jnp.int32) * (chunk // REF)
        lag = lax.broadcasted_iota(jnp.int32, (chunk, 1), 0) // REF + first_lag
        denom = (slab_rows - lag).astype(jnp.float32)
        size = width // len(autos)
        for part in range(2):
            here = half_of(width, part)
            powers, own_refs, _ = sent_powers(ours[part])
            their_powers, their_refs, their_bound = sent_powers(theirs[part])
            total = partial[:, here] + expanded(theirs[part][:chunk], their_bound, ref_column(their_refs))
            scale = 1.0 / jnp.sqrt((powers + their_powers) / slab_rows + 1e-06)
            ref_scale = 1.0 / jnp.sqrt(ref_column(own_refs + their_refs) / slab_rows + 1e-06)
            covariance[:, here] = total * scale * (for_chunk(ref_scale, chunk) / denom)
            for index in range(len(autos)):
                first = index * size - here.start
                if 0 <= first < width // 2:
                    auto = autos[index][...] + edge[...] if index == 0 else autos[index][...]
                    own_scale = scale[:, first : first + size]
                    segment_auto[:, index * size : (index + 1) * size] = auto * (own_scale * own_scale) / segment

    outs = [(partial.shape, jnp.float32), ((LAGS, width), jnp.float32)]
    return call_on_blocks(
        kernel, outs, partial, edge, *ours, *theirs, *autos, name="finished", space=jax.ShapeDtypeStruct
    )


def segment_kernel(first, held, power, tail, out, wide):
    rows = held.shape[0]
    step = rows // 8
    pitch = step + LAGS
    for index in range(out.shape[1] // LANES):
        here = slice(first + index * LANES, first + (index + 1) * LANES)
        there = slice(index * LANES, (index + 1) * LANES)
        for part in range(8):
            end = (part + 1) * step
            wide[part * pitch : part * pitch + step, :] = held[end - step : end, here].astype(jnp.float32)
            if part < 7:
                following = held[end : end + LAGS, here].astype(jnp.float32)
            elif tail is None:
                following = jnp.zeros((LAGS, LANES), jnp.float32)
            else:
                following = tail[:, here].astype(jnp.float32)
            wide[part * pitch + step : (part + 1) * pitch, :] = following
        taken = lambda first: wide[pl.ds(first, 8, stride=pitch), :]

        def advance(index, carry):
            window, sums = carry
            window = window + (taken(index + LAGS - 1),)
            sums = tuple(total + window[0] * window[lag + 1] for lag, total in enumerate(sums))
            return window[1:], sums

        window = tuple(taken(first) for first in range(LAGS - 1))
        zero = jnp.zeros((8, LANES), jnp.float32)
        _, sums = lax.fori_loop(0, step, advance, (window, (zero,) * (LAGS - 1)), unroll=16)
        out[:, there] = jnp.concatenate(
            [power[:, here]] + [jnp.sum(total, axis=0, keepdims=True) for total in sums], axis=0
        )


def segment_rows(held, power, tail, first, size, after=()):
    rows = held.shape[0]
    arrays = (held, power) if tail is None else (held, power, tail)

    def kernel(*refs):
        held, power, *rest = refs
        if tail is None:
            rest = [None] + rest
        segment_kernel(first, held, power, *rest)

    return call_on_blocks(
        kernel,
        [((LAGS, size), jnp.float32)],
        *arrays,
        name="segment_rows",
        after=after,
        scratch=[pltpu.VMEM((rows + 8 * LAGS, LANES), jnp.float32)],
    )[0]


def all_products_kernel(held, own, other, tail, out, shifted):
    chan = lax.axis_index("chan")
    zeros = jnp.zeros((HALF, LANES), jnp.float32)
    for refs, half in ((own, chan), (other, 1 - chan)):
        long = jnp.concatenate([refs[...].astype(jnp.float32), zeros], axis=1)
        for index in range(GROUP):
            start = pl.multiple_of(index * REF + half * HALF, HALF)
            lag = pl.program_id(0) * GROUP + index
            shifted[pl.ds(start, HALF), :] = pltpu.roll(long, lag, 1).astype(jnp.bfloat16)
    edge = edge_of(tail)
    for here in columns(held.shape[1]):
        out[:, here] = product_of(shifted, held, edge, here)


def all_products(held, own, other, tail):
    rows, width = held.shape
    vmem = pl.BlockSpec(memory_space=pltpu.VMEM)
    return pl.pallas_call(
        all_products_kernel,
        grid=(LAGS // GROUP,),
        in_specs=[vmem] * 4,
        out_specs=pl.BlockSpec((GROUP * REF, width), lambda group: (group, 0)),
        out_shape=jax.ShapeDtypeStruct((LAGS * REF, width), jnp.float32),
        scratch_shapes=shifted_scratch(rows),
        compiler_params=pltpu.CompilerParams(vmem_limit_bytes=VMEM_BYTES),
        name="all_products",
    )(held, own, other, tail)


def local(strain):
    rows, width = strain.shape
    count = lax.axis_size("tm")
    slab_rows = rows * count
    chunk = LAGS * REF // count

    own, head = prepared(strain)
    other = exchanged(own, "chan", 1)
    tail = passed_along(head, "tm", -1)
    held, power = loaded(strain, own)
    size = width // 4

    if chunk * 2 == GROUP * REF:
        refs = (own, other, tail)
        autos = [segment_rows(held, power, None, 0, size)]
        keep6, send7 = first_products(held, power, *refs, chunk, after=(autos[0],))
        got7 = exchanged(send7, "tm", 1)
        keep4, send5 = later_products(2, held, *refs, send7, chunk)
        got5 = exchanged(send5, "tm", 1)
        autos.append(segment_rows(held, power, tail, size, size, after=(send5,)))
        sends6 = merge_near(keep6, send7, got7)(after=(autos[1],))
        gots6 = [exchanged(code, "tm", 2) for code in sends6]
        keep2, send3 = later_products(1, held, *refs, send7, chunk, after=tuple(sends6))
        got3 = exchanged(send3, "tm", 1)
        sends4, gots4 = [], []
        for part in range(2):
            after = (sends4[0] if part else send3,)
            sends4.append(merge_far(part, keep4, sends6[part], gots6[part], got5, got7, after))
            gots4.append(exchanged(sends4[part], "tm", 4))
        keep0, send1 = later_products(0, held, *refs, send7, chunk, after=(sends4[1],))
        got1 = exchanged(send1, "tm", 1)
        send2 = resent(keep2, got3, got7, sends6, after=(send1,))
        got2 = exchanged(send2, "tm", 2)
        for index in (2, 3):
            autos.append(segment_rows(held, power, tail, size * index, size, after=(send2,)))
        partial, edge = added(keep0, got1, got7, got2, gots6, held, tail, size, after=tuple(autos[2:]))
        return tuple(finished(slab_rows, rows, partial, edge, sends4, gots4, autos))

    chan = lax.axis_index("chan").astype(jnp.int32)
    time = lax.axis_index("tm").astype(jnp.int32)
    auto = jnp.concatenate(
        [segment_rows(held, power, tail, size * index, size) for index in range(4)], axis=1
    )
    power_other = jnp.sum(jnp.square(other.astype(jnp.float32)), axis=1)
    power = lax.psum(jnp.concatenate([power[0], power_other]), "tm")
    inv = 1.0 / jnp.sqrt(power / slab_rows + 1e-06)
    scale = inv[:width]
    ref_scale = jnp.where(
        chan == 0,
        jnp.concatenate([inv[:HALF], inv[width:]]),
        jnp.concatenate([inv[width:], inv[:HALF]]),
    )
    products = all_products(held, own, other, tail)
    summed = lax.psum_scatter(products, "tm", scatter_dimension=0, tiled=True)
    row = time * chunk + jnp.arange(chunk, dtype=jnp.int32)
    row_scale = ref_scale[row % REF] / (slab_rows - row // REF).astype(jnp.float32)
    covariance = summed * scale[None, :] * row_scale[:, None]
    segment_auto = auto * (scale * scale)[None, :] / rows
    return (covariance, segment_auto)


def solution(mesh):
    in_specs = (P(("groups", "tm"), "chan"),)
    out_specs = (P(("groups", "tm"), "chan"), P(("groups", "tm"), "chan"))
    return jax.shard_map(local, mesh=mesh, in_specs=in_specs, out_specs=out_specs, check_vma=False)
```

```python
import jax
import jax.numpy as jnp
from jax import lax
from jax.experimental import pallas as pl
from jax.experimental.pallas import tpu as pltpu
from jax.sharding import PartitionSpec as P

LAGS = 16
REF = 64
HALF = REF // 2
LANES = 128
EXTRA = 8
FETCHES = 8
STEP = 256
GROUP = 4
POWER = 16
CODE_SCALE = 2.0 ** (126 / POWER)
TINY = 1e-35
PIECES = 4
VMEM_BYTES = 32 * 1024 * 1024
HBM_RATE = 3.69e6
PRODUCT_MICROS = 1.0
SEGMENT_MICROS = 1.2
MERGE_MICROS = 0.3


def lasting(micros):
    return pl.CostEstimate(flops=0, bytes_accessed=int(micros * HBM_RATE), transcendentals=0)


def passed_along(value, axis, steps):
    count = lax.axis_size(axis)
    initial, last = (max(0, -steps), min(count, count - steps))
    return lax.ppermute(value, axis, [(source, source + steps) for source in range(initial, last)])


def exchanged(value, axis, bit):
    count = lax.axis_size(axis)
    return lax.ppermute(value, axis, [(source, source ^ bit) for source in range(count)])


def as_column(row):
    size = row.shape[1]
    eye = lax.broadcasted_iota(jnp.int32, (size, size), 0) == lax.broadcasted_iota(jnp.int32, (size, size), 1)
    return jnp.sum(jnp.where(eye, row, 0.0), axis=1, keepdims=True)


def as_row(column):
    size = column.shape[0]
    eye = lax.broadcasted_iota(jnp.int32, (size, size), 0) == lax.broadcasted_iota(jnp.int32, (size, size), 1)
    return jnp.sum(jnp.where(eye, column, 0.0), axis=0, keepdims=True)


def for_chunk(ref_column, rows):
    return jnp.concatenate([ref_column] * (rows // REF), axis=0)


def bf16_pieces(value):
    high = value.astype(jnp.bfloat16).astype(jnp.float32)
    middle = (value - high).astype(jnp.bfloat16).astype(jnp.float32)
    return high, middle, value - high - middle


def packed(powers, ref_powers, channel_bound):
    rows = list(bf16_pieces(powers))
    refs = jnp.concatenate(bf16_pieces(ref_powers), axis=1)
    pad = jnp.zeros((1, powers.shape[1] - refs.shape[1]), jnp.float32)
    rows += [jnp.concatenate([refs, pad], axis=1), channel_bound]
    rows += [jnp.zeros_like(powers)] * (EXTRA - len(rows))
    return jnp.concatenate(rows, axis=0).astype(jnp.bfloat16)


def unpacked(block):
    wide = block.astype(jnp.float32)
    powers = wide[0:1] + wide[1:2] + wide[2:3]
    refs = wide[3:4, :LANES] + wide[3:4, LANES : 2 * LANES] + wide[3:4, 2 * LANES : 3 * LANES]
    return powers, refs, wide[4:5]


def rounded_up(value):
    return (value * (1.0 + 2.0**-7)).astype(jnp.bfloat16).astype(jnp.float32)


def coded(values, channel_bound, ref_bound):
    channel = lax.rsqrt(jnp.maximum(channel_bound, TINY))
    refs = lax.rsqrt(jnp.maximum(ref_bound, TINY)) * CODE_SCALE
    power = values * channel * for_chunk(refs, values.shape[0])
    for _ in range(4):
        power = power * jnp.abs(power)
    return power.astype(jnp.bfloat16)


def expanded(code, channel_bound, ref_bound):
    channel = jnp.sqrt(jnp.maximum(channel_bound, TINY))
    refs = jnp.sqrt(jnp.maximum(ref_bound, TINY)) * (1.0 / CODE_SCALE)
    wide = code[...].astype(jnp.float32)
    root = jnp.exp2(jnp.log2(jnp.abs(wide)) * (1.0 / POWER))
    return jnp.where(wide < 0.0, -root, root) * channel * for_chunk(refs, code.shape[0])


def ref_column(ref_powers):
    return as_column(ref_powers)[:REF]


def prepare_kernel(strain, own, head, left, sems):
    rows = left.shape[0]
    step = rows // PIECES
    copies = [
        pltpu.make_async_copy(
            strain.at[pl.ds(index * step, step), pl.ds(0, LANES)], left.at[pl.ds(index * step, step)], sems.at[index]
        )
        for index in range(PIECES)
    ]
    copies.append(pltpu.make_async_copy(strain.at[pl.ds(0, LAGS)], head, sems.at[PIECES]))
    for copy in copies:
        copy.start()
    for index in range(PIECES):
        copies[index].wait()
        here = slice(index * step, (index + 1) * step)
        own[:, here] = left[here, :].astype(jnp.float32).T[:HALF].astype(jnp.bfloat16)
    copies[PIECES].wait()


def prepared(strain):
    rows, width = strain.shape
    vmem = pl.BlockSpec(memory_space=pltpu.VMEM)
    return pl.pallas_call(
        prepare_kernel,
        in_specs=[pl.BlockSpec(memory_space=pl.ANY)],
        out_specs=[vmem, vmem],
        out_shape=[pltpu.VMEM((HALF, rows), strain.dtype), pltpu.VMEM((LAGS, width), strain.dtype)],
        scratch_shapes=[pltpu.VMEM((rows, LANES), strain.dtype), pltpu.SemaphoreType.DMA((PIECES + 1,))],
        compiler_params=pltpu.CompilerParams(vmem_limit_bytes=VMEM_BYTES),
        cost_estimate=lasting(PRODUCT_MICROS),
        name="prepared",
    )(pltpu.with_memory_space_constraint(strain, pltpu.HBM))


def lag_rows(own, other, group, shifted):
    chan, near = lax.axis_index("chan"), lax.axis_index("tm") & 1
    zeros = jnp.zeros((HALF, LANES), jnp.float32)
    for refs, half in ((own, chan), (other, 1 - chan)):
        long = jnp.concatenate([refs[...].astype(jnp.float32), zeros], axis=1)
        for index in range(GROUP):
            ahead = near if index < GROUP // 2 else 1 - near
            lag = group * GROUP + ahead * (GROUP // 2) + index % (GROUP // 2)
            start = pl.multiple_of(index * REF + half * HALF, HALF)
            shifted[pl.ds(start, HALF), :] = pltpu.roll(long, lag, 1).astype(jnp.bfloat16)


def own_group(bits):
    return lax.shift_right_logical(lax.axis_index("tm").astype(jnp.int32), 1) ^ bits


def loaded_kernel(strain, held, power, sems):
    step = held.shape[0] // FETCHES
    pieces = [slice(index * step, (index + 1) * step) for index in range(FETCHES)]
    copies = [
        pltpu.make_async_copy(strain.at[pl.ds(here.start, step)], held.at[pl.ds(here.start, step)], sems.at[index])
        for index, here in enumerate(pieces)
    ]
    for copy in copies:
        copy.start()
    total = jnp.zeros((8, held.shape[1]), jnp.float32)
    for copy, here in zip(copies, pieces):
        copy.wait()
        squares = jnp.square(held[here, :].astype(jnp.float32))
        total += jnp.sum(squares.reshape(step // 8, 8, held.shape[1]), axis=0)
    power[...] = jnp.sum(total, axis=0, keepdims=True)


def loaded(strain, after):
    rows, width = strain.shape
    vmem = pl.BlockSpec(memory_space=pltpu.VMEM)

    def kernel(strain, after, held, power, sems):
        loaded_kernel(strain, held, power, sems)

    return pl.pallas_call(
        kernel,
        in_specs=[pl.BlockSpec(memory_space=pl.ANY)] * 2,
        out_specs=[vmem, vmem],
        out_shape=[pltpu.VMEM((rows, width), strain.dtype), pltpu.VMEM((1, width), jnp.float32)],
        scratch_shapes=[pltpu.SemaphoreType.DMA((FETCHES,))],
        compiler_params=pltpu.CompilerParams(vmem_limit_bytes=VMEM_BYTES),
        cost_estimate=lasting(PRODUCT_MICROS),
        name="loaded",
    )(pltpu.with_memory_space_constraint(strain, pltpu.HBM), after)


def edge_of(tail):
    return jnp.concatenate([tail[...], jnp.zeros((LANES - LAGS, tail.shape[1]), tail.dtype)], axis=0)


def product_of(shifted, held, edge, here):
    rows = held.shape[0]
    total = jnp.dot(shifted[:, rows:], edge[:, here], preferred_element_type=jnp.float32)
    return total + jnp.dot(shifted[:, :rows], held[:, here], preferred_element_type=jnp.float32)


def columns(width):
    return [slice(first, first + STEP) for first in range(0, width, STEP)]


def first_products_kernel(held, power, own, other, tail, keep, send, shifted):
    lag_rows(own, other, own_group(3), shifted)
    ours, theirs = [
        jnp.sum(jnp.square(refs[...].astype(jnp.float32)), axis=1, keepdims=True) for refs in (own, other)
    ]
    refs = jnp.where(
        lax.axis_index("chan") == 0,
        jnp.concatenate([ours, theirs], axis=0),
        jnp.concatenate([theirs, ours], axis=0),
    )
    beyond = jnp.sum(jnp.square(tail[...].astype(jnp.float32)), axis=0, keepdims=True)
    bound = rounded_up(power[...] + beyond)
    pad = jnp.zeros((1, LANES - REF), jnp.float32)
    chunk = keep.shape[0]
    send[chunk:] = packed(power[...], jnp.concatenate([as_row(refs), pad], axis=1), bound)
    edge = edge_of(tail)
    for here in columns(held.shape[1]):
        product = product_of(shifted, held, edge, here)
        keep[:, here] = product[:chunk]
        send[:chunk, here] = coded(product[chunk:], bound[:, here], refs)


def shifted_scratch(rows):
    return [pltpu.VMEM((GROUP * REF, rows + LANES), jnp.bfloat16)]


def first_products(held, power, own, other, tail, chunk, after):
    rows, width = held.shape
    outs = [
        ((chunk, width), jnp.float32),
        ((chunk + EXTRA, width), jnp.bfloat16),
    ]
    return call_on_blocks(
        first_products_kernel,
        outs,
        held,
        power,
        own,
        other,
        tail,
        name="first_products",
        micros=PRODUCT_MICROS,
        after=after,
        scratch=shifted_scratch(rows),
    )


def later_products(bits, held, own, other, tail, powers, chunk, after=()):
    rows, width = held.shape

    def kernel(held, own, other, tail, powers, keep, first, second, shifted):
        _, ref_powers, bound = sent_powers(powers)
        refs = ref_column(ref_powers)
        lag_rows(own, other, own_group(bits), shifted)
        edge = edge_of(tail)
        for here in columns(width):
            product = product_of(shifted, held, edge, here)
            keep[:, here] = product[:chunk]
            part, start = divmod(here.start, width // 2)
            send = (first, second)[part]
            send[:, start : start + STEP] = coded(product[chunk:], bound[:, here], refs)

    half = ((chunk, width // 2), jnp.bfloat16)
    keep, *sends = call_on_blocks(
        kernel,
        [((chunk, width), jnp.float32), half, half],
        held,
        own,
        other,
        tail,
        powers,
        name="later_products",
        micros=PRODUCT_MICROS,
        after=after,
        scratch=shifted_scratch(rows),
    )
    return keep, sends


def call_on_blocks(kernel, outs, *arrays, name, micros, after=(), scratch=(), space=pltpu.VMEM):
    vmem = pl.BlockSpec(memory_space=pltpu.VMEM)
    count = len(arrays)

    def body(*refs):
        kernel(*refs[:count], *refs[count + len(after) :])

    return pl.pallas_call(
        body,
        in_specs=[vmem] * count + [pl.BlockSpec(memory_space=pl.ANY)] * len(after),
        out_specs=[vmem] * len(outs),
        out_shape=[space(shape, dtype) for shape, dtype in outs],
        scratch_shapes=list(scratch),
        compiler_params=pltpu.CompilerParams(vmem_limit_bytes=VMEM_BYTES),
        cost_estimate=lasting(micros),
        name=name,
    )(*arrays, *after)


def half_of(width, part):
    return slice(part * width // 2, (part + 1) * width // 2)


def sent_powers(code, here=slice(None)):
    powers, refs, bound = unpacked(code[-EXTRA:])
    return powers[:, here], refs, bound[:, here]


def merge_near(keep, ours, theirs, after):
    chunk, width = keep.shape

    def kernel(keep, ours, theirs, *outs):
        for part, out in enumerate(outs):
            here = half_of(width, part)
            powers, refs, bound = sent_powers(ours, here)
            their_powers, their_refs, their_bound = sent_powers(theirs, here)
            total = keep[:, here] + expanded(theirs[:chunk, here], their_bound, ref_column(their_refs))
            sums, sum_refs, sum_bound = powers + their_powers, refs + their_refs, rounded_up(bound + their_bound)
            out[chunk:] = packed(sums, sum_refs, sum_bound)
            out[:chunk] = coded(total, sum_bound, ref_column(sum_refs))

    outs = [((chunk + EXTRA, width // 2), jnp.bfloat16)] * 2
    return call_on_blocks(
        kernel, outs, keep, ours, theirs, name="merge_near", micros=MERGE_MICROS, after=after
    )


def merge_far(part, keep, ours, theirs, direct, direct_powers, after):
    chunk, width = keep.shape
    here = half_of(width, part)

    def kernel(keep, ours, theirs, direct, direct_powers, out):
        powers, refs, bound = sent_powers(ours)
        their_powers, their_refs, their_bound = sent_powers(theirs)
        total = keep[:, here] + expanded(theirs[:chunk], their_bound, ref_column(their_refs))
        _, direct_refs, direct_bound = sent_powers(direct_powers, here)
        total += expanded(direct, direct_bound, ref_column(direct_refs))
        sums, sum_refs, sum_bound = powers + their_powers, refs + their_refs, rounded_up(bound + their_bound)
        out[chunk:] = packed(sums, sum_refs, sum_bound)
        out[:chunk] = coded(total, sum_bound, ref_column(sum_refs))

    outs = [((chunk + EXTRA, width // 2), jnp.bfloat16)]
    return call_on_blocks(
        kernel, outs, keep, ours, theirs, direct, direct_powers, name="merge_far", micros=MERGE_MICROS, after=after
    )[0]


def resent(keep, direct, direct_powers, ours, after):
    chunk, width = keep.shape

    def kernel(keep, direct_powers, *refs):
        direct, ours, outs = refs[:2], refs[2:4], refs[4:]
        for part in range(2):
            here = half_of(width, part)
            _, direct_refs, direct_bound = sent_powers(direct_powers, here)
            _, refs, bound = sent_powers(ours[part])
            total = keep[:, here] + expanded(direct[part], direct_bound, ref_column(direct_refs))
            outs[part][...] = coded(total, bound, ref_column(refs))

    outs = [((chunk, width // 2), jnp.bfloat16)] * 2
    return call_on_blocks(
        kernel, outs, keep, direct_powers, *direct, *ours, name="resent", micros=MERGE_MICROS, after=after
    )


def added(keep, direct, direct_powers, near, near_powers, held, tail, size, after):
    rows, width = held.shape

    def kernel(keep, direct_powers, held, tail, *refs):
        direct, near, near_powers, (out, edge) = refs[:2], refs[2:4], refs[4:6], refs[6:]
        for part in range(2):
            here = half_of(width, part)
            _, direct_refs, direct_bound = sent_powers(direct_powers, here)
            _, near_refs, near_bound = sent_powers(near_powers[part])
            total = keep[:, here] + expanded(direct[part], direct_bound, ref_column(direct_refs))
            out[:, here] = total + expanded(near[part], near_bound, ref_column(near_refs))
        last = held[rows - LAGS :, :size].astype(jnp.float32)
        beyond = tail[:, :size].astype(jnp.float32)
        place = lax.broadcasted_iota(jnp.int32, last.shape, 0)
        sums = [jnp.zeros((1, size), jnp.float32)]
        for lag in range(1, LAGS):
            pairs = jnp.where(place >= LAGS - lag, last * pltpu.roll(beyond, LAGS - lag, 0), 0.0)
            sums.append(jnp.sum(pairs, axis=0, keepdims=True))
        edge[...] = jnp.concatenate(sums, axis=0)

    outs = [(keep.shape, jnp.float32), ((LAGS, size), jnp.float32)]
    arrays = (keep, direct_powers, held, tail, *direct, *near, *near_powers)
    return call_on_blocks(kernel, outs, *arrays, name="added", micros=MERGE_MICROS, after=after)


def finished(slab_rows, segment, partial, edge, ours, theirs, autos):
    chunk, width = partial.shape

    def kernel(partial, edge, *refs):
        ours, theirs, autos, (covariance, segment_auto) = refs[:2], refs[2:4], refs[4:-2], refs[-2:]
        first_lag = lax.axis_index("tm").astype(jnp.int32) * (chunk // REF)
        lag = lax.broadcasted_iota(jnp.int32, (chunk, 1), 0) // REF + first_lag
        denom = (slab_rows - lag).astype(jnp.float32)
        size = width // len(autos)
        for part in range(2):
            here = half_of(width, part)
            powers, own_refs, _ = sent_powers(ours[part])
            their_powers, their_refs, their_bound = sent_powers(theirs[part])
            total = partial[:, here] + expanded(theirs[part][:chunk], their_bound, ref_column(their_refs))
            scale = 1.0 / jnp.sqrt((powers + their_powers) / slab_rows + 1e-06)
            ref_scale = 1.0 / jnp.sqrt(ref_column(own_refs + their_refs) / slab_rows + 1e-06)
            covariance[:, here] = total * scale * (for_chunk(ref_scale, chunk) / denom)
            for index in range(len(autos)):
                first = index * size - here.start
                if 0 <= first < width // 2:
                    auto = autos[index][...] + edge[...] if index == 0 else autos[index][...]
                    own_scale = scale[:, first : first + size]
                    segment_auto[:, index * size : (index + 1) * size] = auto * (own_scale * own_scale) / segment

    outs = [(partial.shape, jnp.float32), ((LAGS, width), jnp.float32)]
    return call_on_blocks(
        kernel, outs, partial, edge, *ours, *theirs, *autos, name="finished", micros=MERGE_MICROS, space=jax.ShapeDtypeStruct
    )


def segment_kernel(first, held, power, tail, out, wide):
    rows = held.shape[0]
    step = rows // 8
    pitch = step + LAGS
    for index in range(out.shape[1] // LANES):
        here = slice(first + index * LANES, first + (index + 1) * LANES)
        there = slice(index * LANES, (index + 1) * LANES)
        for part in range(8):
            end = (part + 1) * step
            wide[part * pitch : part * pitch + step, :] = held[end - step : end, here].astype(jnp.float32)
            if part < 7:
                following = held[end : end + LAGS, here].astype(jnp.float32)
            elif tail is None:
                following = jnp.zeros((LAGS, LANES), jnp.float32)
            else:
                following = tail[:, here].astype(jnp.float32)
            wide[part * pitch + step : (part + 1) * pitch, :] = following
        taken = lambda first: wide[pl.ds(first, 8, stride=pitch), :]

        def advance(index, carry):
            window, sums = carry
            window = window + (taken(index + LAGS - 1),)
            sums = tuple(total + window[0] * window[lag + 1] for lag, total in enumerate(sums))
            return window[1:], sums

        window = tuple(taken(first) for first in range(LAGS - 1))
        zero = jnp.zeros((8, LANES), jnp.float32)
        _, sums = lax.fori_loop(0, step, advance, (window, (zero,) * (LAGS - 1)), unroll=16)
        out[:, there] = jnp.concatenate(
            [power[:, here]] + [jnp.sum(total, axis=0, keepdims=True) for total in sums], axis=0
        )


def segment_rows(held, power, tail, first, size, after=()):
    rows = held.shape[0]
    arrays = (held, power) if tail is None else (held, power, tail)

    def kernel(*refs):
        held, power, *rest = refs
        if tail is None:
            rest = [None] + rest
        segment_kernel(first, held, power, *rest)

    return call_on_blocks(
        kernel,
        [((LAGS, size), jnp.float32)],
        *arrays,
        name="segment_rows",
        micros=SEGMENT_MICROS,
        after=after,
        scratch=[pltpu.VMEM((rows + 8 * LAGS, LANES), jnp.float32)],
    )[0]


def all_products_kernel(held, own, other, tail, out, shifted):
    chan = lax.axis_index("chan")
    zeros = jnp.zeros((HALF, LANES), jnp.float32)
    for refs, half in ((own, chan), (other, 1 - chan)):
        long = jnp.concatenate([refs[...].astype(jnp.float32), zeros], axis=1)
        for index in range(GROUP):
            start = pl.multiple_of(index * REF + half * HALF, HALF)
            lag = pl.program_id(0) * GROUP + index
            shifted[pl.ds(start, HALF), :] = pltpu.roll(long, lag, 1).astype(jnp.bfloat16)
    edge = edge_of(tail)
    for here in columns(held.shape[1]):
        out[:, here] = product_of(shifted, held, edge, here)


def all_products(held, own, other, tail):
    rows, width = held.shape
    vmem = pl.BlockSpec(memory_space=pltpu.VMEM)
    return pl.pallas_call(
        all_products_kernel,
        grid=(LAGS // GROUP,),
        in_specs=[vmem] * 4,
        out_specs=pl.BlockSpec((GROUP * REF, width), lambda group: (group, 0)),
        out_shape=jax.ShapeDtypeStruct((LAGS * REF, width), jnp.float32),
        scratch_shapes=shifted_scratch(rows),
        compiler_params=pltpu.CompilerParams(vmem_limit_bytes=VMEM_BYTES),
        name="all_products",
    )(held, own, other, tail)


def local(strain):
    rows, width = strain.shape
    count = lax.axis_size("tm")
    slab_rows = rows * count
    chunk = LAGS * REF // count

    own, head = prepared(strain)
    other = exchanged(own, "chan", 1)
    tail = passed_along(head, "tm", -1)
    held, power = loaded(strain, own)
    size = width // 4

    if chunk * 2 == GROUP * REF:
        refs = (own, other, tail)
        autos = [segment_rows(held, power, None, 0, size)]
        keep6, send7 = first_products(held, power, *refs, chunk, after=(autos[0],))
        got7 = exchanged(send7, "tm", 1)
        keep4, sends5 = later_products(2, held, *refs, send7, chunk)
        gots5 = [exchanged(code, "tm", 1) for code in sends5]
        autos.append(segment_rows(held, power, tail, size, size, after=tuple(sends5)))
        sends6 = merge_near(keep6, send7, got7, after=(autos[1],))
        gots6 = [exchanged(code, "tm", 2) for code in sends6]
        keep2, sends3 = later_products(1, held, *refs, send7, chunk, after=tuple(sends6))
        gots3 = [exchanged(code, "tm", 1) for code in sends3]
        keep0, sends1 = later_products(0, held, *refs, send7, chunk, after=tuple(sends3))
        gots1 = [exchanged(code, "tm", 1) for code in sends1]
        sends4, gots4 = [], []
        for part in range(2):
            after = (sends4[0] if part else sends1[0],)
            sends4.append(merge_far(part, keep4, sends6[part], gots6[part], gots5[part], got7, after))
            gots4.append(exchanged(sends4[part], "tm", 4))
        sends2 = resent(keep2, gots3, got7, sends6, after=(sends4[1],))
        gots2 = [exchanged(code, "tm", 2) for code in sends2]
        for index in (2, 3):
            autos.append(segment_rows(held, power, tail, size * index, size, after=tuple(sends2)))
        partial, edge = added(keep0, gots1, got7, gots2, gots6, held, tail, size, after=tuple(autos[2:]))
        return tuple(finished(slab_rows, rows, partial, edge, sends4, gots4, autos))

    chan = lax.axis_index("chan").astype(jnp.int32)
    time = lax.axis_index("tm").astype(jnp.int32)
    auto = jnp.concatenate(
        [segment_rows(held, power, tail, size * index, size) for index in range(4)], axis=1
    )
    power_other = jnp.sum(jnp.square(other.astype(jnp.float32)), axis=1)
    power = lax.psum(jnp.concatenate([power[0], power_other]), "tm")
    inv = 1.0 / jnp.sqrt(power / slab_rows + 1e-06)
    scale = inv[:width]
    ref_scale = jnp.where(
        chan == 0,
        jnp.concatenate([inv[:HALF], inv[width:]]),
        jnp.concatenate([inv[width:], inv[:HALF]]),
    )
    products = all_products(held, own, other, tail)
    summed = lax.psum_scatter(products, "tm", scatter_dimension=0, tiled=True)
    row = time * chunk + jnp.arange(chunk, dtype=jnp.int32)
    row_scale = ref_scale[row % REF] / (slab_rows - row // REF).astype(jnp.float32)
    covariance = summed * scale[None, :] * row_scale[:, None]
    segment_auto = auto * (scale * scale)[None, :] / rows
    return (covariance, segment_auto)


def solution(mesh):
    in_specs = (P(("groups", "tm"), "chan"),)
    out_specs = (P(("groups", "tm"), "chan"), P(("groups", "tm"), "chan"))
    return jax.shard_map(local, mesh=mesh, in_specs=in_specs, out_specs=out_specs, check_vma=False)
```

```python
import jax
import jax.numpy as jnp
from jax import lax
from jax.experimental import pallas as pl
from jax.experimental.pallas import tpu as pltpu
from jax.sharding import PartitionSpec as P

LAGS = 16
REF = 64
HALF = REF // 2
LANES = 128
EXTRA = 8
FETCHES = 8
STEP = 256
GROUP = 4
POWER = 16
CODE_SCALE = 2.0 ** (126 / POWER)
TINY = 1e-35
PIECES = 4
VMEM_BYTES = 32 * 1024 * 1024
HBM_RATE = 3.69e6
PRODUCT_MICROS = 1.0
SEGMENT_MICROS = 1.2
MERGE_MICROS = 0.3


def lasting(micros):
    return pl.CostEstimate(flops=0, bytes_accessed=int(micros * HBM_RATE), transcendentals=0)


def passed_along(value, axis, steps):
    count = lax.axis_size(axis)
    initial, last = (max(0, -steps), min(count, count - steps))
    return lax.ppermute(value, axis, [(source, source + steps) for source in range(initial, last)])


def exchanged(value, axis, bit):
    count = lax.axis_size(axis)
    return lax.ppermute(value, axis, [(source, source ^ bit) for source in range(count)])


def as_column(row):
    size = row.shape[1]
    eye = lax.broadcasted_iota(jnp.int32, (size, size), 0) == lax.broadcasted_iota(jnp.int32, (size, size), 1)
    return jnp.sum(jnp.where(eye, row, 0.0), axis=1, keepdims=True)


def as_row(column):
    size = column.shape[0]
    eye = lax.broadcasted_iota(jnp.int32, (size, size), 0) == lax.broadcasted_iota(jnp.int32, (size, size), 1)
    return jnp.sum(jnp.where(eye, column, 0.0), axis=0, keepdims=True)


def for_chunk(ref_column, rows):
    return jnp.concatenate([ref_column] * (rows // REF), axis=0)


def bf16_pieces(value):
    high = value.astype(jnp.bfloat16).astype(jnp.float32)
    middle = (value - high).astype(jnp.bfloat16).astype(jnp.float32)
    return high, middle, value - high - middle


def packed(powers, ref_powers, channel_bound):
    rows = list(bf16_pieces(powers))
    refs = jnp.concatenate(bf16_pieces(ref_powers), axis=1)
    pad = jnp.zeros((1, powers.shape[1] - refs.shape[1]), jnp.float32)
    rows += [jnp.concatenate([refs, pad], axis=1), channel_bound]
    rows += [jnp.zeros_like(powers)] * (EXTRA - len(rows))
    return jnp.concatenate(rows, axis=0).astype(jnp.bfloat16)


def unpacked(block):
    wide = block.astype(jnp.float32)
    powers = wide[0:1] + wide[1:2] + wide[2:3]
    refs = wide[3:4, :LANES] + wide[3:4, LANES : 2 * LANES] + wide[3:4, 2 * LANES : 3 * LANES]
    return powers, refs, wide[4:5]


def rounded_up(value):
    return (value * (1.0 + 2.0**-7)).astype(jnp.bfloat16).astype(jnp.float32)


def coded(values, channel_bound, ref_bound):
    channel = lax.rsqrt(jnp.maximum(channel_bound, TINY))
    refs = lax.rsqrt(jnp.maximum(ref_bound, TINY)) * CODE_SCALE
    power = values * channel * for_chunk(refs, values.shape[0])
    for _ in range(4):
        power = power * jnp.abs(power)
    return power.astype(jnp.bfloat16)


def expanded(code, channel_bound, ref_bound):
    channel = jnp.sqrt(jnp.maximum(channel_bound, TINY))
    refs = jnp.sqrt(jnp.maximum(ref_bound, TINY)) * (1.0 / CODE_SCALE)
    wide = code[...].astype(jnp.float32)
    root = jnp.exp2(jnp.log2(jnp.abs(wide)) * (1.0 / POWER))
    return jnp.where(wide < 0.0, -root, root) * channel * for_chunk(refs, code.shape[0])


def ref_column(ref_powers):
    return as_column(ref_powers)[:REF]


def prepare_kernel(strain, own, head, left, sems):
    rows = left.shape[0]
    step = rows // PIECES
    copies = [
        pltpu.make_async_copy(
            strain.at[pl.ds(index * step, step), pl.ds(0, LANES)], left.at[pl.ds(index * step, step)], sems.at[index]
        )
        for index in range(PIECES)
    ]
    copies.append(pltpu.make_async_copy(strain.at[pl.ds(0, LAGS)], head, sems.at[PIECES]))
    for copy in copies:
        copy.start()
    for index in range(PIECES):
        copies[index].wait()
        here = slice(index * step, (index + 1) * step)
        own[:, here] = left[here, :].astype(jnp.float32).T[:HALF].astype(jnp.bfloat16)
    copies[PIECES].wait()


def prepared(strain):
    rows, width = strain.shape
    vmem = pl.BlockSpec(memory_space=pltpu.VMEM)
    return pl.pallas_call(
        prepare_kernel,
        in_specs=[pl.BlockSpec(memory_space=pl.ANY)],
        out_specs=[vmem, vmem],
        out_shape=[pltpu.VMEM((HALF, rows), strain.dtype), pltpu.VMEM((LAGS, width), strain.dtype)],
        scratch_shapes=[pltpu.VMEM((rows, LANES), strain.dtype), pltpu.SemaphoreType.DMA((PIECES + 1,))],
        compiler_params=pltpu.CompilerParams(vmem_limit_bytes=VMEM_BYTES),
        cost_estimate=lasting(PRODUCT_MICROS),
        name="prepared",
    )(pltpu.with_memory_space_constraint(strain, pltpu.HBM))


def lag_rows(own, other, group, shifted):
    chan, near = lax.axis_index("chan"), lax.axis_index("tm") & 1
    zeros = jnp.zeros((HALF, LANES), jnp.float32)
    for refs, half in ((own, chan), (other, 1 - chan)):
        long = jnp.concatenate([refs[...].astype(jnp.float32), zeros], axis=1)
        for index in range(GROUP):
            ahead = near if index < GROUP // 2 else 1 - near
            lag = group * GROUP + ahead * (GROUP // 2) + index % (GROUP // 2)
            start = pl.multiple_of(index * REF + half * HALF, HALF)
            shifted[pl.ds(start, HALF), :] = pltpu.roll(long, lag, 1).astype(jnp.bfloat16)


def own_group(bits):
    return lax.shift_right_logical(lax.axis_index("tm").astype(jnp.int32), 1) ^ bits


def loaded_kernel(strain, held, power, sems):
    step = held.shape[0] // FETCHES
    pieces = [slice(index * step, (index + 1) * step) for index in range(FETCHES)]
    copies = [
        pltpu.make_async_copy(strain.at[pl.ds(here.start, step)], held.at[pl.ds(here.start, step)], sems.at[index])
        for index, here in enumerate(pieces)
    ]
    for copy in copies:
        copy.start()
    total = jnp.zeros((8, held.shape[1]), jnp.float32)
    for copy, here in zip(copies, pieces):
        copy.wait()
        squares = jnp.square(held[here, :].astype(jnp.float32))
        total += jnp.sum(squares.reshape(step // 8, 8, held.shape[1]), axis=0)
    power[...] = jnp.sum(total, axis=0, keepdims=True)


def loaded(strain, after):
    rows, width = strain.shape
    vmem = pl.BlockSpec(memory_space=pltpu.VMEM)

    def kernel(strain, after, held, power, sems):
        loaded_kernel(strain, held, power, sems)

    return pl.pallas_call(
        kernel,
        in_specs=[pl.BlockSpec(memory_space=pl.ANY)] * 2,
        out_specs=[vmem, vmem],
        out_shape=[pltpu.VMEM((rows, width), strain.dtype), pltpu.VMEM((1, width), jnp.float32)],
        scratch_shapes=[pltpu.SemaphoreType.DMA((FETCHES,))],
        compiler_params=pltpu.CompilerParams(vmem_limit_bytes=VMEM_BYTES),
        cost_estimate=lasting(PRODUCT_MICROS),
        name="loaded",
    )(pltpu.with_memory_space_constraint(strain, pltpu.HBM), after)


def edge_of(tail):
    return jnp.concatenate([tail[...], jnp.zeros((LANES - LAGS, tail.shape[1]), tail.dtype)], axis=0)


def product_of(shifted, held, edge, here):
    rows = held.shape[0]
    total = jnp.dot(shifted[:, rows:], edge[:, here], preferred_element_type=jnp.float32)
    return total + jnp.dot(shifted[:, :rows], held[:, here], preferred_element_type=jnp.float32)


def columns(width):
    return [slice(first, first + STEP) for first in range(0, width, STEP)]


def first_products_kernel(held, power, own, other, tail, keep, send, shifted):
    lag_rows(own, other, own_group(3), shifted)
    ours, theirs = [
        jnp.sum(jnp.square(refs[...].astype(jnp.float32)), axis=1, keepdims=True) for refs in (own, other)
    ]
    refs = jnp.where(
        lax.axis_index("chan") == 0,
        jnp.concatenate([ours, theirs], axis=0),
        jnp.concatenate([theirs, ours], axis=0),
    )
    beyond = jnp.sum(jnp.square(tail[...].astype(jnp.float32)), axis=0, keepdims=True)
    bound = rounded_up(power[...] + beyond)
    pad = jnp.zeros((1, LANES - REF), jnp.float32)
    chunk = keep.shape[0]
    send[chunk:] = packed(power[...], jnp.concatenate([as_row(refs), pad], axis=1), bound)
    edge = edge_of(tail)
    for here in columns(held.shape[1]):
        product = product_of(shifted, held, edge, here)
        keep[:, here] = product[:chunk]
        send[:chunk, here] = coded(product[chunk:], bound[:, here], refs)


def shifted_scratch(rows, groups=1):
    return [pltpu.VMEM((groups * GROUP * REF, rows + LANES), jnp.bfloat16)]


def first_products(held, power, own, other, tail, chunk, after):
    rows, width = held.shape
    outs = [
        ((chunk, width), jnp.float32),
        ((chunk + EXTRA, width), jnp.bfloat16),
    ]
    return call_on_blocks(
        first_products_kernel,
        outs,
        held,
        power,
        own,
        other,
        tail,
        name="first_products",
        micros=PRODUCT_MICROS,
        after=after,
        scratch=shifted_scratch(rows),
    )


def later_products(groups, held, own, other, tail, powers, chunk, after=()):
    rows, width = held.shape

    def kernel(held, own, other, tail, powers, *rest):
        outs, shifted = rest[:-1], rest[-1]
        _, ref_powers, bound = sent_powers(powers)
        refs = ref_column(ref_powers)
        for index, bits in enumerate(groups):
            lag_rows(own, other, own_group(bits), shifted.at[pl.ds(index * 2 * chunk, 2 * chunk)])
        edge = edge_of(tail)
        for here in columns(width):
            product = product_of(shifted, held, edge, here)
            for index in range(len(groups)):
                keep, send = outs[2 * index : 2 * index + 2]
                first = 2 * index * chunk
                keep[:, here] = product[first : first + chunk]
                send[:, here] = coded(product[first + chunk : first + 2 * chunk], bound[:, here], refs)

    return call_on_blocks(
        kernel,
        [((chunk, width), jnp.float32), ((chunk, width), jnp.bfloat16)] * len(groups),
        held,
        own,
        other,
        tail,
        powers,
        name="later_products",
        micros=PRODUCT_MICROS,
        after=after,
        scratch=shifted_scratch(rows, len(groups)),
    )


def call_on_blocks(kernel, outs, *arrays, name, micros, after=(), scratch=(), space=pltpu.VMEM):
    vmem = pl.BlockSpec(memory_space=pltpu.VMEM)
    count = len(arrays)

    def body(*refs):
        kernel(*refs[:count], *refs[count + len(after) :])

    return pl.pallas_call(
        body,
        in_specs=[vmem] * count + [pl.BlockSpec(memory_space=pl.ANY)] * len(after),
        out_specs=[vmem] * len(outs),
        out_shape=[space(shape, dtype) for shape, dtype in outs],
        scratch_shapes=list(scratch),
        compiler_params=pltpu.CompilerParams(vmem_limit_bytes=VMEM_BYTES),
        cost_estimate=lasting(micros),
        name=name,
    )(*arrays, *after)


def half_of(width, part):
    return slice(part * width // 2, (part + 1) * width // 2)


def sent_powers(code, here=slice(None)):
    powers, refs, bound = unpacked(code[-EXTRA:])
    return powers[:, here], refs, bound[:, here]


def merge_near(keep, ours, theirs, held_back, after):
    chunk, width = keep.shape

    def kernel(keep, ours, theirs, held_back, *outs):
        outs[2][...] = held_back[...]
        for part, out in enumerate(outs[:2]):
            here = half_of(width, part)
            powers, refs, bound = sent_powers(ours, here)
            their_powers, their_refs, their_bound = sent_powers(theirs, here)
            total = keep[:, here] + expanded(theirs[:chunk, here], their_bound, ref_column(their_refs))
            sums, sum_refs, sum_bound = powers + their_powers, refs + their_refs, rounded_up(bound + their_bound)
            out[chunk:] = packed(sums, sum_refs, sum_bound)
            out[:chunk] = coded(total, sum_bound, ref_column(sum_refs))

    outs = [((chunk + EXTRA, width // 2), jnp.bfloat16)] * 2 + [(held_back.shape, jnp.bfloat16)]
    return call_on_blocks(
        kernel, outs, keep, ours, theirs, held_back, name="merge_near", micros=MERGE_MICROS, after=after
    )


def merge_far(part, keep, ours, theirs, direct, direct_powers, *held_back, after):
    chunk, width = keep.shape
    here = half_of(width, part)

    def kernel(keep, ours, theirs, direct, direct_powers, *rest):
        out = rest[len(held_back)]
        if held_back:
            rest[2][...] = rest[0][...]
        powers, refs, bound = sent_powers(ours)
        their_powers, their_refs, their_bound = sent_powers(theirs)
        total = keep[:, here] + expanded(theirs[:chunk], their_bound, ref_column(their_refs))
        _, direct_refs, direct_bound = sent_powers(direct_powers, here)
        total += expanded(direct[:, here], direct_bound, ref_column(direct_refs))
        sums, sum_refs, sum_bound = powers + their_powers, refs + their_refs, rounded_up(bound + their_bound)
        out[chunk:] = packed(sums, sum_refs, sum_bound)
        out[:chunk] = coded(total, sum_bound, ref_column(sum_refs))

    outs = [((chunk + EXTRA, width // 2), jnp.bfloat16)] + [(array.shape, jnp.bfloat16) for array in held_back]
    arrays = (keep, ours, theirs, direct, direct_powers, *held_back)
    return call_on_blocks(kernel, outs, *arrays, name="merge_far", micros=MERGE_MICROS, after=after)


def resent(keep, direct, direct_powers, ours, after):
    chunk, width = keep.shape

    def kernel(keep, direct, direct_powers, first, second, *outs):
        for part, powers in enumerate((first, second)):
            here = half_of(width, part)
            _, direct_refs, direct_bound = sent_powers(direct_powers, here)
            _, refs, bound = sent_powers(powers)
            total = keep[:, here] + expanded(direct[:, here], direct_bound, ref_column(direct_refs))
            outs[part][...] = coded(total, bound, ref_column(refs))

    outs = [((chunk, width // 2), jnp.bfloat16)] * 2
    arrays = (keep, direct, direct_powers, *ours)
    return call_on_blocks(kernel, outs, *arrays, name="resent", micros=MERGE_MICROS, after=after)


def added(keep, direct, direct_powers, near, near_powers, held, tail, size, after):
    rows, width = held.shape

    def kernel(keep, direct, direct_powers, held, tail, *refs):
        near, near_powers, (out, edge) = refs[:2], refs[2:4], refs[4:]
        for part in range(2):
            here = half_of(width, part)
            _, direct_refs, direct_bound = sent_powers(direct_powers, here)
            _, near_refs, near_bound = sent_powers(near_powers[part])
            total = keep[:, here] + expanded(direct[:, here], direct_bound, ref_column(direct_refs))
            out[:, here] = total + expanded(near[part], near_bound, ref_column(near_refs))
        last = held[rows - LAGS :, :size].astype(jnp.float32)
        beyond = tail[:, :size].astype(jnp.float32)
        place = lax.broadcasted_iota(jnp.int32, last.shape, 0)
        sums = [jnp.zeros((1, size), jnp.float32)]
        for lag in range(1, LAGS):
            pairs = jnp.where(place >= LAGS - lag, last * pltpu.roll(beyond, LAGS - lag, 0), 0.0)
            sums.append(jnp.sum(pairs, axis=0, keepdims=True))
        edge[...] = jnp.concatenate(sums, axis=0)

    outs = [(keep.shape, jnp.float32), ((LAGS, size), jnp.float32)]
    arrays = (keep, direct, direct_powers, held, tail, *near, *near_powers)
    return call_on_blocks(kernel, outs, *arrays, name="added", micros=MERGE_MICROS, after=after)


def finished(slab_rows, segment, partial, edge, ours, theirs, autos):
    chunk, width = partial.shape

    def kernel(partial, edge, *refs):
        ours, theirs, autos, (covariance, segment_auto) = refs[:2], refs[2:4], refs[4:-2], refs[-2:]
        first_lag = lax.axis_index("tm").astype(jnp.int32) * (chunk // REF)
        lag = lax.broadcasted_iota(jnp.int32, (chunk, 1), 0) // REF + first_lag
        denom = (slab_rows - lag).astype(jnp.float32)
        for part in range(2):
            here = half_of(width, part)
            powers, own_refs, _ = sent_powers(ours[part])
            their_powers, their_refs, their_bound = sent_powers(theirs[part])
            total = partial[:, here] + expanded(theirs[part][:chunk], their_bound, ref_column(their_refs))
            scale = 1.0 / jnp.sqrt((powers + their_powers) / slab_rows + 1e-06)
            ref_scale = 1.0 / jnp.sqrt(ref_column(own_refs + their_refs) / slab_rows + 1e-06)
            covariance[:, here] = total * scale * (for_chunk(ref_scale, chunk) / denom)
            first = 0
            for auto in autos:
                size = auto.shape[1]
                if here.start <= first < here.stop:
                    own_scale = scale[:, first - here.start : first - here.start + size]
                    sums = auto[...] + edge[...] if first == 0 else auto[...]
                    segment_auto[:, first : first + size] = sums * (own_scale * own_scale) / segment
                first += size

    outs = [(partial.shape, jnp.float32), ((LAGS, width), jnp.float32)]
    return call_on_blocks(
        kernel, outs, partial, edge, *ours, *theirs, *autos, name="finished", micros=MERGE_MICROS, space=jax.ShapeDtypeStruct
    )


def segment_kernel(first, held, power, tail, out, wide):
    rows = held.shape[0]
    step = rows // 8
    pitch = step + LAGS
    for index in range(out.shape[1] // LANES):
        here = slice(first + index * LANES, first + (index + 1) * LANES)
        there = slice(index * LANES, (index + 1) * LANES)
        for part in range(8):
            end = (part + 1) * step
            wide[part * pitch : part * pitch + step, :] = held[end - step : end, here].astype(jnp.float32)
            if part < 7:
                following = held[end : end + LAGS, here].astype(jnp.float32)
            elif tail is None:
                following = jnp.zeros((LAGS, LANES), jnp.float32)
            else:
                following = tail[:, here].astype(jnp.float32)
            wide[part * pitch + step : (part + 1) * pitch, :] = following
        taken = lambda first: wide[pl.ds(first, 8, stride=pitch), :]

        def advance(index, carry):
            window, sums = carry
            window = window + (taken(index + LAGS - 1),)
            sums = tuple(total + window[0] * window[lag + 1] for lag, total in enumerate(sums))
            return window[1:], sums

        window = tuple(taken(first) for first in range(LAGS - 1))
        zero = jnp.zeros((8, LANES), jnp.float32)
        _, sums = lax.fori_loop(0, step, advance, (window, (zero,) * (LAGS - 1)), unroll=16)
        out[:, there] = jnp.concatenate(
            [power[:, here]] + [jnp.sum(total, axis=0, keepdims=True) for total in sums], axis=0
        )


def segment_rows(held, power, tail, first, size, after=()):
    rows = held.shape[0]
    arrays = (held, power) if tail is None else (held, power, tail)

    def kernel(*refs):
        held, power, *rest = refs
        if tail is None:
            rest = [None] + rest
        segment_kernel(first, held, power, *rest)

    return call_on_blocks(
        kernel,
        [((LAGS, size), jnp.float32)],
        *arrays,
        name="segment_rows",
        micros=SEGMENT_MICROS,
        after=after,
        scratch=[pltpu.VMEM((rows + 8 * LAGS, LANES), jnp.float32)],
    )[0]


def all_products_kernel(held, own, other, tail, out, shifted):
    chan = lax.axis_index("chan")
    zeros = jnp.zeros((HALF, LANES), jnp.float32)
    for refs, half in ((own, chan), (other, 1 - chan)):
        long = jnp.concatenate([refs[...].astype(jnp.float32), zeros], axis=1)
        for index in range(GROUP):
            start = pl.multiple_of(index * REF + half * HALF, HALF)
            lag = pl.program_id(0) * GROUP + index
            shifted[pl.ds(start, HALF), :] = pltpu.roll(long, lag, 1).astype(jnp.bfloat16)
    edge = edge_of(tail)
    for here in columns(held.shape[1]):
        out[:, here] = product_of(shifted, held, edge, here)


def all_products(held, own, other, tail):
    rows, width = held.shape
    vmem = pl.BlockSpec(memory_space=pltpu.VMEM)
    return pl.pallas_call(
        all_products_kernel,
        grid=(LAGS // GROUP,),
        in_specs=[vmem] * 4,
        out_specs=pl.BlockSpec((GROUP * REF, width), lambda group: (group, 0)),
        out_shape=jax.ShapeDtypeStruct((LAGS * REF, width), jnp.float32),
        scratch_shapes=shifted_scratch(rows),
        compiler_params=pltpu.CompilerParams(vmem_limit_bytes=VMEM_BYTES),
        name="all_products",
    )(held, own, other, tail)


def local(strain):
    rows, width = strain.shape
    count = lax.axis_size("tm")
    slab_rows = rows * count
    chunk = LAGS * REF // count

    own, head = prepared(strain)
    other = exchanged(own, "chan", 1)
    tail = passed_along(head, "tm", -1)
    held, power = loaded(strain, own)
    size = width // 4

    if chunk * 2 == GROUP * REF:
        refs = (own, other, tail)
        autos = [segment_rows(held, power, None, 0, size)]
        keep6, send7 = first_products(held, power, *refs, chunk, after=(autos[0],))
        got7 = exchanged(send7, "tm", 1)
        keep4, send5, keep2, send3 = later_products((2, 1), held, *refs, send7, chunk)
        got5 = exchanged(send5, "tm", 1)
        keep0, send1 = later_products((0,), held, *refs, send7, chunk, after=(send5,))
        *sends6, send3 = merge_near(keep6, send7, got7, send3, after=(send1,))
        gots6 = [exchanged(code, "tm", 2) for code in sends6]
        got3 = exchanged(send3, "tm", 1)
        autos.append(segment_rows(held, power, tail, size, size, after=(send3,)))
        far = [merge_far(0, keep4, sends6[0], gots6[0], got5, got7, after=(autos[1],))]
        far += [merge_far(1, keep4, sends6[1], gots6[1], got5, got7, send1, after=(far[0][0],))]
        sends4 = [far[0][0], far[1][0]]
        gots4 = [exchanged(code, "tm", 4) for code in sends4]
        got1 = exchanged(far[1][1], "tm", 1)
        sends2 = resent(keep2, got3, got7, sends6, after=(sends4[1],))
        gots2 = [exchanged(code, "tm", 2) for code in sends2]
        autos.append(segment_rows(held, power, tail, 2 * size, 2 * size, after=tuple(sends2)))
        partial, edge = added(keep0, got1, got7, gots2, gots6, held, tail, size, after=(autos[2],))
        return tuple(finished(slab_rows, rows, partial, edge, sends4, gots4, autos))

    chan = lax.axis_index("chan").astype(jnp.int32)
    time = lax.axis_index("tm").astype(jnp.int32)
    auto = jnp.concatenate(
        [segment_rows(held, power, tail, size * index, size) for index in range(4)], axis=1
    )
    power_other = jnp.sum(jnp.square(other.astype(jnp.float32)), axis=1)
    power = lax.psum(jnp.concatenate([power[0], power_other]), "tm")
    inv = 1.0 / jnp.sqrt(power / slab_rows + 1e-06)
    scale = inv[:width]
    ref_scale = jnp.where(
        chan == 0,
        jnp.concatenate([inv[:HALF], inv[width:]]),
        jnp.concatenate([inv[width:], inv[:HALF]]),
    )
    products = all_products(held, own, other, tail)
    summed = lax.psum_scatter(products, "tm", scatter_dimension=0, tiled=True)
    row = time * chunk + jnp.arange(chunk, dtype=jnp.int32)
    row_scale = ref_scale[row % REF] / (slab_rows - row // REF).astype(jnp.float32)
    covariance = summed * scale[None, :] * row_scale[:, None]
    segment_auto = auto * (scale * scale)[None, :] / rows
    return (covariance, segment_auto)


def solution(mesh):
    in_specs = (P(("groups", "tm"), "chan"),)
    out_specs = (P(("groups", "tm"), "chan"), P(("groups", "tm"), "chan"))
    return jax.shard_map(local, mesh=mesh, in_specs=in_specs, out_specs=out_specs, check_vma=False)
```

```python
import jax
import jax.numpy as jnp
from jax import lax
from jax.experimental import pallas as pl
from jax.experimental.pallas import tpu as pltpu
from jax.sharding import PartitionSpec as P

LAGS = 16
REF = 64
HALF = REF // 2
LANES = 128
EXTRA = 8
FETCHES = 8
STEP = 256
GROUP = 4
POWER = 16
CODE_SCALE = 2.0 ** (126 / POWER)
TINY = 1e-35
PIECES = 4
VMEM_BYTES = 32 * 1024 * 1024
HBM_RATE = 3.69e6
PRODUCT_MICROS = 1.0
SEGMENT_MICROS = 1.2
MERGE_MICROS = 0.3


def lasting(micros):
    return pl.CostEstimate(flops=0, bytes_accessed=int(micros * HBM_RATE), transcendentals=0)


def passed_along(value, axis, steps):
    count = lax.axis_size(axis)
    initial, last = (max(0, -steps), min(count, count - steps))
    return lax.ppermute(value, axis, [(source, source + steps) for source in range(initial, last)])


def exchanged(value, axis, bit):
    count = lax.axis_size(axis)
    return lax.ppermute(value, axis, [(source, source ^ bit) for source in range(count)])


def as_column(row):
    size = row.shape[1]
    eye = lax.broadcasted_iota(jnp.int32, (size, size), 0) == lax.broadcasted_iota(jnp.int32, (size, size), 1)
    return jnp.sum(jnp.where(eye, row, 0.0), axis=1, keepdims=True)


def as_row(column):
    size = column.shape[0]
    eye = lax.broadcasted_iota(jnp.int32, (size, size), 0) == lax.broadcasted_iota(jnp.int32, (size, size), 1)
    return jnp.sum(jnp.where(eye, column, 0.0), axis=0, keepdims=True)


def for_chunk(ref_column, rows):
    return jnp.concatenate([ref_column] * (rows // REF), axis=0)


def bf16_pieces(value):
    high = value.astype(jnp.bfloat16).astype(jnp.float32)
    middle = (value - high).astype(jnp.bfloat16).astype(jnp.float32)
    return high, middle, value - high - middle


def packed(powers, ref_powers, channel_bound):
    rows = list(bf16_pieces(powers))
    refs = jnp.concatenate(bf16_pieces(ref_powers), axis=1)
    pad = jnp.zeros((1, powers.shape[1] - refs.shape[1]), jnp.float32)
    rows += [jnp.concatenate([refs, pad], axis=1), channel_bound]
    rows += [jnp.zeros_like(powers)] * (EXTRA - len(rows))
    return jnp.concatenate(rows, axis=0).astype(jnp.bfloat16)


def unpacked(block):
    wide = block.astype(jnp.float32)
    powers = wide[0:1] + wide[1:2] + wide[2:3]
    refs = wide[3:4, :LANES] + wide[3:4, LANES : 2 * LANES] + wide[3:4, 2 * LANES : 3 * LANES]
    return powers, refs, wide[4:5]


def rounded_up(value):
    return (value * (1.0 + 2.0**-7)).astype(jnp.bfloat16).astype(jnp.float32)


def coded(values, channel_bound, ref_bound):
    channel = lax.rsqrt(jnp.maximum(channel_bound, TINY))
    refs = lax.rsqrt(jnp.maximum(ref_bound, TINY)) * CODE_SCALE
    power = values * channel * for_chunk(refs, values.shape[0])
    for _ in range(4):
        power = power * jnp.abs(power)
    return power.astype(jnp.bfloat16)


def expanded(code, channel_bound, ref_bound):
    channel = jnp.sqrt(jnp.maximum(channel_bound, TINY))
    refs = jnp.sqrt(jnp.maximum(ref_bound, TINY)) * (1.0 / CODE_SCALE)
    wide = code[...].astype(jnp.float32)
    root = jnp.exp2(jnp.log2(jnp.abs(wide)) * (1.0 / POWER))
    return jnp.where(wide < 0.0, -root, root) * channel * for_chunk(refs, code.shape[0])


def ref_column(ref_powers):
    return as_column(ref_powers)[:REF]


def prepare_kernel(strain, own, head, left, sems):
    rows = left.shape[0]
    step = rows // PIECES
    copies = [
        pltpu.make_async_copy(
            strain.at[pl.ds(index * step, step), pl.ds(0, LANES)], left.at[pl.ds(index * step, step)], sems.at[index]
        )
        for index in range(PIECES)
    ]
    copies.append(pltpu.make_async_copy(strain.at[pl.ds(0, LAGS)], head, sems.at[PIECES]))
    for copy in copies:
        copy.start()
    for index in range(PIECES):
        copies[index].wait()
        here = slice(index * step, (index + 1) * step)
        own[:, here] = left[here, :].astype(jnp.float32).T[:HALF].astype(jnp.bfloat16)
    copies[PIECES].wait()


def prepared(strain):
    rows, width = strain.shape
    vmem = pl.BlockSpec(memory_space=pltpu.VMEM)
    return pl.pallas_call(
        prepare_kernel,
        in_specs=[pl.BlockSpec(memory_space=pl.ANY)],
        out_specs=[vmem, vmem],
        out_shape=[pltpu.VMEM((HALF, rows), strain.dtype), pltpu.VMEM((LAGS, width), strain.dtype)],
        scratch_shapes=[pltpu.VMEM((rows, LANES), strain.dtype), pltpu.SemaphoreType.DMA((PIECES + 1,))],
        compiler_params=pltpu.CompilerParams(vmem_limit_bytes=VMEM_BYTES),
        cost_estimate=lasting(PRODUCT_MICROS),
        name="prepared",
    )(pltpu.with_memory_space_constraint(strain, pltpu.HBM))


def half_of(width, part):
    return slice(part * width // 2, (part + 1) * width // 2)


def lag_rows(own, other, group, shifted):
    chan, near = lax.axis_index("chan"), lax.axis_index("tm") & 1
    zeros = jnp.zeros((HALF, LANES), jnp.float32)
    for refs, half in ((own, chan), (other, 1 - chan)):
        long = jnp.concatenate([refs[...].astype(jnp.float32), zeros], axis=1)
        for index in range(GROUP):
            ahead = near if index < GROUP // 2 else 1 - near
            lag = group * GROUP + ahead * (GROUP // 2) + index % (GROUP // 2)
            start = pl.multiple_of(index * REF + half * HALF, HALF)
            shifted[pl.ds(start, HALF), :] = pltpu.roll(long, lag, 1).astype(jnp.bfloat16)


def own_group(bits):
    return lax.shift_right_logical(lax.axis_index("tm").astype(jnp.int32), 1) ^ bits


def loaded_kernel(strain, held, power, sems):
    step = held.shape[0] // FETCHES
    pieces = [slice(index * step, (index + 1) * step) for index in range(FETCHES)]
    copies = [
        pltpu.make_async_copy(strain.at[pl.ds(here.start, step)], held.at[pl.ds(here.start, step)], sems.at[index])
        for index, here in enumerate(pieces)
    ]
    for copy in copies:
        copy.start()
    total = jnp.zeros((8, held.shape[1]), jnp.float32)
    for copy, here in zip(copies, pieces):
        copy.wait()
        squares = jnp.square(held[here, :].astype(jnp.float32))
        total += jnp.sum(squares.reshape(step // 8, 8, held.shape[1]), axis=0)
    power[...] = jnp.sum(total, axis=0, keepdims=True)


def loaded(strain, after):
    rows, width = strain.shape
    vmem = pl.BlockSpec(memory_space=pltpu.VMEM)

    def kernel(strain, after, held, power, sems):
        loaded_kernel(strain, held, power, sems)

    return pl.pallas_call(
        kernel,
        in_specs=[pl.BlockSpec(memory_space=pl.ANY)] * 2,
        out_specs=[vmem, vmem],
        out_shape=[pltpu.VMEM((rows, width), strain.dtype), pltpu.VMEM((1, width), jnp.float32)],
        scratch_shapes=[pltpu.SemaphoreType.DMA((FETCHES,))],
        compiler_params=pltpu.CompilerParams(vmem_limit_bytes=VMEM_BYTES),
        cost_estimate=lasting(PRODUCT_MICROS),
        name="loaded",
    )(pltpu.with_memory_space_constraint(strain, pltpu.HBM), after)


def edge_of(tail):
    return jnp.concatenate([tail[...], jnp.zeros((LANES - LAGS, tail.shape[1]), tail.dtype)], axis=0)


def product_of(shifted, held, edge, here):
    rows = held.shape[0]
    total = jnp.dot(shifted[:, rows:], edge[:, here], preferred_element_type=jnp.float32)
    return total + jnp.dot(shifted[:, :rows], held[:, here], preferred_element_type=jnp.float32)


def half_columns(width):
    half = width // 2
    return [
        (part, slice(part * half + first, part * half + first + STEP), slice(first, first + STEP))
        for part in range(2)
        for first in range(0, half, STEP)
    ]


def first_products_kernel(held, power, own, other, tail, keep, first, second, shifted):
    lag_rows(own, other, own_group(3), shifted)
    ours, theirs = [
        jnp.sum(jnp.square(refs[...].astype(jnp.float32)), axis=1, keepdims=True) for refs in (own, other)
    ]
    refs = jnp.where(
        lax.axis_index("chan") == 0,
        jnp.concatenate([ours, theirs], axis=0),
        jnp.concatenate([theirs, ours], axis=0),
    )
    beyond = jnp.sum(jnp.square(tail[...].astype(jnp.float32)), axis=0, keepdims=True)
    bound = rounded_up(power[...] + beyond)
    pad = jnp.zeros((1, LANES - REF), jnp.float32)
    refs_row = jnp.concatenate([as_row(refs), pad], axis=1)
    chunk, width = keep.shape
    sends = (first, second)
    for part, send in enumerate(sends):
        here = half_of(width, part)
        send[chunk:] = packed(power[:, here], refs_row, bound[:, here])
    edge = edge_of(tail)
    for part, here, there in half_columns(width):
        product = product_of(shifted, held, edge, here)
        keep[:, here] = product[:chunk]
        sends[part][:chunk, there] = coded(product[chunk:], bound[:, here], refs)


def shifted_scratch(rows, groups=1):
    return [pltpu.VMEM((groups * GROUP * REF, rows + LANES), jnp.bfloat16)]


def first_products(held, power, own, other, tail, chunk, after):
    rows, width = held.shape
    half = ((chunk + EXTRA, width // 2), jnp.bfloat16)
    keep, *sends = call_on_blocks(
        first_products_kernel,
        [((chunk, width), jnp.float32), half, half],
        held,
        power,
        own,
        other,
        tail,
        name="first_products",
        micros=PRODUCT_MICROS,
        after=after,
        scratch=shifted_scratch(rows),
    )
    return keep, sends


def later_products(groups, held, own, other, tail, powers, chunk, after=()):
    rows, width = held.shape

    def kernel(held, own, other, tail, first, second, *rest):
        outs, shifted = rest[:-1], rest[-1]
        sent = [sent_powers(powers) for powers in (first, second)]
        refs = ref_column(sent[0][1])
        for index, bits in enumerate(groups):
            lag_rows(own, other, own_group(bits), shifted.at[pl.ds(index * 2 * chunk, 2 * chunk)])
        edge = edge_of(tail)
        for part, here, there in half_columns(width):
            product = product_of(shifted, held, edge, here)
            for index in range(len(groups)):
                keep, *sends = outs[3 * index : 3 * index + 3]
                start = 2 * index * chunk
                keep[:, here] = product[start : start + chunk]
                others = product[start + chunk : start + 2 * chunk]
                sends[part][:, there] = coded(others, sent[part][2][:, there], refs)

    half = ((chunk, width // 2), jnp.bfloat16)
    outs = call_on_blocks(
        kernel,
        [((chunk, width), jnp.float32), half, half] * len(groups),
        held,
        own,
        other,
        tail,
        *powers,
        name="later_products",
        micros=PRODUCT_MICROS,
        after=after,
        scratch=shifted_scratch(rows, len(groups)),
    )
    return [(outs[first], outs[first + 1 : first + 3]) for first in range(0, len(outs), 3)]


def call_on_blocks(kernel, outs, *arrays, name, micros, after=(), scratch=(), space=pltpu.VMEM):
    vmem = pl.BlockSpec(memory_space=pltpu.VMEM)
    count = len(arrays)

    def body(*refs):
        kernel(*refs[:count], *refs[count + len(after) :])

    return pl.pallas_call(
        body,
        in_specs=[vmem] * count + [pl.BlockSpec(memory_space=pl.ANY)] * len(after),
        out_specs=[vmem] * len(outs),
        out_shape=[space(shape, dtype) for shape, dtype in outs],
        scratch_shapes=list(scratch),
        compiler_params=pltpu.CompilerParams(vmem_limit_bytes=VMEM_BYTES),
        cost_estimate=lasting(micros),
        name=name,
    )(*arrays, *after)


def sent_powers(code):
    return unpacked(code[-EXTRA:])


def merged(part, keep, ours, theirs, *direct, after):
    chunk, width = keep.shape
    here = half_of(width, part)

    def kernel(keep, ours, theirs, *rest):
        out = rest[-1]
        powers, refs, bound = sent_powers(ours)
        their_powers, their_refs, their_bound = sent_powers(theirs)
        total = keep[:, here] + expanded(theirs[:chunk], their_bound, ref_column(their_refs))
        if direct:
            total += direct_sums(*rest[:2])
        sums, sum_refs, sum_bound = powers + their_powers, refs + their_refs, rounded_up(bound + their_bound)
        out[chunk:] = packed(sums, sum_refs, sum_bound)
        out[:chunk] = coded(total, sum_bound, ref_column(sum_refs))

    outs = [((chunk + EXTRA, width // 2), jnp.bfloat16)]
    return call_on_blocks(
        kernel, outs, keep, ours, theirs, *direct, name="merged", micros=MERGE_MICROS, after=after
    )[0]


def direct_sums(direct, powers):
    _, refs, bound = sent_powers(powers)
    return expanded(direct, bound, ref_column(refs))


def resent(keep, direct, direct_powers, ours, after):
    chunk, width = keep.shape

    def kernel(keep, *refs):
        direct, direct_powers, ours, outs = refs[:2], refs[2:4], refs[4:6], refs[6:]
        for part in range(2):
            _, refs, bound = sent_powers(ours[part])
            total = keep[:, half_of(width, part)] + direct_sums(direct[part], direct_powers[part])
            outs[part][...] = coded(total, bound, ref_column(refs))

    outs = [((chunk, width // 2), jnp.bfloat16)] * 2
    arrays = (keep, *direct, *direct_powers, *ours)
    return call_on_blocks(kernel, outs, *arrays, name="resent", micros=MERGE_MICROS, after=after)


def added(keep, direct, direct_powers, near, near_powers, held, tail, size, after):
    rows, width = held.shape

    def kernel(keep, held, tail, *refs):
        direct, direct_powers, near, near_powers, (out, edge) = (
            refs[:2],
            refs[2:4],
            refs[4:6],
            refs[6:8],
            refs[8:],
        )
        for part in range(2):
            here = half_of(width, part)
            total = keep[:, here] + direct_sums(direct[part], direct_powers[part])
            out[:, here] = total + direct_sums(near[part], near_powers[part])
        last = held[rows - LAGS :, :size].astype(jnp.float32)
        beyond = tail[:, :size].astype(jnp.float32)
        place = lax.broadcasted_iota(jnp.int32, last.shape, 0)
        sums = [jnp.zeros((1, size), jnp.float32)]
        for lag in range(1, LAGS):
            pairs = jnp.where(place >= LAGS - lag, last * pltpu.roll(beyond, LAGS - lag, 0), 0.0)
            sums.append(jnp.sum(pairs, axis=0, keepdims=True))
        edge[...] = jnp.concatenate(sums, axis=0)

    outs = [(keep.shape, jnp.float32), ((LAGS, size), jnp.float32)]
    arrays = (keep, held, tail, *direct, *direct_powers, *near, *near_powers)
    return call_on_blocks(kernel, outs, *arrays, name="added", micros=MERGE_MICROS, after=after)


def finished(slab_rows, segment, partial, edge, ours, theirs, autos):
    chunk, width = partial.shape

    def kernel(partial, edge, *refs):
        ours, theirs, autos, (covariance, segment_auto) = refs[:2], refs[2:4], refs[4:-2], refs[-2:]
        first_lag = lax.axis_index("tm").astype(jnp.int32) * (chunk // REF)
        lag = lax.broadcasted_iota(jnp.int32, (chunk, 1), 0) // REF + first_lag
        denom = (slab_rows - lag).astype(jnp.float32)
        for part in range(2):
            here = half_of(width, part)
            powers, own_refs, _ = sent_powers(ours[part])
            their_powers, their_refs, their_bound = sent_powers(theirs[part])
            total = partial[:, here] + expanded(theirs[part][:chunk], their_bound, ref_column(their_refs))
            scale = 1.0 / jnp.sqrt((powers + their_powers) / slab_rows + 1e-06)
            ref_scale = 1.0 / jnp.sqrt(ref_column(own_refs + their_refs) / slab_rows + 1e-06)
            covariance[:, here] = total * scale * (for_chunk(ref_scale, chunk) / denom)
            first = 0
            for auto in autos:
                size = auto.shape[1]
                if here.start <= first < here.stop:
                    own_scale = scale[:, first - here.start : first - here.start + size]
                    sums = auto[...] + edge[...] if first == 0 else auto[...]
                    segment_auto[:, first : first + size] = sums * (own_scale * own_scale) / segment
                first += size

    outs = [(partial.shape, jnp.float32), ((LAGS, width), jnp.float32)]
    return call_on_blocks(
        kernel, outs, partial, edge, *ours, *theirs, *autos, name="finished", micros=MERGE_MICROS, space=jax.ShapeDtypeStruct
    )


def segment_kernel(first, held, power, tail, out, wide):
    rows = held.shape[0]
    step = rows // 8
    pitch = step + LAGS
    for index in range(out.shape[1] // LANES):
        here = slice(first + index * LANES, first + (index + 1) * LANES)
        there = slice(index * LANES, (index + 1) * LANES)
        for part in range(8):
            end = (part + 1) * step
            wide[part * pitch : part * pitch + step, :] = held[end - step : end, here].astype(jnp.float32)
            if part < 7:
                following = held[end : end + LAGS, here].astype(jnp.float32)
            elif tail is None:
                following = jnp.zeros((LAGS, LANES), jnp.float32)
            else:
                following = tail[:, here].astype(jnp.float32)
            wide[part * pitch + step : (part + 1) * pitch, :] = following
        taken = lambda first: wide[pl.ds(first, 8, stride=pitch), :]

        def advance(index, carry):
            window, sums = carry
            window = window + (taken(index + LAGS - 1),)
            sums = tuple(total + window[0] * window[lag + 1] for lag, total in enumerate(sums))
            return window[1:], sums

        window = tuple(taken(first) for first in range(LAGS - 1))
        zero = jnp.zeros((8, LANES), jnp.float32)
        _, sums = lax.fori_loop(0, step, advance, (window, (zero,) * (LAGS - 1)), unroll=16)
        out[:, there] = jnp.concatenate(
            [power[:, here]] + [jnp.sum(total, axis=0, keepdims=True) for total in sums], axis=0
        )


def segment_rows(held, power, tail, first, size, after=()):
    rows = held.shape[0]
    arrays = (held, power) if tail is None else (held, power, tail)

    def kernel(*refs):
        held, power, *rest = refs
        if tail is None:
            rest = [None] + rest
        segment_kernel(first, held, power, *rest)

    return call_on_blocks(
        kernel,
        [((LAGS, size), jnp.float32)],
        *arrays,
        name="segment_rows",
        micros=SEGMENT_MICROS,
        after=after,
        scratch=[pltpu.VMEM((rows + 8 * LAGS, LANES), jnp.float32)],
    )[0]


def all_products_kernel(held, own, other, tail, out, shifted):
    chan = lax.axis_index("chan")
    zeros = jnp.zeros((HALF, LANES), jnp.float32)
    for refs, half in ((own, chan), (other, 1 - chan)):
        long = jnp.concatenate([refs[...].astype(jnp.float32), zeros], axis=1)
        for index in range(GROUP):
            start = pl.multiple_of(index * REF + half * HALF, HALF)
            lag = pl.program_id(0) * GROUP + index
            shifted[pl.ds(start, HALF), :] = pltpu.roll(long, lag, 1).astype(jnp.bfloat16)
    edge = edge_of(tail)
    for _, here, _ in half_columns(held.shape[1]):
        out[:, here] = product_of(shifted, held, edge, here)


def all_products(held, own, other, tail):
    rows, width = held.shape
    vmem = pl.BlockSpec(memory_space=pltpu.VMEM)
    return pl.pallas_call(
        all_products_kernel,
        grid=(LAGS // GROUP,),
        in_specs=[vmem] * 4,
        out_specs=pl.BlockSpec((GROUP * REF, width), lambda group: (group, 0)),
        out_shape=jax.ShapeDtypeStruct((LAGS * REF, width), jnp.float32),
        scratch_shapes=shifted_scratch(rows),
        compiler_params=pltpu.CompilerParams(vmem_limit_bytes=VMEM_BYTES),
        name="all_products",
    )(held, own, other, tail)


def local(strain):
    rows, width = strain.shape
    count = lax.axis_size("tm")
    slab_rows = rows * count
    chunk = LAGS * REF // count

    own, head = prepared(strain)
    other = exchanged(own, "chan", 1)
    tail = passed_along(head, "tm", -1)
    held, power = loaded(strain, own)
    size = width // 4

    if chunk * 2 == GROUP * REF:
        refs = (own, other, tail)

        def both(codes, bit):
            return [exchanged(code, "tm", bit) for code in codes]

        def piece(index, after):
            return segment_rows(held, power, tail if index else None, size * index, size, after=tuple(after))

        autos = [piece(0, ())]
        keep6, sends7 = first_products(held, power, *refs, chunk, after=(autos[0],))
        gots7 = both(sends7, 1)
        ((keep4, sends5),) = later_products((2,), held, *refs, sends7, chunk)
        gots5 = both(sends5, 1)
        autos.append(piece(1, sends5))
        sends6 = [merged(0, keep6, sends7[0], gots7[0], after=(autos[1],))]
        sends6.append(merged(1, keep6, sends7[1], gots7[1], after=(sends6[0],)))
        gots6 = both(sends6, 2)
        (keep2, sends3), (keep0, sends1) = later_products((1, 0), held, *refs, sends7, chunk, after=tuple(sends6))
        gots3, gots1 = both(sends3, 1), both(sends1, 1)
        sends4 = [merged(0, keep4, sends6[0], gots6[0], gots5[0], gots7[0], after=(sends3[0],))]
        sends4.append(merged(1, keep4, sends6[1], gots6[1], gots5[1], gots7[1], after=(sends4[0],)))
        gots4 = both(sends4, 4)
        autos.append(piece(2, sends4))
        sends2 = resent(keep2, gots3, gots7, sends6, after=(autos[2],))
        gots2 = both(sends2, 2)
        autos.append(piece(3, sends2))
        partial, edge = added(keep0, gots1, gots7, gots2, gots6, held, tail, size, after=(autos[3],))
        return tuple(finished(slab_rows, rows, partial, edge, sends4, gots4, autos))

    chan = lax.axis_index("chan").astype(jnp.int32)
    time = lax.axis_index("tm").astype(jnp.int32)
    auto = jnp.concatenate(
        [segment_rows(held, power, tail, size * index, size) for index in range(4)], axis=1
    )
    power_other = jnp.sum(jnp.square(other.astype(jnp.float32)), axis=1)
    power = lax.psum(jnp.concatenate([power[0], power_other]), "tm")
    inv = 1.0 / jnp.sqrt(power / slab_rows + 1e-06)
    scale = inv[:width]
    ref_scale = jnp.where(
        chan == 0,
        jnp.concatenate([inv[:HALF], inv[width:]]),
        jnp.concatenate([inv[width:], inv[:HALF]]),
    )
    products = all_products(held, own, other, tail)
    summed = lax.psum_scatter(products, "tm", scatter_dimension=0, tiled=True)
    row = time * chunk + jnp.arange(chunk, dtype=jnp.int32)
    row_scale = ref_scale[row % REF] / (slab_rows - row // REF).astype(jnp.float32)
    covariance = summed * scale[None, :] * row_scale[:, None]
    segment_auto = auto * (scale * scale)[None, :] / rows
    return (covariance, segment_auto)


def solution(mesh):
    in_specs = (P(("groups", "tm"), "chan"),)
    out_specs = (P(("groups", "tm"), "chan"), P(("groups", "tm"), "chan"))
    return jax.shard_map(local, mesh=mesh, in_specs=in_specs, out_specs=out_specs, check_vma=False)
```

```python
import jax
import jax.numpy as jnp
from jax import lax
from jax.experimental import pallas as pl
from jax.experimental.pallas import tpu as pltpu
from jax.sharding import PartitionSpec as P

LAGS = 16
REF = 64
HALF = REF // 2
LANES = 128
EXTRA = 8
FETCHES = 8
STEP = 256
GROUP = 4
POWER = 16
CODE_SCALE = 2.0 ** (126 / POWER)
TINY = 1e-35
PIECES = 4
VMEM_BYTES = 32 * 1024 * 1024
HBM_RATE = 3.69e6
PRODUCT_MICROS = 1.0
SEGMENT_MICROS = 1.2
MERGE_MICROS = 0.3


def lasting(micros):
    return pl.CostEstimate(flops=0, bytes_accessed=int(micros * HBM_RATE), transcendentals=0)


def passed_along(value, axis, steps):
    count = lax.axis_size(axis)
    initial, last = (max(0, -steps), min(count, count - steps))
    return lax.ppermute(value, axis, [(source, source + steps) for source in range(initial, last)])


def exchanged(value, axis, bit):
    count = lax.axis_size(axis)
    return lax.ppermute(value, axis, [(source, source ^ bit) for source in range(count)])


def as_column(row):
    size = row.shape[1]
    eye = lax.broadcasted_iota(jnp.int32, (size, size), 0) == lax.broadcasted_iota(jnp.int32, (size, size), 1)
    return jnp.sum(jnp.where(eye, row, 0.0), axis=1, keepdims=True)


def as_row(column):
    size = column.shape[0]
    eye = lax.broadcasted_iota(jnp.int32, (size, size), 0) == lax.broadcasted_iota(jnp.int32, (size, size), 1)
    return jnp.sum(jnp.where(eye, column, 0.0), axis=0, keepdims=True)


def for_chunk(ref_column, rows):
    return jnp.concatenate([ref_column] * (rows // REF), axis=0)


def bf16_pieces(value):
    high = value.astype(jnp.bfloat16).astype(jnp.float32)
    middle = (value - high).astype(jnp.bfloat16).astype(jnp.float32)
    return high, middle, value - high - middle


def packed(powers, ref_powers, channel_bound):
    rows = list(bf16_pieces(powers))
    refs = jnp.concatenate(bf16_pieces(ref_powers), axis=1)
    pad = jnp.zeros((1, powers.shape[1] - refs.shape[1]), jnp.float32)
    rows += [jnp.concatenate([refs, pad], axis=1), channel_bound]
    rows += [jnp.zeros_like(powers)] * (EXTRA - len(rows))
    return jnp.concatenate(rows, axis=0).astype(jnp.bfloat16)


def unpacked(block):
    wide = block.astype(jnp.float32)
    powers = wide[0:1] + wide[1:2] + wide[2:3]
    refs = wide[3:4, :LANES] + wide[3:4, LANES : 2 * LANES] + wide[3:4, 2 * LANES : 3 * LANES]
    return powers, refs, wide[4:5]


def sent_powers(code):
    return unpacked(code[-EXTRA:])


def rounded_up(value):
    return (value * (1.0 + 2.0**-7)).astype(jnp.bfloat16).astype(jnp.float32)


def coded(values, channel_bound, ref_bound):
    channel = lax.rsqrt(jnp.maximum(channel_bound, TINY))
    refs = lax.rsqrt(jnp.maximum(ref_bound, TINY)) * CODE_SCALE
    power = values * channel * for_chunk(refs, values.shape[0])
    for _ in range(4):
        power = power * jnp.abs(power)
    return power.astype(jnp.bfloat16)


def expanded(code, channel_bound, ref_bound):
    channel = jnp.sqrt(jnp.maximum(channel_bound, TINY))
    refs = jnp.sqrt(jnp.maximum(ref_bound, TINY)) * (1.0 / CODE_SCALE)
    wide = code[...].astype(jnp.float32)
    root = jnp.exp2(jnp.log2(jnp.abs(wide)) * (1.0 / POWER))
    return jnp.where(wide < 0.0, -root, root) * channel * for_chunk(refs, code.shape[0])


def ref_column(ref_powers):
    return as_column(ref_powers)[:REF]


def prepare_kernel(strain, own, head, left, sems):
    rows = left.shape[0]
    step = rows // PIECES
    copies = [
        pltpu.make_async_copy(
            strain.at[pl.ds(index * step, step), pl.ds(0, LANES)], left.at[pl.ds(index * step, step)], sems.at[index]
        )
        for index in range(PIECES)
    ]
    copies.append(pltpu.make_async_copy(strain.at[pl.ds(0, LAGS)], head, sems.at[PIECES]))
    for copy in copies:
        copy.start()
    for index in range(PIECES):
        copies[index].wait()
        here = slice(index * step, (index + 1) * step)
        own[:, here] = left[here, :].astype(jnp.float32).T[:HALF].astype(jnp.bfloat16)
    copies[PIECES].wait()


def prepared(strain):
    rows, width = strain.shape
    vmem = pl.BlockSpec(memory_space=pltpu.VMEM)
    return pl.pallas_call(
        prepare_kernel,
        in_specs=[pl.BlockSpec(memory_space=pl.ANY)],
        out_specs=[vmem, vmem],
        out_shape=[pltpu.VMEM((HALF, rows), strain.dtype), pltpu.VMEM((LAGS, width), strain.dtype)],
        scratch_shapes=[pltpu.VMEM((rows, LANES), strain.dtype), pltpu.SemaphoreType.DMA((PIECES + 1,))],
        compiler_params=pltpu.CompilerParams(vmem_limit_bytes=VMEM_BYTES),
        cost_estimate=lasting(PRODUCT_MICROS),
        name="prepared",
    )(pltpu.with_memory_space_constraint(strain, pltpu.HBM))


def lag_rows(own, other, group, shifted):
    chan, near = lax.axis_index("chan"), lax.axis_index("tm") & 1
    rows = own.shape[1]
    zeros = jnp.zeros((HALF, LANES), jnp.float32)
    for refs, half in ((own, chan), (other, 1 - chan)):
        long = jnp.concatenate([zeros, refs[...].astype(jnp.float32)], axis=1)
        for index in range(GROUP):
            ahead = near if index < GROUP // 2 else 1 - near
            lag = group * GROUP + ahead * (GROUP // 2) + index % (GROUP // 2)
            start = pl.multiple_of(index * REF + half * HALF, HALF)
            moved = pltpu.roll(long, lag, 1)[:, LANES : LANES + rows]
            shifted[pl.ds(start, HALF), :] = moved.astype(jnp.bfloat16)


def own_group(bits):
    return lax.shift_right_logical(lax.axis_index("tm").astype(jnp.int32), 1) ^ bits


def loaded_kernel(strain, held, power, sems):
    step = held.shape[0] // FETCHES
    pieces = [slice(index * step, (index + 1) * step) for index in range(FETCHES)]
    copies = [
        pltpu.make_async_copy(strain.at[pl.ds(here.start, step)], held.at[pl.ds(here.start, step)], sems.at[index])
        for index, here in enumerate(pieces)
    ]
    for copy in copies:
        copy.start()
    total = jnp.zeros((8, held.shape[1]), jnp.float32)
    for copy, here in zip(copies, pieces):
        copy.wait()
        squares = jnp.square(held[here, :].astype(jnp.float32))
        total += jnp.sum(squares.reshape(step // 8, 8, held.shape[1]), axis=0)
    power[...] = jnp.sum(total, axis=0, keepdims=True)


def loaded(strain, after):
    rows, width = strain.shape
    vmem = pl.BlockSpec(memory_space=pltpu.VMEM)

    def kernel(strain, after, held, power, sems):
        loaded_kernel(strain, held, power, sems)

    return pl.pallas_call(
        kernel,
        in_specs=[pl.BlockSpec(memory_space=pl.ANY)] * 2,
        out_specs=[vmem, vmem],
        out_shape=[pltpu.VMEM((rows, width), strain.dtype), pltpu.VMEM((1, width), jnp.float32)],
        scratch_shapes=[pltpu.SemaphoreType.DMA((FETCHES,))],
        compiler_params=pltpu.CompilerParams(vmem_limit_bytes=VMEM_BYTES),
        cost_estimate=lasting(PRODUCT_MICROS),
        name="loaded",
    )(pltpu.with_memory_space_constraint(strain, pltpu.HBM), after)


def columns(width):
    return [slice(first, first + STEP) for first in range(0, width, STEP)]


def product_of(shifted, held, here):
    return jnp.dot(shifted[...], held[:, here], preferred_element_type=jnp.float32)


def boundary_rows(group, ends, their_ends, edges):
    chan, near = lax.axis_index("chan"), lax.axis_index("tm") & 1
    zeros = jnp.zeros((HALF, LANES), jnp.float32)
    ours = [(refs[:, refs.shape[1] - LANES :].astype(jnp.float32), half) for refs, half in zip(ends, (chan, 1 - chan))]
    theirs = [(their_ends[half * HALF : (half + 1) * HALF], half) for half in range(2)]
    for side, parts in enumerate((ours, theirs)):
        for end, half in parts:
            long = jnp.concatenate([end, zeros], axis=1)
            for index in range(GROUP // 2):
                lag = group * GROUP + near * (GROUP // 2) + index
                start = pl.multiple_of(index * REF + half * HALF, HALF)
                moved = pltpu.roll(long, lag, 1)[:, LANES:]
                edges[pl.ds(start, HALF), side * LANES : (side + 1) * LANES] = moved.astype(jnp.bfloat16)


def ends_of(code):
    rows = code[LAGS : 2 * LAGS, :LANES].astype(jnp.float32)
    return jnp.concatenate([jnp.zeros((LANES - LAGS, LANES), jnp.float32), rows], axis=0).T[:REF]


def tails_of(sent, arrived, here):
    zeros = jnp.zeros((LANES - LAGS, here.stop - here.start), jnp.bfloat16)
    return jnp.concatenate([arrived[:LAGS, here], zeros, sent[:LAGS, here], zeros], axis=0)


def boundary_of(edges, sent, arrived, here):
    return jnp.dot(edges[...], tails_of(sent, arrived, here), preferred_element_type=jnp.float32)


def first_products_kernel(held, power, own, other, keep, send, shifted):
    lag_rows(own, other, own_group(3), shifted)
    ours, theirs = [
        jnp.sum(jnp.square(refs[...].astype(jnp.float32)), axis=1, keepdims=True) for refs in (own, other)
    ]
    refs = jnp.where(
        lax.axis_index("chan") == 0,
        jnp.concatenate([ours, theirs], axis=0),
        jnp.concatenate([theirs, ours], axis=0),
    )
    bound = rounded_up(power[...])
    pad = jnp.zeros((1, LANES - REF), jnp.float32)
    chunk = keep.shape[0]
    send[chunk:] = packed(power[...], jnp.concatenate([as_row(refs), pad], axis=1), bound)
    for here in columns(held.shape[1]):
        product = product_of(shifted, held, here)
        keep[:, here] = product[:chunk]
        send[:chunk, here] = coded(product[chunk:], bound[:, here], refs)


def shifted_scratch(rows, groups=1):
    return [pltpu.VMEM((groups * GROUP * REF, rows), jnp.bfloat16)]


def first_products(held, power, own, other, chunk):
    rows, width = held.shape
    return call_on_blocks(
        first_products_kernel,
        [((chunk, width), jnp.float32), ((chunk + EXTRA, width), jnp.bfloat16)],
        held,
        power,
        own,
        other,
        name="first_products",
        micros=PRODUCT_MICROS,
        scratch=shifted_scratch(rows),
    )


def later_products(groups, held, own, other, powers, chunk, tails=(), after=()):
    rows, width = held.shape

    def kernel(held, own, other, powers, *rest):
        sides, rest = rest[: len(tails)], rest[len(tails) :]
        outs, shifted, edges = rest[:-2], rest[-2], rest[-1]
        _, ref_powers, bound = sent_powers(powers)
        refs = ref_column(ref_powers)
        for index, bits in enumerate(groups):
            lag_rows(own, other, own_group(bits), shifted.at[pl.ds(index * 2 * chunk, 2 * chunk)])
            if sides:
                boundary_rows(own_group(bits), (own, other), ends_of(sides[1]), edges.at[index])
        for here in columns(width):
            product = product_of(shifted, held, here)
            for index in range(len(groups)):
                keep, send = outs[2 * index : 2 * index + 2]
                first = 2 * index * chunk
                kept = product[first : first + chunk]
                if sides:
                    kept += boundary_of(edges.at[index], *sides, here)
                keep[:, here] = kept
                send[:, here] = coded(product[first + chunk : first + 2 * chunk], bound[:, here], refs)

    return call_on_blocks(
        kernel,
        [((chunk, width), jnp.float32), ((chunk, width), jnp.bfloat16)] * len(groups),
        held,
        own,
        other,
        powers,
        *tails,
        name="later_products",
        micros=PRODUCT_MICROS,
        after=after,
        scratch=shifted_scratch(rows, len(groups)) + edges_scratch(len(groups), chunk),
    )


def edges_scratch(count, chunk):
    return [pltpu.VMEM((count, chunk, 2 * LANES), jnp.bfloat16)]


def sides_to_swap(head, after_next, own, other, held_back):
    def kernel(head, after_next, own, other, held_back, sides, passed):
        chan, near = lax.axis_index("chan"), lax.axis_index("tm") & 1
        passed[...] = widened(held_back[...], LAGS)
        sides[:LAGS] = jnp.where(near == 0, after_next[...], head[...])
        ours, theirs = [
            refs[:, refs.shape[1] - LANES :].astype(jnp.float32) for refs in (own, other)
        ]
        first, second = jnp.where(chan == 0, ours, theirs), jnp.where(chan == 0, theirs, ours)
        square = jnp.concatenate([first, second, jnp.zeros((LANES - REF, LANES), jnp.float32)], axis=0)
        sides[LAGS:, :LANES] = square.T[LANES - LAGS :].astype(jnp.bfloat16)
        sides[LAGS:, LANES:] = jnp.zeros((LAGS, head.shape[1] - LANES), jnp.bfloat16)

    rows, width = held_back.shape
    outs = [((2 * LAGS, width), jnp.bfloat16), ((rows + LAGS, width), jnp.bfloat16)]
    return call_on_blocks(
        kernel, outs, head, after_next, own, other, held_back, name="sides", micros=MERGE_MICROS
    )


def with_boundaries(keeps, groups, own, other, sent, arrived, after):
    chunk, width = keeps[0].shape

    def kernel(own, other, sent, arrived, *rest):
        keeps, rest = rest[: len(groups)], rest[len(groups) :]
        outs, beyond, edges = rest[: len(groups)], rest[-2], rest[-1]
        for index, bits in enumerate(groups):
            boundary_rows(own_group(bits), (own, other), ends_of(arrived), edges.at[index])
        for here in columns(width):
            tails = tails_of(sent, arrived, here)
            for index in range(len(groups)):
                added = jnp.dot(edges[index], tails, preferred_element_type=jnp.float32)
                outs[index][:, here] = keeps[index][:, here] + added
            beyond[:, here] = jnp.sum(jnp.square(tails.astype(jnp.float32)), axis=0, keepdims=True)

    outs = [((chunk, width), jnp.float32)] * len(groups) + [((1, width), jnp.float32)]
    return call_on_blocks(
        kernel,
        outs,
        own,
        other,
        sent,
        arrived,
        *keeps,
        name="with_boundaries",
        micros=MERGE_MICROS,
        after=after,
        scratch=edges_scratch(len(groups), chunk),
    )


def call_on_blocks(kernel, outs, *arrays, name, micros, after=(), scratch=(), space=pltpu.VMEM):
    vmem = pl.BlockSpec(memory_space=pltpu.VMEM)
    count = len(arrays)

    def body(*refs):
        kernel(*refs[:count], *refs[count + len(after) :])

    return pl.pallas_call(
        body,
        in_specs=[vmem] * count + [pl.BlockSpec(memory_space=pl.ANY)] * len(after),
        out_specs=[vmem] * len(outs),
        out_shape=[space(shape, dtype) for shape, dtype in outs],
        scratch_shapes=list(scratch),
        compiler_params=pltpu.CompilerParams(vmem_limit_bytes=VMEM_BYTES),
        cost_estimate=lasting(micros),
        name=name,
    )(*arrays, *after)


def direct_sums(direct, powers):
    _, refs, bound = sent_powers(powers)
    chunk = direct.shape[0] // REF * REF
    return expanded(direct[:chunk], bound, ref_column(refs))


def widened(code, rows):
    return jnp.concatenate([code, jnp.zeros((rows, code.shape[1]), code.dtype)], axis=0)


def merged(keep, ours, theirs, direct=(), beyond=(), held_back=(), after=()):
    chunk, width = keep.shape

    def kernel(keep, ours, theirs, *refs):
        inputs, out, passed = refs[: -1 - len(held_back)], refs[len(arrays) - 3], refs[len(arrays) - 2 :]
        powers, refs, bound = sent_powers(ours)
        their_powers, their_refs, their_bound = sent_powers(theirs)
        sums, sum_refs, sum_bound = powers + their_powers, refs + their_refs, bound + their_bound
        total = keep[...] + expanded(theirs[:chunk], their_bound, ref_column(their_refs))
        if direct:
            total += direct_sums(inputs[0], inputs[1])
        if beyond:
            sum_bound += inputs[len(direct)][...]
        if held_back:
            passed[0][...] = widened(inputs[-1][...], EXTRA)
        sum_bound = rounded_up(sum_bound)
        out[chunk:] = packed(sums, sum_refs, sum_bound)
        out[:chunk] = coded(total, sum_bound, ref_column(sum_refs))

    outs = [((chunk + EXTRA, width), jnp.bfloat16)] * (1 + len(held_back))
    arrays = (keep, ours, theirs, *direct, *beyond, *held_back)
    return call_on_blocks(kernel, outs, *arrays, name="merged", micros=MERGE_MICROS, after=after)


def resent(keep, direct, direct_powers, ours, after):
    def kernel(keep, direct, direct_powers, ours, out):
        _, refs, bound = sent_powers(ours)
        out[...] = coded(keep[...] + direct_sums(direct, direct_powers), bound, ref_column(refs))

    outs = [(keep.shape, jnp.bfloat16)]
    arrays = (keep, direct, direct_powers, ours)
    return call_on_blocks(kernel, outs, *arrays, name="resent", micros=MERGE_MICROS, after=after)[0]


def added(keep, direct, direct_powers, near, near_powers, held, sides, size, after):
    rows, width = held.shape

    def kernel(keep, direct, direct_powers, near, near_powers, held, sides, out, edge):
        out[...] = keep[...] + direct_sums(direct, direct_powers) + direct_sums(near, near_powers)
        last = held[rows - LAGS :, :size].astype(jnp.float32)
        beyond = sides[:LAGS, :size].astype(jnp.float32)
        place = lax.broadcasted_iota(jnp.int32, last.shape, 0)
        sums = [jnp.zeros((1, size), jnp.float32)]
        for lag in range(1, LAGS):
            pairs = jnp.where(place >= LAGS - lag, last * pltpu.roll(beyond, LAGS - lag, 0), 0.0)
            sums.append(jnp.sum(pairs, axis=0, keepdims=True))
        edge[...] = jnp.concatenate(sums, axis=0)

    outs = [(keep.shape, jnp.float32), ((LAGS, size), jnp.float32)]
    arrays = (keep, direct, direct_powers, near, near_powers, held, sides)
    return call_on_blocks(kernel, outs, *arrays, name="added", micros=MERGE_MICROS, after=after)


def finished(slab_rows, segment, partial, edge, ours, theirs, autos):
    chunk, width = partial.shape

    def kernel(partial, edge, ours, theirs, *refs):
        autos, (covariance, segment_auto) = refs[:-2], refs[-2:]
        first_lag = lax.axis_index("tm").astype(jnp.int32) * (chunk // REF)
        lag = lax.broadcasted_iota(jnp.int32, (chunk, 1), 0) // REF + first_lag
        denom = (slab_rows - lag).astype(jnp.float32)
        powers, own_refs, _ = sent_powers(ours)
        their_powers, their_refs, their_bound = sent_powers(theirs)
        total = partial[...] + expanded(theirs[:chunk], their_bound, ref_column(their_refs))
        scale = 1.0 / jnp.sqrt((powers + their_powers) / slab_rows + 1e-06)
        ref_scale = 1.0 / jnp.sqrt(ref_column(own_refs + their_refs) / slab_rows + 1e-06)
        covariance[...] = total * scale * (for_chunk(ref_scale, chunk) / denom)
        first = 0
        for auto in autos:
            here = slice(first, first + auto.shape[1])
            sums = auto[...] + edge[...] if first == 0 else auto[...]
            segment_auto[:, here] = sums * (scale[:, here] * scale[:, here]) / segment
            first = here.stop

    outs = [(partial.shape, jnp.float32), ((LAGS, width), jnp.float32)]
    return call_on_blocks(
        kernel,
        outs,
        partial,
        edge,
        ours,
        theirs,
        *autos,
        name="finished",
        micros=MERGE_MICROS,
        space=jax.ShapeDtypeStruct,
    )


def segment_kernel(first, held, power, tail, out, wide):
    rows = held.shape[0]
    step = rows // 8
    pitch = step + LAGS
    for index in range(out.shape[1] // LANES):
        here = slice(first + index * LANES, first + (index + 1) * LANES)
        there = slice(index * LANES, (index + 1) * LANES)
        for part in range(8):
            end = (part + 1) * step
            wide[part * pitch : part * pitch + step, :] = held[end - step : end, here].astype(jnp.float32)
            if part < 7:
                following = held[end : end + LAGS, here].astype(jnp.float32)
            elif tail is None:
                following = jnp.zeros((LAGS, LANES), jnp.float32)
            else:
                following = tail[:LAGS, here].astype(jnp.float32)
            wide[part * pitch + step : (part + 1) * pitch, :] = following
        taken = lambda first: wide[pl.ds(first, 8, stride=pitch), :]

        def advance(index, carry):
            window, sums = carry
            window = window + (taken(index + LAGS - 1),)
            sums = tuple(total + window[0] * window[lag + 1] for lag, total in enumerate(sums))
            return window[1:], sums

        window = tuple(taken(first) for first in range(LAGS - 1))
        zero = jnp.zeros((8, LANES), jnp.float32)
        _, sums = lax.fori_loop(0, step, advance, (window, (zero,) * (LAGS - 1)), unroll=16)
        out[:, there] = jnp.concatenate(
            [power[:, here]] + [jnp.sum(total, axis=0, keepdims=True) for total in sums], axis=0
        )


def segment_rows(held, power, tail, first, size, after=()):
    rows = held.shape[0]
    arrays = (held, power) if tail is None else (held, power, tail)

    def kernel(*refs):
        held, power, *rest = refs
        if tail is None:
            rest = [None] + rest
        segment_kernel(first, held, power, *rest)

    return call_on_blocks(
        kernel,
        [((LAGS, size), jnp.float32)],
        *arrays,
        name="segment_rows",
        micros=SEGMENT_MICROS,
        after=after,
        scratch=[pltpu.VMEM((rows + 8 * LAGS, LANES), jnp.float32)],
    )[0]


def all_products_kernel(held, own, other, tail, out, shifted):
    chan = lax.axis_index("chan")
    zeros = jnp.zeros((HALF, LANES), jnp.float32)
    for refs, half in ((own, chan), (other, 1 - chan)):
        long = jnp.concatenate([refs[...].astype(jnp.float32), zeros], axis=1)
        for index in range(GROUP):
            start = pl.multiple_of(index * REF + half * HALF, HALF)
            lag = pl.program_id(0) * GROUP + index
            shifted[pl.ds(start, HALF), :] = pltpu.roll(long, lag, 1).astype(jnp.bfloat16)
    rows, width = held.shape
    edge = jnp.concatenate([tail[...], jnp.zeros((LANES - LAGS, width), tail.dtype)], axis=0)
    for here in columns(width):
        total = jnp.dot(shifted[:, rows:], edge[:, here], preferred_element_type=jnp.float32)
        out[:, here] = total + jnp.dot(shifted[:, :rows], held[:, here], preferred_element_type=jnp.float32)


def all_products(held, own, other, tail):
    rows, width = held.shape
    vmem = pl.BlockSpec(memory_space=pltpu.VMEM)
    return pl.pallas_call(
        all_products_kernel,
        grid=(LAGS // GROUP,),
        in_specs=[vmem] * 4,
        out_specs=pl.BlockSpec((GROUP * REF, width), lambda group: (group, 0)),
        out_shape=jax.ShapeDtypeStruct((LAGS * REF, width), jnp.float32),
        scratch_shapes=[pltpu.VMEM((GROUP * REF, rows + LANES), jnp.bfloat16)],
        compiler_params=pltpu.CompilerParams(vmem_limit_bytes=VMEM_BYTES),
        name="all_products",
    )(held, own, other, tail)


def from_pair_ahead(value):
    count = lax.axis_size("tm")
    return lax.ppermute(value, "tm", [(time + 2, time) for time in range(0, count - 2, 2)])


def local(strain):
    rows, width = strain.shape
    count = lax.axis_size("tm")
    slab_rows = rows * count
    chunk = LAGS * REF // count

    own, head = prepared(strain)
    other = exchanged(own, "chan", 1)
    held, power = loaded(strain, own)
    size = width // 4

    if chunk * 2 == GROUP * REF:
        keep6, send7 = first_products(held, power, own, other, chunk)
        got7 = exchanged(send7, "tm", 1)
        after_next = from_pair_ahead(head)
        keep4, send5 = later_products((2,), held, own, other, send7, chunk)
        sides, send5 = sides_to_swap(head, after_next, own, other, send5)
        got5 = exchanged(send5, "tm", 1)
        tails = (sides, exchanged(sides, "tm", 1))
        autos = [segment_rows(held, power, None, 0, size, after=(sides,))]
        keep6, keep4, beyond = with_boundaries((keep6, keep4), (3, 2), own, other, *tails, after=(autos[0],))
        (send6,) = merged(keep6, send7, got7, beyond=(beyond,))
        got6 = exchanged(send6, "tm", 2)
        keep2, send3, keep0, send1 = later_products(
            (1, 0), held, own, other, send7, chunk, tails=tails, after=(send6,)
        )
        got3 = exchanged(send3, "tm", 1)
        send4, send1 = merged(keep4, send6, got6, direct=(got5, got7), held_back=(send1,), after=(send3,))
        got4 = exchanged(send4, "tm", 4)
        got1 = exchanged(send1, "tm", 1)
        autos.append(segment_rows(held, power, tails[1], size, size, after=(send4,)))
        send2 = resent(keep2, got3, got7, send6, after=(autos[1],))
        got2 = exchanged(send2, "tm", 2)
        autos.append(segment_rows(held, power, tails[1], 2 * size, 2 * size, after=(send2,)))
        partial, edge = added(keep0, got1, got7, got2, got6, held, tails[1], size, after=(autos[2],))
        return tuple(finished(slab_rows, rows, partial, edge, send4, got4, autos))

    tail = passed_along(head, "tm", -1)
    chan = lax.axis_index("chan").astype(jnp.int32)
    time = lax.axis_index("tm").astype(jnp.int32)
    auto = jnp.concatenate(
        [segment_rows(held, power, tail, size * index, size) for index in range(4)], axis=1
    )
    power_other = jnp.sum(jnp.square(other.astype(jnp.float32)), axis=1)
    power = lax.psum(jnp.concatenate([power[0], power_other]), "tm")
    inv = 1.0 / jnp.sqrt(power / slab_rows + 1e-06)
    scale = inv[:width]
    ref_scale = jnp.where(
        chan == 0,
        jnp.concatenate([inv[:HALF], inv[width:]]),
        jnp.concatenate([inv[width:], inv[:HALF]]),
    )
    products = all_products(held, own, other, tail)
    summed = lax.psum_scatter(products, "tm", scatter_dimension=0, tiled=True)
    row = time * chunk + jnp.arange(chunk, dtype=jnp.int32)
    row_scale = ref_scale[row % REF] / (slab_rows - row // REF).astype(jnp.float32)
    covariance = summed * scale[None, :] * row_scale[:, None]
    segment_auto = auto * (scale * scale)[None, :] / rows
    return (covariance, segment_auto)


def solution(mesh):
    in_specs = (P(("groups", "tm"), "chan"),)
    out_specs = (P(("groups", "tm"), "chan"), P(("groups", "tm"), "chan"))
    return jax.shard_map(local, mesh=mesh, in_specs=in_specs, out_specs=out_specs, check_vma=False)
```

```python
import jax
import jax.numpy as jnp
from jax import lax
from jax.experimental import pallas as pl
from jax.experimental.pallas import tpu as pltpu
from jax.sharding import PartitionSpec as P

LAGS = 16
REF = 64
HALF = REF // 2
LANES = 128
EXTRA = 8
FETCHES = 8
STEP = 256
GROUP = 4
POWER = 16
CODE_SCALE = 2.0 ** (126 / POWER)
TINY = 1e-35
PIECES = 4
VMEM_BYTES = 32 * 1024 * 1024
HBM_RATE = 3.69e6
PRODUCT_MICROS = 1.0
SEGMENT_MICROS = 1.2
MERGE_MICROS = 0.3


def lasting(micros):
    return pl.CostEstimate(flops=0, bytes_accessed=int(micros * HBM_RATE), transcendentals=0)


def passed_along(value, axis, steps):
    count = lax.axis_size(axis)
    initial, last = (max(0, -steps), min(count, count - steps))
    return lax.ppermute(value, axis, [(source, source + steps) for source in range(initial, last)])


def exchanged(value, axis, bit):
    count = lax.axis_size(axis)
    return lax.ppermute(value, axis, [(source, source ^ bit) for source in range(count)])


def as_column(row):
    size = row.shape[1]
    eye = lax.broadcasted_iota(jnp.int32, (size, size), 0) == lax.broadcasted_iota(jnp.int32, (size, size), 1)
    return jnp.sum(jnp.where(eye, row, 0.0), axis=1, keepdims=True)


def as_row(column):
    size = column.shape[0]
    eye = lax.broadcasted_iota(jnp.int32, (size, size), 0) == lax.broadcasted_iota(jnp.int32, (size, size), 1)
    return jnp.sum(jnp.where(eye, column, 0.0), axis=0, keepdims=True)


def for_chunk(ref_column, rows):
    return jnp.concatenate([ref_column] * (rows // REF), axis=0)


def bf16_pieces(value):
    high = value.astype(jnp.bfloat16).astype(jnp.float32)
    middle = (value - high).astype(jnp.bfloat16).astype(jnp.float32)
    return high, middle, value - high - middle


def packed(powers, ref_powers, channel_bound):
    rows = list(bf16_pieces(powers))
    refs = jnp.concatenate(bf16_pieces(ref_powers), axis=1)
    pad = jnp.zeros((1, powers.shape[1] - refs.shape[1]), jnp.float32)
    rows += [jnp.concatenate([refs, pad], axis=1), channel_bound]
    rows += [jnp.zeros_like(powers)] * (EXTRA - len(rows))
    return jnp.concatenate(rows, axis=0).astype(jnp.bfloat16)


def unpacked(block):
    wide = block.astype(jnp.float32)
    powers = wide[0:1] + wide[1:2] + wide[2:3]
    refs = wide[3:4, :LANES] + wide[3:4, LANES : 2 * LANES] + wide[3:4, 2 * LANES : 3 * LANES]
    return powers, refs, wide[4:5]


def sent_powers(code):
    return unpacked(code[-EXTRA:])


def rounded_up(value):
    return (value * (1.0 + 2.0**-7)).astype(jnp.bfloat16).astype(jnp.float32)


def coded(values, channel_bound, ref_bound):
    channel = lax.rsqrt(jnp.maximum(channel_bound, TINY))
    refs = lax.rsqrt(jnp.maximum(ref_bound, TINY)) * CODE_SCALE
    power = values * channel * for_chunk(refs, values.shape[0])
    for _ in range(4):
        power = power * jnp.abs(power)
    return power.astype(jnp.bfloat16)


def expanded(code, channel_bound, ref_bound):
    channel = jnp.sqrt(jnp.maximum(channel_bound, TINY))
    refs = jnp.sqrt(jnp.maximum(ref_bound, TINY)) * (1.0 / CODE_SCALE)
    wide = code[...].astype(jnp.float32)
    root = jnp.exp2(jnp.log2(jnp.abs(wide)) * (1.0 / POWER))
    return jnp.where(wide < 0.0, -root, root) * channel * for_chunk(refs, code.shape[0])


def ref_column(ref_powers):
    return as_column(ref_powers)[:REF]


def prepare_kernel(strain, own, head, left, sems):
    rows = left.shape[0]
    step = rows // PIECES
    copies = [
        pltpu.make_async_copy(
            strain.at[pl.ds(index * step, step), pl.ds(0, LANES)], left.at[pl.ds(index * step, step)], sems.at[index]
        )
        for index in range(PIECES)
    ]
    copies.append(pltpu.make_async_copy(strain.at[pl.ds(0, LAGS)], head, sems.at[PIECES]))
    for copy in copies:
        copy.start()
    for index in range(PIECES):
        copies[index].wait()
        here = slice(index * step, (index + 1) * step)
        own[:, here] = left[here, :].astype(jnp.float32).T[:HALF].astype(jnp.bfloat16)
    copies[PIECES].wait()


def prepared(strain):
    rows, width = strain.shape
    vmem = pl.BlockSpec(memory_space=pltpu.VMEM)
    return pl.pallas_call(
        prepare_kernel,
        in_specs=[pl.BlockSpec(memory_space=pl.ANY)],
        out_specs=[vmem, vmem],
        out_shape=[pltpu.VMEM((HALF, rows), strain.dtype), pltpu.VMEM((LAGS, width), strain.dtype)],
        scratch_shapes=[pltpu.VMEM((rows, LANES), strain.dtype), pltpu.SemaphoreType.DMA((PIECES + 1,))],
        compiler_params=pltpu.CompilerParams(vmem_limit_bytes=VMEM_BYTES),
        cost_estimate=lasting(PRODUCT_MICROS),
        name="prepared",
    )(pltpu.with_memory_space_constraint(strain, pltpu.HBM))


def lag_rows(own, other, group, shifted):
    chan, near = lax.axis_index("chan"), lax.axis_index("tm") & 1
    rows = own.shape[1]
    zeros = jnp.zeros((HALF, LANES), jnp.float32)
    for refs, half in ((own, chan), (other, 1 - chan)):
        long = jnp.concatenate([zeros, refs[...].astype(jnp.float32)], axis=1)
        for index in range(GROUP):
            ahead = near if index < GROUP // 2 else 1 - near
            lag = group * GROUP + ahead * (GROUP // 2) + index % (GROUP // 2)
            start = pl.multiple_of(index * REF + half * HALF, HALF)
            moved = pltpu.roll(long, lag, 1)[:, LANES : LANES + rows]
            shifted[pl.ds(start, HALF), :] = moved.astype(jnp.bfloat16)


def own_group(bits):
    return lax.shift_right_logical(lax.axis_index("tm").astype(jnp.int32), 1) ^ bits


def loaded_kernel(strain, held, power, sems):
    step = held.shape[0] // FETCHES
    pieces = [slice(index * step, (index + 1) * step) for index in range(FETCHES)]
    copies = [
        pltpu.make_async_copy(strain.at[pl.ds(here.start, step)], held.at[pl.ds(here.start, step)], sems.at[index])
        for index, here in enumerate(pieces)
    ]
    for copy in copies:
        copy.start()
    total = jnp.zeros((8, held.shape[1]), jnp.float32)
    for copy, here in zip(copies, pieces):
        copy.wait()
        squares = jnp.square(held[here, :].astype(jnp.float32))
        total += jnp.sum(squares.reshape(step // 8, 8, held.shape[1]), axis=0)
    power[...] = jnp.sum(total, axis=0, keepdims=True)


def loaded(strain, after):
    rows, width = strain.shape
    vmem = pl.BlockSpec(memory_space=pltpu.VMEM)

    def kernel(strain, after, held, power, sems):
        loaded_kernel(strain, held, power, sems)

    return pl.pallas_call(
        kernel,
        in_specs=[pl.BlockSpec(memory_space=pl.ANY)] * 2,
        out_specs=[vmem, vmem],
        out_shape=[pltpu.VMEM((rows, width), strain.dtype), pltpu.VMEM((1, width), jnp.float32)],
        scratch_shapes=[pltpu.SemaphoreType.DMA((FETCHES,))],
        compiler_params=pltpu.CompilerParams(vmem_limit_bytes=VMEM_BYTES),
        cost_estimate=lasting(PRODUCT_MICROS),
        name="loaded",
    )(pltpu.with_memory_space_constraint(strain, pltpu.HBM), after)


def columns(width):
    return [slice(first, first + STEP) for first in range(0, width, STEP)]


def product_of(shifted, held, here):
    return jnp.dot(shifted[...], held[:, here], preferred_element_type=jnp.float32)


def boundary_rows(group, ends, their_ends, edges):
    chan, near = lax.axis_index("chan"), lax.axis_index("tm") & 1
    zeros = jnp.zeros((HALF, LANES), jnp.float32)
    ours = [(refs[:, refs.shape[1] - LANES :].astype(jnp.float32), half) for refs, half in zip(ends, (chan, 1 - chan))]
    theirs = [(their_ends[half * HALF : (half + 1) * HALF], half) for half in range(2)]
    for side, parts in enumerate((ours, theirs)):
        for end, half in parts:
            long = jnp.concatenate([end, zeros], axis=1)
            for index in range(GROUP // 2):
                lag = group * GROUP + near * (GROUP // 2) + index
                start = pl.multiple_of(index * REF + half * HALF, HALF)
                moved = pltpu.roll(long, lag, 1)[:, LANES:]
                edges[pl.ds(start, HALF), side * LANES : (side + 1) * LANES] = moved.astype(jnp.bfloat16)


def ends_of(code):
    rows = code[LAGS : 2 * LAGS, :LANES].astype(jnp.float32)
    return jnp.concatenate([jnp.zeros((LANES - LAGS, LANES), jnp.float32), rows], axis=0).T[:REF]


def tails_of(sent, arrived, here):
    zeros = jnp.zeros((LANES - LAGS, here.stop - here.start), jnp.bfloat16)
    return jnp.concatenate([arrived[:LAGS, here], zeros, sent[:LAGS, here], zeros], axis=0)


def first_products_kernel(held, power, own, other, keep, send, shifted):
    lag_rows(own, other, own_group(3), shifted)
    ours, theirs = [
        jnp.sum(jnp.square(refs[...].astype(jnp.float32)), axis=1, keepdims=True) for refs in (own, other)
    ]
    refs = jnp.where(
        lax.axis_index("chan") == 0,
        jnp.concatenate([ours, theirs], axis=0),
        jnp.concatenate([theirs, ours], axis=0),
    )
    bound = rounded_up(power[...])
    pad = jnp.zeros((1, LANES - REF), jnp.float32)
    chunk = keep.shape[0]
    send[chunk:] = packed(power[...], jnp.concatenate([as_row(refs), pad], axis=1), bound)
    for here in columns(held.shape[1]):
        product = product_of(shifted, held, here)
        keep[:, here] = product[:chunk]
        send[:chunk, here] = coded(product[chunk:], bound[:, here], refs)


def shifted_scratch(rows, groups=1):
    return [pltpu.VMEM((groups * GROUP * REF, rows), jnp.bfloat16)]


def first_products(held, power, own, other, chunk, after):
    rows, width = held.shape
    return call_on_blocks(
        first_products_kernel,
        [((chunk, width), jnp.float32), ((chunk + EXTRA, width), jnp.bfloat16)],
        held,
        power,
        own,
        other,
        name="first_products",
        micros=PRODUCT_MICROS,
        after=after,
        scratch=shifted_scratch(rows),
    )


def later_products(groups, held, own, other, powers, chunk, spare=0, after=()):
    rows, width = held.shape

    def kernel(held, own, other, powers, *rest):
        outs, shifted = rest[:-1], rest[-1]
        _, ref_powers, bound = sent_powers(powers)
        refs = ref_column(ref_powers)
        for index, bits in enumerate(groups):
            lag_rows(own, other, own_group(bits), shifted.at[pl.ds(index * 2 * chunk, 2 * chunk)])
            if spare:
                outs[2 * index + 1][chunk:] = jnp.zeros((spare, width), jnp.bfloat16)
        for here in columns(width):
            product = product_of(shifted, held, here)
            for index in range(len(groups)):
                keep, send = outs[2 * index : 2 * index + 2]
                first = 2 * index * chunk
                keep[:, here] = product[first : first + chunk]
                send[:chunk, here] = coded(product[first + chunk : first + 2 * chunk], bound[:, here], refs)

    return call_on_blocks(
        kernel,
        [((chunk, width), jnp.float32), ((chunk + spare, width), jnp.bfloat16)] * len(groups),
        held,
        own,
        other,
        powers,
        name="later_products",
        micros=PRODUCT_MICROS,
        after=after,
        scratch=shifted_scratch(rows, len(groups)),
    )


def edges_scratch(count, chunk):
    return [pltpu.VMEM((count, chunk, 2 * LANES), jnp.bfloat16)]


def sides_to_swap(head, after_next, own, other):
    width = head.shape[1]

    def kernel(head, after_next, own, other, sides):
        chan, near = lax.axis_index("chan"), lax.axis_index("tm") & 1
        sides[:LAGS] = jnp.where(near == 0, after_next[...], head[...])
        ours, theirs = [refs[:, refs.shape[1] - LANES :].astype(jnp.float32) for refs in (own, other)]
        first, second = jnp.where(chan == 0, ours, theirs), jnp.where(chan == 0, theirs, ours)
        square = jnp.concatenate([first, second, jnp.zeros((LANES - REF, LANES), jnp.float32)], axis=0)
        sides[LAGS:, :LANES] = square.T[LANES - LAGS :].astype(jnp.bfloat16)
        sides[LAGS:, LANES:] = jnp.zeros((LAGS, width - LANES), jnp.bfloat16)

    outs = [((2 * LAGS, width), jnp.bfloat16)]
    return call_on_blocks(kernel, outs, head, after_next, own, other, name="sides", micros=MERGE_MICROS)[0]


def with_boundaries(keeps, groups, own, other, sent, arrived):
    chunk, width = keeps[0].shape

    def kernel(own, other, sent, arrived, *rest):
        keeps, rest = rest[: len(groups)], rest[len(groups) :]
        outs, beyond, edges = rest[: len(groups)], rest[-2], rest[-1]
        for index, bits in enumerate(groups):
            boundary_rows(own_group(bits), (own, other), ends_of(arrived), edges.at[index])
        for here in columns(width):
            tails = tails_of(sent, arrived, here)
            for index in range(len(groups)):
                added = jnp.dot(edges[index], tails, preferred_element_type=jnp.float32)
                outs[index][:, here] = keeps[index][:, here] + added
            beyond[:, here] = jnp.sum(jnp.square(tails.astype(jnp.float32)), axis=0, keepdims=True)

    outs = [((chunk, width), jnp.float32)] * len(groups) + [((1, width), jnp.float32)]
    return call_on_blocks(
        kernel,
        outs,
        own,
        other,
        sent,
        arrived,
        *keeps,
        name="with_boundaries",
        micros=MERGE_MICROS,
        scratch=edges_scratch(len(groups), chunk),
    )


def call_on_blocks(kernel, outs, *arrays, name, micros, after=(), scratch=(), space=pltpu.VMEM):
    vmem = pl.BlockSpec(memory_space=pltpu.VMEM)
    count = len(arrays)

    def body(*refs):
        kernel(*refs[:count], *refs[count + len(after) :])

    return pl.pallas_call(
        body,
        in_specs=[vmem] * count + [pl.BlockSpec(memory_space=pl.ANY)] * len(after),
        out_specs=[vmem] * len(outs),
        out_shape=[space(shape, dtype) for shape, dtype in outs],
        scratch_shapes=list(scratch),
        compiler_params=pltpu.CompilerParams(vmem_limit_bytes=VMEM_BYTES),
        cost_estimate=lasting(micros),
        name=name,
    )(*arrays, *after)


def direct_sums(direct, powers):
    _, refs, bound = sent_powers(powers)
    chunk = direct.shape[0] // REF * REF
    return expanded(direct[:chunk], bound, ref_column(refs))


def merged(keep, ours, theirs, direct=(), beyond=(), held_back=(), after=()):
    chunk, width = keep.shape

    def kernel(keep, ours, theirs, *refs):
        inputs, out, passed = refs[: -1 - len(held_back)], refs[len(arrays) - 3], refs[len(arrays) - 2 :]
        powers, refs, bound = sent_powers(ours)
        their_powers, their_refs, their_bound = sent_powers(theirs)
        sums, sum_refs, sum_bound = powers + their_powers, refs + their_refs, bound + their_bound
        total = keep[...] + expanded(theirs[:chunk], their_bound, ref_column(their_refs))
        if direct:
            total += direct_sums(inputs[0], inputs[1])
        if beyond:
            sum_bound += inputs[len(direct)][...]
        if held_back:
            passed[0][...] = inputs[-1][...]
        sum_bound = rounded_up(sum_bound)
        out[chunk:] = packed(sums, sum_refs, sum_bound)
        out[:chunk] = coded(total, sum_bound, ref_column(sum_refs))

    outs = [((chunk + EXTRA, width), jnp.bfloat16)] + [(code.shape, code.dtype) for code in held_back]
    arrays = (keep, ours, theirs, *direct, *beyond, *held_back)
    return call_on_blocks(kernel, outs, *arrays, name="merged", micros=MERGE_MICROS, after=after)


def resent(keep, direct, direct_powers, ours, after):
    def kernel(keep, direct, direct_powers, ours, out):
        _, refs, bound = sent_powers(ours)
        out[...] = coded(keep[...] + direct_sums(direct, direct_powers), bound, ref_column(refs))

    outs = [(keep.shape, jnp.bfloat16)]
    arrays = (keep, direct, direct_powers, ours)
    return call_on_blocks(kernel, outs, *arrays, name="resent", micros=MERGE_MICROS, after=after)[0]


def added(keep, direct, direct_powers, near, near_powers, after):
    def kernel(keep, direct, direct_powers, near, near_powers, out):
        out[...] = keep[...] + direct_sums(direct, direct_powers) + direct_sums(near, near_powers)

    outs = [(keep.shape, jnp.float32)]
    arrays = (keep, direct, direct_powers, near, near_powers)
    return call_on_blocks(kernel, outs, *arrays, name="added", micros=MERGE_MICROS, after=after)[0]


def finished(slab_rows, segment, partial, ours, theirs, autos):
    chunk, width = partial.shape

    def kernel(partial, ours, theirs, *refs):
        autos, (covariance, segment_auto) = refs[:-2], refs[-2:]
        first_lag = lax.axis_index("tm").astype(jnp.int32) * (chunk // REF)
        lag = lax.broadcasted_iota(jnp.int32, (chunk, 1), 0) // REF + first_lag
        denom = (slab_rows - lag).astype(jnp.float32)
        powers, own_refs, _ = sent_powers(ours)
        their_powers, their_refs, their_bound = sent_powers(theirs)
        total = partial[...] + expanded(theirs[:chunk], their_bound, ref_column(their_refs))
        scale = 1.0 / jnp.sqrt((powers + their_powers) / slab_rows + 1e-06)
        ref_scale = 1.0 / jnp.sqrt(ref_column(own_refs + their_refs) / slab_rows + 1e-06)
        covariance[...] = total * scale * (for_chunk(ref_scale, chunk) / denom)
        first = 0
        for auto in autos:
            here = slice(first, first + auto.shape[1])
            segment_auto[:, here] = auto[...] * (scale[:, here] * scale[:, here]) / segment
            first = here.stop

    outs = [(partial.shape, jnp.float32), ((LAGS, width), jnp.float32)]
    return call_on_blocks(
        kernel,
        outs,
        partial,
        ours,
        theirs,
        *autos,
        name="finished",
        micros=MERGE_MICROS,
        space=jax.ShapeDtypeStruct,
    )


def segment_kernel(first, held, power, tail, out, wide):
    rows = held.shape[0]
    step = rows // 8
    pitch = step + LAGS
    for index in range(out.shape[1] // LANES):
        here = slice(first + index * LANES, first + (index + 1) * LANES)
        there = slice(index * LANES, (index + 1) * LANES)
        for part in range(8):
            end = (part + 1) * step
            wide[part * pitch : part * pitch + step, :] = held[end - step : end, here].astype(jnp.float32)
            if part < 7:
                following = held[end : end + LAGS, here].astype(jnp.float32)
            else:
                following = tail[:LAGS, here].astype(jnp.float32)
            wide[part * pitch + step : (part + 1) * pitch, :] = following
        taken = lambda first: wide[pl.ds(first, 8, stride=pitch), :]

        def advance(index, carry):
            window, sums = carry
            window = window + (taken(index + LAGS - 1),)
            sums = tuple(total + window[0] * window[lag + 1] for lag, total in enumerate(sums))
            return window[1:], sums

        window = tuple(taken(first) for first in range(LAGS - 1))
        zero = jnp.zeros((8, LANES), jnp.float32)
        _, sums = lax.fori_loop(0, step, advance, (window, (zero,) * (LAGS - 1)), unroll=16)
        out[:, there] = jnp.concatenate(
            [power[:, here]] + [jnp.sum(total, axis=0, keepdims=True) for total in sums], axis=0
        )


def segment_rows(held, power, tail, first, size, after=()):
    rows = held.shape[0]

    def kernel(*refs):
        segment_kernel(first, *refs)

    return call_on_blocks(
        kernel,
        [((LAGS, size), jnp.float32)],
        held,
        power,
        tail,
        name="segment_rows",
        micros=SEGMENT_MICROS,
        after=after,
        scratch=[pltpu.VMEM((rows + 8 * LAGS, LANES), jnp.float32)],
    )[0]


def all_products_kernel(held, own, other, tail, out, shifted):
    chan = lax.axis_index("chan")
    zeros = jnp.zeros((HALF, LANES), jnp.float32)
    for refs, half in ((own, chan), (other, 1 - chan)):
        long = jnp.concatenate([refs[...].astype(jnp.float32), zeros], axis=1)
        for index in range(GROUP):
            start = pl.multiple_of(index * REF + half * HALF, HALF)
            lag = pl.program_id(0) * GROUP + index
            shifted[pl.ds(start, HALF), :] = pltpu.roll(long, lag, 1).astype(jnp.bfloat16)
    rows, width = held.shape
    edge = jnp.concatenate([tail[...], jnp.zeros((LANES - LAGS, width), tail.dtype)], axis=0)
    for here in columns(width):
        total = jnp.dot(shifted[:, rows:], edge[:, here], preferred_element_type=jnp.float32)
        out[:, here] = total + jnp.dot(shifted[:, :rows], held[:, here], preferred_element_type=jnp.float32)


def all_products(held, own, other, tail):
    rows, width = held.shape
    vmem = pl.BlockSpec(memory_space=pltpu.VMEM)
    return pl.pallas_call(
        all_products_kernel,
        grid=(LAGS // GROUP,),
        in_specs=[vmem] * 4,
        out_specs=pl.BlockSpec((GROUP * REF, width), lambda group: (group, 0)),
        out_shape=jax.ShapeDtypeStruct((LAGS * REF, width), jnp.float32),
        scratch_shapes=[pltpu.VMEM((GROUP * REF, rows + LANES), jnp.bfloat16)],
        compiler_params=pltpu.CompilerParams(vmem_limit_bytes=VMEM_BYTES),
        name="all_products",
    )(held, own, other, tail)


def from_pair_ahead(value):
    count = lax.axis_size("tm")
    return lax.ppermute(value, "tm", [(time + 2, time) for time in range(0, count - 2, 2)])


def local(strain):
    rows, width = strain.shape
    count = lax.axis_size("tm")
    slab_rows = rows * count
    chunk = LAGS * REF // count

    own, head = prepared(strain)
    other = exchanged(own, "chan", 1)
    held, power = loaded(strain, own)
    size = width // 2

    if chunk * 2 == GROUP * REF:
        after_next = from_pair_ahead(head)
        keep6, send7 = first_products(held, power, own, other, chunk, after=(after_next,))
        got7 = exchanged(send7, "tm", 1)
        keep4, send5 = later_products((2,), held, own, other, send7, chunk, spare=LAGS)
        got5 = exchanged(send5, "tm", 1)
        sides = sides_to_swap(head, after_next, own, other)
        tails = (sides, exchanged(sides, "tm", 1))
        keep2, send3, keep0, send1 = later_products(
            (1, 0), held, own, other, send7, chunk, after=(send5, sides)
        )
        *keeps, beyond = with_boundaries((keep6, keep4, keep2, keep0), (3, 2, 1, 0), own, other, *tails)
        keep6, keep4, keep2, keep0 = keeps
        send6, send3 = merged(keep6, send7, got7, beyond=(beyond,), held_back=(send3,))
        got6 = exchanged(send6, "tm", 2)
        got3 = exchanged(send3, "tm", 1)
        autos = [segment_rows(held, power, tails[1], 0, size, after=(send6,))]
        send4, send1 = merged(
            keep4, send6, got6, direct=(got5, got7), held_back=(send1,), after=(autos[0],)
        )
        got4 = exchanged(send4, "tm", 4)
        got1 = exchanged(send1, "tm", 1)
        send2 = resent(keep2, got3, got7, send6, after=(send4,))
        got2 = exchanged(send2, "tm", 2)
        autos.append(segment_rows(held, power, tails[1], size, size, after=(send2,)))
        partial = added(keep0, got1, got7, got2, got6, after=(autos[1],))
        return tuple(finished(slab_rows, rows, partial, send4, got4, autos))

    tail = passed_along(head, "tm", -1)
    chan = lax.axis_index("chan").astype(jnp.int32)
    time = lax.axis_index("tm").astype(jnp.int32)
    auto = jnp.concatenate(
        [segment_rows(held, power, tail, size * index, size) for index in range(2)], axis=1
    )
    power_other = jnp.sum(jnp.square(other.astype(jnp.float32)), axis=1)
    power = lax.psum(jnp.concatenate([power[0], power_other]), "tm")
    inv = 1.0 / jnp.sqrt(power / slab_rows + 1e-06)
    scale = inv[:width]
    ref_scale = jnp.where(
        chan == 0,
        jnp.concatenate([inv[:HALF], inv[width:]]),
        jnp.concatenate([inv[width:], inv[:HALF]]),
    )
    products = all_products(held, own, other, tail)
    summed = lax.psum_scatter(products, "tm", scatter_dimension=0, tiled=True)
    row = time * chunk + jnp.arange(chunk, dtype=jnp.int32)
    row_scale = ref_scale[row % REF] / (slab_rows - row // REF).astype(jnp.float32)
    covariance = summed * scale[None, :] * row_scale[:, None]
    segment_auto = auto * (scale * scale)[None, :] / rows
    return (covariance, segment_auto)


def solution(mesh):
    in_specs = (P(("groups", "tm"), "chan"),)
    out_specs = (P(("groups", "tm"), "chan"), P(("groups", "tm"), "chan"))
    return jax.shard_map(local, mesh=mesh, in_specs=in_specs, out_specs=out_specs, check_vma=False)
```

```python
import jax
import jax.numpy as jnp
from jax import lax
from jax.experimental import pallas as pl
from jax.experimental.pallas import tpu as pltpu
from jax.sharding import PartitionSpec as P

LAGS = 16
REF = 64
HALF = REF // 2
LANES = 128
EXTRA = 8
FETCHES = 8
STEP = 256
GROUP = 4
POWER = 16
CODE_SCALE = 2.0 ** (126 / POWER)
TINY = 1e-35
PIECES = 4
VMEM_BYTES = 32 * 1024 * 1024
HBM_RATE = 3.69e6
PRODUCT_MICROS = 1.0
SEGMENT_MICROS = 1.2
MERGE_MICROS = 0.3


def lasting(micros):
    return pl.CostEstimate(flops=0, bytes_accessed=int(micros * HBM_RATE), transcendentals=0)


def passed_along(value, axis, steps):
    count = lax.axis_size(axis)
    initial, last = (max(0, -steps), min(count, count - steps))
    return lax.ppermute(value, axis, [(source, source + steps) for source in range(initial, last)])


def exchanged(value, axis, bit):
    count = lax.axis_size(axis)
    return lax.ppermute(value, axis, [(source, source ^ bit) for source in range(count)])


def as_column(row):
    size = row.shape[1]
    eye = lax.broadcasted_iota(jnp.int32, (size, size), 0) == lax.broadcasted_iota(jnp.int32, (size, size), 1)
    return jnp.sum(jnp.where(eye, row, 0.0), axis=1, keepdims=True)


def as_row(column):
    size = column.shape[0]
    eye = lax.broadcasted_iota(jnp.int32, (size, size), 0) == lax.broadcasted_iota(jnp.int32, (size, size), 1)
    return jnp.sum(jnp.where(eye, column, 0.0), axis=0, keepdims=True)


def for_chunk(ref_column, rows):
    return jnp.concatenate([ref_column] * (rows // REF), axis=0)


def bf16_pieces(value):
    high = value.astype(jnp.bfloat16).astype(jnp.float32)
    middle = (value - high).astype(jnp.bfloat16).astype(jnp.float32)
    return high, middle, value - high - middle


def packed(powers, ref_powers, channel_bound):
    rows = list(bf16_pieces(powers))
    refs = jnp.concatenate(bf16_pieces(ref_powers), axis=1)
    pad = jnp.zeros((1, powers.shape[1] - refs.shape[1]), jnp.float32)
    rows += [jnp.concatenate([refs, pad], axis=1), channel_bound]
    rows += [jnp.zeros_like(powers)] * (EXTRA - len(rows))
    return jnp.concatenate(rows, axis=0).astype(jnp.bfloat16)


def unpacked(block):
    wide = block.astype(jnp.float32)
    powers = wide[0:1] + wide[1:2] + wide[2:3]
    refs = wide[3:4, :LANES] + wide[3:4, LANES : 2 * LANES] + wide[3:4, 2 * LANES : 3 * LANES]
    return powers, refs, wide[4:5]


def sent_powers(code):
    return unpacked(code[-EXTRA:])


def rounded_up(value):
    return (value * (1.0 + 2.0**-7)).astype(jnp.bfloat16).astype(jnp.float32)


def coded(values, channel_bound, ref_bound):
    channel = lax.rsqrt(jnp.maximum(channel_bound, TINY))
    refs = lax.rsqrt(jnp.maximum(ref_bound, TINY)) * CODE_SCALE
    power = values * channel * for_chunk(refs, values.shape[0])
    for _ in range(4):
        power = power * jnp.abs(power)
    return power.astype(jnp.bfloat16)


def expanded(code, channel_bound, ref_bound):
    channel = jnp.sqrt(jnp.maximum(channel_bound, TINY))
    refs = jnp.sqrt(jnp.maximum(ref_bound, TINY)) * (1.0 / CODE_SCALE)
    wide = code[...].astype(jnp.float32)
    root = jnp.exp2(jnp.log2(jnp.abs(wide)) * (1.0 / POWER))
    return jnp.where(wide < 0.0, -root, root) * channel * for_chunk(refs, code.shape[0])


def ref_column(ref_powers):
    return as_column(ref_powers)[:REF]


def prepare_kernel(strain, own, head, left, sems):
    rows = left.shape[0]
    step = rows // PIECES
    copies = [
        pltpu.make_async_copy(
            strain.at[pl.ds(index * step, step), pl.ds(0, LANES)], left.at[pl.ds(index * step, step)], sems.at[index]
        )
        for index in range(PIECES)
    ]
    copies.append(pltpu.make_async_copy(strain.at[pl.ds(0, LAGS)], head, sems.at[PIECES]))
    for copy in copies:
        copy.start()
    for index in range(PIECES):
        copies[index].wait()
        here = slice(index * step, (index + 1) * step)
        own[:, here] = left[here, :].astype(jnp.float32).T[:HALF].astype(jnp.bfloat16)
    copies[PIECES].wait()


def prepared(strain):
    rows, width = strain.shape
    vmem = pl.BlockSpec(memory_space=pltpu.VMEM)
    return pl.pallas_call(
        prepare_kernel,
        in_specs=[pl.BlockSpec(memory_space=pl.ANY)],
        out_specs=[vmem, vmem],
        out_shape=[pltpu.VMEM((HALF, rows), strain.dtype), pltpu.VMEM((LAGS, width), strain.dtype)],
        scratch_shapes=[pltpu.VMEM((rows, LANES), strain.dtype), pltpu.SemaphoreType.DMA((PIECES + 1,))],
        compiler_params=pltpu.CompilerParams(vmem_limit_bytes=VMEM_BYTES),
        cost_estimate=lasting(PRODUCT_MICROS),
        name="prepared",
    )(pltpu.with_memory_space_constraint(strain, pltpu.HBM))


def lag_rows(own, other, group, shifted):
    chan, near = lax.axis_index("chan"), lax.axis_index("tm") & 1
    rows = own.shape[1]
    zeros = jnp.zeros((HALF, LANES), jnp.float32)
    for refs, half in ((own, chan), (other, 1 - chan)):
        long = jnp.concatenate([zeros, refs[...].astype(jnp.float32)], axis=1)
        for index in range(GROUP):
            ahead = near if index < GROUP // 2 else 1 - near
            lag = group * GROUP + ahead * (GROUP // 2) + index % (GROUP // 2)
            start = pl.multiple_of(index * REF + half * HALF, HALF)
            moved = pltpu.roll(long, lag, 1)[:, LANES : LANES + rows]
            shifted[pl.ds(start, HALF), :] = moved.astype(jnp.bfloat16)


def own_group(bits):
    return lax.shift_right_logical(lax.axis_index("tm").astype(jnp.int32), 1) ^ bits


def loaded_kernel(strain, held, power, sems):
    step = held.shape[0] // FETCHES
    pieces = [slice(index * step, (index + 1) * step) for index in range(FETCHES)]
    copies = [
        pltpu.make_async_copy(strain.at[pl.ds(here.start, step)], held.at[pl.ds(here.start, step)], sems.at[index])
        for index, here in enumerate(pieces)
    ]
    for copy in copies:
        copy.start()
    total = jnp.zeros((8, held.shape[1]), jnp.float32)
    for copy, here in zip(copies, pieces):
        copy.wait()
        squares = jnp.square(held[here, :].astype(jnp.float32))
        total += jnp.sum(squares.reshape(step // 8, 8, held.shape[1]), axis=0)
    power[...] = jnp.sum(total, axis=0, keepdims=True)


def loaded(strain, after):
    rows, width = strain.shape
    vmem = pl.BlockSpec(memory_space=pltpu.VMEM)

    def kernel(strain, after, held, power, sems):
        loaded_kernel(strain, held, power, sems)

    return pl.pallas_call(
        kernel,
        in_specs=[pl.BlockSpec(memory_space=pl.ANY)] * 2,
        out_specs=[vmem, vmem],
        out_shape=[pltpu.VMEM((rows, width), strain.dtype), pltpu.VMEM((1, width), jnp.float32)],
        scratch_shapes=[pltpu.SemaphoreType.DMA((FETCHES,))],
        compiler_params=pltpu.CompilerParams(vmem_limit_bytes=VMEM_BYTES),
        cost_estimate=lasting(PRODUCT_MICROS),
        name="loaded",
    )(pltpu.with_memory_space_constraint(strain, pltpu.HBM), after)


def columns(width):
    return [slice(first, first + STEP) for first in range(0, width, STEP)]


def product_of(shifted, held, here):
    return jnp.dot(shifted[...], held[:, here], preferred_element_type=jnp.float32)


def boundary_rows(group, ends, their_ends, edges):
    chan, near = lax.axis_index("chan"), lax.axis_index("tm") & 1
    zeros = jnp.zeros((HALF, LANES), jnp.float32)
    ours = [(refs[:, refs.shape[1] - LANES :].astype(jnp.float32), half) for refs, half in zip(ends, (chan, 1 - chan))]
    theirs = [(their_ends[half * HALF : (half + 1) * HALF], half) for half in range(2)]
    for side, parts in enumerate((ours, theirs)):
        for end, half in parts:
            long = jnp.concatenate([end, zeros], axis=1)
            for index in range(GROUP // 2):
                lag = group * GROUP + near * (GROUP // 2) + index
                start = pl.multiple_of(index * REF + half * HALF, HALF)
                moved = pltpu.roll(long, lag, 1)[:, LANES:]
                edges[pl.ds(start, HALF), side * LANES : (side + 1) * LANES] = moved.astype(jnp.bfloat16)


def ends_of(code):
    rows = code[LAGS : 2 * LAGS, :LANES].astype(jnp.float32)
    return jnp.concatenate([jnp.zeros((LANES - LAGS, LANES), jnp.float32), rows], axis=0).T[:REF]


def tails_of(sent, arrived, here):
    zeros = jnp.zeros((LANES - LAGS, here.stop - here.start), jnp.bfloat16)
    return jnp.concatenate([arrived[:LAGS, here], zeros, sent[:LAGS, here], zeros], axis=0)


def first_products_kernel(held, power, own, other, keep, send, shifted):
    lag_rows(own, other, own_group(3), shifted)
    ours, theirs = [
        jnp.sum(jnp.square(refs[...].astype(jnp.float32)), axis=1, keepdims=True) for refs in (own, other)
    ]
    refs = jnp.where(
        lax.axis_index("chan") == 0,
        jnp.concatenate([ours, theirs], axis=0),
        jnp.concatenate([theirs, ours], axis=0),
    )
    bound = rounded_up(power[...])
    pad = jnp.zeros((1, LANES - REF), jnp.float32)
    chunk = keep.shape[0]
    send[chunk:] = packed(power[...], jnp.concatenate([as_row(refs), pad], axis=1), bound)
    for here in columns(held.shape[1]):
        product = product_of(shifted, held, here)
        keep[:, here] = product[:chunk]
        send[:chunk, here] = coded(product[chunk:], bound[:, here], refs)


def shifted_scratch(rows, groups=1):
    return [pltpu.VMEM((groups * GROUP * REF, rows), jnp.bfloat16)]


def first_products(held, power, own, other, chunk):
    rows, width = held.shape
    return call_on_blocks(
        first_products_kernel,
        [((chunk, width), jnp.float32), ((chunk + EXTRA, width), jnp.bfloat16)],
        held,
        power,
        own,
        other,
        name="first_products",
        micros=PRODUCT_MICROS,
        scratch=shifted_scratch(rows),
    )


def later_products(groups, held, own, other, powers, chunk):
    rows, width = held.shape

    def kernel(held, own, other, powers, *rest):
        outs, shifted = rest[:-1], rest[-1]
        _, ref_powers, bound = sent_powers(powers)
        refs = ref_column(ref_powers)
        for index, bits in enumerate(groups):
            lag_rows(own, other, own_group(bits), shifted.at[pl.ds(index * 2 * chunk, 2 * chunk)])
        for here in columns(width):
            product = product_of(shifted, held, here)
            for index in range(len(groups)):
                keep, send = outs[2 * index : 2 * index + 2]
                first = 2 * index * chunk
                keep[:, here] = product[first : first + chunk]
                send[:, here] = coded(product[first + chunk : first + 2 * chunk], bound[:, here], refs)

    return call_on_blocks(
        kernel,
        [((chunk, width), jnp.float32), ((chunk, width), jnp.bfloat16)] * len(groups),
        held,
        own,
        other,
        powers,
        name="later_products",
        micros=PRODUCT_MICROS,
        scratch=shifted_scratch(rows, len(groups)),
    )


def edges_scratch(count, chunk):
    return [pltpu.VMEM((count, chunk, 2 * LANES), jnp.bfloat16)]


def sides_to_swap(head, after_next, own, other, held_back):
    rows, width = held_back.shape

    def kernel(head, after_next, own, other, held_back, sides, passed):
        chan, near = lax.axis_index("chan"), lax.axis_index("tm") & 1
        passed[:rows] = held_back[...]
        passed[rows:] = jnp.zeros((LAGS, width), jnp.bfloat16)
        sides[:LAGS] = jnp.where(near == 0, after_next[...], head[...])
        ours, theirs = [refs[:, refs.shape[1] - LANES :].astype(jnp.float32) for refs in (own, other)]
        first, second = jnp.where(chan == 0, ours, theirs), jnp.where(chan == 0, theirs, ours)
        square = jnp.concatenate([first, second, jnp.zeros((LANES - REF, LANES), jnp.float32)], axis=0)
        sides[LAGS:, :LANES] = square.T[LANES - LAGS :].astype(jnp.bfloat16)
        sides[LAGS:, LANES:] = jnp.zeros((LAGS, width - LANES), jnp.bfloat16)

    outs = [((2 * LAGS, width), jnp.bfloat16), ((rows + LAGS, width), jnp.bfloat16)]
    arrays = (head, after_next, own, other, held_back)
    return call_on_blocks(kernel, outs, *arrays, name="sides", micros=MERGE_MICROS)


def with_boundaries(keeps, groups, own, other, sent, arrived):
    chunk, width = keeps[0].shape

    def kernel(own, other, sent, arrived, *rest):
        keeps, rest = rest[: len(groups)], rest[len(groups) :]
        outs, beyond, edges = rest[: len(groups)], rest[-2], rest[-1]
        for index, bits in enumerate(groups):
            boundary_rows(own_group(bits), (own, other), ends_of(arrived), edges.at[index])
        for here in columns(width):
            tails = tails_of(sent, arrived, here)
            for index in range(len(groups)):
                added = jnp.dot(edges[index], tails, preferred_element_type=jnp.float32)
                outs[index][:, here] = keeps[index][:, here] + added
            beyond[:, here] = jnp.sum(jnp.square(tails.astype(jnp.float32)), axis=0, keepdims=True)

    outs = [((chunk, width), jnp.float32)] * len(groups) + [((1, width), jnp.float32)]
    return call_on_blocks(
        kernel,
        outs,
        own,
        other,
        sent,
        arrived,
        *keeps,
        name="with_boundaries",
        micros=MERGE_MICROS,
        scratch=edges_scratch(len(groups), chunk),
    )


def call_on_blocks(kernel, outs, *arrays, name, micros, after=(), scratch=(), space=pltpu.VMEM):
    vmem = pl.BlockSpec(memory_space=pltpu.VMEM)
    count = len(arrays)

    def body(*refs):
        kernel(*refs[:count], *refs[count + len(after) :])

    return pl.pallas_call(
        body,
        in_specs=[vmem] * count + [pl.BlockSpec(memory_space=pl.ANY)] * len(after),
        out_specs=[vmem] * len(outs),
        out_shape=[space(shape, dtype) for shape, dtype in outs],
        scratch_shapes=list(scratch),
        compiler_params=pltpu.CompilerParams(vmem_limit_bytes=VMEM_BYTES),
        cost_estimate=lasting(micros),
        name=name,
    )(*arrays, *after)


def direct_sums(direct, powers):
    _, refs, bound = sent_powers(powers)
    chunk = direct.shape[0] // REF * REF
    return expanded(direct[:chunk], bound, ref_column(refs))


def merged(keep, ours, theirs, direct=(), beyond=(), held_back=(), after=()):
    chunk, width = keep.shape

    def kernel(keep, ours, theirs, *refs):
        inputs, out, passed = refs[: -1 - len(held_back)], refs[len(arrays) - 3], refs[len(arrays) - 2 :]
        powers, refs, bound = sent_powers(ours)
        their_powers, their_refs, their_bound = sent_powers(theirs)
        sums, sum_refs, sum_bound = powers + their_powers, refs + their_refs, bound + their_bound
        total = keep[...] + expanded(theirs[:chunk], their_bound, ref_column(their_refs))
        if direct:
            total += direct_sums(inputs[0], inputs[1])
        if beyond:
            sum_bound += inputs[len(direct)][...]
        if held_back:
            passed[0][...] = inputs[-1][...]
        sum_bound = rounded_up(sum_bound)
        out[chunk:] = packed(sums, sum_refs, sum_bound)
        out[:chunk] = coded(total, sum_bound, ref_column(sum_refs))

    outs = [((chunk + EXTRA, width), jnp.bfloat16)] + [(code.shape, code.dtype) for code in held_back]
    arrays = (keep, ours, theirs, *direct, *beyond, *held_back)
    return call_on_blocks(kernel, outs, *arrays, name="merged", micros=MERGE_MICROS, after=after)


def resent(keep, direct, direct_powers, ours, after):
    def kernel(keep, direct, direct_powers, ours, out):
        _, refs, bound = sent_powers(ours)
        out[...] = coded(keep[...] + direct_sums(direct, direct_powers), bound, ref_column(refs))

    outs = [(keep.shape, jnp.bfloat16)]
    arrays = (keep, direct, direct_powers, ours)
    return call_on_blocks(kernel, outs, *arrays, name="resent", micros=MERGE_MICROS, after=after)[0]


def added(keep, direct, direct_powers, near, near_powers, after):
    def kernel(keep, direct, direct_powers, near, near_powers, out):
        out[...] = keep[...] + direct_sums(direct, direct_powers) + direct_sums(near, near_powers)

    outs = [(keep.shape, jnp.float32)]
    arrays = (keep, direct, direct_powers, near, near_powers)
    return call_on_blocks(kernel, outs, *arrays, name="added", micros=MERGE_MICROS, after=after)[0]


def finished(slab_rows, segment, partial, ours, theirs, autos):
    chunk, width = partial.shape

    def kernel(partial, ours, theirs, *refs):
        autos, (covariance, segment_auto) = refs[:-2], refs[-2:]
        first_lag = lax.axis_index("tm").astype(jnp.int32) * (chunk // REF)
        lag = lax.broadcasted_iota(jnp.int32, (chunk, 1), 0) // REF + first_lag
        denom = (slab_rows - lag).astype(jnp.float32)
        powers, own_refs, _ = sent_powers(ours)
        their_powers, their_refs, their_bound = sent_powers(theirs)
        total = partial[...] + expanded(theirs[:chunk], their_bound, ref_column(their_refs))
        scale = 1.0 / jnp.sqrt((powers + their_powers) / slab_rows + 1e-06)
        ref_scale = 1.0 / jnp.sqrt(ref_column(own_refs + their_refs) / slab_rows + 1e-06)
        covariance[...] = total * scale * (for_chunk(ref_scale, chunk) / denom)
        first = 0
        for auto in autos:
            here = slice(first, first + auto.shape[1])
            segment_auto[:, here] = auto[...] * (scale[:, here] * scale[:, here]) / segment
            first = here.stop

    outs = [(partial.shape, jnp.float32), ((LAGS, width), jnp.float32)]
    return call_on_blocks(
        kernel,
        outs,
        partial,
        ours,
        theirs,
        *autos,
        name="finished",
        micros=MERGE_MICROS,
        space=jax.ShapeDtypeStruct,
    )


def segment_kernel(first, held, power, tail, out, wide):
    rows = held.shape[0]
    step = rows // 8
    pitch = step + LAGS
    for index in range(out.shape[1] // LANES):
        here = slice(first + index * LANES, first + (index + 1) * LANES)
        there = slice(index * LANES, (index + 1) * LANES)
        for part in range(8):
            end = (part + 1) * step
            wide[part * pitch : part * pitch + step, :] = held[end - step : end, here].astype(jnp.float32)
            if part < 7:
                following = held[end : end + LAGS, here].astype(jnp.float32)
            else:
                following = tail[:LAGS, here].astype(jnp.float32)
            wide[part * pitch + step : (part + 1) * pitch, :] = following
        taken = lambda first: wide[pl.ds(first, 8, stride=pitch), :]

        def advance(index, carry):
            window, sums = carry
            window = window + (taken(index + LAGS - 1),)
            sums = tuple(total + window[0] * window[lag + 1] for lag, total in enumerate(sums))
            return window[1:], sums

        window = tuple(taken(first) for first in range(LAGS - 1))
        zero = jnp.zeros((8, LANES), jnp.float32)
        _, sums = lax.fori_loop(0, step, advance, (window, (zero,) * (LAGS - 1)), unroll=16)
        out[:, there] = jnp.concatenate(
            [power[:, here]] + [jnp.sum(total, axis=0, keepdims=True) for total in sums], axis=0
        )


def segment_rows(held, power, tail, first, size, after=()):
    rows = held.shape[0]

    def kernel(*refs):
        segment_kernel(first, *refs)

    return call_on_blocks(
        kernel,
        [((LAGS, size), jnp.float32)],
        held,
        power,
        tail,
        name="segment_rows",
        micros=SEGMENT_MICROS,
        after=after,
        scratch=[pltpu.VMEM((rows + 8 * LAGS, LANES), jnp.float32)],
    )[0]


def all_products_kernel(held, own, other, tail, out, shifted):
    chan = lax.axis_index("chan")
    zeros = jnp.zeros((HALF, LANES), jnp.float32)
    for refs, half in ((own, chan), (other, 1 - chan)):
        long = jnp.concatenate([refs[...].astype(jnp.float32), zeros], axis=1)
        for index in range(GROUP):
            start = pl.multiple_of(index * REF + half * HALF, HALF)
            lag = pl.program_id(0) * GROUP + index
            shifted[pl.ds(start, HALF), :] = pltpu.roll(long, lag, 1).astype(jnp.bfloat16)
    rows, width = held.shape
    edge = jnp.concatenate([tail[...], jnp.zeros((LANES - LAGS, width), tail.dtype)], axis=0)
    for here in columns(width):
        total = jnp.dot(shifted[:, rows:], edge[:, here], preferred_element_type=jnp.float32)
        out[:, here] = total + jnp.dot(shifted[:, :rows], held[:, here], preferred_element_type=jnp.float32)


def all_products(held, own, other, tail):
    rows, width = held.shape
    vmem = pl.BlockSpec(memory_space=pltpu.VMEM)
    return pl.pallas_call(
        all_products_kernel,
        grid=(LAGS // GROUP,),
        in_specs=[vmem] * 4,
        out_specs=pl.BlockSpec((GROUP * REF, width), lambda group: (group, 0)),
        out_shape=jax.ShapeDtypeStruct((LAGS * REF, width), jnp.float32),
        scratch_shapes=[pltpu.VMEM((GROUP * REF, rows + LANES), jnp.bfloat16)],
        compiler_params=pltpu.CompilerParams(vmem_limit_bytes=VMEM_BYTES),
        name="all_products",
    )(held, own, other, tail)


def from_pair_ahead(value):
    count = lax.axis_size("tm")
    return lax.ppermute(value, "tm", [(time + 2, time) for time in range(0, count - 2, 2)])


def local(strain):
    rows, width = strain.shape
    count = lax.axis_size("tm")
    slab_rows = rows * count
    chunk = LAGS * REF // count

    own, head = prepared(strain)
    other = exchanged(own, "chan", 1)
    held, power = loaded(strain, own)
    size = width // 2

    if chunk * 2 == GROUP * REF:
        keep6, send7 = first_products(held, power, own, other, chunk)
        got7 = exchanged(send7, "tm", 1)
        after_next = from_pair_ahead(head)
        keep4, send5, keep2, send3, keep0, send1 = later_products(
            (2, 1, 0), held, own, other, send7, chunk
        )
        sides, send5 = sides_to_swap(head, after_next, own, other, send5)
        tails = (sides, exchanged(sides, "tm", 1))
        got5 = exchanged(send5, "tm", 1)
        *keeps, beyond = with_boundaries((keep6, keep4, keep2, keep0), (3, 2, 1, 0), own, other, *tails)
        keep6, keep4, keep2, keep0 = keeps
        send6, send3 = merged(keep6, send7, got7, beyond=(beyond,), held_back=(send3,))
        got6 = exchanged(send6, "tm", 2)
        got3 = exchanged(send3, "tm", 1)
        autos = [segment_rows(held, power, tails[1], 0, size, after=(send6,))]
        send4, send1 = merged(
            keep4, send6, got6, direct=(got5, got7), held_back=(send1,), after=(autos[0],)
        )
        got4 = exchanged(send4, "tm", 4)
        got1 = exchanged(send1, "tm", 1)
        send2 = resent(keep2, got3, got7, send6, after=(send4,))
        got2 = exchanged(send2, "tm", 2)
        autos.append(segment_rows(held, power, tails[1], size, size, after=(send2,)))
        partial = added(keep0, got1, got7, got2, got6, after=(autos[1],))
        return tuple(finished(slab_rows, rows, partial, send4, got4, autos))

    tail = passed_along(head, "tm", -1)
    chan = lax.axis_index("chan").astype(jnp.int32)
    time = lax.axis_index("tm").astype(jnp.int32)
    auto = jnp.concatenate(
        [segment_rows(held, power, tail, size * index, size) for index in range(2)], axis=1
    )
    power_other = jnp.sum(jnp.square(other.astype(jnp.float32)), axis=1)
    power = lax.psum(jnp.concatenate([power[0], power_other]), "tm")
    inv = 1.0 / jnp.sqrt(power / slab_rows + 1e-06)
    scale = inv[:width]
    ref_scale = jnp.where(
        chan == 0,
        jnp.concatenate([inv[:HALF], inv[width:]]),
        jnp.concatenate([inv[width:], inv[:HALF]]),
    )
    products = all_products(held, own, other, tail)
    summed = lax.psum_scatter(products, "tm", scatter_dimension=0, tiled=True)
    row = time * chunk + jnp.arange(chunk, dtype=jnp.int32)
    row_scale = ref_scale[row % REF] / (slab_rows - row // REF).astype(jnp.float32)
    covariance = summed * scale[None, :] * row_scale[:, None]
    segment_auto = auto * (scale * scale)[None, :] / rows
    return (covariance, segment_auto)


def solution(mesh):
    in_specs = (P(("groups", "tm"), "chan"),)
    out_specs = (P(("groups", "tm"), "chan"), P(("groups", "tm"), "chan"))
    return jax.shard_map(local, mesh=mesh, in_specs=in_specs, out_specs=out_specs, check_vma=False)
```

```python
import jax
import jax.numpy as jnp
from jax import lax
from jax.experimental import pallas as pl
from jax.experimental.pallas import tpu as pltpu
from jax.sharding import PartitionSpec as P

LAGS = 16
REF = 64
HALF = REF // 2
LANES = 128
EXTRA = 8
FETCHES = 8
STEP = 256
GROUP = 4
POWER = 16
CODE_SCALE = 2.0 ** (126 / POWER)
TINY = 1e-35
PIECES = 4
VMEM_BYTES = 32 * 1024 * 1024
HBM_RATE = 3.69e6
PRODUCT_MICROS = 1.0
SEGMENT_MICROS = 1.2
MERGE_MICROS = 0.3


def lasting(micros):
    return pl.CostEstimate(flops=0, bytes_accessed=int(micros * HBM_RATE), transcendentals=0)


def passed_along(value, axis, steps):
    count = lax.axis_size(axis)
    initial, last = (max(0, -steps), min(count, count - steps))
    return lax.ppermute(value, axis, [(source, source + steps) for source in range(initial, last)])


def exchanged(value, axis, bit):
    count = lax.axis_size(axis)
    return lax.ppermute(value, axis, [(source, source ^ bit) for source in range(count)])


def as_column(row):
    size = row.shape[1]
    eye = lax.broadcasted_iota(jnp.int32, (size, size), 0) == lax.broadcasted_iota(jnp.int32, (size, size), 1)
    return jnp.sum(jnp.where(eye, row, 0.0), axis=1, keepdims=True)


def as_row(column):
    size = column.shape[0]
    eye = lax.broadcasted_iota(jnp.int32, (size, size), 0) == lax.broadcasted_iota(jnp.int32, (size, size), 1)
    return jnp.sum(jnp.where(eye, column, 0.0), axis=0, keepdims=True)


def for_chunk(ref_column, rows):
    return jnp.concatenate([ref_column] * (rows // REF), axis=0)


def bf16_pieces(value):
    high = value.astype(jnp.bfloat16).astype(jnp.float32)
    middle = (value - high).astype(jnp.bfloat16).astype(jnp.float32)
    return high, middle, value - high - middle


def packed(powers, ref_powers, channel_bound):
    rows = list(bf16_pieces(powers))
    refs = jnp.concatenate(bf16_pieces(ref_powers), axis=1)
    pad = jnp.zeros((1, powers.shape[1] - refs.shape[1]), jnp.float32)
    rows += [jnp.concatenate([refs, pad], axis=1), channel_bound]
    rows += [jnp.zeros_like(powers)] * (EXTRA - len(rows))
    return jnp.concatenate(rows, axis=0).astype(jnp.bfloat16)


def unpacked(block):
    wide = block.astype(jnp.float32)
    powers = wide[0:1] + wide[1:2] + wide[2:3]
    refs = wide[3:4, :LANES] + wide[3:4, LANES : 2 * LANES] + wide[3:4, 2 * LANES : 3 * LANES]
    return powers, refs, wide[4:5]


def sent_powers(code):
    return unpacked(code[-EXTRA:])


def rounded_up(value):
    return (value * (1.0 + 2.0**-7)).astype(jnp.bfloat16).astype(jnp.float32)


def coded(values, channel_bound, ref_bound):
    channel = lax.rsqrt(jnp.maximum(channel_bound, TINY))
    refs = lax.rsqrt(jnp.maximum(ref_bound, TINY)) * CODE_SCALE
    power = values * channel * for_chunk(refs, values.shape[0])
    for _ in range(4):
        power = power * jnp.abs(power)
    return power.astype(jnp.bfloat16)


def expanded(code, channel_bound, ref_bound):
    channel = jnp.sqrt(jnp.maximum(channel_bound, TINY))
    refs = jnp.sqrt(jnp.maximum(ref_bound, TINY)) * (1.0 / CODE_SCALE)
    wide = code[...].astype(jnp.float32)
    root = jnp.exp2(jnp.log2(jnp.abs(wide)) * (1.0 / POWER))
    return jnp.where(wide < 0.0, -root, root) * channel * for_chunk(refs, code.shape[0])


def ref_column(ref_powers):
    return as_column(ref_powers)[:REF]


def prepare_kernel(strain, own, head, left, sems):
    rows = left.shape[0]
    step = rows // PIECES
    copies = [
        pltpu.make_async_copy(
            strain.at[pl.ds(index * step, step), pl.ds(0, LANES)], left.at[pl.ds(index * step, step)], sems.at[index]
        )
        for index in range(PIECES)
    ]
    copies.append(pltpu.make_async_copy(strain.at[pl.ds(0, LAGS)], head, sems.at[PIECES]))
    for copy in copies:
        copy.start()
    for index in range(PIECES):
        copies[index].wait()
        here = slice(index * step, (index + 1) * step)
        own[:, here] = left[here, :].astype(jnp.float32).T[:HALF].astype(jnp.bfloat16)
    copies[PIECES].wait()


def prepared(strain):
    rows, width = strain.shape
    vmem = pl.BlockSpec(memory_space=pltpu.VMEM)
    return pl.pallas_call(
        prepare_kernel,
        in_specs=[pl.BlockSpec(memory_space=pl.ANY)],
        out_specs=[vmem, vmem],
        out_shape=[pltpu.VMEM((HALF, rows), strain.dtype), pltpu.VMEM((LAGS, width), strain.dtype)],
        scratch_shapes=[pltpu.VMEM((rows, LANES), strain.dtype), pltpu.SemaphoreType.DMA((PIECES + 1,))],
        compiler_params=pltpu.CompilerParams(vmem_limit_bytes=VMEM_BYTES),
        cost_estimate=lasting(PRODUCT_MICROS),
        name="prepared",
    )(pltpu.with_memory_space_constraint(strain, pltpu.HBM))


def lag_rows(own, other, group, shifted):
    chan, near = lax.axis_index("chan"), lax.axis_index("tm") & 1
    rows = own.shape[1]
    zeros = jnp.zeros((HALF, LANES), jnp.float32)
    for refs, half in ((own, chan), (other, 1 - chan)):
        long = jnp.concatenate([zeros, refs[...].astype(jnp.float32)], axis=1)
        for index in range(GROUP):
            ahead = near if index < GROUP // 2 else 1 - near
            lag = group * GROUP + ahead * (GROUP // 2) + index % (GROUP // 2)
            start = pl.multiple_of(index * REF + half * HALF, HALF)
            moved = pltpu.roll(long, lag, 1)[:, LANES : LANES + rows]
            shifted[pl.ds(start, HALF), :] = moved.astype(jnp.bfloat16)


def own_group(bits):
    return lax.shift_right_logical(lax.axis_index("tm").astype(jnp.int32), 1) ^ bits


def loaded_kernel(strain, held, power, sems):
    step = held.shape[0] // FETCHES
    pieces = [slice(index * step, (index + 1) * step) for index in range(FETCHES)]
    copies = [
        pltpu.make_async_copy(strain.at[pl.ds(here.start, step)], held.at[pl.ds(here.start, step)], sems.at[index])
        for index, here in enumerate(pieces)
    ]
    for copy in copies:
        copy.start()
    total = jnp.zeros((8, held.shape[1]), jnp.float32)
    for copy, here in zip(copies, pieces):
        copy.wait()
        squares = jnp.square(held[here, :].astype(jnp.float32))
        total += jnp.sum(squares.reshape(step // 8, 8, held.shape[1]), axis=0)
    power[...] = jnp.sum(total, axis=0, keepdims=True)


def loaded(strain, after):
    rows, width = strain.shape
    vmem = pl.BlockSpec(memory_space=pltpu.VMEM)

    def kernel(strain, after, held, power, sems):
        loaded_kernel(strain, held, power, sems)

    return pl.pallas_call(
        kernel,
        in_specs=[pl.BlockSpec(memory_space=pl.ANY)] * 2,
        out_specs=[vmem, vmem],
        out_shape=[pltpu.VMEM((rows, width), strain.dtype), pltpu.VMEM((1, width), jnp.float32)],
        scratch_shapes=[pltpu.SemaphoreType.DMA((FETCHES,))],
        compiler_params=pltpu.CompilerParams(vmem_limit_bytes=VMEM_BYTES),
        cost_estimate=lasting(PRODUCT_MICROS),
        name="loaded",
    )(pltpu.with_memory_space_constraint(strain, pltpu.HBM), after)


def columns(width):
    return [slice(first, first + STEP) for first in range(0, width, STEP)]


def product_of(shifted, held, here):
    return jnp.dot(shifted[...], held[:, here], preferred_element_type=jnp.float32)


def boundary_rows(group, ends, their_ends, edges):
    chan, near = lax.axis_index("chan"), lax.axis_index("tm") & 1
    zeros = jnp.zeros((HALF, LANES), jnp.float32)
    ours = [(refs[:, refs.shape[1] - LANES :].astype(jnp.float32), half) for refs, half in zip(ends, (chan, 1 - chan))]
    theirs = [(their_ends[half * HALF : (half + 1) * HALF], half) for half in range(2)]
    for side, parts in enumerate((ours, theirs)):
        for end, half in parts:
            long = jnp.concatenate([end, zeros], axis=1)
            for index in range(GROUP // 2):
                lag = group * GROUP + near * (GROUP // 2) + index
                start = pl.multiple_of(index * REF + half * HALF, HALF)
                moved = pltpu.roll(long, lag, 1)[:, LANES:]
                edges[pl.ds(start, HALF), side * LANES : (side + 1) * LANES] = moved.astype(jnp.bfloat16)


def ends_of(code):
    rows = code[LAGS : 2 * LAGS, :LANES].astype(jnp.float32)
    return jnp.concatenate([jnp.zeros((LANES - LAGS, LANES), jnp.float32), rows], axis=0).T[:REF]


def tails_of(sent, arrived, here):
    zeros = jnp.zeros((LANES - LAGS, here.stop - here.start), jnp.bfloat16)
    return jnp.concatenate([arrived[:LAGS, here], zeros, sent[:LAGS, here], zeros], axis=0)


def first_products_kernel(held, power, own, other, keep, send, shifted):
    lag_rows(own, other, own_group(3), shifted)
    ours, theirs = [
        jnp.sum(jnp.square(refs[...].astype(jnp.float32)), axis=1, keepdims=True) for refs in (own, other)
    ]
    refs = jnp.where(
        lax.axis_index("chan") == 0,
        jnp.concatenate([ours, theirs], axis=0),
        jnp.concatenate([theirs, ours], axis=0),
    )
    bound = rounded_up(power[...])
    pad = jnp.zeros((1, LANES - REF), jnp.float32)
    chunk = keep.shape[0]
    send[chunk:] = packed(power[...], jnp.concatenate([as_row(refs), pad], axis=1), bound)
    for here in columns(held.shape[1]):
        product = product_of(shifted, held, here)
        keep[:, here] = product[:chunk]
        send[:chunk, here] = coded(product[chunk:], bound[:, here], refs)


def shifted_scratch(rows, groups=1):
    return [pltpu.VMEM((groups * GROUP * REF, rows), jnp.bfloat16)]


def first_products(held, power, own, other, chunk):
    rows, width = held.shape
    return call_on_blocks(
        first_products_kernel,
        [((chunk, width), jnp.float32), ((chunk + EXTRA, width), jnp.bfloat16)],
        held,
        power,
        own,
        other,
        name="first_products",
        micros=PRODUCT_MICROS,
        scratch=shifted_scratch(rows),
    )


def later_products(groups, held, own, other, powers, chunk):
    rows, width = held.shape

    def kernel(held, own, other, powers, *rest):
        outs, shifted = rest[:-1], rest[-1]
        _, ref_powers, bound = sent_powers(powers)
        refs = ref_column(ref_powers)
        for index, bits in enumerate(groups):
            lag_rows(own, other, own_group(bits), shifted.at[pl.ds(index * 2 * chunk, 2 * chunk)])
        for here in columns(width):
            product = product_of(shifted, held, here)
            for index in range(len(groups)):
                keep, send = outs[2 * index : 2 * index + 2]
                first = 2 * index * chunk
                keep[:, here] = product[first : first + chunk]
                send[:, here] = coded(product[first + chunk : first + 2 * chunk], bound[:, here], refs)

    return call_on_blocks(
        kernel,
        [((chunk, width), jnp.float32), ((chunk, width), jnp.bfloat16)] * len(groups),
        held,
        own,
        other,
        powers,
        name="later_products",
        micros=PRODUCT_MICROS,
        scratch=shifted_scratch(rows, len(groups)),
    )


def edges_scratch(count, chunk):
    return [pltpu.VMEM((count, chunk, 2 * LANES), jnp.bfloat16)]


def sides_to_swap(head, after_next, own, other, held_back):
    width = head.shape[1]

    def kernel(head, after_next, own, other, held_back, sides, passed):
        chan, near = lax.axis_index("chan"), lax.axis_index("tm") & 1
        passed[...] = held_back[...]
        sides[:LAGS] = jnp.where(near == 0, after_next[...], head[...])
        ours, theirs = [refs[:, refs.shape[1] - LANES :].astype(jnp.float32) for refs in (own, other)]
        first, second = jnp.where(chan == 0, ours, theirs), jnp.where(chan == 0, theirs, ours)
        square = jnp.concatenate([first, second, jnp.zeros((LANES - REF, LANES), jnp.float32)], axis=0)
        sides[LAGS:, :LANES] = square.T[LANES - LAGS :].astype(jnp.bfloat16)
        sides[LAGS:, LANES:] = jnp.zeros((LAGS, width - LANES), jnp.bfloat16)

    outs = [((2 * LAGS, width), jnp.bfloat16), (held_back.shape, jnp.bfloat16)]
    arrays = (head, after_next, own, other, held_back)
    return call_on_blocks(kernel, outs, *arrays, name="sides", micros=MERGE_MICROS)


def with_boundaries(keeps, groups, own, other, sent, arrived, held_back):
    chunk, width = keeps[0].shape

    def kernel(own, other, sent, arrived, held_back, *rest):
        keeps, rest = rest[: len(groups)], rest[len(groups) :]
        outs, beyond, passed, edges = rest[: len(groups)], rest[-3], rest[-2], rest[-1]
        passed[:chunk] = held_back[...]
        passed[chunk:] = jnp.zeros((LAGS, width), jnp.bfloat16)
        for index, bits in enumerate(groups):
            boundary_rows(own_group(bits), (own, other), ends_of(arrived), edges.at[index])
        for here in columns(width):
            tails = tails_of(sent, arrived, here)
            for index in range(len(groups)):
                added = jnp.dot(edges[index], tails, preferred_element_type=jnp.float32)
                outs[index][:, here] = keeps[index][:, here] + added
            beyond[:, here] = jnp.sum(jnp.square(tails.astype(jnp.float32)), axis=0, keepdims=True)

    outs = [((chunk, width), jnp.float32)] * len(groups) + [((1, width), jnp.float32), ((chunk + LAGS, width), jnp.bfloat16)]
    return call_on_blocks(
        kernel,
        outs,
        own,
        other,
        sent,
        arrived,
        held_back,
        *keeps,
        name="with_boundaries",
        micros=MERGE_MICROS,
        scratch=edges_scratch(len(groups), chunk),
    )


def call_on_blocks(kernel, outs, *arrays, name, micros, after=(), scratch=(), space=pltpu.VMEM):
    vmem = pl.BlockSpec(memory_space=pltpu.VMEM)
    count = len(arrays)

    def body(*refs):
        kernel(*refs[:count], *refs[count + len(after) :])

    return pl.pallas_call(
        body,
        in_specs=[vmem] * count + [pl.BlockSpec(memory_space=pl.ANY)] * len(after),
        out_specs=[vmem] * len(outs),
        out_shape=[space(shape, dtype) for shape, dtype in outs],
        scratch_shapes=list(scratch),
        compiler_params=pltpu.CompilerParams(vmem_limit_bytes=VMEM_BYTES),
        cost_estimate=lasting(micros),
        name=name,
    )(*arrays, *after)


def direct_sums(direct, powers):
    _, refs, bound = sent_powers(powers)
    chunk = direct.shape[0] // REF * REF
    return expanded(direct[:chunk], bound, ref_column(refs))


def merged(keep, ours, theirs, direct=(), beyond=(), held_back=(), after=()):
    chunk, width = keep.shape

    def kernel(keep, ours, theirs, *refs):
        inputs, out, passed = refs[: -1 - len(held_back)], refs[len(arrays) - 3], refs[len(arrays) - 2 :]
        powers, refs, bound = sent_powers(ours)
        their_powers, their_refs, their_bound = sent_powers(theirs)
        sums, sum_refs, sum_bound = powers + their_powers, refs + their_refs, bound + their_bound
        total = keep[...] + expanded(theirs[:chunk], their_bound, ref_column(their_refs))
        if direct:
            total += direct_sums(inputs[0], inputs[1])
        if beyond:
            sum_bound += inputs[len(direct)][...]
        if held_back:
            passed[0][...] = inputs[-1][...]
        sum_bound = rounded_up(sum_bound)
        out[chunk:] = packed(sums, sum_refs, sum_bound)
        out[:chunk] = coded(total, sum_bound, ref_column(sum_refs))

    outs = [((chunk + EXTRA, width), jnp.bfloat16)] + [(code.shape, code.dtype) for code in held_back]
    arrays = (keep, ours, theirs, *direct, *beyond, *held_back)
    return call_on_blocks(kernel, outs, *arrays, name="merged", micros=MERGE_MICROS, after=after)


def resent(keep, direct, direct_powers, ours, after):
    def kernel(keep, direct, direct_powers, ours, out):
        _, refs, bound = sent_powers(ours)
        out[...] = coded(keep[...] + direct_sums(direct, direct_powers), bound, ref_column(refs))

    outs = [(keep.shape, jnp.bfloat16)]
    arrays = (keep, direct, direct_powers, ours)
    return call_on_blocks(kernel, outs, *arrays, name="resent", micros=MERGE_MICROS, after=after)[0]


def added(keep, direct, direct_powers, after):
    def kernel(keep, direct, direct_powers, out):
        out[...] = keep[...] + direct_sums(direct, direct_powers)

    outs = [(keep.shape, jnp.float32)]
    arrays = (keep, direct, direct_powers)
    return call_on_blocks(kernel, outs, *arrays, name="added", micros=MERGE_MICROS, after=after)[0]


def finished(slab_rows, segment, partial, near, near_powers, ours, theirs, autos):
    chunk, width = partial.shape

    def kernel(partial, near, near_powers, ours, theirs, *refs):
        autos, (covariance, segment_auto) = refs[:-2], refs[-2:]
        first_lag = lax.axis_index("tm").astype(jnp.int32) * (chunk // REF)
        lag = lax.broadcasted_iota(jnp.int32, (chunk, 1), 0) // REF + first_lag
        denom = (slab_rows - lag).astype(jnp.float32)
        powers, own_refs, _ = sent_powers(ours)
        their_powers, their_refs, their_bound = sent_powers(theirs)
        total = partial[...] + direct_sums(near, near_powers)
        total += expanded(theirs[:chunk], their_bound, ref_column(their_refs))
        scale = 1.0 / jnp.sqrt((powers + their_powers) / slab_rows + 1e-06)
        ref_scale = 1.0 / jnp.sqrt(ref_column(own_refs + their_refs) / slab_rows + 1e-06)
        covariance[...] = total * scale * (for_chunk(ref_scale, chunk) / denom)
        first = 0
        for auto in autos:
            here = slice(first, first + auto.shape[1])
            segment_auto[:, here] = auto[...] * (scale[:, here] * scale[:, here]) / segment
            first = here.stop

    outs = [(partial.shape, jnp.float32), ((LAGS, width), jnp.float32)]
    return call_on_blocks(
        kernel,
        outs,
        partial,
        near,
        near_powers,
        ours,
        theirs,
        *autos,
        name="finished",
        micros=MERGE_MICROS,
        space=jax.ShapeDtypeStruct,
    )


def segment_kernel(first, held, power, tail, out, wide):
    rows = held.shape[0]
    step = rows // 8
    pitch = step + LAGS
    for index in range(out.shape[1] // LANES):
        here = slice(first + index * LANES, first + (index + 1) * LANES)
        there = slice(index * LANES, (index + 1) * LANES)
        for part in range(8):
            end = (part + 1) * step
            wide[part * pitch : part * pitch + step, :] = held[end - step : end, here].astype(jnp.float32)
            if part < 7:
                following = held[end : end + LAGS, here].astype(jnp.float32)
            else:
                following = tail[:LAGS, here].astype(jnp.float32)
            wide[part * pitch + step : (part + 1) * pitch, :] = following
        taken = lambda first: wide[pl.ds(first, 8, stride=pitch), :]

        def advance(index, carry):
            window, sums = carry
            window = window + (taken(index + LAGS - 1),)
            sums = tuple(total + window[0] * window[lag + 1] for lag, total in enumerate(sums))
            return window[1:], sums

        window = tuple(taken(first) for first in range(LAGS - 1))
        zero = jnp.zeros((8, LANES), jnp.float32)
        _, sums = lax.fori_loop(0, step, advance, (window, (zero,) * (LAGS - 1)), unroll=16)
        out[:, there] = jnp.concatenate(
            [power[:, here]] + [jnp.sum(total, axis=0, keepdims=True) for total in sums], axis=0
        )


def segment_rows(held, power, tail, first, size, after=()):
    rows = held.shape[0]

    def kernel(*refs):
        segment_kernel(first, *refs)

    return call_on_blocks(
        kernel,
        [((LAGS, size), jnp.float32)],
        held,
        power,
        tail,
        name="segment_rows",
        micros=SEGMENT_MICROS,
        after=after,
        scratch=[pltpu.VMEM((rows + 8 * LAGS, LANES), jnp.float32)],
    )[0]


def all_products_kernel(held, own, other, tail, out, shifted):
    chan = lax.axis_index("chan")
    zeros = jnp.zeros((HALF, LANES), jnp.float32)
    for refs, half in ((own, chan), (other, 1 - chan)):
        long = jnp.concatenate([refs[...].astype(jnp.float32), zeros], axis=1)
        for index in range(GROUP):
            start = pl.multiple_of(index * REF + half * HALF, HALF)
            lag = pl.program_id(0) * GROUP + index
            shifted[pl.ds(start, HALF), :] = pltpu.roll(long, lag, 1).astype(jnp.bfloat16)
    rows, width = held.shape
    edge = jnp.concatenate([tail[...], jnp.zeros((LANES - LAGS, width), tail.dtype)], axis=0)
    for here in columns(width):
        total = jnp.dot(shifted[:, rows:], edge[:, here], preferred_element_type=jnp.float32)
        out[:, here] = total + jnp.dot(shifted[:, :rows], held[:, here], preferred_element_type=jnp.float32)


def all_products(held, own, other, tail):
    rows, width = held.shape
    vmem = pl.BlockSpec(memory_space=pltpu.VMEM)
    return pl.pallas_call(
        all_products_kernel,
        grid=(LAGS // GROUP,),
        in_specs=[vmem] * 4,
        out_specs=pl.BlockSpec((GROUP * REF, width), lambda group: (group, 0)),
        out_shape=jax.ShapeDtypeStruct((LAGS * REF, width), jnp.float32),
        scratch_shapes=[pltpu.VMEM((GROUP * REF, rows + LANES), jnp.bfloat16)],
        compiler_params=pltpu.CompilerParams(vmem_limit_bytes=VMEM_BYTES),
        name="all_products",
    )(held, own, other, tail)


def from_pair_ahead(value):
    count = lax.axis_size("tm")
    return lax.ppermute(value, "tm", [(time + 2, time) for time in range(0, count - 2, 2)])


def local(strain):
    rows, width = strain.shape
    count = lax.axis_size("tm")
    slab_rows = rows * count
    chunk = LAGS * REF // count

    own, head = prepared(strain)
    other = exchanged(own, "chan", 1)
    held, power = loaded(strain, own)
    size = width // 2

    if chunk * 2 == GROUP * REF:
        keep6, send7 = first_products(held, power, own, other, chunk)
        after_next = from_pair_ahead(head)
        sides, send7 = sides_to_swap(head, after_next, own, other, send7)
        got7 = exchanged(send7, "tm", 1)
        tails = (sides, exchanged(sides, "tm", 1))
        keep4, send5, keep2, send3, keep0, send1 = later_products(
            (2, 1, 0), held, own, other, send7, chunk
        )
        *keeps, beyond, send5 = with_boundaries(
            (keep6, keep4, keep2, keep0), (3, 2, 1, 0), own, other, *tails, send5
        )
        got5 = exchanged(send5, "tm", 1)
        keep6, keep4, keep2, keep0 = keeps
        send6, send3 = merged(keep6, send7, got7, beyond=(beyond,), held_back=(send3,))
        got6 = exchanged(send6, "tm", 2)
        got3 = exchanged(send3, "tm", 1)
        autos = [segment_rows(held, power, tails[1], 0, size, after=(send6,))]
        send4, send1 = merged(
            keep4, send6, got6, direct=(got5, got7), held_back=(send1,), after=(autos[0],)
        )
        got4 = exchanged(send4, "tm", 4)
        got1 = exchanged(send1, "tm", 1)
        send2 = resent(keep2, got3, got7, send6, after=(send4,))
        got2 = exchanged(send2, "tm", 2)
        autos.append(segment_rows(held, power, tails[1], size, size, after=(send2,)))
        partial = added(keep0, got1, got7, after=(autos[1],))
        return tuple(finished(slab_rows, rows, partial, got2, got6, send4, got4, autos))

    tail = passed_along(head, "tm", -1)
    chan = lax.axis_index("chan").astype(jnp.int32)
    time = lax.axis_index("tm").astype(jnp.int32)
    auto = jnp.concatenate(
        [segment_rows(held, power, tail, size * index, size) for index in range(2)], axis=1
    )
    power_other = jnp.sum(jnp.square(other.astype(jnp.float32)), axis=1)
    power = lax.psum(jnp.concatenate([power[0], power_other]), "tm")
    inv = 1.0 / jnp.sqrt(power / slab_rows + 1e-06)
    scale = inv[:width]
    ref_scale = jnp.where(
        chan == 0,
        jnp.concatenate([inv[:HALF], inv[width:]]),
        jnp.concatenate([inv[width:], inv[:HALF]]),
    )
    products = all_products(held, own, other, tail)
    summed = lax.psum_scatter(products, "tm", scatter_dimension=0, tiled=True)
    row = time * chunk + jnp.arange(chunk, dtype=jnp.int32)
    row_scale = ref_scale[row % REF] / (slab_rows - row // REF).astype(jnp.float32)
    covariance = summed * scale[None, :] * row_scale[:, None]
    segment_auto = auto * (scale * scale)[None, :] / rows
    return (covariance, segment_auto)


def solution(mesh):
    in_specs = (P(("groups", "tm"), "chan"),)
    out_specs = (P(("groups", "tm"), "chan"), P(("groups", "tm"), "chan"))
    return jax.shard_map(local, mesh=mesh, in_specs=in_specs, out_specs=out_specs, check_vma=False)
```

```python
import jax
import jax.numpy as jnp
from jax import lax
from jax.experimental import pallas as pl
from jax.experimental.pallas import tpu as pltpu
from jax.sharding import PartitionSpec as P

LAGS = 16
REF = 64
HALF = REF // 2
LANES = 128
EXTRA = 8
FETCHES = 8
STEP = 256
GROUP = 4
POWER = 16
CODE_SCALE = 2.0 ** (126 / POWER)
TINY = 1e-35
PIECES = 4
VMEM_BYTES = 32 * 1024 * 1024
HBM_RATE = 3.69e6
PRODUCT_MICROS = 1.0
SEGMENT_MICROS = 1.2
MERGE_MICROS = 0.3


def lasting(micros):
    return pl.CostEstimate(flops=0, bytes_accessed=int(micros * HBM_RATE), transcendentals=0)


def passed_along(value, axis, steps):
    count = lax.axis_size(axis)
    initial, last = (max(0, -steps), min(count, count - steps))
    return lax.ppermute(value, axis, [(source, source + steps) for source in range(initial, last)])


def exchanged(value, axis, bit):
    count = lax.axis_size(axis)
    return lax.ppermute(value, axis, [(source, source ^ bit) for source in range(count)])


def as_column(row):
    size = row.shape[1]
    eye = lax.broadcasted_iota(jnp.int32, (size, size), 0) == lax.broadcasted_iota(jnp.int32, (size, size), 1)
    return jnp.sum(jnp.where(eye, row, 0.0), axis=1, keepdims=True)


def as_row(column):
    size = column.shape[0]
    eye = lax.broadcasted_iota(jnp.int32, (size, size), 0) == lax.broadcasted_iota(jnp.int32, (size, size), 1)
    return jnp.sum(jnp.where(eye, column, 0.0), axis=0, keepdims=True)


def for_chunk(ref_column, rows):
    return jnp.concatenate([ref_column] * (rows // REF), axis=0)


def bf16_pieces(value):
    high = value.astype(jnp.bfloat16).astype(jnp.float32)
    middle = (value - high).astype(jnp.bfloat16).astype(jnp.float32)
    return high, middle, value - high - middle


def packed(powers, ref_powers, channel_bound, *more):
    rows = list(bf16_pieces(powers))
    refs = jnp.concatenate(bf16_pieces(ref_powers), axis=1)
    pad = jnp.zeros((1, powers.shape[1] - refs.shape[1]), jnp.float32)
    rows += [jnp.concatenate([refs, pad], axis=1), channel_bound] + list(more)
    rows += [jnp.zeros_like(powers)] * (EXTRA - len(rows))
    return jnp.concatenate(rows, axis=0).astype(jnp.bfloat16)


def unpacked(block):
    wide = block.astype(jnp.float32)
    powers = wide[0:1] + wide[1:2] + wide[2:3]
    refs = wide[3:4, :LANES] + wide[3:4, LANES : 2 * LANES] + wide[3:4, 2 * LANES : 3 * LANES]
    return powers, refs, wide[4:5]


def sent_powers(code):
    return unpacked(code[-EXTRA:])


def rounded_up(value):
    return (value * (1.0 + 2.0**-7)).astype(jnp.bfloat16).astype(jnp.float32)


def coded(values, channel_bound, ref_bound):
    channel = lax.rsqrt(jnp.maximum(channel_bound, TINY))
    refs = lax.rsqrt(jnp.maximum(ref_bound, TINY)) * CODE_SCALE
    power = values * channel * for_chunk(refs, values.shape[0])
    for _ in range(4):
        power = power * jnp.abs(power)
    return power.astype(jnp.bfloat16)


def expanded(code, channel_bound, ref_bound):
    channel = jnp.sqrt(jnp.maximum(channel_bound, TINY))
    refs = jnp.sqrt(jnp.maximum(ref_bound, TINY)) * (1.0 / CODE_SCALE)
    wide = code[...].astype(jnp.float32)
    root = jnp.exp2(jnp.log2(jnp.abs(wide)) * (1.0 / POWER))
    return jnp.where(wide < 0.0, -root, root) * channel * for_chunk(refs, code.shape[0])


def ref_column(ref_powers):
    return as_column(ref_powers)[:REF]


def prepare_kernel(strain, own, head, left, sems):
    rows = left.shape[0]
    step = rows // PIECES
    copies = [
        pltpu.make_async_copy(
            strain.at[pl.ds(index * step, step), pl.ds(0, LANES)], left.at[pl.ds(index * step, step)], sems.at[index]
        )
        for index in range(PIECES)
    ]
    copies.append(pltpu.make_async_copy(strain.at[pl.ds(0, LAGS)], head, sems.at[PIECES]))
    for copy in copies:
        copy.start()
    for index in range(PIECES):
        copies[index].wait()
        here = slice(index * step, (index + 1) * step)
        own[:, here] = left[here, :].astype(jnp.float32).T[:HALF].astype(jnp.bfloat16)
    copies[PIECES].wait()


def prepared(strain):
    rows, width = strain.shape
    vmem = pl.BlockSpec(memory_space=pltpu.VMEM)
    return pl.pallas_call(
        prepare_kernel,
        in_specs=[pl.BlockSpec(memory_space=pl.ANY)],
        out_specs=[vmem, vmem],
        out_shape=[pltpu.VMEM((HALF, rows), strain.dtype), pltpu.VMEM((LAGS, width), strain.dtype)],
        scratch_shapes=[pltpu.VMEM((rows, LANES), strain.dtype), pltpu.SemaphoreType.DMA((PIECES + 1,))],
        compiler_params=pltpu.CompilerParams(vmem_limit_bytes=VMEM_BYTES),
        cost_estimate=lasting(PRODUCT_MICROS),
        name="prepared",
    )(pltpu.with_memory_space_constraint(strain, pltpu.HBM))


def lag_rows(own, other, group, shifted):
    chan, near = lax.axis_index("chan"), lax.axis_index("tm") & 1
    rows = own.shape[1]
    zeros = jnp.zeros((HALF, LANES), jnp.float32)
    for refs, half in ((own, chan), (other, 1 - chan)):
        long = jnp.concatenate([zeros, refs[...].astype(jnp.float32)], axis=1)
        for index in range(GROUP):
            ahead = near if index < GROUP // 2 else 1 - near
            lag = group * GROUP + ahead * (GROUP // 2) + index % (GROUP // 2)
            start = pl.multiple_of(index * REF + half * HALF, HALF)
            moved = pltpu.roll(long, lag, 1)[:, LANES : LANES + rows]
            shifted[pl.ds(start, HALF), :] = moved.astype(jnp.bfloat16)


def own_group(bits):
    return lax.shift_right_logical(lax.axis_index("tm").astype(jnp.int32), 1) ^ bits


def loaded_kernel(strain, held, power, sems):
    step = held.shape[0] // FETCHES
    pieces = [slice(index * step, (index + 1) * step) for index in range(FETCHES)]
    copies = [
        pltpu.make_async_copy(strain.at[pl.ds(here.start, step)], held.at[pl.ds(here.start, step)], sems.at[index])
        for index, here in enumerate(pieces)
    ]
    for copy in copies:
        copy.start()
    total = jnp.zeros((8, held.shape[1]), jnp.float32)
    for copy, here in zip(copies, pieces):
        copy.wait()
        squares = jnp.square(held[here, :].astype(jnp.float32))
        total += jnp.sum(squares.reshape(step // 8, 8, held.shape[1]), axis=0)
    power[...] = jnp.sum(total, axis=0, keepdims=True)


def loaded(strain, after):
    rows, width = strain.shape
    vmem = pl.BlockSpec(memory_space=pltpu.VMEM)

    def kernel(strain, after, held, power, sems):
        loaded_kernel(strain, held, power, sems)

    return pl.pallas_call(
        kernel,
        in_specs=[pl.BlockSpec(memory_space=pl.ANY)] * 2,
        out_specs=[vmem, vmem],
        out_shape=[pltpu.VMEM((rows, width), strain.dtype), pltpu.VMEM((1, width), jnp.float32)],
        scratch_shapes=[pltpu.SemaphoreType.DMA((FETCHES,))],
        compiler_params=pltpu.CompilerParams(vmem_limit_bytes=VMEM_BYTES),
        cost_estimate=lasting(PRODUCT_MICROS),
        name="loaded",
    )(pltpu.with_memory_space_constraint(strain, pltpu.HBM), after)


def columns(width):
    return [slice(first, first + STEP) for first in range(0, width, STEP)]


def product_of(shifted, held, here):
    return jnp.dot(shifted[...], held[:, here], preferred_element_type=jnp.float32)


def boundary_rows(group, ends, their_ends, edges):
    chan, near = lax.axis_index("chan"), lax.axis_index("tm") & 1
    zeros = jnp.zeros((HALF, LANES), jnp.float32)
    ours = [(refs[:, refs.shape[1] - LANES :].astype(jnp.float32), half) for refs, half in zip(ends, (chan, 1 - chan))]
    theirs = [(their_ends[half * HALF : (half + 1) * HALF], half) for half in range(2)]
    for side, parts in enumerate((ours, theirs)):
        for end, half in parts:
            long = jnp.concatenate([end, zeros], axis=1)
            for index in range(GROUP // 2):
                lag = group * GROUP + near * (GROUP // 2) + index
                start = pl.multiple_of(index * REF + half * HALF, HALF)
                moved = pltpu.roll(long, lag, 1)[:, LANES:]
                edges[pl.ds(start, HALF), side * LANES : (side + 1) * LANES] = moved.astype(jnp.bfloat16)


def last_samples(own, other):
    chan = lax.axis_index("chan")
    ours, theirs = [refs[:, refs.shape[1] - LANES :].astype(jnp.float32) for refs in (own, other)]
    first, second = jnp.where(chan == 0, ours, theirs), jnp.where(chan == 0, theirs, ours)
    square = jnp.concatenate([first, second, jnp.zeros((LANES - REF, LANES), jnp.float32)], axis=0)
    rows = square.T[LANES - LAGS :, :REF]
    return jnp.concatenate([rows[index : index + 1] for index in range(LAGS)], axis=1)


def ends_of(code):
    row = code[-EXTRA:].astype(jnp.float32)[5:6]
    rows = jnp.concatenate([row[:, index * REF : (index + 1) * REF] for index in range(LAGS)], axis=0)
    rows = jnp.concatenate([rows, jnp.zeros((LAGS, LANES - REF), jnp.float32)], axis=1)
    return jnp.concatenate([jnp.zeros((LANES - LAGS, LANES), jnp.float32), rows], axis=0).T[:REF]


def tail_of(code, here):
    first = code.shape[0] // REF * REF
    return code[first : first + LAGS, here]


def tails_of(sent, arrived, here):
    zeros = jnp.zeros((LANES - LAGS, here.stop - here.start), jnp.bfloat16)
    return jnp.concatenate([tail_of(arrived, here), zeros, tail_of(sent, here), zeros], axis=0)


def first_products_kernel(held, power, own, other, keep, send, shifted):
    lag_rows(own, other, own_group(3), shifted)
    ours, theirs = [
        jnp.sum(jnp.square(refs[...].astype(jnp.float32)), axis=1, keepdims=True) for refs in (own, other)
    ]
    refs = jnp.where(
        lax.axis_index("chan") == 0,
        jnp.concatenate([ours, theirs], axis=0),
        jnp.concatenate([theirs, ours], axis=0),
    )
    bound = rounded_up(power[...])
    pad = jnp.zeros((1, LANES - REF), jnp.float32)
    chunk = keep.shape[0]
    refs_row = jnp.concatenate([as_row(refs), pad], axis=1)
    send[chunk:] = packed(power[...], refs_row, bound, last_samples(own, other))
    for here in columns(held.shape[1]):
        product = product_of(shifted, held, here)
        keep[:, here] = product[:chunk]
        send[:chunk, here] = coded(product[chunk:], bound[:, here], refs)


def shifted_scratch(rows, groups=1):
    return [pltpu.VMEM((groups * GROUP * REF, rows), jnp.bfloat16)]


def first_products(held, power, own, other, chunk):
    rows, width = held.shape
    return call_on_blocks(
        first_products_kernel,
        [((chunk, width), jnp.float32), ((chunk + EXTRA, width), jnp.bfloat16)],
        held,
        power,
        own,
        other,
        name="first_products",
        micros=PRODUCT_MICROS,
        scratch=shifted_scratch(rows),
    )


def later_products(groups, held, own, other, powers, chunk, spare=0, after=()):
    rows, width = held.shape

    def kernel(held, own, other, powers, *rest):
        outs, shifted = rest[:-1], rest[-1]
        _, ref_powers, bound = sent_powers(powers)
        refs = ref_column(ref_powers)
        for index, bits in enumerate(groups):
            lag_rows(own, other, own_group(bits), shifted.at[pl.ds(index * 2 * chunk, 2 * chunk)])
            if spare:
                outs[2 * index + 1][chunk:] = jnp.zeros((spare, width), jnp.bfloat16)
        for here in columns(width):
            product = product_of(shifted, held, here)
            for index in range(len(groups)):
                keep, send = outs[2 * index : 2 * index + 2]
                first = 2 * index * chunk
                keep[:, here] = product[first : first + chunk]
                send[:chunk, here] = coded(product[first + chunk : first + 2 * chunk], bound[:, here], refs)

    return call_on_blocks(
        kernel,
        [((chunk, width), jnp.float32), ((chunk + spare, width), jnp.bfloat16)] * len(groups),
        held,
        own,
        other,
        powers,
        name="later_products",
        micros=PRODUCT_MICROS,
        after=after,
        scratch=shifted_scratch(rows, len(groups)),
    )


def edges_scratch(count, chunk):
    return [pltpu.VMEM((count, chunk, 2 * LANES), jnp.bfloat16)]


def call_on_blocks(kernel, outs, *arrays, name, micros, after=(), scratch=(), space=pltpu.VMEM):
    vmem = pl.BlockSpec(memory_space=pltpu.VMEM)
    count = len(arrays)

    def body(*refs):
        kernel(*refs[:count], *refs[count + len(after) :])

    return pl.pallas_call(
        body,
        in_specs=[vmem] * count + [pl.BlockSpec(memory_space=pl.ANY)] * len(after),
        out_specs=[vmem] * len(outs),
        out_shape=[space(shape, dtype) for shape, dtype in outs],
        scratch_shapes=list(scratch),
        compiler_params=pltpu.CompilerParams(vmem_limit_bytes=VMEM_BYTES),
        cost_estimate=lasting(micros),
        name=name,
    )(*arrays, *after)


def with_tails(head, after_next, send):
    rows, width = send.shape
    chunk = rows - EXTRA

    def kernel(head, after_next, send, out):
        near = lax.axis_index("tm") & 1
        out[:chunk] = send[:chunk]
        out[chunk : chunk + LAGS] = jnp.where(near == 0, after_next[...], head[...])
        out[chunk + LAGS :] = send[chunk:]

    outs = [((rows + LAGS, width), jnp.bfloat16)]
    return call_on_blocks(kernel, outs, head, after_next, send, name="with_tails", micros=MERGE_MICROS)[0]


def with_boundaries(keeps, groups, own, other, sent, arrived, after):
    chunk, width = keeps[0].shape

    def kernel(own, other, sent, arrived, *rest):
        keeps, outs, edges = rest[: len(groups)], rest[len(groups) : -1], rest[-1]
        for index, bits in enumerate(groups):
            boundary_rows(own_group(bits), (own, other), ends_of(arrived), edges.at[index])
        for here in columns(width):
            tails = tails_of(sent, arrived, here)
            for index in range(len(groups)):
                added = jnp.dot(edges[index], tails, preferred_element_type=jnp.float32)
                outs[index][:, here] = keeps[index][:, here] + added

    return call_on_blocks(
        kernel,
        [((chunk, width), jnp.float32)] * len(groups),
        own,
        other,
        sent,
        arrived,
        *keeps,
        name="with_boundaries",
        micros=MERGE_MICROS,
        after=after,
        scratch=edges_scratch(len(groups), chunk),
    )


def merged_near(keep, group, own, other, ours, theirs, held_back):
    chunk, width = keep.shape

    def kernel(keep, own, other, ours, theirs, held_back, out, passed, edges):
        passed[...] = held_back[...]
        boundary_rows(own_group(group), (own, other), ends_of(theirs), edges.at[0])
        powers, refs, bound = sent_powers(ours)
        their_powers, their_refs, their_bound = sent_powers(theirs)
        their_refs_column, sum_refs = ref_column(their_refs), refs + their_refs
        sum_refs_column = ref_column(sum_refs)
        bounds = []
        for here in columns(width):
            tails = tails_of(ours, theirs, here)
            total = keep[:, here] + jnp.dot(edges[0], tails, preferred_element_type=jnp.float32)
            total += expanded(theirs[:chunk, here], their_bound[:, here], their_refs_column)
            beyond = jnp.sum(jnp.square(tails.astype(jnp.float32)), axis=0, keepdims=True)
            bounds.append(rounded_up(bound[:, here] + their_bound[:, here] + beyond))
            out[:chunk, here] = coded(total, bounds[-1], sum_refs_column)
        out[chunk:] = packed(powers + their_powers, sum_refs, jnp.concatenate(bounds, axis=1))

    return call_on_blocks(
        kernel,
        [((chunk + EXTRA, width), jnp.bfloat16), (held_back.shape, jnp.bfloat16)],
        keep,
        own,
        other,
        ours,
        theirs,
        held_back,
        name="merged_near",
        micros=MERGE_MICROS,
        scratch=edges_scratch(1, chunk),
    )


def direct_sums(direct, powers):
    _, refs, bound = sent_powers(powers)
    chunk = direct.shape[0] // REF * REF
    return expanded(direct[:chunk], bound, ref_column(refs))


def merged(keep, ours, theirs, direct, direct_powers, held_back, after):
    chunk, width = keep.shape

    def kernel(keep, ours, theirs, direct, direct_powers, held_back, out, passed):
        passed[...] = held_back[...]
        powers, refs, bound = sent_powers(ours)
        their_powers, their_refs, their_bound = sent_powers(theirs)
        sum_refs, sum_bound = refs + their_refs, rounded_up(bound + their_bound)
        total = keep[...] + expanded(theirs[:chunk], their_bound, ref_column(their_refs))
        total += direct_sums(direct, direct_powers)
        out[chunk:] = packed(powers + their_powers, sum_refs, sum_bound)
        out[:chunk] = coded(total, sum_bound, ref_column(sum_refs))

    outs = [((chunk + EXTRA, width), jnp.bfloat16), (held_back.shape, jnp.bfloat16)]
    arrays = (keep, ours, theirs, direct, direct_powers, held_back)
    return call_on_blocks(kernel, outs, *arrays, name="merged", micros=MERGE_MICROS, after=after)


def resent(keep, direct, direct_powers, ours, after):
    def kernel(keep, direct, direct_powers, ours, out):
        _, refs, bound = sent_powers(ours)
        out[...] = coded(keep[...] + direct_sums(direct, direct_powers), bound, ref_column(refs))

    outs = [(keep.shape, jnp.bfloat16)]
    arrays = (keep, direct, direct_powers, ours)
    return call_on_blocks(kernel, outs, *arrays, name="resent", micros=MERGE_MICROS, after=after)[0]


def added(keep, direct, direct_powers, after):
    def kernel(keep, direct, direct_powers, out):
        out[...] = keep[...] + direct_sums(direct, direct_powers)

    outs = [(keep.shape, jnp.float32)]
    arrays = (keep, direct, direct_powers)
    return call_on_blocks(kernel, outs, *arrays, name="added", micros=MERGE_MICROS, after=after)[0]


def finished(slab_rows, segment, partial, near, near_powers, ours, theirs, autos):
    chunk, width = partial.shape

    def kernel(partial, near, near_powers, ours, theirs, *refs):
        autos, (covariance, segment_auto) = refs[:-2], refs[-2:]
        first_lag = lax.axis_index("tm").astype(jnp.int32) * (chunk // REF)
        lag = lax.broadcasted_iota(jnp.int32, (chunk, 1), 0) // REF + first_lag
        denom = (slab_rows - lag).astype(jnp.float32)
        powers, own_refs, _ = sent_powers(ours)
        their_powers, their_refs, their_bound = sent_powers(theirs)
        total = partial[...] + direct_sums(near, near_powers)
        total += expanded(theirs[:chunk], their_bound, ref_column(their_refs))
        scale = 1.0 / jnp.sqrt((powers + their_powers) / slab_rows + 1e-06)
        ref_scale = 1.0 / jnp.sqrt(ref_column(own_refs + their_refs) / slab_rows + 1e-06)
        covariance[...] = total * scale * (for_chunk(ref_scale, chunk) / denom)
        first = 0
        for auto in autos:
            here = slice(first, first + auto.shape[1])
            segment_auto[:, here] = auto[...] * (scale[:, here] * scale[:, here]) / segment
            first = here.stop

    outs = [(partial.shape, jnp.float32), ((LAGS, width), jnp.float32)]
    return call_on_blocks(
        kernel,
        outs,
        partial,
        near,
        near_powers,
        ours,
        theirs,
        *autos,
        name="finished",
        micros=MERGE_MICROS,
        space=jax.ShapeDtypeStruct,
    )


def segment_kernel(first, held, power, tail, out, wide):
    rows = held.shape[0]
    step = rows // 8
    pitch = step + LAGS
    for index in range(out.shape[1] // LANES):
        here = slice(first + index * LANES, first + (index + 1) * LANES)
        there = slice(index * LANES, (index + 1) * LANES)
        for part in range(8):
            end = (part + 1) * step
            wide[part * pitch : part * pitch + step, :] = held[end - step : end, here].astype(jnp.float32)
            if part < 7:
                following = held[end : end + LAGS, here].astype(jnp.float32)
            else:
                following = tail_of(tail, here).astype(jnp.float32)
            wide[part * pitch + step : (part + 1) * pitch, :] = following
        taken = lambda first: wide[pl.ds(first, 8, stride=pitch), :]

        def advance(index, carry):
            window, sums = carry
            window = window + (taken(index + LAGS - 1),)
            sums = tuple(total + window[0] * window[lag + 1] for lag, total in enumerate(sums))
            return window[1:], sums

        window = tuple(taken(first) for first in range(LAGS - 1))
        zero = jnp.zeros((8, LANES), jnp.float32)
        _, sums = lax.fori_loop(0, step, advance, (window, (zero,) * (LAGS - 1)), unroll=16)
        out[:, there] = jnp.concatenate(
            [power[:, here]] + [jnp.sum(total, axis=0, keepdims=True) for total in sums], axis=0
        )


def segment_rows(held, power, tail, first, size, after=()):
    rows = held.shape[0]

    def kernel(*refs):
        segment_kernel(first, *refs)

    return call_on_blocks(
        kernel,
        [((LAGS, size), jnp.float32)],
        held,
        power,
        tail,
        name="segment_rows",
        micros=SEGMENT_MICROS,
        after=after,
        scratch=[pltpu.VMEM((rows + 8 * LAGS, LANES), jnp.float32)],
    )[0]


def all_products_kernel(held, own, other, tail, out, shifted):
    chan = lax.axis_index("chan")
    zeros = jnp.zeros((HALF, LANES), jnp.float32)
    for refs, half in ((own, chan), (other, 1 - chan)):
        long = jnp.concatenate([refs[...].astype(jnp.float32), zeros], axis=1)
        for index in range(GROUP):
            start = pl.multiple_of(index * REF + half * HALF, HALF)
            lag = pl.program_id(0) * GROUP + index
            shifted[pl.ds(start, HALF), :] = pltpu.roll(long, lag, 1).astype(jnp.bfloat16)
    rows, width = held.shape
    edge = jnp.concatenate([tail[...], jnp.zeros((LANES - LAGS, width), tail.dtype)], axis=0)
    for here in columns(width):
        total = jnp.dot(shifted[:, rows:], edge[:, here], preferred_element_type=jnp.float32)
        out[:, here] = total + jnp.dot(shifted[:, :rows], held[:, here], preferred_element_type=jnp.float32)


def all_products(held, own, other, tail):
    rows, width = held.shape
    vmem = pl.BlockSpec(memory_space=pltpu.VMEM)
    return pl.pallas_call(
        all_products_kernel,
        grid=(LAGS // GROUP,),
        in_specs=[vmem] * 4,
        out_specs=pl.BlockSpec((GROUP * REF, width), lambda group: (group, 0)),
        out_shape=jax.ShapeDtypeStruct((LAGS * REF, width), jnp.float32),
        scratch_shapes=[pltpu.VMEM((GROUP * REF, rows + LANES), jnp.bfloat16)],
        compiler_params=pltpu.CompilerParams(vmem_limit_bytes=VMEM_BYTES),
        name="all_products",
    )(held, own, other, tail)


def from_pair_ahead(value):
    count = lax.axis_size("tm")
    return lax.ppermute(value, "tm", [(time + 2, time) for time in range(0, count - 2, 2)])


def local(strain):
    rows, width = strain.shape
    count = lax.axis_size("tm")
    slab_rows = rows * count
    chunk = LAGS * REF // count

    own, head = prepared(strain)
    other = exchanged(own, "chan", 1)
    held, power = loaded(strain, own)
    size = width // 2

    if chunk * 2 == GROUP * REF:
        keep6, send7 = first_products(held, power, own, other, chunk)
        after_next = from_pair_ahead(head)
        send7 = with_tails(head, after_next, send7)
        got7 = exchanged(send7, "tm", 1)
        keep4, send5 = later_products((2,), held, own, other, send7, chunk, spare=LAGS)
        got5 = exchanged(send5, "tm", 1)
        keep2, send3, keep0, send1 = later_products(
            (1, 0), held, own, other, send7, chunk, after=(send5,)
        )
        send6, send3 = merged_near(keep6, 3, own, other, send7, got7, send3)
        got6 = exchanged(send6, "tm", 2)
        got3 = exchanged(send3, "tm", 1)
        keep4, keep2, keep0 = with_boundaries(
            (keep4, keep2, keep0), (2, 1, 0), own, other, send7, got7, after=(send6,)
        )
        autos = [segment_rows(held, power, got7, 0, size, after=(keep4,))]
        send4, send1 = merged(keep4, send6, got6, got5, got7, send1, after=(autos[0],))
        got4 = exchanged(send4, "tm", 4)
        got1 = exchanged(send1, "tm", 1)
        send2 = resent(keep2, got3, got7, send6, after=(send4,))
        got2 = exchanged(send2, "tm", 2)
        autos.append(segment_rows(held, power, got7, size, size, after=(send2,)))
        partial = added(keep0, got1, got7, after=(autos[1],))
        return tuple(finished(slab_rows, rows, partial, got2, got6, send4, got4, autos))

    tail = passed_along(head, "tm", -1)
    chan = lax.axis_index("chan").astype(jnp.int32)
    time = lax.axis_index("tm").astype(jnp.int32)
    auto = jnp.concatenate(
        [segment_rows(held, power, tail, size * index, size) for index in range(2)], axis=1
    )
    power_other = jnp.sum(jnp.square(other.astype(jnp.float32)), axis=1)
    power = lax.psum(jnp.concatenate([power[0], power_other]), "tm")
    inv = 1.0 / jnp.sqrt(power / slab_rows + 1e-06)
    scale = inv[:width]
    ref_scale = jnp.where(
        chan == 0,
        jnp.concatenate([inv[:HALF], inv[width:]]),
        jnp.concatenate([inv[width:], inv[:HALF]]),
    )
    products = all_products(held, own, other, tail)
    summed = lax.psum_scatter(products, "tm", scatter_dimension=0, tiled=True)
    row = time * chunk + jnp.arange(chunk, dtype=jnp.int32)
    row_scale = ref_scale[row % REF] / (slab_rows - row // REF).astype(jnp.float32)
    covariance = summed * scale[None, :] * row_scale[:, None]
    segment_auto = auto * (scale * scale)[None, :] / rows
    return (covariance, segment_auto)


def solution(mesh):
    in_specs = (P(("groups", "tm"), "chan"),)
    out_specs = (P(("groups", "tm"), "chan"), P(("groups", "tm"), "chan"))
    return jax.shard_map(local, mesh=mesh, in_specs=in_specs, out_specs=out_specs, check_vma=False)
```

```python
import jax
import jax.numpy as jnp
from jax import lax
from jax.experimental import pallas as pl
from jax.experimental.pallas import tpu as pltpu
from jax.sharding import PartitionSpec as P

LAGS = 16
REF = 64
HALF = REF // 2
LANES = 128
EXTRA = 8
FETCHES = 8
STEP = 256
GROUP = 4
POWER = 16
CODE_SCALE = 2.0 ** (126 / POWER)
TINY = 1e-35
PIECES = 4
VMEM_BYTES = 32 * 1024 * 1024
HBM_RATE = 3.69e6
PRODUCT_MICROS = 1.0
SEGMENT_MICROS = 1.2
MERGE_MICROS = 0.3


def lasting(micros):
    return pl.CostEstimate(flops=0, bytes_accessed=int(micros * HBM_RATE), transcendentals=0)


def passed_along(value, axis, steps):
    count = lax.axis_size(axis)
    initial, last = (max(0, -steps), min(count, count - steps))
    return lax.ppermute(value, axis, [(source, source + steps) for source in range(initial, last)])


def exchanged(value, axis, bit):
    count = lax.axis_size(axis)
    return lax.ppermute(value, axis, [(source, source ^ bit) for source in range(count)])


def as_column(row):
    size = row.shape[1]
    eye = lax.broadcasted_iota(jnp.int32, (size, size), 0) == lax.broadcasted_iota(jnp.int32, (size, size), 1)
    return jnp.sum(jnp.where(eye, row, 0.0), axis=1, keepdims=True)


def as_row(column):
    size = column.shape[0]
    eye = lax.broadcasted_iota(jnp.int32, (size, size), 0) == lax.broadcasted_iota(jnp.int32, (size, size), 1)
    return jnp.sum(jnp.where(eye, column, 0.0), axis=0, keepdims=True)


def for_chunk(ref_column, rows):
    return jnp.concatenate([ref_column] * (rows // REF), axis=0)


def bf16_pieces(value):
    high = value.astype(jnp.bfloat16).astype(jnp.float32)
    middle = (value - high).astype(jnp.bfloat16).astype(jnp.float32)
    return high, middle, value - high - middle


def packed(powers, ref_powers, channel_bound, *more):
    rows = list(bf16_pieces(powers))
    refs = jnp.concatenate(bf16_pieces(ref_powers), axis=1)
    pad = jnp.zeros((1, powers.shape[1] - refs.shape[1]), jnp.float32)
    rows += [jnp.concatenate([refs, pad], axis=1), channel_bound] + list(more)
    rows += [jnp.zeros_like(powers)] * (EXTRA - len(rows))
    return jnp.concatenate(rows, axis=0).astype(jnp.bfloat16)


def unpacked(block):
    wide = block.astype(jnp.float32)
    powers = wide[0:1] + wide[1:2] + wide[2:3]
    refs = wide[3:4, :LANES] + wide[3:4, LANES : 2 * LANES] + wide[3:4, 2 * LANES : 3 * LANES]
    return powers, refs, wide[4:5]


def sent_powers(code):
    return unpacked(code[-EXTRA:])


def rounded_up(value):
    return (value * (1.0 + 2.0**-7)).astype(jnp.bfloat16).astype(jnp.float32)


def coded(values, channel_bound, ref_bound):
    channel = lax.rsqrt(jnp.maximum(channel_bound, TINY))
    refs = lax.rsqrt(jnp.maximum(ref_bound, TINY)) * CODE_SCALE
    power = values * channel * for_chunk(refs, values.shape[0])
    for _ in range(4):
        power = power * jnp.abs(power)
    return power.astype(jnp.bfloat16)


def expanded(code, channel_bound, ref_bound):
    channel = jnp.sqrt(jnp.maximum(channel_bound, TINY))
    refs = jnp.sqrt(jnp.maximum(ref_bound, TINY)) * (1.0 / CODE_SCALE)
    wide = code[...].astype(jnp.float32)
    root = jnp.exp2(jnp.log2(jnp.abs(wide)) * (1.0 / POWER))
    return jnp.where(wide < 0.0, -root, root) * channel * for_chunk(refs, code.shape[0])


def ref_column(ref_powers):
    return as_column(ref_powers)[:REF]


def prepare_kernel(strain, own, head, left, sems):
    rows = left.shape[0]
    step = rows // PIECES
    copies = [
        pltpu.make_async_copy(
            strain.at[pl.ds(index * step, step), pl.ds(0, LANES)], left.at[pl.ds(index * step, step)], sems.at[index]
        )
        for index in range(PIECES)
    ]
    copies.append(pltpu.make_async_copy(strain.at[pl.ds(0, LAGS)], head, sems.at[PIECES]))
    for copy in copies:
        copy.start()
    for index in range(PIECES):
        copies[index].wait()
        here = slice(index * step, (index + 1) * step)
        own[:, here] = left[here, :].astype(jnp.float32).T[:HALF].astype(jnp.bfloat16)
    copies[PIECES].wait()


def prepared(strain):
    rows, width = strain.shape
    vmem = pl.BlockSpec(memory_space=pltpu.VMEM)
    return pl.pallas_call(
        prepare_kernel,
        in_specs=[pl.BlockSpec(memory_space=pl.ANY)],
        out_specs=[vmem, vmem],
        out_shape=[pltpu.VMEM((HALF, rows), strain.dtype), pltpu.VMEM((LAGS, width), strain.dtype)],
        scratch_shapes=[pltpu.VMEM((rows, LANES), strain.dtype), pltpu.SemaphoreType.DMA((PIECES + 1,))],
        compiler_params=pltpu.CompilerParams(vmem_limit_bytes=VMEM_BYTES),
        cost_estimate=lasting(PRODUCT_MICROS),
        name="prepared",
    )(pltpu.with_memory_space_constraint(strain, pltpu.HBM))


def lag_rows(own, other, group, shifted):
    chan, near = lax.axis_index("chan"), lax.axis_index("tm") & 1
    rows = own.shape[1]
    zeros = jnp.zeros((HALF, LANES), jnp.float32)
    for refs, half in ((own, chan), (other, 1 - chan)):
        long = jnp.concatenate([zeros, refs[...].astype(jnp.float32)], axis=1)
        for index in range(GROUP):
            ahead = near if index < GROUP // 2 else 1 - near
            lag = group * GROUP + ahead * (GROUP // 2) + index % (GROUP // 2)
            start = pl.multiple_of(index * REF + half * HALF, HALF)
            moved = pltpu.roll(long, lag, 1)[:, LANES : LANES + rows]
            shifted[pl.ds(start, HALF), :] = moved.astype(jnp.bfloat16)


def own_group(bits):
    return lax.shift_right_logical(lax.axis_index("tm").astype(jnp.int32), 1) ^ bits


def loaded_kernel(strain, held, power, sems):
    step = held.shape[0] // FETCHES
    pieces = [slice(index * step, (index + 1) * step) for index in range(FETCHES)]
    copies = [
        pltpu.make_async_copy(strain.at[pl.ds(here.start, step)], held.at[pl.ds(here.start, step)], sems.at[index])
        for index, here in enumerate(pieces)
    ]
    for copy in copies:
        copy.start()
    total = jnp.zeros((8, held.shape[1]), jnp.float32)
    for copy, here in zip(copies, pieces):
        copy.wait()
        squares = jnp.square(held[here, :].astype(jnp.float32))
        total += jnp.sum(squares.reshape(step // 8, 8, held.shape[1]), axis=0)
    power[...] = jnp.sum(total, axis=0, keepdims=True)


def loaded(strain, after):
    rows, width = strain.shape
    vmem = pl.BlockSpec(memory_space=pltpu.VMEM)

    def kernel(strain, after, held, power, sems):
        loaded_kernel(strain, held, power, sems)

    return pl.pallas_call(
        kernel,
        in_specs=[pl.BlockSpec(memory_space=pl.ANY)] * 2,
        out_specs=[vmem, vmem],
        out_shape=[pltpu.VMEM((rows, width), strain.dtype), pltpu.VMEM((1, width), jnp.float32)],
        scratch_shapes=[pltpu.SemaphoreType.DMA((FETCHES,))],
        compiler_params=pltpu.CompilerParams(vmem_limit_bytes=VMEM_BYTES),
        cost_estimate=lasting(PRODUCT_MICROS),
        name="loaded",
    )(pltpu.with_memory_space_constraint(strain, pltpu.HBM), after)


def columns(width):
    return [slice(first, first + STEP) for first in range(0, width, STEP)]


def product_of(shifted, held, here):
    return jnp.dot(shifted[...], held[:, here], preferred_element_type=jnp.float32)


def boundary_rows(group, ends, their_ends, edges):
    chan, near = lax.axis_index("chan"), lax.axis_index("tm") & 1
    zeros = jnp.zeros((HALF, LANES), jnp.float32)
    ours = [(refs[:, refs.shape[1] - LANES :].astype(jnp.float32), half) for refs, half in zip(ends, (chan, 1 - chan))]
    theirs = [(their_ends[half * HALF : (half + 1) * HALF], half) for half in range(2)]
    for side, parts in enumerate((ours, theirs)):
        for end, half in parts:
            long = jnp.concatenate([end, zeros], axis=1)
            for index in range(GROUP // 2):
                lag = group * GROUP + near * (GROUP // 2) + index
                start = pl.multiple_of(index * REF + half * HALF, HALF)
                moved = pltpu.roll(long, lag, 1)[:, LANES:]
                edges[pl.ds(start, HALF), side * LANES : (side + 1) * LANES] = moved.astype(jnp.bfloat16)


def last_samples(own, other):
    chan = lax.axis_index("chan")
    ours, theirs = [refs[:, refs.shape[1] - LANES :].astype(jnp.float32) for refs in (own, other)]
    first, second = jnp.where(chan == 0, ours, theirs), jnp.where(chan == 0, theirs, ours)
    square = jnp.concatenate([first, second, jnp.zeros((LANES - REF, LANES), jnp.float32)], axis=0)
    rows = square.T[LANES - LAGS :, :REF]
    return jnp.concatenate([rows[index : index + 1] for index in range(LAGS)], axis=1)


def ends_of(code):
    row = code[-EXTRA:].astype(jnp.float32)[5:6]
    rows = jnp.concatenate([row[:, index * REF : (index + 1) * REF] for index in range(LAGS)], axis=0)
    rows = jnp.concatenate([rows, jnp.zeros((LAGS, LANES - REF), jnp.float32)], axis=1)
    return jnp.concatenate([jnp.zeros((LANES - LAGS, LANES), jnp.float32), rows], axis=0).T[:REF]


def tail_of(code, here):
    first = code.shape[0] // REF * REF
    return code[first : first + LAGS, here]


def tails_of(sent, arrived, here):
    zeros = jnp.zeros((LANES - LAGS, here.stop - here.start), jnp.bfloat16)
    return jnp.concatenate([tail_of(arrived, here), zeros, tail_of(sent, here), zeros], axis=0)


def first_products_kernel(held, power, own, other, keep, send, shifted):
    lag_rows(own, other, own_group(3), shifted)
    ours, theirs = [
        jnp.sum(jnp.square(refs[...].astype(jnp.float32)), axis=1, keepdims=True) for refs in (own, other)
    ]
    refs = jnp.where(
        lax.axis_index("chan") == 0,
        jnp.concatenate([ours, theirs], axis=0),
        jnp.concatenate([theirs, ours], axis=0),
    )
    bound = rounded_up(power[...])
    pad = jnp.zeros((1, LANES - REF), jnp.float32)
    chunk = keep.shape[0]
    refs_row = jnp.concatenate([as_row(refs), pad], axis=1)
    send[chunk:] = packed(power[...], refs_row, bound, last_samples(own, other))
    for here in columns(held.shape[1]):
        product = product_of(shifted, held, here)
        keep[:, here] = product[:chunk]
        send[:chunk, here] = coded(product[chunk:], bound[:, here], refs)


def shifted_scratch(rows, groups=1):
    return [pltpu.VMEM((groups * GROUP * REF, rows), jnp.bfloat16)]


def first_products(held, power, own, other, chunk):
    rows, width = held.shape
    return call_on_blocks(
        first_products_kernel,
        [((chunk, width), jnp.float32), ((chunk + EXTRA, width), jnp.bfloat16)],
        held,
        power,
        own,
        other,
        name="first_products",
        micros=PRODUCT_MICROS,
        scratch=shifted_scratch(rows),
    )


def later_products(groups, held, own, other, powers, chunk, spare=0, after=()):
    rows, width = held.shape

    def kernel(held, own, other, powers, *rest):
        outs, shifted = rest[:-1], rest[-1]
        _, ref_powers, bound = sent_powers(powers)
        refs = ref_column(ref_powers)
        for index, bits in enumerate(groups):
            lag_rows(own, other, own_group(bits), shifted.at[pl.ds(index * 2 * chunk, 2 * chunk)])
            if spare:
                outs[2 * index + 1][chunk:] = jnp.zeros((spare, width), jnp.bfloat16)
        for here in columns(width):
            product = product_of(shifted, held, here)
            for index in range(len(groups)):
                keep, send = outs[2 * index : 2 * index + 2]
                first = 2 * index * chunk
                keep[:, here] = product[first : first + chunk]
                send[:chunk, here] = coded(product[first + chunk : first + 2 * chunk], bound[:, here], refs)

    return call_on_blocks(
        kernel,
        [((chunk, width), jnp.float32), ((chunk + spare, width), jnp.bfloat16)] * len(groups),
        held,
        own,
        other,
        powers,
        name="later_products",
        micros=PRODUCT_MICROS,
        after=after,
        scratch=shifted_scratch(rows, len(groups)),
    )


def edges_scratch(count, chunk):
    return [pltpu.VMEM((count, chunk, 2 * LANES), jnp.bfloat16)]


def call_on_blocks(kernel, outs, *arrays, name, micros, after=(), scratch=(), space=pltpu.VMEM):
    vmem = pl.BlockSpec(memory_space=pltpu.VMEM)
    count = len(arrays)

    def body(*refs):
        kernel(*refs[:count], *refs[count + len(after) :])

    return pl.pallas_call(
        body,
        in_specs=[vmem] * count + [pl.BlockSpec(memory_space=pl.ANY)] * len(after),
        out_specs=[vmem] * len(outs),
        out_shape=[space(shape, dtype) for shape, dtype in outs],
        scratch_shapes=list(scratch),
        compiler_params=pltpu.CompilerParams(vmem_limit_bytes=VMEM_BYTES),
        cost_estimate=lasting(micros),
        name=name,
    )(*arrays, *after)


def with_tails(head, after_next, send):
    rows, width = send.shape
    chunk = rows - EXTRA

    def kernel(head, after_next, send, out):
        near = lax.axis_index("tm") & 1
        out[:chunk] = send[:chunk]
        out[chunk : chunk + LAGS] = jnp.where(near == 0, after_next[...], head[...])
        out[chunk + LAGS :] = send[chunk:]

    outs = [((rows + LAGS, width), jnp.bfloat16)]
    return call_on_blocks(kernel, outs, head, after_next, send, name="with_tails", micros=MERGE_MICROS)[0]


def with_boundaries(keeps, groups, own, other, sent, arrived, after):
    chunk, width = keeps[0].shape

    def kernel(own, other, sent, arrived, *rest):
        keeps, outs, edges = rest[: len(groups)], rest[len(groups) : -1], rest[-1]
        for index, bits in enumerate(groups):
            boundary_rows(own_group(bits), (own, other), ends_of(arrived), edges.at[index])
        for here in columns(width):
            tails = tails_of(sent, arrived, here)
            for index in range(len(groups)):
                added = jnp.dot(edges[index], tails, preferred_element_type=jnp.float32)
                outs[index][:, here] = keeps[index][:, here] + added

    return call_on_blocks(
        kernel,
        [((chunk, width), jnp.float32)] * len(groups),
        own,
        other,
        sent,
        arrived,
        *keeps,
        name="with_boundaries",
        micros=MERGE_MICROS,
        after=after,
        scratch=edges_scratch(len(groups), chunk),
    )


def merged_near(keep, group, own, other, ours, theirs, held_back):
    chunk, width = keep.shape

    def kernel(keep, own, other, ours, theirs, held_back, out, passed, edges):
        passed[...] = held_back[...]
        boundary_rows(own_group(group), (own, other), ends_of(theirs), edges.at[0])
        powers, refs, bound = sent_powers(ours)
        their_powers, their_refs, their_bound = sent_powers(theirs)
        their_refs_column, sum_refs = ref_column(their_refs), refs + their_refs
        sum_refs_column = ref_column(sum_refs)
        bounds = []
        for here in columns(width):
            tails = tails_of(ours, theirs, here)
            total = keep[:, here] + jnp.dot(edges[0], tails, preferred_element_type=jnp.float32)
            total += expanded(theirs[:chunk, here], their_bound[:, here], their_refs_column)
            beyond = jnp.sum(jnp.square(tails.astype(jnp.float32)), axis=0, keepdims=True)
            bounds.append(rounded_up(bound[:, here] + their_bound[:, here] + beyond))
            out[:chunk, here] = coded(total, bounds[-1], sum_refs_column)
        out[chunk:] = packed(powers + their_powers, sum_refs, jnp.concatenate(bounds, axis=1))

    return call_on_blocks(
        kernel,
        [((chunk + EXTRA, width), jnp.bfloat16), (held_back.shape, jnp.bfloat16)],
        keep,
        own,
        other,
        ours,
        theirs,
        held_back,
        name="merged_near",
        micros=MERGE_MICROS,
        scratch=edges_scratch(1, chunk),
    )


def direct_sums(direct, powers):
    _, refs, bound = sent_powers(powers)
    chunk = direct.shape[0] // REF * REF
    return expanded(direct[:chunk], bound, ref_column(refs))


def merged(keep, ours, theirs, direct, direct_powers, after):
    chunk, width = keep.shape

    def kernel(keep, ours, theirs, direct, direct_powers, out):
        powers, refs, bound = sent_powers(ours)
        their_powers, their_refs, their_bound = sent_powers(theirs)
        sum_refs, sum_bound = refs + their_refs, rounded_up(bound + their_bound)
        total = keep[...] + expanded(theirs[:chunk], their_bound, ref_column(their_refs))
        total += direct_sums(direct, direct_powers)
        out[chunk:] = packed(powers + their_powers, sum_refs, sum_bound)
        out[:chunk] = coded(total, sum_bound, ref_column(sum_refs))

    outs = [((chunk + EXTRA, width), jnp.bfloat16)]
    arrays = (keep, ours, theirs, direct, direct_powers)
    return call_on_blocks(kernel, outs, *arrays, name="merged", micros=MERGE_MICROS, after=after)[0]


def resent(keep, direct, direct_powers, ours, after):
    def kernel(keep, direct, direct_powers, ours, out):
        _, refs, bound = sent_powers(ours)
        out[...] = coded(keep[...] + direct_sums(direct, direct_powers), bound, ref_column(refs))

    outs = [(keep.shape, jnp.bfloat16)]
    arrays = (keep, direct, direct_powers, ours)
    return call_on_blocks(kernel, outs, *arrays, name="resent", micros=MERGE_MICROS, after=after)[0]


def added(keep, direct, direct_powers, after):
    def kernel(keep, direct, direct_powers, out):
        out[...] = keep[...] + direct_sums(direct, direct_powers)

    outs = [(keep.shape, jnp.float32)]
    arrays = (keep, direct, direct_powers)
    return call_on_blocks(kernel, outs, *arrays, name="added", micros=MERGE_MICROS, after=after)[0]


def finished(slab_rows, segment, partial, near, near_powers, ours, theirs, autos):
    chunk, width = partial.shape

    def kernel(partial, near, near_powers, ours, theirs, *refs):
        autos, (covariance, segment_auto) = refs[:-2], refs[-2:]
        first_lag = lax.axis_index("tm").astype(jnp.int32) * (chunk // REF)
        lag = lax.broadcasted_iota(jnp.int32, (chunk, 1), 0) // REF + first_lag
        denom = (slab_rows - lag).astype(jnp.float32)
        powers, own_refs, _ = sent_powers(ours)
        their_powers, their_refs, their_bound = sent_powers(theirs)
        total = partial[...] + direct_sums(near, near_powers)
        total += expanded(theirs[:chunk], their_bound, ref_column(their_refs))
        scale = 1.0 / jnp.sqrt((powers + their_powers) / slab_rows + 1e-06)
        ref_scale = 1.0 / jnp.sqrt(ref_column(own_refs + their_refs) / slab_rows + 1e-06)
        covariance[...] = total * scale * (for_chunk(ref_scale, chunk) / denom)
        first = 0
        for auto in autos:
            here = slice(first, first + auto.shape[1])
            segment_auto[:, here] = auto[...] * (scale[:, here] * scale[:, here]) / segment
            first = here.stop

    outs = [(partial.shape, jnp.float32), ((LAGS, width), jnp.float32)]
    return call_on_blocks(
        kernel,
        outs,
        partial,
        near,
        near_powers,
        ours,
        theirs,
        *autos,
        name="finished",
        micros=MERGE_MICROS,
        space=jax.ShapeDtypeStruct,
    )


def segment_kernel(first, held, power, tail, out, wide):
    rows = held.shape[0]
    step = rows // 8
    pitch = step + LAGS
    for index in range(out.shape[1] // LANES):
        here = slice(first + index * LANES, first + (index + 1) * LANES)
        there = slice(index * LANES, (index + 1) * LANES)
        for part in range(8):
            end = (part + 1) * step
            wide[part * pitch : part * pitch + step, :] = held[end - step : end, here].astype(jnp.float32)
            if part < 7:
                following = held[end : end + LAGS, here].astype(jnp.float32)
            else:
                following = tail_of(tail, here).astype(jnp.float32)
            wide[part * pitch + step : (part + 1) * pitch, :] = following
        taken = lambda first: wide[pl.ds(first, 8, stride=pitch), :]

        def advance(index, carry):
            window, sums = carry
            window = window + (taken(index + LAGS - 1),)
            sums = tuple(total + window[0] * window[lag + 1] for lag, total in enumerate(sums))
            return window[1:], sums

        window = tuple(taken(first) for first in range(LAGS - 1))
        zero = jnp.zeros((8, LANES), jnp.float32)
        _, sums = lax.fori_loop(0, step, advance, (window, (zero,) * (LAGS - 1)), unroll=16)
        out[:, there] = jnp.concatenate(
            [power[:, here]] + [jnp.sum(total, axis=0, keepdims=True) for total in sums], axis=0
        )


def segment_rows(held, power, tail, first, size, held_back=(), after=()):
    rows = held.shape[0]

    def kernel(held, power, tail, *refs):
        codes, out, passed, wide = refs[: len(held_back)], refs[len(held_back)], refs[len(held_back) + 1 : -1], refs[-1]
        for code, to in zip(codes, passed):
            to[...] = code[...]
        segment_kernel(first, held, power, tail, out, wide)

    return call_on_blocks(
        kernel,
        [((LAGS, size), jnp.float32)] + [(code.shape, code.dtype) for code in held_back],
        held,
        power,
        tail,
        *held_back,
        name="segment_rows",
        micros=SEGMENT_MICROS,
        after=after,
        scratch=[pltpu.VMEM((rows + 8 * LAGS, LANES), jnp.float32)],
    )


def all_products_kernel(held, own, other, tail, out, shifted):
    chan = lax.axis_index("chan")
    zeros = jnp.zeros((HALF, LANES), jnp.float32)
    for refs, half in ((own, chan), (other, 1 - chan)):
        long = jnp.concatenate([refs[...].astype(jnp.float32), zeros], axis=1)
        for index in range(GROUP):
            start = pl.multiple_of(index * REF + half * HALF, HALF)
            lag = pl.program_id(0) * GROUP + index
            shifted[pl.ds(start, HALF), :] = pltpu.roll(long, lag, 1).astype(jnp.bfloat16)
    rows, width = held.shape
    edge = jnp.concatenate([tail[...], jnp.zeros((LANES - LAGS, width), tail.dtype)], axis=0)
    for here in columns(width):
        total = jnp.dot(shifted[:, rows:], edge[:, here], preferred_element_type=jnp.float32)
        out[:, here] = total + jnp.dot(shifted[:, :rows], held[:, here], preferred_element_type=jnp.float32)


def all_products(held, own, other, tail):
    rows, width = held.shape
    vmem = pl.BlockSpec(memory_space=pltpu.VMEM)
    return pl.pallas_call(
        all_products_kernel,
        grid=(LAGS // GROUP,),
        in_specs=[vmem] * 4,
        out_specs=pl.BlockSpec((GROUP * REF, width), lambda group: (group, 0)),
        out_shape=jax.ShapeDtypeStruct((LAGS * REF, width), jnp.float32),
        scratch_shapes=[pltpu.VMEM((GROUP * REF, rows + LANES), jnp.bfloat16)],
        compiler_params=pltpu.CompilerParams(vmem_limit_bytes=VMEM_BYTES),
        name="all_products",
    )(held, own, other, tail)


def from_pair_ahead(value):
    count = lax.axis_size("tm")
    return lax.ppermute(value, "tm", [(time + 2, time) for time in range(0, count - 2, 2)])


def local(strain):
    rows, width = strain.shape
    count = lax.axis_size("tm")
    slab_rows = rows * count
    chunk = LAGS * REF // count

    own, head = prepared(strain)
    other = exchanged(own, "chan", 1)
    held, power = loaded(strain, own)
    if chunk * 2 == GROUP * REF:
        keep6, send7 = first_products(held, power, own, other, chunk)
        after_next = from_pair_ahead(head)
        send7 = with_tails(head, after_next, send7)
        got7 = exchanged(send7, "tm", 1)
        keep4, send5 = later_products((2,), held, own, other, send7, chunk, spare=LAGS)
        got5 = exchanged(send5, "tm", 1)
        keep2, send3, keep0, send1 = later_products(
            (1, 0), held, own, other, send7, chunk, after=(send5,)
        )
        send6, send3 = merged_near(keep6, 3, own, other, send7, got7, send3)
        got6 = exchanged(send6, "tm", 2)
        got3 = exchanged(send3, "tm", 1)
        keep4, keep2, keep0 = with_boundaries(
            (keep4, keep2, keep0), (2, 1, 0), own, other, send7, got7, after=(send6,)
        )
        size = width // 4
        auto, send1 = segment_rows(held, power, got7, 0, size, held_back=(send1,), after=(keep4,))
        got1 = exchanged(send1, "tm", 1)
        send4 = merged(keep4, send6, got6, got5, got7, after=(auto,))
        got4 = exchanged(send4, "tm", 4)
        send2 = resent(keep2, got3, got7, send6, after=(send4,))
        got2 = exchanged(send2, "tm", 2)
        autos = [auto, *segment_rows(held, power, got7, size, width - size, after=(send2,))]
        partial = added(keep0, got1, got7, after=(autos[1],))
        return tuple(finished(slab_rows, rows, partial, got2, got6, send4, got4, autos))

    tail = passed_along(head, "tm", -1)
    chan = lax.axis_index("chan").astype(jnp.int32)
    time = lax.axis_index("tm").astype(jnp.int32)
    (auto,) = segment_rows(held, power, tail, 0, width)
    power_other = jnp.sum(jnp.square(other.astype(jnp.float32)), axis=1)
    power = lax.psum(jnp.concatenate([power[0], power_other]), "tm")
    inv = 1.0 / jnp.sqrt(power / slab_rows + 1e-06)
    scale = inv[:width]
    ref_scale = jnp.where(
        chan == 0,
        jnp.concatenate([inv[:HALF], inv[width:]]),
        jnp.concatenate([inv[width:], inv[:HALF]]),
    )
    products = all_products(held, own, other, tail)
    summed = lax.psum_scatter(products, "tm", scatter_dimension=0, tiled=True)
    row = time * chunk + jnp.arange(chunk, dtype=jnp.int32)
    row_scale = ref_scale[row % REF] / (slab_rows - row // REF).astype(jnp.float32)
    covariance = summed * scale[None, :] * row_scale[:, None]
    segment_auto = auto * (scale * scale)[None, :] / rows
    return (covariance, segment_auto)


def solution(mesh):
    in_specs = (P(("groups", "tm"), "chan"),)
    out_specs = (P(("groups", "tm"), "chan"), P(("groups", "tm"), "chan"))
    return jax.shard_map(local, mesh=mesh, in_specs=in_specs, out_specs=out_specs, check_vma=False)
```

```python
import jax
import jax.numpy as jnp
from jax import lax
from jax.experimental import pallas as pl
from jax.experimental.pallas import tpu as pltpu
from jax.sharding import PartitionSpec as P

LAGS = 16
REF = 64
HALF = REF // 2
LANES = 128
EXTRA = 8
FETCHES = 8
STEP = 256
GROUP = 4
POWER = 16
CODE_SCALE = 2.0 ** (126 / POWER)
TINY = 1e-35
PIECES = 4
VMEM_BYTES = 32 * 1024 * 1024
HBM_RATE = 3.69e6
PRODUCT_MICROS = 1.0
SEGMENT_MICROS = 1.2
MERGE_MICROS = 0.3


def lasting(micros):
    return pl.CostEstimate(flops=0, bytes_accessed=int(micros * HBM_RATE), transcendentals=0)


def passed_along(value, axis, steps):
    count = lax.axis_size(axis)
    initial, last = (max(0, -steps), min(count, count - steps))
    return lax.ppermute(value, axis, [(source, source + steps) for source in range(initial, last)])


def exchanged(value, axis, bit):
    count = lax.axis_size(axis)
    return lax.ppermute(value, axis, [(source, source ^ bit) for source in range(count)])


def as_column(row):
    size = row.shape[1]
    eye = lax.broadcasted_iota(jnp.int32, (size, size), 0) == lax.broadcasted_iota(jnp.int32, (size, size), 1)
    return jnp.sum(jnp.where(eye, row, 0.0), axis=1, keepdims=True)


def as_row(column):
    size = column.shape[0]
    eye = lax.broadcasted_iota(jnp.int32, (size, size), 0) == lax.broadcasted_iota(jnp.int32, (size, size), 1)
    return jnp.sum(jnp.where(eye, column, 0.0), axis=0, keepdims=True)


def for_chunk(ref_column, rows):
    return jnp.concatenate([ref_column] * (rows // REF), axis=0)


def bf16_pieces(value):
    high = value.astype(jnp.bfloat16).astype(jnp.float32)
    middle = (value - high).astype(jnp.bfloat16).astype(jnp.float32)
    return high, middle, value - high - middle


def packed(powers, ref_powers, channel_bound, *more):
    rows = list(bf16_pieces(powers))
    refs = jnp.concatenate(bf16_pieces(ref_powers), axis=1)
    pad = jnp.zeros((1, powers.shape[1] - refs.shape[1]), jnp.float32)
    rows += [jnp.concatenate([refs, pad], axis=1), channel_bound] + list(more)
    rows += [jnp.zeros_like(powers)] * (EXTRA - len(rows))
    return jnp.concatenate(rows, axis=0).astype(jnp.bfloat16)


def unpacked(block):
    wide = block.astype(jnp.float32)
    powers = wide[0:1] + wide[1:2] + wide[2:3]
    refs = wide[3:4, :LANES] + wide[3:4, LANES : 2 * LANES] + wide[3:4, 2 * LANES : 3 * LANES]
    return powers, refs, wide[4:5]


def sent_powers(code):
    return unpacked(code[-EXTRA:])


def rounded_up(value):
    return (value * (1.0 + 2.0**-7)).astype(jnp.bfloat16).astype(jnp.float32)


def coded(values, channel_bound, ref_bound):
    channel = lax.rsqrt(jnp.maximum(channel_bound, TINY))
    refs = lax.rsqrt(jnp.maximum(ref_bound, TINY)) * CODE_SCALE
    power = values * channel * for_chunk(refs, values.shape[0])
    for _ in range(4):
        power = power * jnp.abs(power)
    return power.astype(jnp.bfloat16)


def expanded(code, channel_bound, ref_bound):
    channel = jnp.sqrt(jnp.maximum(channel_bound, TINY))
    refs = jnp.sqrt(jnp.maximum(ref_bound, TINY)) * (1.0 / CODE_SCALE)
    wide = code[...].astype(jnp.float32)
    root = jnp.exp2(jnp.log2(jnp.abs(wide)) * (1.0 / POWER))
    return jnp.where(wide < 0.0, -root, root) * channel * for_chunk(refs, code.shape[0])


def ref_column(ref_powers):
    return as_column(ref_powers)[:REF]


def prepare_kernel(strain, own, head, left, sems):
    rows = left.shape[0]
    step = rows // PIECES
    copies = [
        pltpu.make_async_copy(
            strain.at[pl.ds(index * step, step), pl.ds(0, LANES)], left.at[pl.ds(index * step, step)], sems.at[index]
        )
        for index in range(PIECES)
    ]
    copies.append(pltpu.make_async_copy(strain.at[pl.ds(0, LAGS)], head, sems.at[PIECES]))
    for copy in copies:
        copy.start()
    for index in range(PIECES):
        copies[index].wait()
        here = slice(index * step, (index + 1) * step)
        own[:, here] = left[here, :].astype(jnp.float32).T[:HALF].astype(jnp.bfloat16)
    copies[PIECES].wait()


def prepared(strain):
    rows, width = strain.shape
    vmem = pl.BlockSpec(memory_space=pltpu.VMEM)
    return pl.pallas_call(
        prepare_kernel,
        in_specs=[pl.BlockSpec(memory_space=pl.ANY)],
        out_specs=[vmem, vmem],
        out_shape=[pltpu.VMEM((HALF, rows), strain.dtype), pltpu.VMEM((LAGS, width), strain.dtype)],
        scratch_shapes=[pltpu.VMEM((rows, LANES), strain.dtype), pltpu.SemaphoreType.DMA((PIECES + 1,))],
        compiler_params=pltpu.CompilerParams(vmem_limit_bytes=VMEM_BYTES),
        cost_estimate=lasting(PRODUCT_MICROS),
        name="prepared",
    )(pltpu.with_memory_space_constraint(strain, pltpu.HBM))


def lag_rows(own, other, group, shifted):
    chan, near = lax.axis_index("chan"), lax.axis_index("tm") & 1
    rows = own.shape[1]
    zeros = jnp.zeros((HALF, LANES), jnp.float32)
    for refs, half in ((own, chan), (other, 1 - chan)):
        long = jnp.concatenate([zeros, refs[...].astype(jnp.float32)], axis=1)
        for index in range(GROUP):
            ahead = near if index < GROUP // 2 else 1 - near
            lag = group * GROUP + ahead * (GROUP // 2) + index % (GROUP // 2)
            start = pl.multiple_of(index * REF + half * HALF, HALF)
            moved = pltpu.roll(long, lag, 1)[:, LANES : LANES + rows]
            shifted[pl.ds(start, HALF), :] = moved.astype(jnp.bfloat16)


def own_group(bits):
    return lax.shift_right_logical(lax.axis_index("tm").astype(jnp.int32), 1) ^ bits


def loaded_kernel(strain, held, power, sems):
    step = held.shape[0] // FETCHES
    pieces = [slice(index * step, (index + 1) * step) for index in range(FETCHES)]
    copies = [
        pltpu.make_async_copy(strain.at[pl.ds(here.start, step)], held.at[pl.ds(here.start, step)], sems.at[index])
        for index, here in enumerate(pieces)
    ]
    for copy in copies:
        copy.start()
    total = jnp.zeros((8, held.shape[1]), jnp.float32)
    for copy, here in zip(copies, pieces):
        copy.wait()
        squares = jnp.square(held[here, :].astype(jnp.float32))
        total += jnp.sum(squares.reshape(step // 8, 8, held.shape[1]), axis=0)
    power[...] = jnp.sum(total, axis=0, keepdims=True)


def loaded(strain, after):
    rows, width = strain.shape
    vmem = pl.BlockSpec(memory_space=pltpu.VMEM)

    def kernel(strain, after, held, power, sems):
        loaded_kernel(strain, held, power, sems)

    return pl.pallas_call(
        kernel,
        in_specs=[pl.BlockSpec(memory_space=pl.ANY)] * 2,
        out_specs=[vmem, vmem],
        out_shape=[pltpu.VMEM((rows, width), strain.dtype), pltpu.VMEM((1, width), jnp.float32)],
        scratch_shapes=[pltpu.SemaphoreType.DMA((FETCHES,))],
        compiler_params=pltpu.CompilerParams(vmem_limit_bytes=VMEM_BYTES),
        cost_estimate=lasting(PRODUCT_MICROS),
        name="loaded",
    )(pltpu.with_memory_space_constraint(strain, pltpu.HBM), after)


def columns(width):
    return [slice(first, first + STEP) for first in range(0, width, STEP)]


def product_of(shifted, held, here):
    return jnp.dot(shifted[...], held[:, here], preferred_element_type=jnp.float32)


def boundary_rows(group, ends, their_ends, edges):
    chan, near = lax.axis_index("chan"), lax.axis_index("tm") & 1
    zeros = jnp.zeros((HALF, LANES), jnp.float32)
    ours = [(refs[:, refs.shape[1] - LANES :].astype(jnp.float32), half) for refs, half in zip(ends, (chan, 1 - chan))]
    theirs = [(their_ends[half * HALF : (half + 1) * HALF], half) for half in range(2)]
    for side, parts in enumerate((ours, theirs)):
        for end, half in parts:
            long = jnp.concatenate([end, zeros], axis=1)
            for index in range(GROUP // 2):
                lag = group * GROUP + near * (GROUP // 2) + index
                start = pl.multiple_of(index * REF + half * HALF, HALF)
                moved = pltpu.roll(long, lag, 1)[:, LANES:]
                edges[pl.ds(start, HALF), side * LANES : (side + 1) * LANES] = moved.astype(jnp.bfloat16)


def last_samples(own, other):
    chan = lax.axis_index("chan")
    ours, theirs = [refs[:, refs.shape[1] - LANES :].astype(jnp.float32) for refs in (own, other)]
    first, second = jnp.where(chan == 0, ours, theirs), jnp.where(chan == 0, theirs, ours)
    square = jnp.concatenate([first, second, jnp.zeros((LANES - REF, LANES), jnp.float32)], axis=0)
    rows = square.T[LANES - LAGS :, :REF]
    return jnp.concatenate([rows[index : index + 1] for index in range(LAGS)], axis=1)


def ends_of(code):
    row = code[-EXTRA:].astype(jnp.float32)[5:6]
    rows = jnp.concatenate([row[:, index * REF : (index + 1) * REF] for index in range(LAGS)], axis=0)
    rows = jnp.concatenate([rows, jnp.zeros((LAGS, LANES - REF), jnp.float32)], axis=1)
    return jnp.concatenate([jnp.zeros((LANES - LAGS, LANES), jnp.float32), rows], axis=0).T[:REF]


def tail_of(code, here):
    first = code.shape[0] // REF * REF
    return code[first : first + LAGS, here]


def tails_of(sent, arrived, here):
    zeros = jnp.zeros((LANES - LAGS, here.stop - here.start), jnp.bfloat16)
    return jnp.concatenate([tail_of(arrived, here), zeros, tail_of(sent, here), zeros], axis=0)


def first_products_kernel(held, power, own, other, keep, send, shifted):
    lag_rows(own, other, own_group(3), shifted)
    ours, theirs = [
        jnp.sum(jnp.square(refs[...].astype(jnp.float32)), axis=1, keepdims=True) for refs in (own, other)
    ]
    refs = jnp.where(
        lax.axis_index("chan") == 0,
        jnp.concatenate([ours, theirs], axis=0),
        jnp.concatenate([theirs, ours], axis=0),
    )
    bound = rounded_up(power[...])
    pad = jnp.zeros((1, LANES - REF), jnp.float32)
    chunk = keep.shape[0]
    refs_row = jnp.concatenate([as_row(refs), pad], axis=1)
    send[chunk:] = packed(power[...], refs_row, bound, last_samples(own, other))
    for here in columns(held.shape[1]):
        product = product_of(shifted, held, here)
        keep[:, here] = product[:chunk]
        send[:chunk, here] = coded(product[chunk:], bound[:, here], refs)


def shifted_scratch(rows, groups=1):
    return [pltpu.VMEM((groups * GROUP * REF, rows), jnp.bfloat16)]


def first_products(held, power, own, other, chunk):
    rows, width = held.shape
    return call_on_blocks(
        first_products_kernel,
        [((chunk, width), jnp.float32), ((chunk + EXTRA, width), jnp.bfloat16)],
        held,
        power,
        own,
        other,
        name="first_products",
        micros=PRODUCT_MICROS,
        scratch=shifted_scratch(rows),
    )


def later_products(groups, held, own, other, powers, chunk, spare=0, after=()):
    rows, width = held.shape

    def kernel(held, own, other, powers, *rest):
        outs, shifted = rest[:-1], rest[-1]
        _, ref_powers, bound = sent_powers(powers)
        refs = ref_column(ref_powers)
        for index, bits in enumerate(groups):
            lag_rows(own, other, own_group(bits), shifted.at[pl.ds(index * 2 * chunk, 2 * chunk)])
            if spare:
                outs[2 * index + 1][chunk:] = jnp.zeros((spare, width), jnp.bfloat16)
        for here in columns(width):
            product = product_of(shifted, held, here)
            for index in range(len(groups)):
                keep, send = outs[2 * index : 2 * index + 2]
                first = 2 * index * chunk
                keep[:, here] = product[first : first + chunk]
                send[:chunk, here] = coded(product[first + chunk : first + 2 * chunk], bound[:, here], refs)

    return call_on_blocks(
        kernel,
        [((chunk, width), jnp.float32), ((chunk + spare, width), jnp.bfloat16)] * len(groups),
        held,
        own,
        other,
        powers,
        name="later_products",
        micros=PRODUCT_MICROS,
        after=after,
        scratch=shifted_scratch(rows, len(groups)),
    )


def edges_scratch(count, chunk):
    return [pltpu.VMEM((count, chunk, 2 * LANES), jnp.bfloat16)]


def call_on_blocks(kernel, outs, *arrays, name, micros, after=(), scratch=(), space=pltpu.VMEM):
    vmem = pl.BlockSpec(memory_space=pltpu.VMEM)
    count = len(arrays)

    def body(*refs):
        kernel(*refs[:count], *refs[count + len(after) :])

    return pl.pallas_call(
        body,
        in_specs=[vmem] * count + [pl.BlockSpec(memory_space=pl.ANY)] * len(after),
        out_specs=[vmem] * len(outs),
        out_shape=[space(shape, dtype) for shape, dtype in outs],
        scratch_shapes=list(scratch),
        compiler_params=pltpu.CompilerParams(vmem_limit_bytes=VMEM_BYTES),
        cost_estimate=lasting(micros),
        name=name,
    )(*arrays, *after)


def with_tails(head, after_next, send):
    rows, width = send.shape
    chunk = rows - EXTRA

    def kernel(head, after_next, send, out):
        near = lax.axis_index("tm") & 1
        out[:chunk] = send[:chunk]
        out[chunk : chunk + LAGS] = jnp.where(near == 0, after_next[...], head[...])
        out[chunk + LAGS :] = send[chunk:]

    outs = [((rows + LAGS, width), jnp.bfloat16)]
    return call_on_blocks(kernel, outs, head, after_next, send, name="with_tails", micros=MERGE_MICROS)[0]


def with_boundaries(keeps, groups, own, other, sent, arrived, after):
    chunk, width = keeps[0].shape

    def kernel(own, other, sent, arrived, *rest):
        keeps, outs, edges = rest[: len(groups)], rest[len(groups) : -1], rest[-1]
        for index, bits in enumerate(groups):
            boundary_rows(own_group(bits), (own, other), ends_of(arrived), edges.at[index])
        for here in columns(width):
            tails = tails_of(sent, arrived, here)
            for index in range(len(groups)):
                added = jnp.dot(edges[index], tails, preferred_element_type=jnp.float32)
                outs[index][:, here] = keeps[index][:, here] + added

    return call_on_blocks(
        kernel,
        [((chunk, width), jnp.float32)] * len(groups),
        own,
        other,
        sent,
        arrived,
        *keeps,
        name="with_boundaries",
        micros=MERGE_MICROS,
        after=after,
        scratch=edges_scratch(len(groups), chunk),
    )


def merged_near(keep, group, own, other, ours, theirs, held_back):
    chunk, width = keep.shape

    def kernel(keep, own, other, ours, theirs, held_back, out, passed, edges):
        passed[...] = held_back[...]
        boundary_rows(own_group(group), (own, other), ends_of(theirs), edges.at[0])
        powers, refs, bound = sent_powers(ours)
        their_powers, their_refs, their_bound = sent_powers(theirs)
        their_refs_column, sum_refs = ref_column(their_refs), refs + their_refs
        sum_refs_column = ref_column(sum_refs)
        bounds = []
        for here in columns(width):
            tails = tails_of(ours, theirs, here)
            total = keep[:, here] + jnp.dot(edges[0], tails, preferred_element_type=jnp.float32)
            total += expanded(theirs[:chunk, here], their_bound[:, here], their_refs_column)
            beyond = jnp.sum(jnp.square(tails.astype(jnp.float32)), axis=0, keepdims=True)
            bounds.append(rounded_up(bound[:, here] + their_bound[:, here] + beyond))
            out[:chunk, here] = coded(total, bounds[-1], sum_refs_column)
        out[chunk:] = packed(powers + their_powers, sum_refs, jnp.concatenate(bounds, axis=1))

    return call_on_blocks(
        kernel,
        [((chunk + EXTRA, width), jnp.bfloat16), (held_back.shape, jnp.bfloat16)],
        keep,
        own,
        other,
        ours,
        theirs,
        held_back,
        name="merged_near",
        micros=MERGE_MICROS,
        scratch=edges_scratch(1, chunk),
    )


def direct_sums(direct, powers):
    _, refs, bound = sent_powers(powers)
    chunk = direct.shape[0] // REF * REF
    return expanded(direct[:chunk], bound, ref_column(refs))


def merged(keep, ours, theirs, direct, direct_powers, after):
    chunk, width = keep.shape

    def kernel(keep, ours, theirs, direct, direct_powers, out):
        powers, refs, bound = sent_powers(ours)
        their_powers, their_refs, their_bound = sent_powers(theirs)
        sum_refs, sum_bound = refs + their_refs, rounded_up(bound + their_bound)
        total = keep[...] + expanded(theirs[:chunk], their_bound, ref_column(their_refs))
        total += direct_sums(direct, direct_powers)
        out[chunk:] = packed(powers + their_powers, sum_refs, sum_bound)
        out[:chunk] = coded(total, sum_bound, ref_column(sum_refs))

    outs = [((chunk + EXTRA, width), jnp.bfloat16)]
    arrays = (keep, ours, theirs, direct, direct_powers)
    return call_on_blocks(kernel, outs, *arrays, name="merged", micros=MERGE_MICROS, after=after)[0]


def resent(keep, direct, direct_powers, ours, held_back, after):
    def kernel(keep, direct, direct_powers, ours, held_back, out, passed):
        passed[...] = held_back[...]
        _, refs, bound = sent_powers(ours)
        out[...] = coded(keep[...] + direct_sums(direct, direct_powers), bound, ref_column(refs))

    outs = [(keep.shape, jnp.bfloat16), (held_back.shape, jnp.bfloat16)]
    arrays = (keep, direct, direct_powers, ours, held_back)
    return call_on_blocks(kernel, outs, *arrays, name="resent", micros=MERGE_MICROS, after=after)


def added(keep, direct, direct_powers, after):
    def kernel(keep, direct, direct_powers, out):
        out[...] = keep[...] + direct_sums(direct, direct_powers)

    outs = [(keep.shape, jnp.float32)]
    arrays = (keep, direct, direct_powers)
    return call_on_blocks(kernel, outs, *arrays, name="added", micros=MERGE_MICROS, after=after)[0]


def finished(slab_rows, segment, partial, near, near_powers, ours, theirs, autos):
    chunk, width = partial.shape

    def kernel(partial, near, near_powers, ours, theirs, *refs):
        autos, (covariance, segment_auto) = refs[:-2], refs[-2:]
        first_lag = lax.axis_index("tm").astype(jnp.int32) * (chunk // REF)
        lag = lax.broadcasted_iota(jnp.int32, (chunk, 1), 0) // REF + first_lag
        denom = (slab_rows - lag).astype(jnp.float32)
        powers, own_refs, _ = sent_powers(ours)
        their_powers, their_refs, their_bound = sent_powers(theirs)
        total = partial[...] + direct_sums(near, near_powers)
        total += expanded(theirs[:chunk], their_bound, ref_column(their_refs))
        scale = 1.0 / jnp.sqrt((powers + their_powers) / slab_rows + 1e-06)
        ref_scale = 1.0 / jnp.sqrt(ref_column(own_refs + their_refs) / slab_rows + 1e-06)
        covariance[...] = total * scale * (for_chunk(ref_scale, chunk) / denom)
        first = 0
        for auto in autos:
            here = slice(first, first + auto.shape[1])
            segment_auto[:, here] = auto[...] * (scale[:, here] * scale[:, here]) / segment
            first = here.stop

    outs = [(partial.shape, jnp.float32), ((LAGS, width), jnp.float32)]
    return call_on_blocks(
        kernel,
        outs,
        partial,
        near,
        near_powers,
        ours,
        theirs,
        *autos,
        name="finished",
        micros=MERGE_MICROS,
        space=jax.ShapeDtypeStruct,
    )


def segment_kernel(first, held, power, tail, out, wide):
    rows = held.shape[0]
    step = rows // 8
    pitch = step + LAGS
    for index in range(out.shape[1] // LANES):
        here = slice(first + index * LANES, first + (index + 1) * LANES)
        there = slice(index * LANES, (index + 1) * LANES)
        for part in range(8):
            end = (part + 1) * step
            wide[part * pitch : part * pitch + step, :] = held[end - step : end, here].astype(jnp.float32)
            if part < 7:
                following = held[end : end + LAGS, here].astype(jnp.float32)
            else:
                following = tail_of(tail, here).astype(jnp.float32)
            wide[part * pitch + step : (part + 1) * pitch, :] = following
        taken = lambda first: wide[pl.ds(first, 8, stride=pitch), :]

        def advance(index, carry):
            window, sums = carry
            window = window + (taken(index + LAGS - 1),)
            sums = tuple(total + window[0] * window[lag + 1] for lag, total in enumerate(sums))
            return window[1:], sums

        window = tuple(taken(first) for first in range(LAGS - 1))
        zero = jnp.zeros((8, LANES), jnp.float32)
        _, sums = lax.fori_loop(0, step, advance, (window, (zero,) * (LAGS - 1)), unroll=16)
        out[:, there] = jnp.concatenate(
            [power[:, here]] + [jnp.sum(total, axis=0, keepdims=True) for total in sums], axis=0
        )


def segment_rows(held, power, tail, first, size, held_back=(), after=()):
    rows = held.shape[0]

    def kernel(held, power, tail, *refs):
        codes, out, passed, wide = refs[: len(held_back)], refs[len(held_back)], refs[len(held_back) + 1 : -1], refs[-1]
        for code, to in zip(codes, passed):
            to[...] = code[...]
        segment_kernel(first, held, power, tail, out, wide)

    return call_on_blocks(
        kernel,
        [((LAGS, size), jnp.float32)] + [(code.shape, code.dtype) for code in held_back],
        held,
        power,
        tail,
        *held_back,
        name="segment_rows",
        micros=SEGMENT_MICROS,
        after=after,
        scratch=[pltpu.VMEM((rows + 8 * LAGS, LANES), jnp.float32)],
    )


def all_products_kernel(held, own, other, tail, out, shifted):
    chan = lax.axis_index("chan")
    zeros = jnp.zeros((HALF, LANES), jnp.float32)
    for refs, half in ((own, chan), (other, 1 - chan)):
        long = jnp.concatenate([refs[...].astype(jnp.float32), zeros], axis=1)
        for index in range(GROUP):
            start = pl.multiple_of(index * REF + half * HALF, HALF)
            lag = pl.program_id(0) * GROUP + index
            shifted[pl.ds(start, HALF), :] = pltpu.roll(long, lag, 1).astype(jnp.bfloat16)
    rows, width = held.shape
    edge = jnp.concatenate([tail[...], jnp.zeros((LANES - LAGS, width), tail.dtype)], axis=0)
    for here in columns(width):
        total = jnp.dot(shifted[:, rows:], edge[:, here], preferred_element_type=jnp.float32)
        out[:, here] = total + jnp.dot(shifted[:, :rows], held[:, here], preferred_element_type=jnp.float32)


def all_products(held, own, other, tail):
    rows, width = held.shape
    vmem = pl.BlockSpec(memory_space=pltpu.VMEM)
    return pl.pallas_call(
        all_products_kernel,
        grid=(LAGS // GROUP,),
        in_specs=[vmem] * 4,
        out_specs=pl.BlockSpec((GROUP * REF, width), lambda group: (group, 0)),
        out_shape=jax.ShapeDtypeStruct((LAGS * REF, width), jnp.float32),
        scratch_shapes=[pltpu.VMEM((GROUP * REF, rows + LANES), jnp.bfloat16)],
        compiler_params=pltpu.CompilerParams(vmem_limit_bytes=VMEM_BYTES),
        name="all_products",
    )(held, own, other, tail)


def from_pair_ahead(value):
    count = lax.axis_size("tm")
    return lax.ppermute(value, "tm", [(time + 2, time) for time in range(0, count - 2, 2)])


def local(strain):
    rows, width = strain.shape
    count = lax.axis_size("tm")
    slab_rows = rows * count
    chunk = LAGS * REF // count

    own, head = prepared(strain)
    other = exchanged(own, "chan", 1)
    held, power = loaded(strain, own)
    if chunk * 2 == GROUP * REF:
        keep6, send7 = first_products(held, power, own, other, chunk)
        after_next = from_pair_ahead(head)
        send7 = with_tails(head, after_next, send7)
        got7 = exchanged(send7, "tm", 1)
        keep4, send5 = later_products((2,), held, own, other, send7, chunk, spare=LAGS)
        got5 = exchanged(send5, "tm", 1)
        keep2, send3, keep0, send1 = later_products(
            (1, 0), held, own, other, send7, chunk, after=(send5,)
        )
        send6, send3 = merged_near(keep6, 3, own, other, send7, got7, send3)
        got6 = exchanged(send6, "tm", 2)
        got3 = exchanged(send3, "tm", 1)
        keep4, keep2, keep0 = with_boundaries(
            (keep4, keep2, keep0), (2, 1, 0), own, other, send7, got7, after=(send6,)
        )
        size = width // 4
        (auto,) = segment_rows(held, power, got7, 0, size, after=(keep4,))
        send4 = merged(keep4, send6, got6, got5, got7, after=(auto,))
        got4 = exchanged(send4, "tm", 4)
        send2, send1 = resent(keep2, got3, got7, send6, send1, after=(send4,))
        got2 = exchanged(send2, "tm", 2)
        got1 = exchanged(send1, "tm", 1)
        autos = [auto, *segment_rows(held, power, got7, size, width - size, after=(send2,))]
        partial = added(keep0, got2, got6, after=(autos[1],))
        return tuple(finished(slab_rows, rows, partial, got1, got7, send4, got4, autos))

    tail = passed_along(head, "tm", -1)
    chan = lax.axis_index("chan").astype(jnp.int32)
    time = lax.axis_index("tm").astype(jnp.int32)
    (auto,) = segment_rows(held, power, tail, 0, width)
    power_other = jnp.sum(jnp.square(other.astype(jnp.float32)), axis=1)
    power = lax.psum(jnp.concatenate([power[0], power_other]), "tm")
    inv = 1.0 / jnp.sqrt(power / slab_rows + 1e-06)
    scale = inv[:width]
    ref_scale = jnp.where(
        chan == 0,
        jnp.concatenate([inv[:HALF], inv[width:]]),
        jnp.concatenate([inv[width:], inv[:HALF]]),
    )
    products = all_products(held, own, other, tail)
    summed = lax.psum_scatter(products, "tm", scatter_dimension=0, tiled=True)
    row = time * chunk + jnp.arange(chunk, dtype=jnp.int32)
    row_scale = ref_scale[row % REF] / (slab_rows - row // REF).astype(jnp.float32)
    covariance = summed * scale[None, :] * row_scale[:, None]
    segment_auto = auto * (scale * scale)[None, :] / rows
    return (covariance, segment_auto)


def solution(mesh):
    in_specs = (P(("groups", "tm"), "chan"),)
    out_specs = (P(("groups", "tm"), "chan"), P(("groups", "tm"), "chan"))
    return jax.shard_map(local, mesh=mesh, in_specs=in_specs, out_specs=out_specs, check_vma=False)
```

```python
import jax
import jax.numpy as jnp
from jax import lax
from jax.experimental import pallas as pl
from jax.experimental.pallas import tpu as pltpu
from jax.sharding import PartitionSpec as P

LAGS = 16
REF = 64
HALF = REF // 2
LANES = 128
EXTRA = 8
FETCHES = 8
STEP = 256
GROUP = 4
POWER = 16
CODE_SCALE = 2.0 ** (126 / POWER)
TINY = 1e-35
PIECES = 4
VMEM_BYTES = 32 * 1024 * 1024
HBM_RATE = 3.69e6
PRODUCT_MICROS = 1.0
SEGMENT_MICROS = 1.2
MERGE_MICROS = 0.3


def lasting(micros):
    return pl.CostEstimate(flops=0, bytes_accessed=int(micros * HBM_RATE), transcendentals=0)


def passed_along(value, axis, steps):
    count = lax.axis_size(axis)
    initial, last = (max(0, -steps), min(count, count - steps))
    return lax.ppermute(value, axis, [(source, source + steps) for source in range(initial, last)])


def exchanged(value, axis, bit):
    count = lax.axis_size(axis)
    return lax.ppermute(value, axis, [(source, source ^ bit) for source in range(count)])


def as_column(row):
    size = row.shape[1]
    eye = lax.broadcasted_iota(jnp.int32, (size, size), 0) == lax.broadcasted_iota(jnp.int32, (size, size), 1)
    return jnp.sum(jnp.where(eye, row, 0.0), axis=1, keepdims=True)


def as_row(column):
    size = column.shape[0]
    eye = lax.broadcasted_iota(jnp.int32, (size, size), 0) == lax.broadcasted_iota(jnp.int32, (size, size), 1)
    return jnp.sum(jnp.where(eye, column, 0.0), axis=0, keepdims=True)


def for_chunk(ref_column, rows):
    return jnp.concatenate([ref_column] * (rows // REF), axis=0)


def bf16_pieces(value):
    high = value.astype(jnp.bfloat16).astype(jnp.float32)
    middle = (value - high).astype(jnp.bfloat16).astype(jnp.float32)
    return high, middle, value - high - middle


def packed(powers, ref_powers, channel_bound, *more):
    rows = list(bf16_pieces(powers))
    refs = jnp.concatenate(bf16_pieces(ref_powers), axis=1)
    pad = jnp.zeros((1, powers.shape[1] - refs.shape[1]), jnp.float32)
    rows += [jnp.concatenate([refs, pad], axis=1), channel_bound] + list(more)
    rows += [jnp.zeros_like(powers)] * (EXTRA - len(rows))
    return jnp.concatenate(rows, axis=0).astype(jnp.bfloat16)


def unpacked(block):
    wide = block.astype(jnp.float32)
    powers = wide[0:1] + wide[1:2] + wide[2:3]
    refs = wide[3:4, :LANES] + wide[3:4, LANES : 2 * LANES] + wide[3:4, 2 * LANES : 3 * LANES]
    return powers, refs, wide[4:5]


def sent_powers(code):
    return unpacked(code[-EXTRA:])


def rounded_up(value):
    return (value * (1.0 + 2.0**-7)).astype(jnp.bfloat16).astype(jnp.float32)


def coded(values, channel_bound, ref_bound):
    channel = lax.rsqrt(jnp.maximum(channel_bound, TINY))
    refs = lax.rsqrt(jnp.maximum(ref_bound, TINY)) * CODE_SCALE
    power = values * channel * for_chunk(refs, values.shape[0])
    for _ in range(4):
        power = power * jnp.abs(power)
    return power.astype(jnp.bfloat16)


def expanded(code, channel_bound, ref_bound):
    channel = jnp.sqrt(jnp.maximum(channel_bound, TINY))
    refs = jnp.sqrt(jnp.maximum(ref_bound, TINY)) * (1.0 / CODE_SCALE)
    wide = code[...].astype(jnp.float32)
    root = jnp.exp2(jnp.log2(jnp.abs(wide)) * (1.0 / POWER))
    return jnp.where(wide < 0.0, -root, root) * channel * for_chunk(refs, code.shape[0])


def ref_column(ref_powers):
    return as_column(ref_powers)[:REF]


def prepare_kernel(strain, own, head, left, sems):
    rows = left.shape[0]
    step = rows // PIECES
    copies = [
        pltpu.make_async_copy(
            strain.at[pl.ds(index * step, step), pl.ds(0, LANES)], left.at[pl.ds(index * step, step)], sems.at[index]
        )
        for index in range(PIECES)
    ]
    copies.append(pltpu.make_async_copy(strain.at[pl.ds(0, LAGS)], head, sems.at[PIECES]))
    for copy in copies:
        copy.start()
    for index in range(PIECES):
        copies[index].wait()
        here = slice(index * step, (index + 1) * step)
        own[:, here] = left[here, :].astype(jnp.float32).T[:HALF].astype(jnp.bfloat16)
    copies[PIECES].wait()


def prepared(strain):
    rows, width = strain.shape
    vmem = pl.BlockSpec(memory_space=pltpu.VMEM)
    return pl.pallas_call(
        prepare_kernel,
        in_specs=[pl.BlockSpec(memory_space=pl.ANY)],
        out_specs=[vmem, vmem],
        out_shape=[pltpu.VMEM((HALF, rows), strain.dtype), pltpu.VMEM((LAGS, width), strain.dtype)],
        scratch_shapes=[pltpu.VMEM((rows, LANES), strain.dtype), pltpu.SemaphoreType.DMA((PIECES + 1,))],
        compiler_params=pltpu.CompilerParams(vmem_limit_bytes=VMEM_BYTES),
        cost_estimate=lasting(PRODUCT_MICROS),
        name="prepared",
    )(pltpu.with_memory_space_constraint(strain, pltpu.HBM))


def lag_rows(own, other, group, shifted):
    chan, near = lax.axis_index("chan"), lax.axis_index("tm") & 1
    rows = own.shape[1]
    zeros = jnp.zeros((HALF, LANES), jnp.float32)
    for refs, half in ((own, chan), (other, 1 - chan)):
        long = jnp.concatenate([zeros, refs[...].astype(jnp.float32)], axis=1)
        for index in range(GROUP):
            ahead = near if index < GROUP // 2 else 1 - near
            lag = group * GROUP + ahead * (GROUP // 2) + index % (GROUP // 2)
            start = pl.multiple_of(index * REF + half * HALF, HALF)
            moved = pltpu.roll(long, lag, 1)[:, LANES : LANES + rows]
            shifted[pl.ds(start, HALF), :] = moved.astype(jnp.bfloat16)


def own_group(bits):
    return lax.shift_right_logical(lax.axis_index("tm").astype(jnp.int32), 1) ^ bits


def loaded_kernel(strain, held, power, sems):
    step = held.shape[0] // FETCHES
    pieces = [slice(index * step, (index + 1) * step) for index in range(FETCHES)]
    copies = [
        pltpu.make_async_copy(strain.at[pl.ds(here.start, step)], held.at[pl.ds(here.start, step)], sems.at[index])
        for index, here in enumerate(pieces)
    ]
    for copy in copies:
        copy.start()
    total = jnp.zeros((8, held.shape[1]), jnp.float32)
    for copy, here in zip(copies, pieces):
        copy.wait()
        squares = jnp.square(held[here, :].astype(jnp.float32))
        total += jnp.sum(squares.reshape(step // 8, 8, held.shape[1]), axis=0)
    power[...] = jnp.sum(total, axis=0, keepdims=True)


def loaded(strain, after):
    rows, width = strain.shape
    vmem = pl.BlockSpec(memory_space=pltpu.VMEM)

    def kernel(strain, after, held, power, sems):
        loaded_kernel(strain, held, power, sems)

    return pl.pallas_call(
        kernel,
        in_specs=[pl.BlockSpec(memory_space=pl.ANY)] * 2,
        out_specs=[vmem, vmem],
        out_shape=[pltpu.VMEM((rows, width), strain.dtype), pltpu.VMEM((1, width), jnp.float32)],
        scratch_shapes=[pltpu.SemaphoreType.DMA((FETCHES,))],
        compiler_params=pltpu.CompilerParams(vmem_limit_bytes=VMEM_BYTES),
        cost_estimate=lasting(PRODUCT_MICROS),
        name="loaded",
    )(pltpu.with_memory_space_constraint(strain, pltpu.HBM), after)


def columns(width):
    return [slice(first, first + STEP) for first in range(0, width, STEP)]


def product_of(shifted, held, here):
    return jnp.dot(shifted[...], held[:, here], preferred_element_type=jnp.float32)


def boundary_rows(group, ends, their_ends, edges):
    chan, near = lax.axis_index("chan"), lax.axis_index("tm") & 1
    zeros = jnp.zeros((HALF, LANES), jnp.float32)
    ours = [(refs[:, refs.shape[1] - LANES :].astype(jnp.float32), half) for refs, half in zip(ends, (chan, 1 - chan))]
    theirs = [(their_ends[half * HALF : (half + 1) * HALF], half) for half in range(2)]
    for side, parts in enumerate((ours, theirs)):
        for end, half in parts:
            long = jnp.concatenate([end, zeros], axis=1)
            for index in range(GROUP // 2):
                lag = group * GROUP + near * (GROUP // 2) + index
                start = pl.multiple_of(index * REF + half * HALF, HALF)
                moved = pltpu.roll(long, lag, 1)[:, LANES:]
                edges[pl.ds(start, HALF), side * LANES : (side + 1) * LANES] = moved.astype(jnp.bfloat16)


def last_samples(own, other):
    chan = lax.axis_index("chan")
    ours, theirs = [refs[:, refs.shape[1] - LANES :].astype(jnp.float32) for refs in (own, other)]
    first, second = jnp.where(chan == 0, ours, theirs), jnp.where(chan == 0, theirs, ours)
    square = jnp.concatenate([first, second, jnp.zeros((LANES - REF, LANES), jnp.float32)], axis=0)
    rows = square.T[LANES - LAGS :, :REF]
    return jnp.concatenate([rows[index : index + 1] for index in range(LAGS)], axis=1)


def ends_of(code):
    row = code[-EXTRA:].astype(jnp.float32)[5:6]
    rows = jnp.concatenate([row[:, index * REF : (index + 1) * REF] for index in range(LAGS)], axis=0)
    rows = jnp.concatenate([rows, jnp.zeros((LAGS, LANES - REF), jnp.float32)], axis=1)
    return jnp.concatenate([jnp.zeros((LANES - LAGS, LANES), jnp.float32), rows], axis=0).T[:REF]


def tail_of(code, here):
    first = code.shape[0] // REF * REF
    return code[first : first + LAGS, here]


def tails_of(sent, arrived, here):
    zeros = jnp.zeros((LANES - LAGS, here.stop - here.start), jnp.bfloat16)
    return jnp.concatenate([tail_of(arrived, here), zeros, tail_of(sent, here), zeros], axis=0)


def first_products_kernel(held, power, own, other, keep, send, shifted):
    lag_rows(own, other, own_group(3), shifted)
    ours, theirs = [
        jnp.sum(jnp.square(refs[...].astype(jnp.float32)), axis=1, keepdims=True) for refs in (own, other)
    ]
    refs = jnp.where(
        lax.axis_index("chan") == 0,
        jnp.concatenate([ours, theirs], axis=0),
        jnp.concatenate([theirs, ours], axis=0),
    )
    bound = rounded_up(power[...])
    pad = jnp.zeros((1, LANES - REF), jnp.float32)
    chunk = keep.shape[0]
    refs_row = jnp.concatenate([as_row(refs), pad], axis=1)
    send[chunk:] = packed(power[...], refs_row, bound, last_samples(own, other))
    for here in columns(held.shape[1]):
        product = product_of(shifted, held, here)
        keep[:, here] = product[:chunk]
        send[:chunk, here] = coded(product[chunk:], bound[:, here], refs)


def shifted_scratch(rows, groups=1):
    return [pltpu.VMEM((groups * GROUP * REF, rows), jnp.bfloat16)]


def first_products(held, power, own, other, chunk):
    rows, width = held.shape
    return call_on_blocks(
        first_products_kernel,
        [((chunk, width), jnp.float32), ((chunk + EXTRA, width), jnp.bfloat16)],
        held,
        power,
        own,
        other,
        name="first_products",
        micros=PRODUCT_MICROS,
        scratch=shifted_scratch(rows),
    )


def later_products(groups, held, own, other, powers, chunk, spare=0, after=()):
    rows, width = held.shape

    def kernel(held, own, other, powers, *rest):
        outs, shifted = rest[:-1], rest[-1]
        _, ref_powers, bound = sent_powers(powers)
        refs = ref_column(ref_powers)
        for index, bits in enumerate(groups):
            lag_rows(own, other, own_group(bits), shifted.at[pl.ds(index * 2 * chunk, 2 * chunk)])
            if spare and index == 0:
                outs[1][chunk:] = jnp.zeros((spare, width), jnp.bfloat16)
        for here in columns(width):
            product = product_of(shifted, held, here)
            for index in range(len(groups)):
                keep, send = outs[2 * index : 2 * index + 2]
                first = 2 * index * chunk
                keep[:, here] = product[first : first + chunk]
                send[:chunk, here] = coded(product[first + chunk : first + 2 * chunk], bound[:, here], refs)

    return call_on_blocks(
        kernel,
        [
            (shape, dtype)
            for index in range(len(groups))
            for shape, dtype in (
                ((chunk, width), jnp.float32),
                ((chunk + (0 if index else spare), width), jnp.bfloat16),
            )
        ],
        held,
        own,
        other,
        powers,
        name="later_products",
        micros=PRODUCT_MICROS,
        after=after,
        scratch=shifted_scratch(rows, len(groups)),
    )


def edges_scratch(count, chunk):
    return [pltpu.VMEM((count, chunk, 2 * LANES), jnp.bfloat16)]


def call_on_blocks(kernel, outs, *arrays, name, micros, after=(), scratch=(), space=pltpu.VMEM):
    vmem = pl.BlockSpec(memory_space=pltpu.VMEM)
    count = len(arrays)

    def body(*refs):
        kernel(*refs[:count], *refs[count + len(after) :])

    return pl.pallas_call(
        body,
        in_specs=[vmem] * count + [pl.BlockSpec(memory_space=pl.ANY)] * len(after),
        out_specs=[vmem] * len(outs),
        out_shape=[space(shape, dtype) for shape, dtype in outs],
        scratch_shapes=list(scratch),
        compiler_params=pltpu.CompilerParams(vmem_limit_bytes=VMEM_BYTES),
        cost_estimate=lasting(micros),
        name=name,
    )(*arrays, *after)


def with_tails(head, after_next, send):
    rows, width = send.shape
    chunk = rows - EXTRA

    def kernel(head, after_next, send, out):
        near = lax.axis_index("tm") & 1
        out[:chunk] = send[:chunk]
        out[chunk : chunk + LAGS] = jnp.where(near == 0, after_next[...], head[...])
        out[chunk + LAGS :] = send[chunk:]

    outs = [((rows + LAGS, width), jnp.bfloat16)]
    return call_on_blocks(kernel, outs, head, after_next, send, name="with_tails", micros=MERGE_MICROS)[0]


def with_boundaries(keeps, groups, own, other, sent, arrived, after):
    chunk, width = keeps[0].shape

    def kernel(own, other, sent, arrived, *rest):
        keeps, outs, edges = rest[: len(groups)], rest[len(groups) : -1], rest[-1]
        for index, bits in enumerate(groups):
            boundary_rows(own_group(bits), (own, other), ends_of(arrived), edges.at[index])
        for here in columns(width):
            tails = tails_of(sent, arrived, here)
            for index in range(len(groups)):
                added = jnp.dot(edges[index], tails, preferred_element_type=jnp.float32)
                outs[index][:, here] = keeps[index][:, here] + added

    return call_on_blocks(
        kernel,
        [((chunk, width), jnp.float32)] * len(groups),
        own,
        other,
        sent,
        arrived,
        *keeps,
        name="with_boundaries",
        micros=MERGE_MICROS,
        after=after,
        scratch=edges_scratch(len(groups), chunk),
    )


def merged_near(keep, group, own, other, ours, theirs, held_back):
    chunk, width = keep.shape

    def kernel(keep, own, other, ours, theirs, held_back, out, passed, edges):
        passed[...] = held_back[...]
        boundary_rows(own_group(group), (own, other), ends_of(theirs), edges.at[0])
        powers, refs, bound = sent_powers(ours)
        their_powers, their_refs, their_bound = sent_powers(theirs)
        their_refs_column, sum_refs = ref_column(their_refs), refs + their_refs
        sum_refs_column = ref_column(sum_refs)
        bounds = []
        for here in columns(width):
            tails = tails_of(ours, theirs, here)
            total = keep[:, here] + jnp.dot(edges[0], tails, preferred_element_type=jnp.float32)
            total += expanded(theirs[:chunk, here], their_bound[:, here], their_refs_column)
            beyond = jnp.sum(jnp.square(tails.astype(jnp.float32)), axis=0, keepdims=True)
            bounds.append(rounded_up(bound[:, here] + their_bound[:, here] + beyond))
            out[:chunk, here] = coded(total, bounds[-1], sum_refs_column)
        out[chunk:] = packed(powers + their_powers, sum_refs, jnp.concatenate(bounds, axis=1))

    return call_on_blocks(
        kernel,
        [((chunk + EXTRA, width), jnp.bfloat16), (held_back.shape, jnp.bfloat16)],
        keep,
        own,
        other,
        ours,
        theirs,
        held_back,
        name="merged_near",
        micros=MERGE_MICROS,
        scratch=edges_scratch(1, chunk),
    )


def direct_sums(direct, powers):
    _, refs, bound = sent_powers(powers)
    chunk = direct.shape[0] // REF * REF
    return expanded(direct[:chunk], bound, ref_column(refs))


def merged(keep, ours, theirs, direct, direct_powers, after):
    chunk, width = keep.shape

    def kernel(keep, ours, theirs, direct, direct_powers, out):
        powers, refs, bound = sent_powers(ours)
        their_powers, their_refs, their_bound = sent_powers(theirs)
        sum_refs, sum_bound = refs + their_refs, rounded_up(bound + their_bound)
        total = keep[...] + expanded(theirs[:chunk], their_bound, ref_column(their_refs))
        total += direct_sums(direct, direct_powers)
        out[chunk:] = packed(powers + their_powers, sum_refs, sum_bound)
        out[:chunk] = coded(total, sum_bound, ref_column(sum_refs))

    outs = [((chunk + EXTRA, width), jnp.bfloat16)]
    arrays = (keep, ours, theirs, direct, direct_powers)
    return call_on_blocks(kernel, outs, *arrays, name="merged", micros=MERGE_MICROS, after=after)[0]


def resent(keep, direct, direct_powers, ours, held_back, after):
    def kernel(keep, direct, direct_powers, ours, held_back, out, passed):
        passed[...] = held_back[...]
        _, refs, bound = sent_powers(ours)
        out[...] = coded(keep[...] + direct_sums(direct, direct_powers), bound, ref_column(refs))

    outs = [(keep.shape, jnp.bfloat16), (held_back.shape, jnp.bfloat16)]
    arrays = (keep, direct, direct_powers, ours, held_back)
    return call_on_blocks(kernel, outs, *arrays, name="resent", micros=MERGE_MICROS, after=after)


def added(keep, direct, direct_powers, after):
    def kernel(keep, direct, direct_powers, out):
        out[...] = keep[...] + direct_sums(direct, direct_powers)

    outs = [(keep.shape, jnp.float32)]
    arrays = (keep, direct, direct_powers)
    return call_on_blocks(kernel, outs, *arrays, name="added", micros=MERGE_MICROS, after=after)[0]


def finished(slab_rows, segment, partial, near, near_powers, ours, theirs, autos):
    chunk, width = partial.shape

    def kernel(partial, near, near_powers, ours, theirs, *refs):
        autos, (covariance, segment_auto) = refs[:-2], refs[-2:]
        first_lag = lax.axis_index("tm").astype(jnp.int32) * (chunk // REF)
        lag = lax.broadcasted_iota(jnp.int32, (chunk, 1), 0) // REF + first_lag
        denom = (slab_rows - lag).astype(jnp.float32)
        powers, own_refs, _ = sent_powers(ours)
        their_powers, their_refs, their_bound = sent_powers(theirs)
        total = partial[...] + direct_sums(near, near_powers)
        total += expanded(theirs[:chunk], their_bound, ref_column(their_refs))
        scale = 1.0 / jnp.sqrt((powers + their_powers) / slab_rows + 1e-06)
        ref_scale = 1.0 / jnp.sqrt(ref_column(own_refs + their_refs) / slab_rows + 1e-06)
        covariance[...] = total * scale * (for_chunk(ref_scale, chunk) / denom)
        first = 0
        for auto in autos:
            here = slice(first, first + auto.shape[1])
            segment_auto[:, here] = auto[...] * (scale[:, here] * scale[:, here]) / segment
            first = here.stop

    outs = [(partial.shape, jnp.float32), ((LAGS, width), jnp.float32)]
    return call_on_blocks(
        kernel,
        outs,
        partial,
        near,
        near_powers,
        ours,
        theirs,
        *autos,
        name="finished",
        micros=MERGE_MICROS,
        space=jax.ShapeDtypeStruct,
    )


def segment_kernel(first, held, power, tail, out, wide):
    rows = held.shape[0]
    step = rows // 8
    pitch = step + LAGS
    for index in range(out.shape[1] // LANES):
        here = slice(first + index * LANES, first + (index + 1) * LANES)
        there = slice(index * LANES, (index + 1) * LANES)
        for part in range(8):
            end = (part + 1) * step
            wide[part * pitch : part * pitch + step, :] = held[end - step : end, here].astype(jnp.float32)
            if part < 7:
                following = held[end : end + LAGS, here].astype(jnp.float32)
            else:
                following = tail_of(tail, here).astype(jnp.float32)
            wide[part * pitch + step : (part + 1) * pitch, :] = following
        taken = lambda first: wide[pl.ds(first, 8, stride=pitch), :]

        def advance(index, carry):
            window, sums = carry
            window = window + (taken(index + LAGS - 1),)
            sums = tuple(total + window[0] * window[lag + 1] for lag, total in enumerate(sums))
            return window[1:], sums

        window = tuple(taken(first) for first in range(LAGS - 1))
        zero = jnp.zeros((8, LANES), jnp.float32)
        _, sums = lax.fori_loop(0, step, advance, (window, (zero,) * (LAGS - 1)), unroll=16)
        out[:, there] = jnp.concatenate(
            [power[:, here]] + [jnp.sum(total, axis=0, keepdims=True) for total in sums], axis=0
        )


def segment_rows(held, power, tail, first, size, held_back=(), after=()):
    rows = held.shape[0]

    def kernel(held, power, tail, *refs):
        codes, out, passed, wide = refs[: len(held_back)], refs[len(held_back)], refs[len(held_back) + 1 : -1], refs[-1]
        for code, to in zip(codes, passed):
            to[...] = code[...]
        segment_kernel(first, held, power, tail, out, wide)

    return call_on_blocks(
        kernel,
        [((LAGS, size), jnp.float32)] + [(code.shape, code.dtype) for code in held_back],
        held,
        power,
        tail,
        *held_back,
        name="segment_rows",
        micros=SEGMENT_MICROS,
        after=after,
        scratch=[pltpu.VMEM((rows + 8 * LAGS, LANES), jnp.float32)],
    )


def all_products_kernel(held, own, other, tail, out, shifted):
    chan = lax.axis_index("chan")
    zeros = jnp.zeros((HALF, LANES), jnp.float32)
    for refs, half in ((own, chan), (other, 1 - chan)):
        long = jnp.concatenate([refs[...].astype(jnp.float32), zeros], axis=1)
        for index in range(GROUP):
            start = pl.multiple_of(index * REF + half * HALF, HALF)
            lag = pl.program_id(0) * GROUP + index
            shifted[pl.ds(start, HALF), :] = pltpu.roll(long, lag, 1).astype(jnp.bfloat16)
    rows, width = held.shape
    edge = jnp.concatenate([tail[...], jnp.zeros((LANES - LAGS, width), tail.dtype)], axis=0)
    for here in columns(width):
        total = jnp.dot(shifted[:, rows:], edge[:, here], preferred_element_type=jnp.float32)
        out[:, here] = total + jnp.dot(shifted[:, :rows], held[:, here], preferred_element_type=jnp.float32)


def all_products(held, own, other, tail):
    rows, width = held.shape
    vmem = pl.BlockSpec(memory_space=pltpu.VMEM)
    return pl.pallas_call(
        all_products_kernel,
        grid=(LAGS // GROUP,),
        in_specs=[vmem] * 4,
        out_specs=pl.BlockSpec((GROUP * REF, width), lambda group: (group, 0)),
        out_shape=jax.ShapeDtypeStruct((LAGS * REF, width), jnp.float32),
        scratch_shapes=[pltpu.VMEM((GROUP * REF, rows + LANES), jnp.bfloat16)],
        compiler_params=pltpu.CompilerParams(vmem_limit_bytes=VMEM_BYTES),
        name="all_products",
    )(held, own, other, tail)


def from_pair_ahead(value):
    count = lax.axis_size("tm")
    return lax.ppermute(value, "tm", [(time + 2, time) for time in range(0, count - 2, 2)])


def local(strain):
    rows, width = strain.shape
    count = lax.axis_size("tm")
    slab_rows = rows * count
    chunk = LAGS * REF // count

    own, head = prepared(strain)
    other = exchanged(own, "chan", 1)
    held, power = loaded(strain, own)
    if chunk * 2 == GROUP * REF:
        keep6, send7 = first_products(held, power, own, other, chunk)
        after_next = from_pair_ahead(head)
        send7 = with_tails(head, after_next, send7)
        got7 = exchanged(send7, "tm", 1)
        keep4, send5, keep2, send3, keep0, send1 = later_products(
            (2, 1, 0), held, own, other, send7, chunk, spare=LAGS
        )
        got5 = exchanged(send5, "tm", 1)
        send6, send3 = merged_near(keep6, 3, own, other, send7, got7, send3)
        got6 = exchanged(send6, "tm", 2)
        got3 = exchanged(send3, "tm", 1)
        keep4, keep2, keep0 = with_boundaries(
            (keep4, keep2, keep0), (2, 1, 0), own, other, send7, got7, after=(send6,)
        )
        size = width // 4
        (auto,) = segment_rows(held, power, got7, 0, size, after=(keep4,))
        send4 = merged(keep4, send6, got6, got5, got7, after=(auto,))
        got4 = exchanged(send4, "tm", 4)
        send2, send1 = resent(keep2, got3, got7, send6, send1, after=(send4,))
        got2 = exchanged(send2, "tm", 2)
        got1 = exchanged(send1, "tm", 1)
        autos = [auto, *segment_rows(held, power, got7, size, width - size, after=(send2,))]
        partial = added(keep0, got2, got6, after=(autos[1],))
        return tuple(finished(slab_rows, rows, partial, got1, got7, send4, got4, autos))

    tail = passed_along(head, "tm", -1)
    chan = lax.axis_index("chan").astype(jnp.int32)
    time = lax.axis_index("tm").astype(jnp.int32)
    (auto,) = segment_rows(held, power, tail, 0, width)
    power_other = jnp.sum(jnp.square(other.astype(jnp.float32)), axis=1)
    power = lax.psum(jnp.concatenate([power[0], power_other]), "tm")
    inv = 1.0 / jnp.sqrt(power / slab_rows + 1e-06)
    scale = inv[:width]
    ref_scale = jnp.where(
        chan == 0,
        jnp.concatenate([inv[:HALF], inv[width:]]),
        jnp.concatenate([inv[width:], inv[:HALF]]),
    )
    products = all_products(held, own, other, tail)
    summed = lax.psum_scatter(products, "tm", scatter_dimension=0, tiled=True)
    row = time * chunk + jnp.arange(chunk, dtype=jnp.int32)
    row_scale = ref_scale[row % REF] / (slab_rows - row // REF).astype(jnp.float32)
    covariance = summed * scale[None, :] * row_scale[:, None]
    segment_auto = auto * (scale * scale)[None, :] / rows
    return (covariance, segment_auto)


def solution(mesh):
    in_specs = (P(("groups", "tm"), "chan"),)
    out_specs = (P(("groups", "tm"), "chan"), P(("groups", "tm"), "chan"))
    return jax.shard_map(local, mesh=mesh, in_specs=in_specs, out_specs=out_specs, check_vma=False)
```

```python
import jax
import jax.numpy as jnp
from jax import lax
from jax.experimental import pallas as pl
from jax.experimental.pallas import tpu as pltpu
from jax.sharding import PartitionSpec as P

LAGS = 16
REF = 64
HALF = REF // 2
LANES = 128
EXTRA = 8
FETCHES = 8
STEP = 512
GROUP = 4
POWER = 16
CODE_SCALE = 2.0 ** (126 / POWER)
TINY = 1e-35
PIECES = 4
VMEM_BYTES = 32 * 1024 * 1024
HBM_RATE = 3.69e6
PRODUCT_MICROS = 1.0
SEGMENT_MICROS = 1.2
MERGE_MICROS = 0.3


def lasting(micros):
    return pl.CostEstimate(flops=0, bytes_accessed=int(micros * HBM_RATE), transcendentals=0)


def passed_along(value, axis, steps):
    count = lax.axis_size(axis)
    initial, last = (max(0, -steps), min(count, count - steps))
    return lax.ppermute(value, axis, [(source, source + steps) for source in range(initial, last)])


def exchanged(value, axis, bit):
    count = lax.axis_size(axis)
    return lax.ppermute(value, axis, [(source, source ^ bit) for source in range(count)])


def as_column(row):
    size = row.shape[1]
    eye = lax.broadcasted_iota(jnp.int32, (size, size), 0) == lax.broadcasted_iota(jnp.int32, (size, size), 1)
    return jnp.sum(jnp.where(eye, row, 0.0), axis=1, keepdims=True)


def as_row(column):
    size = column.shape[0]
    eye = lax.broadcasted_iota(jnp.int32, (size, size), 0) == lax.broadcasted_iota(jnp.int32, (size, size), 1)
    return jnp.sum(jnp.where(eye, column, 0.0), axis=0, keepdims=True)


def for_chunk(ref_column, rows):
    return jnp.concatenate([ref_column] * (rows // REF), axis=0)


def bf16_pieces(value):
    high = value.astype(jnp.bfloat16).astype(jnp.float32)
    middle = (value - high).astype(jnp.bfloat16).astype(jnp.float32)
    return high, middle, value - high - middle


def packed(powers, ref_powers, channel_bound, *more):
    rows = list(bf16_pieces(powers))
    refs = jnp.concatenate(bf16_pieces(ref_powers), axis=1)
    pad = jnp.zeros((1, powers.shape[1] - refs.shape[1]), jnp.float32)
    rows += [jnp.concatenate([refs, pad], axis=1), channel_bound] + list(more)
    rows += [jnp.zeros_like(powers)] * (EXTRA - len(rows))
    return jnp.concatenate(rows, axis=0).astype(jnp.bfloat16)


def unpacked(block):
    wide = block.astype(jnp.float32)
    powers = wide[0:1] + wide[1:2] + wide[2:3]
    refs = wide[3:4, :LANES] + wide[3:4, LANES : 2 * LANES] + wide[3:4, 2 * LANES : 3 * LANES]
    return powers, refs, wide[4:5]


def sent_powers(code):
    return unpacked(code[-EXTRA:])


def rounded_up(value):
    return (value * (1.0 + 2.0**-7)).astype(jnp.bfloat16).astype(jnp.float32)


def coded(values, channel_bound, ref_bound):
    channel = lax.rsqrt(jnp.maximum(channel_bound, TINY))
    refs = lax.rsqrt(jnp.maximum(ref_bound, TINY)) * CODE_SCALE
    power = values * channel * for_chunk(refs, values.shape[0])
    for _ in range(4):
        power = power * jnp.abs(power)
    return power.astype(jnp.bfloat16)


def expanded(code, channel_bound, ref_bound):
    channel = jnp.sqrt(jnp.maximum(channel_bound, TINY))
    refs = jnp.sqrt(jnp.maximum(ref_bound, TINY)) * (1.0 / CODE_SCALE)
    wide = code[...].astype(jnp.float32)
    root = jnp.exp2(jnp.log2(jnp.abs(wide)) * (1.0 / POWER))
    return jnp.where(wide < 0.0, -root, root) * channel * for_chunk(refs, code.shape[0])


def ref_column(ref_powers):
    return as_column(ref_powers)[:REF]


def prepare_kernel(strain, own, head, left, sems):
    rows = left.shape[0]
    step = rows // PIECES
    copies = [
        pltpu.make_async_copy(
            strain.at[pl.ds(index * step, step), pl.ds(0, LANES)], left.at[pl.ds(index * step, step)], sems.at[index]
        )
        for index in range(PIECES)
    ]
    copies.append(pltpu.make_async_copy(strain.at[pl.ds(0, LAGS)], head, sems.at[PIECES]))
    for copy in copies:
        copy.start()
    for index in range(PIECES):
        copies[index].wait()
        here = slice(index * step, (index + 1) * step)
        own[:, here] = left[here, :].astype(jnp.float32).T[:HALF].astype(jnp.bfloat16)
    copies[PIECES].wait()


def prepared(strain):
    rows, width = strain.shape
    vmem = pl.BlockSpec(memory_space=pltpu.VMEM)
    return pl.pallas_call(
        prepare_kernel,
        in_specs=[pl.BlockSpec(memory_space=pl.ANY)],
        out_specs=[vmem, vmem],
        out_shape=[pltpu.VMEM((HALF, rows), strain.dtype), pltpu.VMEM((LAGS, width), strain.dtype)],
        scratch_shapes=[pltpu.VMEM((rows, LANES), strain.dtype), pltpu.SemaphoreType.DMA((PIECES + 1,))],
        compiler_params=pltpu.CompilerParams(vmem_limit_bytes=VMEM_BYTES),
        cost_estimate=lasting(PRODUCT_MICROS),
        name="prepared",
    )(pltpu.with_memory_space_constraint(strain, pltpu.HBM))


def lag_rows(own, other, group, shifted):
    chan, near = lax.axis_index("chan"), lax.axis_index("tm") & 1
    rows = own.shape[1]
    zeros = jnp.zeros((HALF, LANES), jnp.float32)
    for refs, half in ((own, chan), (other, 1 - chan)):
        long = jnp.concatenate([zeros, refs[...].astype(jnp.float32)], axis=1)
        for index in range(GROUP):
            ahead = near if index < GROUP // 2 else 1 - near
            lag = group * GROUP + ahead * (GROUP // 2) + index % (GROUP // 2)
            start = pl.multiple_of(index * REF + half * HALF, HALF)
            moved = pltpu.roll(long, lag, 1)[:, LANES : LANES + rows]
            shifted[pl.ds(start, HALF), :] = moved.astype(jnp.bfloat16)


def own_group(bits):
    return lax.shift_right_logical(lax.axis_index("tm").astype(jnp.int32), 1) ^ bits


def loaded_kernel(strain, held, power, sems):
    step = held.shape[0] // FETCHES
    pieces = [slice(index * step, (index + 1) * step) for index in range(FETCHES)]
    copies = [
        pltpu.make_async_copy(strain.at[pl.ds(here.start, step)], held.at[pl.ds(here.start, step)], sems.at[index])
        for index, here in enumerate(pieces)
    ]
    for copy in copies:
        copy.start()
    total = jnp.zeros((8, held.shape[1]), jnp.float32)
    for copy, here in zip(copies, pieces):
        copy.wait()
        squares = jnp.square(held[here, :].astype(jnp.float32))
        total += jnp.sum(squares.reshape(step // 8, 8, held.shape[1]), axis=0)
    power[...] = jnp.sum(total, axis=0, keepdims=True)


def loaded(strain, after):
    rows, width = strain.shape
    vmem = pl.BlockSpec(memory_space=pltpu.VMEM)

    def kernel(strain, after, held, power, sems):
        loaded_kernel(strain, held, power, sems)

    return pl.pallas_call(
        kernel,
        in_specs=[pl.BlockSpec(memory_space=pl.ANY)] * 2,
        out_specs=[vmem, vmem],
        out_shape=[pltpu.VMEM((rows, width), strain.dtype), pltpu.VMEM((1, width), jnp.float32)],
        scratch_shapes=[pltpu.SemaphoreType.DMA((FETCHES,))],
        compiler_params=pltpu.CompilerParams(vmem_limit_bytes=VMEM_BYTES),
        cost_estimate=lasting(PRODUCT_MICROS),
        name="loaded",
    )(pltpu.with_memory_space_constraint(strain, pltpu.HBM), after)


def columns(width):
    return [slice(first, first + STEP) for first in range(0, width, STEP)]


def product_of(shifted, held, here):
    return jnp.dot(shifted[...], held[:, here], preferred_element_type=jnp.float32)


def boundary_rows(group, ends, their_ends, edges):
    chan, near = lax.axis_index("chan"), lax.axis_index("tm") & 1
    zeros = jnp.zeros((HALF, LANES), jnp.float32)
    ours = [(refs[:, refs.shape[1] - LANES :].astype(jnp.float32), half) for refs, half in zip(ends, (chan, 1 - chan))]
    theirs = [(their_ends[half * HALF : (half + 1) * HALF], half) for half in range(2)]
    for side, parts in enumerate((ours, theirs)):
        for end, half in parts:
            long = jnp.concatenate([end, zeros], axis=1)
            for index in range(GROUP // 2):
                lag = group * GROUP + near * (GROUP // 2) + index
                start = pl.multiple_of(index * REF + half * HALF, HALF)
                moved = pltpu.roll(long, lag, 1)[:, LANES:]
                edges[pl.ds(start, HALF), side * LANES : (side + 1) * LANES] = moved.astype(jnp.bfloat16)


def last_samples(own, other):
    chan = lax.axis_index("chan")
    ours, theirs = [refs[:, refs.shape[1] - LANES :].astype(jnp.float32) for refs in (own, other)]
    first, second = jnp.where(chan == 0, ours, theirs), jnp.where(chan == 0, theirs, ours)
    square = jnp.concatenate([first, second, jnp.zeros((LANES - REF, LANES), jnp.float32)], axis=0)
    rows = square.T[LANES - LAGS :, :REF]
    return jnp.concatenate([rows[index : index + 1] for index in range(LAGS)], axis=1)


def ends_of(code):
    row = code[-EXTRA:].astype(jnp.float32)[5:6]
    rows = jnp.concatenate([row[:, index * REF : (index + 1) * REF] for index in range(LAGS)], axis=0)
    rows = jnp.concatenate([rows, jnp.zeros((LAGS, LANES - REF), jnp.float32)], axis=1)
    return jnp.concatenate([jnp.zeros((LANES - LAGS, LANES), jnp.float32), rows], axis=0).T[:REF]


def tail_of(code, here):
    first = code.shape[0] // REF * REF
    return code[first : first + LAGS, here]


def tails_of(sent, arrived, here):
    zeros = jnp.zeros((LANES - LAGS, here.stop - here.start), jnp.bfloat16)
    return jnp.concatenate([tail_of(arrived, here), zeros, tail_of(sent, here), zeros], axis=0)


def first_products_kernel(held, power, own, other, keep, send, shifted):
    lag_rows(own, other, own_group(3), shifted)
    ours, theirs = [
        jnp.sum(jnp.square(refs[...].astype(jnp.float32)), axis=1, keepdims=True) for refs in (own, other)
    ]
    refs = jnp.where(
        lax.axis_index("chan") == 0,
        jnp.concatenate([ours, theirs], axis=0),
        jnp.concatenate([theirs, ours], axis=0),
    )
    bound = rounded_up(power[...])
    pad = jnp.zeros((1, LANES - REF), jnp.float32)
    chunk = keep.shape[0]
    refs_row = jnp.concatenate([as_row(refs), pad], axis=1)
    send[chunk:] = packed(power[...], refs_row, bound, last_samples(own, other))
    for here in columns(held.shape[1]):
        product = product_of(shifted, held, here)
        keep[:, here] = product[:chunk]
        send[:chunk, here] = coded(product[chunk:], bound[:, here], refs)


def shifted_scratch(rows, groups=1):
    return [pltpu.VMEM((groups * GROUP * REF, rows), jnp.bfloat16)]


def first_products(held, power, own, other, chunk):
    rows, width = held.shape
    return call_on_blocks(
        first_products_kernel,
        [((chunk, width), jnp.float32), ((chunk + EXTRA, width), jnp.bfloat16)],
        held,
        power,
        own,
        other,
        name="first_products",
        micros=PRODUCT_MICROS,
        scratch=shifted_scratch(rows),
    )


def later_products(groups, held, own, other, powers, chunk, spare=0, after=()):
    rows, width = held.shape

    def kernel(held, own, other, powers, *rest):
        outs, shifted = rest[:-1], rest[-1]
        _, ref_powers, bound = sent_powers(powers)
        refs = ref_column(ref_powers)
        for index, bits in enumerate(groups):
            lag_rows(own, other, own_group(bits), shifted.at[pl.ds(index * 2 * chunk, 2 * chunk)])
            if spare and index == 0:
                outs[1][chunk:] = jnp.zeros((spare, width), jnp.bfloat16)
        for here in columns(width):
            product = product_of(shifted, held, here)
            for index in range(len(groups)):
                keep, send = outs[2 * index : 2 * index + 2]
                first = 2 * index * chunk
                keep[:, here] = product[first : first + chunk]
                send[:chunk, here] = coded(product[first + chunk : first + 2 * chunk], bound[:, here], refs)

    return call_on_blocks(
        kernel,
        [
            (shape, dtype)
            for index in range(len(groups))
            for shape, dtype in (
                ((chunk, width), jnp.float32),
                ((chunk + (0 if index else spare), width), jnp.bfloat16),
            )
        ],
        held,
        own,
        other,
        powers,
        name="later_products",
        micros=PRODUCT_MICROS,
        after=after,
        scratch=shifted_scratch(rows, len(groups)),
    )


def edges_scratch(count, chunk):
    return [pltpu.VMEM((count, chunk, 2 * LANES), jnp.bfloat16)]


def call_on_blocks(kernel, outs, *arrays, name, micros, after=(), scratch=(), space=pltpu.VMEM):
    vmem = pl.BlockSpec(memory_space=pltpu.VMEM)
    count = len(arrays)

    def body(*refs):
        kernel(*refs[:count], *refs[count + len(after) :])

    return pl.pallas_call(
        body,
        in_specs=[vmem] * count + [pl.BlockSpec(memory_space=pl.ANY)] * len(after),
        out_specs=[vmem] * len(outs),
        out_shape=[space(shape, dtype) for shape, dtype in outs],
        scratch_shapes=list(scratch),
        compiler_params=pltpu.CompilerParams(vmem_limit_bytes=VMEM_BYTES),
        cost_estimate=lasting(micros),
        name=name,
    )(*arrays, *after)


def with_tails(head, after_next, send):
    rows, width = send.shape
    chunk = rows - EXTRA

    def kernel(head, after_next, send, out):
        near = lax.axis_index("tm") & 1
        out[:chunk] = send[:chunk]
        out[chunk : chunk + LAGS] = jnp.where(near == 0, after_next[...], head[...])
        out[chunk + LAGS :] = send[chunk:]

    outs = [((rows + LAGS, width), jnp.bfloat16)]
    return call_on_blocks(kernel, outs, head, after_next, send, name="with_tails", micros=MERGE_MICROS)[0]


def with_boundaries(keeps, groups, own, other, sent, arrived, after):
    chunk, width = keeps[0].shape

    def kernel(own, other, sent, arrived, *rest):
        keeps, outs, edges = rest[: len(groups)], rest[len(groups) : -1], rest[-1]
        for index, bits in enumerate(groups):
            boundary_rows(own_group(bits), (own, other), ends_of(arrived), edges.at[index])
        for here in columns(width):
            tails = tails_of(sent, arrived, here)
            for index in range(len(groups)):
                added = jnp.dot(edges[index], tails, preferred_element_type=jnp.float32)
                outs[index][:, here] = keeps[index][:, here] + added

    return call_on_blocks(
        kernel,
        [((chunk, width), jnp.float32)] * len(groups),
        own,
        other,
        sent,
        arrived,
        *keeps,
        name="with_boundaries",
        micros=MERGE_MICROS,
        after=after,
        scratch=edges_scratch(len(groups), chunk),
    )


def merged_near(keep, group, own, other, ours, theirs, held_back):
    chunk, width = keep.shape

    def kernel(keep, own, other, ours, theirs, held_back, out, passed, edges):
        passed[...] = held_back[...]
        boundary_rows(own_group(group), (own, other), ends_of(theirs), edges.at[0])
        powers, refs, bound = sent_powers(ours)
        their_powers, their_refs, their_bound = sent_powers(theirs)
        their_refs_column, sum_refs = ref_column(their_refs), refs + their_refs
        sum_refs_column = ref_column(sum_refs)
        bounds = []
        for here in columns(width):
            tails = tails_of(ours, theirs, here)
            total = keep[:, here] + jnp.dot(edges[0], tails, preferred_element_type=jnp.float32)
            total += expanded(theirs[:chunk, here], their_bound[:, here], their_refs_column)
            beyond = jnp.sum(jnp.square(tails.astype(jnp.float32)), axis=0, keepdims=True)
            bounds.append(rounded_up(bound[:, here] + their_bound[:, here] + beyond))
            out[:chunk, here] = coded(total, bounds[-1], sum_refs_column)
        out[chunk:] = packed(powers + their_powers, sum_refs, jnp.concatenate(bounds, axis=1))

    return call_on_blocks(
        kernel,
        [((chunk + EXTRA, width), jnp.bfloat16), (held_back.shape, jnp.bfloat16)],
        keep,
        own,
        other,
        ours,
        theirs,
        held_back,
        name="merged_near",
        micros=MERGE_MICROS,
        scratch=edges_scratch(1, chunk),
    )


def direct_sums(direct, powers):
    _, refs, bound = sent_powers(powers)
    chunk = direct.shape[0] // REF * REF
    return expanded(direct[:chunk], bound, ref_column(refs))


def merged(keep, ours, theirs, direct, direct_powers, after):
    chunk, width = keep.shape

    def kernel(keep, ours, theirs, direct, direct_powers, out):
        powers, refs, bound = sent_powers(ours)
        their_powers, their_refs, their_bound = sent_powers(theirs)
        sum_refs, sum_bound = refs + their_refs, rounded_up(bound + their_bound)
        total = keep[...] + expanded(theirs[:chunk], their_bound, ref_column(their_refs))
        total += direct_sums(direct, direct_powers)
        out[chunk:] = packed(powers + their_powers, sum_refs, sum_bound)
        out[:chunk] = coded(total, sum_bound, ref_column(sum_refs))

    outs = [((chunk + EXTRA, width), jnp.bfloat16)]
    arrays = (keep, ours, theirs, direct, direct_powers)
    return call_on_blocks(kernel, outs, *arrays, name="merged", micros=MERGE_MICROS, after=after)[0]


def resent(keep, direct, direct_powers, ours, held_back, after):
    def kernel(keep, direct, direct_powers, ours, held_back, out, passed):
        passed[...] = held_back[...]
        _, refs, bound = sent_powers(ours)
        out[...] = coded(keep[...] + direct_sums(direct, direct_powers), bound, ref_column(refs))

    outs = [(keep.shape, jnp.bfloat16), (held_back.shape, jnp.bfloat16)]
    arrays = (keep, direct, direct_powers, ours, held_back)
    return call_on_blocks(kernel, outs, *arrays, name="resent", micros=MERGE_MICROS, after=after)


def added(keep, direct, direct_powers, after):
    def kernel(keep, direct, direct_powers, out):
        out[...] = keep[...] + direct_sums(direct, direct_powers)

    outs = [(keep.shape, jnp.float32)]
    arrays = (keep, direct, direct_powers)
    return call_on_blocks(kernel, outs, *arrays, name="added", micros=MERGE_MICROS, after=after)[0]


def finished(slab_rows, segment, partial, near, near_powers, ours, theirs, autos):
    chunk, width = partial.shape

    def kernel(partial, near, near_powers, ours, theirs, *refs):
        autos, (covariance, segment_auto) = refs[:-2], refs[-2:]
        first_lag = lax.axis_index("tm").astype(jnp.int32) * (chunk // REF)
        lag = lax.broadcasted_iota(jnp.int32, (chunk, 1), 0) // REF + first_lag
        denom = (slab_rows - lag).astype(jnp.float32)
        powers, own_refs, _ = sent_powers(ours)
        their_powers, their_refs, their_bound = sent_powers(theirs)
        total = partial[...] + direct_sums(near, near_powers)
        total += expanded(theirs[:chunk], their_bound, ref_column(their_refs))
        scale = 1.0 / jnp.sqrt((powers + their_powers) / slab_rows + 1e-06)
        ref_scale = 1.0 / jnp.sqrt(ref_column(own_refs + their_refs) / slab_rows + 1e-06)
        covariance[...] = total * scale * (for_chunk(ref_scale, chunk) / denom)
        first = 0
        for auto in autos:
            here = slice(first, first + auto.shape[1])
            segment_auto[:, here] = auto[...] * (scale[:, here] * scale[:, here]) / segment
            first = here.stop

    outs = [(partial.shape, jnp.float32), ((LAGS, width), jnp.float32)]
    return call_on_blocks(
        kernel,
        outs,
        partial,
        near,
        near_powers,
        ours,
        theirs,
        *autos,
        name="finished",
        micros=MERGE_MICROS,
        space=jax.ShapeDtypeStruct,
    )


def segment_kernel(first, held, power, tail, out, wide):
    rows = held.shape[0]
    step = rows // 8
    pitch = step + LAGS
    for index in range(out.shape[1] // LANES):
        here = slice(first + index * LANES, first + (index + 1) * LANES)
        there = slice(index * LANES, (index + 1) * LANES)
        for part in range(8):
            end = (part + 1) * step
            wide[part * pitch : part * pitch + step, :] = held[end - step : end, here].astype(jnp.float32)
            if part < 7:
                following = held[end : end + LAGS, here].astype(jnp.float32)
            else:
                following = tail_of(tail, here).astype(jnp.float32)
            wide[part * pitch + step : (part + 1) * pitch, :] = following
        taken = lambda first: wide[pl.ds(first, 8, stride=pitch), :]

        def advance(index, carry):
            window, sums = carry
            window = window + (taken(index + LAGS - 1),)
            sums = tuple(total + window[0] * window[lag + 1] for lag, total in enumerate(sums))
            return window[1:], sums

        window = tuple(taken(first) for first in range(LAGS - 1))
        zero = jnp.zeros((8, LANES), jnp.float32)
        _, sums = lax.fori_loop(0, step, advance, (window, (zero,) * (LAGS - 1)), unroll=16)
        out[:, there] = jnp.concatenate(
            [power[:, here]] + [jnp.sum(total, axis=0, keepdims=True) for total in sums], axis=0
        )


def segment_rows(held, power, tail, first, size, held_back=(), after=()):
    rows = held.shape[0]

    def kernel(held, power, tail, *refs):
        codes, out, passed, wide = refs[: len(held_back)], refs[len(held_back)], refs[len(held_back) + 1 : -1], refs[-1]
        for code, to in zip(codes, passed):
            to[...] = code[...]
        segment_kernel(first, held, power, tail, out, wide)

    return call_on_blocks(
        kernel,
        [((LAGS, size), jnp.float32)] + [(code.shape, code.dtype) for code in held_back],
        held,
        power,
        tail,
        *held_back,
        name="segment_rows",
        micros=SEGMENT_MICROS,
        after=after,
        scratch=[pltpu.VMEM((rows + 8 * LAGS, LANES), jnp.float32)],
    )


def all_products_kernel(held, own, other, tail, out, shifted):
    chan = lax.axis_index("chan")
    zeros = jnp.zeros((HALF, LANES), jnp.float32)
    for refs, half in ((own, chan), (other, 1 - chan)):
        long = jnp.concatenate([refs[...].astype(jnp.float32), zeros], axis=1)
        for index in range(GROUP):
            start = pl.multiple_of(index * REF + half * HALF, HALF)
            lag = pl.program_id(0) * GROUP + index
            shifted[pl.ds(start, HALF), :] = pltpu.roll(long, lag, 1).astype(jnp.bfloat16)
    rows, width = held.shape
    edge = jnp.concatenate([tail[...], jnp.zeros((LANES - LAGS, width), tail.dtype)], axis=0)
    for here in columns(width):
        total = jnp.dot(shifted[:, rows:], edge[:, here], preferred_element_type=jnp.float32)
        out[:, here] = total + jnp.dot(shifted[:, :rows], held[:, here], preferred_element_type=jnp.float32)


def all_products(held, own, other, tail):
    rows, width = held.shape
    vmem = pl.BlockSpec(memory_space=pltpu.VMEM)
    return pl.pallas_call(
        all_products_kernel,
        grid=(LAGS // GROUP,),
        in_specs=[vmem] * 4,
        out_specs=pl.BlockSpec((GROUP * REF, width), lambda group: (group, 0)),
        out_shape=jax.ShapeDtypeStruct((LAGS * REF, width), jnp.float32),
        scratch_shapes=[pltpu.VMEM((GROUP * REF, rows + LANES), jnp.bfloat16)],
        compiler_params=pltpu.CompilerParams(vmem_limit_bytes=VMEM_BYTES),
        name="all_products",
    )(held, own, other, tail)


def from_pair_ahead(value):
    count = lax.axis_size("tm")
    return lax.ppermute(value, "tm", [(time + 2, time) for time in range(0, count - 2, 2)])


def local(strain):
    rows, width = strain.shape
    count = lax.axis_size("tm")
    slab_rows = rows * count
    chunk = LAGS * REF // count

    own, head = prepared(strain)
    other = exchanged(own, "chan", 1)
    held, power = loaded(strain, own)
    if chunk * 2 == GROUP * REF:
        keep6, send7 = first_products(held, power, own, other, chunk)
        after_next = from_pair_ahead(head)
        send7 = with_tails(head, after_next, send7)
        got7 = exchanged(send7, "tm", 1)
        keep4, send5, keep2, send3, keep0, send1 = later_products(
            (2, 1, 0), held, own, other, send7, chunk, spare=LAGS
        )
        got5 = exchanged(send5, "tm", 1)
        send6, send3 = merged_near(keep6, 3, own, other, send7, got7, send3)
        got6 = exchanged(send6, "tm", 2)
        got3 = exchanged(send3, "tm", 1)
        keep4, keep2, keep0 = with_boundaries(
            (keep4, keep2, keep0), (2, 1, 0), own, other, send7, got7, after=(send6,)
        )
        size = width // 4
        (auto,) = segment_rows(held, power, got7, 0, size, after=(keep4,))
        send4 = merged(keep4, send6, got6, got5, got7, after=(auto,))
        got4 = exchanged(send4, "tm", 4)
        send2, send1 = resent(keep2, got3, got7, send6, send1, after=(send4,))
        got2 = exchanged(send2, "tm", 2)
        got1 = exchanged(send1, "tm", 1)
        autos = [auto, *segment_rows(held, power, got7, size, width - size, after=(send2,))]
        partial = added(keep0, got2, got6, after=(autos[1],))
        return tuple(finished(slab_rows, rows, partial, got1, got7, send4, got4, autos))

    tail = passed_along(head, "tm", -1)
    chan = lax.axis_index("chan").astype(jnp.int32)
    time = lax.axis_index("tm").astype(jnp.int32)
    (auto,) = segment_rows(held, power, tail, 0, width)
    power_other = jnp.sum(jnp.square(other.astype(jnp.float32)), axis=1)
    power = lax.psum(jnp.concatenate([power[0], power_other]), "tm")
    inv = 1.0 / jnp.sqrt(power / slab_rows + 1e-06)
    scale = inv[:width]
    ref_scale = jnp.where(
        chan == 0,
        jnp.concatenate([inv[:HALF], inv[width:]]),
        jnp.concatenate([inv[width:], inv[:HALF]]),
    )
    products = all_products(held, own, other, tail)
    summed = lax.psum_scatter(products, "tm", scatter_dimension=0, tiled=True)
    row = time * chunk + jnp.arange(chunk, dtype=jnp.int32)
    row_scale = ref_scale[row % REF] / (slab_rows - row // REF).astype(jnp.float32)
    covariance = summed * scale[None, :] * row_scale[:, None]
    segment_auto = auto * (scale * scale)[None, :] / rows
    return (covariance, segment_auto)


def solution(mesh):
    in_specs = (P(("groups", "tm"), "chan"),)
    out_specs = (P(("groups", "tm"), "chan"), P(("groups", "tm"), "chan"))
    return jax.shard_map(local, mesh=mesh, in_specs=in_specs, out_specs=out_specs, check_vma=False)
```
